128 devices in a mesh: dp: 2 (over z_hi), latent: 64 (over z_lo, x, y, core).
Axes of the slice: x: 4, y: 4, z: 4 (z_hi: 2, z_lo: 2; z = z_hi * 2 + z_lo), core: 2. Of those that a mesh axis runs over, the one named last changes fastest.
Arguments:
- inputs: bfloat16 [1152, 4096], P('dp', 'latent'), may hold values from -36 to 36
- dictionary: float32 [16384, 4096], P('latent')
- offset: float32 [16384], P('latent'), may hold values from -3 to 3
- center: float32 [4096], P('latent'), may hold values from -3 to 3
- dict_mean: float32 [16384, 4096], P('latent'), may hold values from -0.12 to 0.12
- dict_var: float32 [16384, 4096], P('latent'), may hold values from 1e-05 to 0.001
- offset_mean: float32 [16384], P('latent'), may hold values from -0.12 to 0.12
- offset_var: float32 [16384], P('latent'), may hold values from 0.01 to 1000
- center_mean: float32 [4096], P('latent'), may hold values from -250 to 250
- center_var: float32 [4096], P('latent'), may hold values from 0.1 to 10000
Outputs:
- fresh_dict: float32 [16384, 4096], P('latent')
- fresh_offset: float32 [16384], P('latent')
- fresh_center: float32 [4096], P('latent')
- mean_dict: float32 [16384, 4096], P('latent')
- var_dict: float32 [16384, 4096], P('latent')
- mean_offset: float32 [16384], P('latent')
- var_offset: float32 [16384], P('latent')
- mean_center: float32 [4096], P('latent')
- var_center: float32 [4096], P('latent')
- loss_value: float32 [], replicated
The draws below stay inside these ranges and needn't reach their ends.
All inputs are finite; a program needn't handle non-finite values.
Results may differ from the reference program's by a relative error of at most 0.0064.
Values may be sent and summed in bfloat16 or wider, within the bound.
A program may use at most 128 MiB of HBM per device.

```python
import math
import jax
import jax.numpy as jnp
from jax import lax

D = 4096
STEP = 1000
LATENTS = 16384
TOKENS = 1152


def rising_factors(key, count):
    place = jnp.arange(count, dtype=jnp.float32) / count
    jitter = jax.random.uniform(key, (count,), jnp.float32, 0.0, math.log(2.0))
    return 0.5 * jnp.exp(math.log(3.0) * place + jitter)


def draw_inputs(key, part):
    key = jax.random.fold_in(key, 11)
    keys = jax.random.split(key, 3)
    row_factor = rising_factors(keys[1], TOKENS)
    col_factor = rising_factors(keys[2], D)
    base = jnp.clip(jax.random.normal(keys[0], (TOKENS, D), jnp.float32), -4.0, 4.0)
    return (base * row_factor[:, None] * col_factor[None, :]).astype(jnp.bfloat16)


def draw_dictionary(key, part):
    key = jax.random.fold_in(key, 23)
    keys = jax.random.split(key, 2)
    row_factor = rising_factors(keys[1], LATENTS)
    base = jnp.clip(jax.random.normal(keys[0], (LATENTS, D), jnp.float32), -4.0, 4.0)
    return base * row_factor[:, None] * (1.0 / math.sqrt(D))


def shard_levels(key, extent, cuts, low, high):
    def one(position, parts):
        steps = jax.random.uniform(jax.random.fold_in(jax.random.fold_in(key, 6), position), (parts,), jnp.float32, low / len(cuts), high / len(cuts))
        return jnp.repeat(jnp.exp(steps), extent[position] // parts).reshape((-1,) + (1,) * (len(extent) - position - 1))

    level = one(*cuts[0])
    for cut in cuts[1:]:
        level = level * one(*cut)
    return level


def scatter_about(rng, dims, scale, limit, cuts=(), kind=jnp.bfloat16):
    level = shard_levels(rng, dims, cuts, -0.22, 0.18) if cuts else 1.0
    array = jax.random.normal(rng, dims, jnp.float32) * scale * level
    return jnp.minimum(jnp.maximum(array, -limit), limit).astype(kind)


def setup_inputs(seed: int = 0) -> dict:
    streams_of = jax.random.split(jax.random.key(seed), 11)
    return {
        "inputs": draw_inputs(jax.random.fold_in(streams_of[10], 71), 0),
        "dictionary": draw_dictionary(jax.random.fold_in(streams_of[10], 71), 0),
        "offset": scatter_about(streams_of[2], (LATENTS,), 0.5, 3.0, ((0, 64),), jnp.float32),
        "center": scatter_about(streams_of[3], (D,), 0.5, 3.0, ((0, 64),), jnp.float32),
        "dict_mean": scatter_about(streams_of[4], (LATENTS, D), 0.02, 0.12, ((0, 64),), jnp.float32),
        "dict_var": jnp.clip(jnp.exp(math.log(0.001) - 4.6051703 * jax.random.uniform(streams_of[5], (LATENTS, D), jnp.float32) ** shard_levels(streams_of[5], (LATENTS, D), ((0, 64),), -0.2, 0.2)), 9.999999747378752e-06, 0.001),
        "offset_mean": scatter_about(streams_of[6], (LATENTS,), 0.02, 0.12, ((0, 64),), jnp.float32),
        "offset_var": jnp.clip(jnp.exp(math.log(1000.0) - 11.512925 * jax.random.uniform(streams_of[7], (LATENTS,), jnp.float32) ** shard_levels(streams_of[7], (LATENTS,), ((0, 64),), -0.2, 0.2)), 0.01, 1000.0),
        "center_mean": scatter_about(streams_of[8], (D,), 50.0, 250.0, ((0, 64),), jnp.float32),
        "center_var": jnp.clip(jnp.exp(math.log(10000.0) - 11.512925 * jax.random.uniform(streams_of[9], (D,), jnp.float32) ** shard_levels(streams_of[9], (D,), ((0, 64),), -0.2, 0.2)), 0.1, 10000.0),
    }


sparsity_coeff = 5.0
beta_one = 0.9
beta_two = 0.999
learn_rate = 0.001
adam_eps = 1e-08
norm_eps = 1e-06

def adam_update(param, grad, mean, var):
    mean_new = beta_one * mean + (1.0 - beta_one) * grad
    var_new = beta_two * var + (1.0 - beta_two) * grad * grad
    corr_one = 1.0 - beta_one ** STEP
    corr_two = 1.0 - beta_two ** STEP
    param_new = param - learn_rate * (mean_new / corr_one) / (jnp.sqrt(var_new / corr_two) + adam_eps)
    return (param_new, mean_new, var_new)

def reference(inputs, dictionary, offset, center, dict_mean, dict_var, offset_mean, offset_var, center_mean, center_var):
    weights = dictionary.astype(jnp.bfloat16)
    centered = (inputs.astype(jnp.float32) - center).astype(jnp.bfloat16)
    pre = jnp.dot(centered, weights.T, preferred_element_type=jnp.float32) + offset
    acts = jnp.maximum(pre, 0.0).astype(jnp.bfloat16)
    norms = jnp.sqrt(lax.optimization_barrier(jnp.sum(dictionary * dictionary, axis=1)) + norm_eps)
    recon = jnp.dot(acts, weights, preferred_element_type=jnp.float32)
    err = recon + center - inputs.astype(jnp.float32)
    acts_wide = acts.astype(jnp.float32)
    sq_total = jnp.sum(err * err)
    spars = jnp.sum(acts_wide * norms[None, :])
    loss_value = (sq_total + sparsity_coeff * spars) / (TOKENS * D)
    derr = (2.0 / TOKENS * err).astype(jnp.bfloat16)
    dacts = jnp.dot(derr, weights.T, preferred_element_type=jnp.float32) + sparsity_coeff / TOKENS * norms[None, :]
    dpre = jnp.where(pre > 0, dacts, 0.0).astype(jnp.bfloat16)
    g_offset = lax.optimization_barrier(jnp.sum(dpre.astype(jnp.float32), axis=0))
    g_center = 2.0 / TOKENS * lax.optimization_barrier(jnp.sum(err, axis=0)) - jnp.dot(g_offset, weights.astype(jnp.float32), precision=lax.Precision.HIGHEST)
    act_sums = lax.optimization_barrier(jnp.sum(acts_wide, axis=0))
    g_dict = jnp.dot(dpre.T, centered, preferred_element_type=jnp.float32)
    g_dict = g_dict + jnp.dot(acts.T, derr, preferred_element_type=jnp.float32)
    g_dict = g_dict + sparsity_coeff / TOKENS * act_sums[:, None] * dictionary / norms[:, None]
    fresh_dict, mean_dict, var_dict = adam_update(dictionary, g_dict, dict_mean, dict_var)
    fresh_offset, mean_offset, var_offset = adam_update(offset, g_offset, offset_mean, offset_var)
    fresh_center, mean_center, var_center = adam_update(center, g_center, center_mean, center_var)
    return (fresh_dict, fresh_offset, fresh_center, mean_dict, var_dict, mean_offset, var_offset, mean_center, var_center, loss_value)
```

```python
import jax
import jax.numpy as jnp
from jax import lax
from jax.experimental import pallas as pl
from jax.experimental.pallas import tpu as pltpu
from jax.sharding import PartitionSpec as P

STEP = 1000
sparsity_coeff = 5.0
beta_one = 0.9
beta_two = 0.999
learn_rate = 0.001
adam_eps = 1e-08
norm_eps = 1e-06

TOK = 1152
WIDTH = 4096
ROWS = 288
PART = 96
HALF = 144
LAT = 256
F32 = jnp.float32
BF16 = jnp.bfloat16
MESH = pl.DeviceIdType.MESH


def adam_update(param, grad, mean, var):
    mean_new = beta_one * mean + (1.0 - beta_one) * grad
    var_new = beta_two * var + (1.0 - beta_two) * grad * grad
    corr_one = 1.0 - beta_one**STEP
    corr_two = 1.0 - beta_two**STEP
    param_new = param - learn_rate * (mean_new / corr_one) / (
        jnp.sqrt(var_new / corr_two) + adam_eps
    )
    return (param_new, mean_new, var_new)


def mod4(v):
    return lax.rem(v + 4, 4)


def dot(a, b):
    return jnp.dot(a, b, preferred_element_type=F32)


def dot_nt(a, b):
    return lax.dot_general(a, b, (((1,), (1,)), ((), ())), preferred_element_type=F32)


def kernel(
    inputs_ref, center_ref, offset_ref, dict_ref,
    grad_ref, small_ref,
    stage, weights, gx, ge, pre, dacc, acts, acts_t, dpre_t,
    raw, raw_in, cen, cen_in, sm, sm_in, sums, sums_in,
    part, b0_out, b0_in, a0_out, a0_in, b1_out, b1_in, a1_out, a1_in, z_out, z_in,
    own, g_out, g_in,
    vx, vx_in, vy, vy_in, vz, vz_in, vc, vc_in,
    dict_sem, grad_sem, pair_send, pair_recv,
    gx_send, gx_recv, ge_send, ge_recv, rs_send, rs_recv,
    g_send, g_recv, v_send, v_recv,
):
    h = lax.axis_index("dp")
    i = lax.axis_index("latent")
    core = lax.rem(i, 2)
    y = lax.rem(i // 2, 4)
    x = lax.rem(i // 8, 4)
    zl = i // 32
    z = 2 * h + zl

    def dev(xx, yy, zz, cc):
        return (zz // 2, ((lax.rem(zz, 2) * 4 + xx) * 4 + yy) * 2 + cc)

    def along(axis, step):
        if axis == "x":
            return dev(mod4(x + step), y, z, core)
        if axis == "y":
            return dev(x, mod4(y + step), z, core)
        return dev(x, y, mod4(z + step), core)

    sibling = dev(x, y, z, 1 - core)
    coord = {"x": x, "y": y, "z": z}

    def rcopy(src, dst, ssem, rsem, device):
        return pltpu.make_async_remote_copy(
            src_ref=src, dst_ref=dst, send_sem=ssem, recv_sem=rsem,
            device_id=device, device_id_type=MESH,
        )

    def load(j):
        return pltpu.make_async_copy(
            dict_ref.at[:, pl.ds(512 * j, 512)], stage.at[j], dict_sem.at[j]
        )

    for j in range(8):
        load(j).start()

    barrier = pltpu.get_barrier_semaphore()
    partners = [sibling] + [along(a, s) for a in ("x", "y", "z") for s in (1, 2, 3)]
    for partner in partners:
        pl.semaphore_signal(barrier, inc=1, device_id=partner, device_id_type=MESH)

    lane = lax.broadcasted_iota(jnp.int32, (1, 128), 1)
    mine = (lane // 64) == core
    both = inputs_ref[...].astype(F32)
    both = jnp.where(mine, jnp.concatenate([both, both], axis=1), 0.0)
    raw[...] = both.astype(BF16).reshape(2, ROWS, 128)
    cboth = jnp.concatenate([center_ref[...], center_ref[...]], axis=1)
    cen[...] = jnp.broadcast_to(jnp.where(mine, cboth, 0.0), (8, 128))
    pl.semaphore_wait(barrier, len(partners))

    pair = [
        rcopy(raw.at[1 - core], raw_in, pair_send.at[0], pair_recv.at[0], sibling),
        rcopy(cen, cen_in, pair_send.at[1], pair_recv.at[1], sibling),
    ]
    for c in pair:
        c.start()
    for c in pair:
        c.wait_recv()
    center = cen[0:1, :] + cen_in[0:1, :]
    xin = raw[core].astype(F32) + raw_in[...].astype(F32)
    centered = (xin - center).astype(BF16)

    orders = (("y", "x", "z"), ("x", "z", "y"), ("z", "y", "x"))

    def gather(buf, block, ssem, rsem, between):
        at = [tuple(coord[a] for a in reversed(o)) for o in orders]
        for p in range(3):
            buf[(p,) + at[p]] = block[PART * p : PART * (p + 1)]
        sent = []
        for f in range(3):
            def chunk(p, step):
                q = mod4(coord[orders[p][f]] + step)
                return (p,) + at[p][: 2 - f] + (q,)

            def halves(p, step, k):
                idx = chunk(p, step)
                return idx + ((pl.ds(48 * k, 48),) if f == 0 else (pl.ds(2 * k, 2),))

            def move(p, idx, k, step):
                ref = buf.at[idx]
                return rcopy(ref, ref, ssem.at[p, f, k], rsem.at[p, f, k], along(orders[p][f], step))

            for p in range(3):
                for k, step in ((0, 1), (1, -1)):
                    c = move(p, chunk(p, 0), k, step)
                    c.start()
                    sent.append(c)
            between(f)
            for p in range(3):
                for k, step in ((0, 1), (1, -1)):
                    move(p, chunk(p, -step), k, step).wait_recv()
                    c = move(p, halves(p, -step, k), 2 + k, step)
                    c.start()
                    sent.append(c)
            for p in range(3):
                for k, step in ((0, 1), (1, -1)):
                    move(p, halves(p, 2, k), 2 + k, step).wait_recv()
        return sent

    def weight_copy(j):
        return rcopy(
            weights.at[0, j], weights.at[1, j], pair_send.at[2 + j], pair_recv.at[2 + j], sibling
        )

    small_copy = rcopy(sm, sm_in, pair_send.at[10], pair_recv.at[10], sibling)

    def prepare(f):
        if f != 1:
            return
        sq = jnp.zeros((LAT, 1), F32)
        for j in range(8):
            load(j).wait()
            block = stage[j]
            weights[0, j] = block.astype(BF16)
            weight_copy(j).start()
            sq = sq + jnp.sum(block * block, axis=1, keepdims=True)
        norm = jnp.sqrt(sq + norm_eps)
        sm[...] = jnp.zeros((8, LAT), F32)
        sm[0:1, :] = offset_ref[...]
        sm[1:2, :] = jnp.broadcast_to(norm, (LAT, 128)).T[0:1, :]
        small_copy.start()

    sent = gather(gx, centered, gx_send, gx_recv, prepare)
    for j in range(8):
        weight_copy(j).wait_recv()
    small_copy.wait_recv()

    bias = jnp.concatenate([sm[0:1, :], sm_in[0:1, :]], axis=1)
    norms = jnp.concatenate([sm[1:2, :], sm_in[1:2, :]], axis=1)

    def slab(buf, j):
        jz, jx = j // 4, lax.rem(j, 4)
        rows = []
        for r in range(2):
            zz = 2 * (h if r == 0 else 1 - h) + jz
            for p in range(3):
                cols = []
                for yy in range(4):
                    idx = ((zz, jx, yy), (yy, zz, jx), (jx, yy, zz))[p]
                    cols.append(buf[(p,) + idx])
                rows.append(jnp.concatenate(cols, axis=1))
        return jnp.concatenate(rows, axis=0)

    def all_weights(j):
        return jnp.concatenate([weights[0, j], weights[1, j]], axis=0)

    def project(buf, acc):
        acc[...] = jnp.zeros_like(acc)

        @pl.loop(0, 8)
        def _(j):
            acc[...] += dot_nt(slab(buf, j), all_weights(j))

    project(gx, pre)
    pre[...] = pre[...] + bias
    act = jnp.maximum(pre[...], 0.0).astype(BF16)
    acts[...] = act[:ROWS]
    acts_t[...] = act.T
    act_own = jnp.sum(act[:ROWS].astype(F32), axis=0, keepdims=True)
    act_all = act_own + jnp.sum(act[ROWS:].astype(F32), axis=0, keepdims=True)
    spars = jnp.sum(act_own * norms)

    @pl.loop(0, 8)
    def _(j):
        jz, jx = j // 4, lax.rem(j, 4)
        out = dot(acts[...], all_weights(j))
        for yy in range(4):
            part[0, jx, yy, jz] = out[:HALF, 128 * yy : 128 * (yy + 1)]
            part[1, yy, jx, jz] = out[HALF:, 128 * yy : 128 * (yy + 1)]

    rs_orders = (("x", "y"), ("y", "x"))
    for s in range(2):
        b_out, b_in, a_out, a_in = (
            (b0_out, b0_in, a0_out, a0_in) if s == 0 else (b1_out, b1_in, a1_out, a1_in)
        )
        n = 2 if s == 0 else 1

        def where_of(p, step):
            q = mod4(coord[rs_orders[p][s]] + step)
            return (p, q) if s == 0 else (p, coord[rs_orders[p][0]], q)

        def rs_move(src, dst, p, k, base):
            step = 1 if k == 0 else -1
            e = 4 * s + base + k
            return rcopy(
                src.at[p, k], dst.at[p, k], rs_send.at[p, e], rs_recv.at[p, e],
                along(rs_orders[p][s], step),
            )

        for p in range(2):
            for k in range(2):
                b_out[p, k] = part[where_of(p, 2) + (pl.ds(n * k, n),)].astype(BF16)
                c = rs_move(b_out, b_in, p, k, 0)
                c.start()
                sent.append(c)
        for p in range(2):
            for k in range(2):
                step = 1 if k == 0 else -1
                rs_move(b_out, b_in, p, k, 0).wait_recv()
                here = where_of(p, step)
                far = n * (1 - k)
                a_out[p, k, pl.ds(n * k, n)] = (
                    part[here + (pl.ds(n * k, n),)] + b_in[p, k].astype(F32)
                ).astype(BF16)
                a_out[p, k, pl.ds(far, n)] = part[here + (pl.ds(far, n),)].astype(BF16)
                c = rs_move(a_out, a_in, p, k, 2)
                c.start()
                sent.append(c)
        for p in range(2):
            for k in range(2):
                rs_move(a_out, a_in, p, k, 2).wait_recv()
            here = where_of(p, 0)
            part[here] = part[here] + a_in[p, 0].astype(F32) + a_in[p, 1].astype(F32)

    other_z = dev(x, y, 2 * h + 1 - zl, core)
    recon = []
    for p in range(2):
        z_out[p] = part[p, coord[rs_orders[p][0]], coord[rs_orders[p][1]], 1 - zl].astype(BF16)
        c = rcopy(z_out.at[p], z_in.at[p], rs_send.at[p, 8], rs_recv.at[p, 8], other_z)
        c.start()
        sent.append(c)
    for p in range(2):
        rcopy(z_out.at[p], z_in.at[p], rs_send.at[p, 8], rs_recv.at[p, 8], other_z).wait_recv()
        recon.append(
            part[p, coord[rs_orders[p][0]], coord[rs_orders[p][1]], zl] + z_in[p].astype(F32)
        )

    err = jnp.concatenate(recon, axis=0) + center - (
        raw[core].astype(F32) + raw_in[...].astype(F32)
    )
    sq = jnp.sum(err * err)
    err_sum = jnp.sum(err, axis=0, keepdims=True)
    derr = (2.0 / TOK * err).astype(BF16)

    sent += gather(ge, derr, ge_send, ge_recv, lambda f: None)

    project(ge, dacc)
    dacts = dacc[...] + sparsity_coeff / TOK * norms
    dpre = jnp.where(pre[...] > 0, dacts, 0.0).astype(BF16)
    dpre_t[...] = dpre.T
    off_own = jnp.sum(dpre[:ROWS].astype(F32), axis=0, keepdims=True)
    off_all = off_own + jnp.sum(dpre[ROWS:].astype(F32), axis=0, keepdims=True)

    sums[...] = jnp.zeros((2, 8, LAT), F32)
    for k in range(2):
        sums[k, 0:1, :] = off_all[:, LAT * k : LAT * (k + 1)]
        sums[k, 1:2, :] = act_all[:, LAT * k : LAT * (k + 1)]
    sums_copy = rcopy(sums.at[1], sums_in, pair_send.at[11], pair_recv.at[11], sibling)
    sums_copy.start()

    hi = off_own.astype(BF16)
    rest = off_own - hi.astype(F32)
    mid = rest.astype(BF16)
    low = (rest - mid.astype(F32)).astype(BF16)
    row = lax.broadcasted_iota(jnp.int32, (16, 512), 0)
    terms = jnp.where(
        row == 0, hi.astype(F32),
        jnp.where(row == 1, mid.astype(F32), jnp.where(row == 2, low.astype(F32), 0.0)),
    ).astype(BF16)
    for j in range(8):
        enc = jnp.sum(dot(terms, all_weights(j)), axis=0, keepdims=True)
        for yy in range(4):
            vx[j % 4, (j // 4) * 4 + yy : (j // 4) * 4 + yy + 1, :] = -enc[:, 128 * yy : 128 * (yy + 1)]
    scalars = jnp.where(lane == 0, sq, jnp.where(lane == 1, spars, 0.0))
    for k in range(4):
        vx[k, 8:16, :] = jnp.broadcast_to(scalars, (8, 128))
    sub = lax.broadcasted_iota(jnp.int32, (16, 128), 0)
    vx[x] = vx[x] + jnp.where(sub == zl * 4 + y, 2.0 / TOK * err_sum, 0.0)

    def g_copy(j):
        return rcopy(g_out.at[j], g_in.at[j], g_send.at[j], g_recv.at[j], sibling)

    def gradient(first, last):
        @pl.loop(first, last)
        def _(j):
            xs, es = slab(gx, j), slab(ge, j)
            g_out[j] = (dot(dpre_t[LAT:, :], xs) + dot(acts_t[LAT:, :], es)).astype(BF16)
            g_copy(j).start()
            own[j] = dot(dpre_t[:LAT, :], xs) + dot(acts_t[:LAT, :], es)

    def v_move(src, dst, e, device):
        return rcopy(src, dst, v_send.at[e], v_recv.at[e], device)

    for s in (1, 2, 3):
        c = v_move(vx.at[mod4(x + s)], vx_in.at[s - 1], s - 1, along("x", s))
        c.start()
        sent.append(c)
    gradient(0, 3)
    total = vx[x]
    for s in (1, 2, 3):
        v_move(vx.at[mod4(x + s)], vx_in.at[s - 1], s - 1, along("x", s)).wait_recv()
        total = total + vx_in[s - 1]
    for k in range(4):
        vy[k] = jnp.zeros((8, 128), F32)
        vy[k, 0:1, :] = total[k : k + 1]
        vy[k, 1:2, :] = total[4 + k : 5 + k]
        vy[k, 2:3, :] = total[8:9]
    for s in (1, 2, 3):
        c = v_move(vy.at[mod4(y + s)], vy_in.at[s - 1], 2 + s, along("y", s))
        c.start()
        sent.append(c)
    gradient(3, 5)
    total = vy[y]
    for s in (1, 2, 3):
        v_move(vy.at[mod4(y + s)], vy_in.at[s - 1], 2 + s, along("y", s)).wait_recv()
        total = total + vy_in[s - 1]
    vz[...] = total
    for s in (1, 2, 3):
        c = v_move(vz, vz_in.at[s - 1], 5 + s, along("z", s))
        c.start()
        sent.append(c)
    gradient(5, 7)
    for s in (1, 2, 3):
        v_move(vz, vz_in.at[s - 1], 5 + s, along("z", s)).wait_recv()
        total = total + vz_in[s - 1]
    vc[...] = total
    last = v_move(vc, vc_in, 9, sibling)
    last.start()
    sent.append(last)
    gradient(7, 8)
    last.wait_recv()
    total = vc[...] + vc_in[...]
    sums_copy.wait_recv()

    small_ref[...] = jnp.zeros((8, LAT), F32)
    small_ref[0:2, :] = sums[0, 0:2, :] + sums_in[0:2, :]
    small_ref[2:3, :] = sm[1:2, :]
    small_ref[3:4, 0:128] = jnp.where(zl == 0, total[0:1], total[1:2])
    small_ref[4:5, 0:128] = total[2:3]

    def store(j):
        return pltpu.make_async_copy(
            own.at[j], grad_ref.at[:, pl.ds(512 * j, 512)], grad_sem.at[j]
        )

    for j in range(8):
        g_copy(j).wait_recv()
        own[j] = own[j] + g_in[j].astype(F32)
        store(j).start()
    for j in range(8):
        store(j).wait()
        g_copy(j).wait_send()
        weight_copy(j).wait_send()
    for c in pair + [small_copy, sums_copy] + sent:
        c.wait_send()


def step_kernel(inputs, center, offset, dictionary):
    vm = pltpu.VMEM
    dma = pltpu.SemaphoreType.DMA
    block = (HALF, 128)
    return pl.pallas_call(
        kernel,
        out_shape=(
            jax.ShapeDtypeStruct((LAT, WIDTH), F32),
            jax.ShapeDtypeStruct((8, LAT), F32),
        ),
        in_specs=[pl.BlockSpec(memory_space=pltpu.VMEM)] * 3 + [pl.BlockSpec(memory_space=pl.ANY)],
        out_specs=(pl.BlockSpec(memory_space=pl.ANY), pl.BlockSpec(memory_space=pltpu.VMEM)),
        scratch_shapes=[
            vm((8, LAT, 512), F32),
            vm((2, 8, LAT, 512), BF16),
            vm((3, 4, 4, 4, PART, 128), BF16),
            vm((3, 4, 4, 4, PART, 128), BF16),
            vm((2 * ROWS, 512), F32),
            vm((2 * ROWS, 512), F32),
            vm((ROWS, 512), BF16),
            vm((512, 2 * ROWS), BF16),
            vm((512, 2 * ROWS), BF16),
            vm((2, ROWS, 128), BF16),
            vm((ROWS, 128), BF16),
            vm((8, 128), F32),
            vm((8, 128), F32),
            vm((8, LAT), F32),
            vm((8, LAT), F32),
            vm((2, 8, LAT), F32),
            vm((8, LAT), F32),
            vm((2, 4, 4, 2) + block, F32),
            vm((2, 2, 2, 2) + block, BF16),
            vm((2, 2, 2, 2) + block, BF16),
            vm((2, 2, 4, 2) + block, BF16),
            vm((2, 2, 4, 2) + block, BF16),
            vm((2, 2, 1) + block, BF16),
            vm((2, 2, 1) + block, BF16),
            vm((2, 2, 2) + block, BF16),
            vm((2, 2, 2) + block, BF16),
            vm((2,) + block, BF16),
            vm((2,) + block, BF16),
            vm((8, LAT, 512), F32),
            vm((8, LAT, 512), BF16),
            vm((8, LAT, 512), BF16),
            vm((4, 16, 128), F32),
            vm((3, 16, 128), F32),
            vm((4, 8, 128), F32),
            vm((3, 8, 128), F32),
            vm((8, 128), F32),
            vm((3, 8, 128), F32),
            vm((8, 128), F32),
            vm((8, 128), F32),
            dma((8,)),
            dma((8,)),
            dma((12,)),
            dma((12,)),
            dma((3, 3, 4)),
            dma((3, 3, 4)),
            dma((3, 3, 4)),
            dma((3, 3, 4)),
            dma((2, 9)),
            dma((2, 9)),
            dma((8,)),
            dma((8,)),
            dma((10,)),
            dma((10,)),
        ],
        compiler_params=pltpu.CompilerParams(
            collective_id=0, has_side_effects=True, vmem_limit_bytes=56 * 1024 * 1024
        ),
        name="step",
    )(inputs, center, offset, dictionary)


def body(
    inputs,
    dictionary,
    offset,
    center,
    dict_mean,
    dict_var,
    offset_mean,
    offset_var,
    center_mean,
    center_var,
):
    grad, small = step_kernel(
        inputs, center.reshape(1, -1), offset.reshape(1, -1), dictionary
    )
    g_offset, act_sums, norms = small[0], small[1], small[2]
    core = lax.rem(lax.axis_index("latent"), 2)
    g_center = lax.dynamic_slice(small[3], (core * 64,), (64,))
    sq_total, spars_total = small[4, 0], small[4, 1]
    g_dict = grad + sparsity_coeff / TOK * act_sums[:, None] * dictionary / norms[:, None]
    loss_value = (sq_total + sparsity_coeff * spars_total) / (TOK * WIDTH)
    fresh_dict, mean_dict, var_dict = adam_update(dictionary, g_dict, dict_mean, dict_var)
    fresh_offset, mean_offset, var_offset = adam_update(offset, g_offset, offset_mean, offset_var)
    fresh_center, mean_center, var_center = adam_update(center, g_center, center_mean, center_var)
    return (
        fresh_dict,
        fresh_offset,
        fresh_center,
        mean_dict,
        var_dict,
        mean_offset,
        var_offset,
        mean_center,
        var_center,
        loss_value,
    )


def solution(mesh):
    return jax.shard_map(
        body,
        mesh=mesh,
        in_specs=(
            P("dp", "latent"),
            P("latent", None),
            P("latent"),
            P("latent"),
            P("latent", None),
            P("latent", None),
            P("latent"),
            P("latent"),
            P("latent"),
            P("latent"),
        ),
        out_specs=(
            P("latent", None),
            P("latent"),
            P("latent"),
            P("latent", None),
            P("latent", None),
            P("latent"),
            P("latent"),
            P("latent"),
            P("latent"),
            P(),
        ),
        check_vma=False,
    )
```

```python
import jax
import jax.numpy as jnp
from jax import lax
from jax.experimental import pallas as pl
from jax.experimental.pallas import tpu as pltpu
from jax.sharding import PartitionSpec as P

STEP = 1000
sparsity_coeff = 5.0
beta_one = 0.9
beta_two = 0.999
learn_rate = 0.001
adam_eps = 1e-08
norm_eps = 1e-06

TOK = 1152
WIDTH = 4096
ROWS = 288
CHUNK = 144
PART = 48
LAT = 256
VMEM_LIMIT = 44 * 1024 * 1024
F32 = jnp.float32
BF16 = jnp.bfloat16
MESH = pl.DeviceIdType.MESH


def adam_update(param, grad, mean, var):
    mean_new = beta_one * mean + (1.0 - beta_one) * grad
    var_new = beta_two * var + (1.0 - beta_two) * grad * grad
    corr_one = 1.0 - beta_one**STEP
    corr_two = 1.0 - beta_two**STEP
    param_new = param - learn_rate * (mean_new / corr_one) / (
        jnp.sqrt(var_new / corr_two) + adam_eps
    )
    return (param_new, mean_new, var_new)


def mod4(v):
    return lax.rem(v + 4, 4)


def dot(a, b):
    return jnp.dot(a, b, preferred_element_type=F32)


def dot_nt(a, b):
    return lax.dot_general(a, b, (((1,), (1,)), ((), ())), preferred_element_type=F32)


def kernel(
    inputs_ref, center_ref, offset_ref, dict_ref,
    grad_ref, small_ref,
    weights, gx, ge, pre, dacc, acts, tmat, gacc,
    raw, raw_in, cen, cen_in, sm, sm_in, sums, sums_in,
    part, b0_out, b0_in, a0_out, a0_in, b1_out, b1_in, z_out, z_in,
    side, y_out, y_in, c1_out, c1_in, c2_out, c2_in,
    g_out, g_in,
    vx, vx_in, vy, vy_in, vz, vz_in, vc, vc_in,
    grad_sem, pair_send, pair_recv,
    gx_send, gx_recv, ge_send, ge_recv, rs_send, rs_recv,
    g_send, g_recv, v_send, v_recv,
):
    h = lax.axis_index("dp")
    i = lax.axis_index("latent")
    core = lax.rem(i, 2)
    y = lax.rem(i // 2, 4)
    x = lax.rem(i // 8, 4)
    zl = i // 32
    z = 2 * h + zl

    def dev(xx, yy, zz, cc):
        return (zz // 2, ((lax.rem(zz, 2) * 4 + xx) * 4 + yy) * 2 + cc)

    coord = {"x": x, "y": y, "z": z}
    place = {(a, s): mod4(coord[a] + s) for a in coord for s in range(4)}
    near = {}
    for s in range(1, 4):
        near["x", s] = dev(place["x", s], y, z, core)
        near["y", s] = dev(x, place["y", s], z, core)
        near["z", s] = dev(x, y, place["z", s], core)

    def along(axis, step):
        return near[axis, step % 4]

    sibling = dev(x, y, z, 1 - core)
    other_z = dev(x, y, 2 * h + 1 - zl, core)

    def rcopy(src, dst, ssem, rsem, device):
        return pltpu.make_async_remote_copy(
            src_ref=src, dst_ref=dst, send_sem=ssem, recv_sem=rsem,
            device_id=device, device_id_type=MESH,
        )

    barrier = pltpu.get_barrier_semaphore()
    partners = [sibling] + [along(a, s) for a in ("x", "y", "z") for s in (1, 2, 3)]
    for partner in partners:
        pl.semaphore_signal(barrier, inc=1, device_id=partner, device_id_type=MESH)

    lane = lax.broadcasted_iota(jnp.int32, (1, 128), 1)
    mine = (lane // 64) == core
    both = inputs_ref[...].astype(F32)
    both = jnp.concatenate([both, both], axis=0).T
    raw[...] = jnp.where(mine, both, 0.0).astype(BF16).reshape(2, ROWS, 128)
    cboth = jnp.concatenate([center_ref[...], center_ref[...]], axis=1)
    cen[...] = jnp.broadcast_to(jnp.where(mine, cboth, 0.0), (8, 128))
    pl.semaphore_wait(barrier, len(partners))

    pair = [
        rcopy(raw.at[1 - core], raw_in, pair_send.at[0], pair_recv.at[0], sibling),
        rcopy(cen, cen_in, pair_send.at[1], pair_recv.at[1], sibling),
    ]
    for c in pair:
        c.start()
    for c in pair:
        c.wait_recv()
    center = cen[0:1, :] + cen_in[0:1, :]

    def own_rows(t):
        rows = pl.ds(CHUNK * t, CHUNK)
        return raw[core, rows].astype(F32) + raw_in[rows].astype(F32)

    sent = []

    def flush(log):
        for c in log:
            c.wait_send()
        log.clear()

    orders = (("y", "x", "z"), ("x", "z", "y"), ("z", "y", "x"))
    dirs = ((0, 1), (1, -1))

    def gather(buf, t, block, ssem, rsem, log):
        at = [tuple(coord[a] for a in reversed(o)) for o in orders]
        for p in range(3):
            buf[(t, p) + at[p]] = block[PART * p : PART * (p + 1)]

        def chunk(p, f, step):
            q = place[orders[p][f], step % 4]
            return (t, p) + at[p][: 2 - f] + (q,)

        def move(p, f, idx, k, step):
            ref = buf.at[idx]
            return rcopy(
                ref, ref, ssem.at[t, p, f, k], rsem.at[t, p, f, k], along(orders[p][f], step)
            )

        for f in range(2):
            for p in range(3):
                for k in range(3):
                    c = move(p, f, chunk(p, f, 0), k, k + 1)
                    c.start()
                    log.append(c)
            yield
            for p in range(3):
                for k in range(3):
                    move(p, f, chunk(p, f, -k - 1), k, k + 1).wait_recv()
        for p in range(3):
            for k, step in dirs:
                c = move(p, 2, chunk(p, 2, 0), k, step)
                c.start()
                log.append(c)
        yield
        for p in range(3):
            for k, step in dirs:
                move(p, 2, chunk(p, 2, -step), k, step).wait_recv()
                c = move(p, 2, chunk(p, 2, -step) + (pl.ds(2 * k, 2),), 2 + k, step)
                c.start()
                log.append(c)
        yield
        for p in range(3):
            for k, step in dirs:
                move(p, 2, chunk(p, 2, 2) + (pl.ds(2 * k, 2),), 2 + k, step).wait_recv()

    def weight_copy(j):
        return rcopy(
            weights.at[0, j], weights.at[1, j], pair_send.at[2 + j], pair_recv.at[2 + j], sibling
        )

    small_copy = rcopy(sm, sm_in, pair_send.at[10], pair_recv.at[10], sibling)

    def prepare():
        sq = jnp.zeros((LAT, 1), F32)
        for j in range(8):
            block = dict_ref[:, 512 * j : 512 * (j + 1)]
            weights[0, j] = block.astype(BF16)
            weight_copy(j).start()
            sq = sq + jnp.sum(block * block, axis=1, keepdims=True)
        norm = jnp.sqrt(sq + norm_eps)
        sm[...] = jnp.zeros((8, LAT), F32)
        sm[0:1, :] = offset_ref[...]
        sm[1:2, :] = jnp.broadcast_to(norm, (LAT, 128)).T[0:1, :]
        small_copy.start()

    def slab(buf, t, j):
        jz, jx = j // 4, lax.rem(j, 4)
        rows = []
        for r in range(2):
            zz = 2 * (h if r == 0 else 1 - h) + jz
            for p in range(3):
                cols = []
                for yy in range(4):
                    idx = ((zz, jx, yy), (yy, zz, jx), (jx, yy, zz))[p]
                    cols.append(buf[(t, p) + idx])
                rows.append(jnp.concatenate(cols, axis=1))
        return jnp.concatenate(rows, axis=0)

    def all_weights(j):
        return jnp.concatenate([weights[0, j], weights[1, j]], axis=0)

    def project(buf, t, acc, first, last):
        if first == 0:
            acc[t] = jnp.zeros((2 * CHUNK, 512), F32)

        @pl.loop(first, last, unroll=2)
        def _(j):
            acc[t] += dot_nt(slab(buf, t, j), all_weights(j))

    def ring_first(src, lead, axis, b_out, b_in, sems, log):
        q = place[axis, 2]
        for k, step in dirs:
            b_out[k][...] = src[lead + (q, pl.ds(2 * k, 2))].astype(BF16)
            c = rcopy(b_out[k], b_in[k], sems[0][k], sems[1][k], along(axis, step))
            c.start()
            log.append(c)

    def ring_second(src, lead, axis, b_out, b_in, a_out, a_in, sems, log):
        for k, step in dirs:
            q = place[axis, step % 4]
            mix, rest = pl.ds(2 * k, 2), pl.ds(2 - 2 * k, 2)
            a_out[k][rest] = src[lead + (q, rest)].astype(BF16)
            rcopy(b_out[k], b_in[k], sems[0][k], sems[1][k], along(axis, step)).wait_recv()
            a_out[k][mix] = (src[lead + (q, mix)] + b_in[k][...].astype(F32)).astype(BF16)
            c = rcopy(a_out[k], a_in[k], sems[0][2 + k], sems[1][2 + k], along(axis, step))
            c.start()
            log.append(c)

    def ring_last(src, lead, axis, a_out, a_in, sems):
        for k, step in dirs:
            rcopy(a_out[k], a_in[k], sems[0][2 + k], sems[1][2 + k], along(axis, step)).wait_recv()
        return src[lead + (coord[axis],)] + a_in[0][...].astype(F32) + a_in[1][...].astype(F32)

    def direct_first(value, axis, out, into, sems, log):
        for k in range(3):
            out[k][...] = value(place[axis, k + 1]).astype(BF16)
            c = rcopy(out[k], into[k], sems[0][k], sems[1][k], along(axis, k + 1))
            c.start()
            log.append(c)

    def direct_last(value, axis, out, into, sems):
        for k in range(3):
            rcopy(out[k], into[k], sems[0][k], sems[1][k], along(axis, k + 1)).wait_recv()
        total = value(coord[axis])
        for k in range(3):
            total = total + into[k][...].astype(F32)
        return total

    def scatter(t, log):
        side_axes = ("x", "y") if t == 0 else ("y", "x")
        axes = (("x", "y"), ("y", "x"), side_axes)

        def some(ref, *lead):
            return [ref.at[lead + (k,)] for k in range(ref.shape[len(lead)])]

        def sems(p, s):
            return (
                [rs_send.at[t, p, 4 * s + e] for e in range(4)],
                [rs_recv.at[t, p, 4 * s + e] for e in range(4)],
            )

        def pair_copy(p):
            out, into = (y_out.at[t], y_in.at[t]) if p == 2 else (z_out.at[t, p], z_in.at[t, p])
            return rcopy(out, into, rs_send.at[t, p, 8], rs_recv.at[t, p, 8], other_z)

        y_out[t] = side[t, 1 - zl].astype(BF16)
        pair_copy(2).start()
        ring = [
            (part, (t, p), axes[p][0], some(b0_out, t, p), some(b0_in, t, p), some(a0_out, t, p), some(a0_in, t, p), sems(p, 0))
            for p in range(2)
        ]
        for a in ring:
            ring_first(*a[:5], a[7], log)
        yield
        pair_copy(2).wait_recv()
        side[t, zl] = side[t, zl] + y_in[t].astype(F32)
        wide = (lambda q: side[t, zl, q], axes[2][0], some(c1_out, t), some(c1_in, t), sems(2, 0))
        direct_first(*wide, log)
        for a in ring:
            ring_second(*a, log)
        yield
        here = coord[axes[2][0]]
        side[t, zl, here] = direct_last(*wide)
        thin = (lambda q: side[t, zl, here, q], axes[2][1], some(c2_out, t), some(c2_in, t), sems(2, 1))
        direct_first(*thin, log)
        line = []
        for p in range(2):
            first = coord[axes[p][0]]
            part[t, p, first] = ring_last(*ring[p][:3], *ring[p][5:])
            line.append(
                (lambda q, p=p, first=first: part[t, p, first, q], axes[p][1], some(b1_out, t, p), some(b1_in, t, p), sems(p, 1))
            )
            direct_first(*line[p], log)
        yield
        sums_z = []
        for p in range(2):
            part[t, p, coord[axes[p][0]], coord[axes[p][1]]] = direct_last(*line[p])
            z_out[t, p] = part[t, p, coord[axes[p][0]], coord[axes[p][1]], 1 - zl].astype(BF16)
            pair_copy(p).start()
        last = direct_last(*thin)
        yield
        for p in range(2):
            pair_copy(p).wait_recv()
            sums_z.append(
                part[t, p, coord[axes[p][0]], coord[axes[p][1]], zl] + z_in[t, p].astype(F32)
            )
        log.extend(pair_copy(p) for p in range(3))
        result[t] = jnp.concatenate(sums_z + [last], axis=0)

    result, sq, err_sum, act_own, act_all, off_own, off_all = {}, {}, {}, {}, {}, {}, {}
    shared = {}

    def g_copy(j):
        return rcopy(g_out.at[j], g_in.at[j], g_send.at[j], g_recv.at[j], sibling)

    def gradient(t, first, last):
        @pl.loop(first, last)
        def _(j):
            both = jnp.concatenate([slab(gx, t, j), slab(ge, t, j)], axis=0)
            if t == 0:
                gacc[1, j] = dot(tmat[t, LAT:, :], both)
                gacc[0, j] = dot(tmat[t, :LAT, :], both)
            else:
                g_out[j] = (gacc[1, j] + dot(tmat[t, LAT:, :], both)).astype(BF16)
                g_copy(j).start()
                gacc[0, j] = gacc[0, j] + dot(tmat[t, :LAT, :], both)

    def steps(t):
        centered = (own_rows(t) - center).astype(BF16)
        log_x, log_r, log_e = [], [], []
        yield from gather(gx, t, centered, gx_send, gx_recv, log_x)
        if t == 0:
            for j in range(8):
                weight_copy(j).wait_recv()
            small_copy.wait_recv()
            shared["bias"] = jnp.concatenate([sm[0:1, :], sm_in[0:1, :]], axis=1)
            shared["norms"] = jnp.concatenate([sm[1:2, :], sm_in[1:2, :]], axis=1)
        norms = shared["norms"]
        project(gx, t, pre, 0, 4)
        yield
        project(gx, t, pre, 4, 8)
        yield
        pre[t] = pre[t] + shared["bias"]
        acts[t] = jnp.maximum(pre[t], 0.0).astype(BF16)

        @pl.loop(0, 8, unroll=2)
        def _(j):
            jz, jx = j // 4, lax.rem(j, 4)
            out = dot(acts[t, :CHUNK], all_weights(j))
            for yy in range(4):
                cols = slice(128 * yy, 128 * (yy + 1))
                part[t, 0, jx, yy, jz] = out[:PART, cols]
                part[t, 1, yy, jx, jz] = out[PART : 2 * PART, cols]
                if t == 0:
                    side[t, jz, jx, yy] = out[2 * PART :, cols]
                else:
                    side[t, jz, yy, jx] = out[2 * PART :, cols]

        ready = scatter(t, log_r)
        next(ready)
        flush(log_x)
        yield
        yield from ready
        err = result[t] + center - own_rows(t)
        sq[t] = jnp.sum(err * err)
        err_sum[t] = jnp.sum(err, axis=0, keepdims=True)
        derr = (2.0 / TOK * err).astype(BF16)
        ready = gather(ge, t, derr, ge_send, ge_recv, log_e)
        next(ready)
        flush(log_r)
        yield
        yield from ready
        sent.extend(log_e)
        project(ge, t, dacc, 0, 4)
        yield
        project(ge, t, dacc, 4, 8)
        yield
        dacts = dacc[t] + sparsity_coeff / TOK * norms
        dpre = jnp.where(pre[t] > 0, dacts, 0.0).astype(BF16)
        act = acts[t]
        tmat[t] = jnp.concatenate([dpre, act], axis=0).T
        off_own[t] = jnp.sum(dpre[:CHUNK].astype(F32), axis=0, keepdims=True)
        off_all[t] = off_own[t] + jnp.sum(dpre[CHUNK:].astype(F32), axis=0, keepdims=True)
        act_own[t] = jnp.sum(act[:CHUNK].astype(F32), axis=0, keepdims=True)
        act_all[t] = act_own[t] + jnp.sum(act[CHUNK:].astype(F32), axis=0, keepdims=True)
        yield
        if t == 0:
            gradient(0, 0, 4)
            yield
            gradient(0, 4, 8)
            yield

    run = [steps(0), steps(1)]
    plan = ["01" * 2, "0w0", "1", "00", "1", "01" * 6, "1", "01" * 2, "00", "1", "000", "111"]
    for who in "".join(plan):
        if who == "w":
            prepare()
        else:
            next(run[int(who)])
    for one in run:
        assert next(one, one) is one
    off = off_own[0] + off_own[1]
    offs = off_all[0] + off_all[1]
    act_tot = act_all[0] + act_all[1]
    spars = jnp.sum((act_own[0] + act_own[1]) * shared["norms"])

    sums[...] = jnp.zeros((2, 8, LAT), F32)
    for k in range(2):
        sums[k, 0:1, :] = offs[:, LAT * k : LAT * (k + 1)]
        sums[k, 1:2, :] = act_tot[:, LAT * k : LAT * (k + 1)]
    sums_copy = rcopy(sums.at[1], sums_in, pair_send.at[11], pair_recv.at[11], sibling)
    sums_copy.start()

    hi = off.astype(BF16)
    rest = off - hi.astype(F32)
    mid = rest.astype(BF16)
    low = (rest - mid.astype(F32)).astype(BF16)
    row = lax.broadcasted_iota(jnp.int32, (16, 512), 0)
    terms = jnp.where(
        row == 0, hi.astype(F32),
        jnp.where(row == 1, mid.astype(F32), jnp.where(row == 2, low.astype(F32), 0.0)),
    ).astype(BF16)
    for j in range(8):
        enc = jnp.sum(dot(terms, all_weights(j)), axis=0, keepdims=True)
        for yy in range(4):
            vx[j % 4, (j // 4) * 4 + yy : (j // 4) * 4 + yy + 1, :] = -enc[:, 128 * yy : 128 * (yy + 1)]
    scalars = jnp.where(lane == 0, sq[0] + sq[1], jnp.where(lane == 1, spars, 0.0))
    for k in range(4):
        vx[k, 8:16, :] = jnp.broadcast_to(scalars, (8, 128))
    sub = lax.broadcasted_iota(jnp.int32, (16, 128), 0)
    vx[x] = vx[x] + jnp.where(sub == zl * 4 + y, 2.0 / TOK * (err_sum[0] + err_sum[1]), 0.0)

    def v_move(src, dst, e, device):
        return rcopy(src, dst, v_send.at[e], v_recv.at[e], device)

    for s in (1, 2, 3):
        c = v_move(vx.at[mod4(x + s)], vx_in.at[s - 1], s - 1, along("x", s))
        c.start()
        sent.append(c)
    gradient(1, 0, 3)
    total = vx[x]
    for s in (1, 2, 3):
        v_move(vx.at[mod4(x + s)], vx_in.at[s - 1], s - 1, along("x", s)).wait_recv()
        total = total + vx_in[s - 1]
    for k in range(4):
        vy[k] = jnp.zeros((8, 128), F32)
        vy[k, 0:1, :] = total[k : k + 1]
        vy[k, 1:2, :] = total[4 + k : 5 + k]
        vy[k, 2:3, :] = total[8:9]
    for s in (1, 2, 3):
        c = v_move(vy.at[mod4(y + s)], vy_in.at[s - 1], 2 + s, along("y", s))
        c.start()
        sent.append(c)
    gradient(1, 3, 5)
    total = vy[y]
    for s in (1, 2, 3):
        v_move(vy.at[mod4(y + s)], vy_in.at[s - 1], 2 + s, along("y", s)).wait_recv()
        total = total + vy_in[s - 1]
    vz[...] = total
    for s in (1, 2, 3):
        c = v_move(vz, vz_in.at[s - 1], 5 + s, along("z", s))
        c.start()
        sent.append(c)
    gradient(1, 5, 7)
    for s in (1, 2, 3):
        v_move(vz, vz_in.at[s - 1], 5 + s, along("z", s)).wait_recv()
        total = total + vz_in[s - 1]
    vc[...] = total
    last = v_move(vc, vc_in, 9, sibling)
    last.start()
    sent.append(last)
    gradient(1, 7, 8)
    last.wait_recv()
    total = vc[...] + vc_in[...]
    sums_copy.wait_recv()

    small_ref[...] = jnp.zeros((8, LAT), F32)
    small_ref[0:1, :] = sums[0, 0:1, :] + sums_in[0:1, :]
    small_ref[1:2, :] = sparsity_coeff / TOK * (sums[0, 1:2, :] + sums_in[1:2, :]) / sm[1:2, :]
    slot = jnp.where(zl == 0, total[0:1], total[1:2])
    small_ref[2:3, 0:64] = jnp.where(core == 0, slot[:, :64], slot[:, 64:])
    small_ref[3:4, 0:128] = total[2:3]

    def store(j):
        return pltpu.make_async_copy(
            gacc.at[0, j], grad_ref.at[:, pl.ds(512 * j, 512)], grad_sem.at[j]
        )

    for j in range(8):
        g_copy(j).wait_recv()
        gacc[0, j] = gacc[0, j] + g_in[j].astype(F32)
        store(j).start()
    for j in range(8):
        store(j).wait()
        g_copy(j).wait_send()
        weight_copy(j).wait_send()
    for c in pair + [small_copy, sums_copy] + sent:
        c.wait_send()


def step_kernel(inputs, center, offset, dictionary):
    vm = pltpu.VMEM
    dma = pltpu.SemaphoreType.DMA
    block = (PART, 128)
    return pl.pallas_call(
        kernel,
        out_shape=(
            jax.ShapeDtypeStruct((LAT, WIDTH), F32),
            jax.ShapeDtypeStruct((8, LAT), F32),
        ),
        in_specs=[pl.BlockSpec(memory_space=pltpu.VMEM)] * 4,
        out_specs=(pl.BlockSpec(memory_space=pl.ANY), pl.BlockSpec(memory_space=pltpu.VMEM)),
        scratch_shapes=[
            vm((2, 8, LAT, 512), BF16),
            vm((2, 3, 4, 4, 4) + block, BF16),
            vm((2, 3, 4, 4, 4) + block, BF16),
            vm((2, 2 * CHUNK, 512), F32),
            vm((2, 2 * CHUNK, 512), F32),
            vm((2, 2 * CHUNK, 512), BF16),
            vm((2, 512, 4 * CHUNK), BF16),
            vm((2, 8, LAT, 512), F32),
            vm((2, ROWS, 128), BF16),
            vm((ROWS, 128), BF16),
            vm((8, 128), F32),
            vm((8, 128), F32),
            vm((8, LAT), F32),
            vm((8, LAT), F32),
            vm((2, 8, LAT), F32),
            vm((8, LAT), F32),
            vm((2, 2, 4, 4, 2) + block, F32),
            vm((2, 2, 2, 2, 2) + block, BF16),
            vm((2, 2, 2, 2, 2) + block, BF16),
            vm((2, 2, 2, 4, 2) + block, BF16),
            vm((2, 2, 2, 4, 2) + block, BF16),
            vm((2, 2, 3, 2) + block, BF16),
            vm((2, 2, 3, 2) + block, BF16),
            vm((2, 2) + block, BF16),
            vm((2, 2) + block, BF16),
            vm((2, 2, 4, 4) + block, F32),
            vm((2, 4, 4) + block, BF16),
            vm((2, 4, 4) + block, BF16),
            vm((2, 3, 4) + block, BF16),
            vm((2, 3, 4) + block, BF16),
            vm((2, 3) + block, BF16),
            vm((2, 3) + block, BF16),
            vm((8, LAT, 512), BF16),
            vm((8, LAT, 512), BF16),
            vm((4, 16, 128), F32),
            vm((3, 16, 128), F32),
            vm((4, 8, 128), F32),
            vm((3, 8, 128), F32),
            vm((8, 128), F32),
            vm((3, 8, 128), F32),
            vm((8, 128), F32),
            vm((8, 128), F32),
            dma((8,)),
            dma((12,)),
            dma((12,)),
            dma((2, 3, 3, 4)),
            dma((2, 3, 3, 4)),
            dma((2, 3, 3, 4)),
            dma((2, 3, 3, 4)),
            dma((2, 3, 9)),
            dma((2, 3, 9)),
            dma((8,)),
            dma((8,)),
            dma((10,)),
            dma((10,)),
        ],
        compiler_params=pltpu.CompilerParams(
            collective_id=0, has_side_effects=True, vmem_limit_bytes=VMEM_LIMIT
        ),
        cost_estimate=pl.CostEstimate(
            flops=12 * 2**30, bytes_accessed=160 * 2**20, transcendentals=0
        ),
        name="step",
    )(inputs, center, offset, dictionary)


def small_kernel(small, offset, offset_mean, offset_var, center, center_mean, center_var, *outs):
    rows = (
        (offset, small[0:1, :], offset_mean, offset_var),
        (center, small[2:3, 0:64], center_mean, center_var),
    )
    for k, (param, grad, mean, var) in enumerate(rows):
        new = adam_update(param[...], grad, mean[...], var[...])
        for n in range(3):
            outs[3 * k + n][...] = new[n]
    scalars = small[3:4, 0:128]
    lane = lax.broadcasted_iota(jnp.int32, (1, 128), 1)
    weight = jnp.where(lane == 0, 1.0, jnp.where(lane == 1, sparsity_coeff, 0.0))
    outs[6][...] = jnp.sum(scalars * weight, axis=1, keepdims=True) / (TOK * WIDTH)


def small_step(small, *rows):
    shapes = [(1, LAT)] * 3 + [(1, 64)] * 3 + [(1, 1)]
    return pl.pallas_call(
        small_kernel,
        out_shape=[jax.ShapeDtypeStruct(s, F32) for s in shapes],
        in_specs=[pl.BlockSpec(memory_space=pltpu.VMEM)] * 7,
        out_specs=[pl.BlockSpec(memory_space=pltpu.VMEM)] * 7,
        name="small",
    )(small, *[r.reshape(1, -1) for r in rows])


def body(
    inputs,
    dictionary,
    offset,
    center,
    dict_mean,
    dict_var,
    offset_mean,
    offset_var,
    center_mean,
    center_var,
):
    grad, small = step_kernel(
        inputs.T, center.reshape(1, -1), offset.reshape(1, -1), dictionary
    )
    g_dict = grad + small[1][:, None] * dictionary
    fresh_dict, mean_dict, var_dict = adam_update(dictionary, g_dict, dict_mean, dict_var)
    *rows, loss = small_step(
        small, offset, offset_mean, offset_var, center, center_mean, center_var
    )
    fresh_offset, mean_offset, var_offset, fresh_center, mean_center, var_center = [
        r.reshape(-1) for r in rows
    ]
    loss_value = loss.reshape(())
    return (
        fresh_dict,
        fresh_offset,
        fresh_center,
        mean_dict,
        var_dict,
        mean_offset,
        var_offset,
        mean_center,
        var_center,
        loss_value,
    )


def solution(mesh):
    return jax.shard_map(
        body,
        mesh=mesh,
        in_specs=(
            P("dp", "latent"),
            P("latent", None),
            P("latent"),
            P("latent"),
            P("latent", None),
            P("latent", None),
            P("latent"),
            P("latent"),
            P("latent"),
            P("latent"),
        ),
        out_specs=(
            P("latent", None),
            P("latent"),
            P("latent"),
            P("latent", None),
            P("latent", None),
            P("latent"),
            P("latent"),
            P("latent"),
            P("latent"),
            P(),
        ),
        check_vma=False,
    )
```

```python
import jax
import jax.numpy as jnp
from jax import lax
from jax.experimental import pallas as pl
from jax.experimental.pallas import tpu as pltpu
from jax.sharding import PartitionSpec as P

STEP = 1000
sparsity_coeff = 5.0
beta_one = 0.9
beta_two = 0.999
learn_rate = 0.001
adam_eps = 1e-08
norm_eps = 1e-06

TOK = 1152
WIDTH = 4096
ROWS = 288
CHUNK = 144
PART = 48
LAT = 256
VMEM_LIMIT = 42 * 1024 * 1024
F32 = jnp.float32
BF16 = jnp.bfloat16
MESH = pl.DeviceIdType.MESH


def adam_update(param, grad, mean, var):
    mean_new = beta_one * mean + (1.0 - beta_one) * grad
    var_new = beta_two * var + (1.0 - beta_two) * grad * grad
    corr_one = 1.0 - beta_one**STEP
    corr_two = 1.0 - beta_two**STEP
    param_new = param - learn_rate * (mean_new / corr_one) / (
        jnp.sqrt(var_new / corr_two) + adam_eps
    )
    return (param_new, mean_new, var_new)


def mod4(v):
    return lax.rem(v + 4, 4)


def dot(a, b):
    return jnp.dot(a, b, preferred_element_type=F32)


def dot_nt(a, b):
    return lax.dot_general(a, b, (((1,), (1,)), ((), ())), preferred_element_type=F32)


def kernel(
    inputs_hbm, center_hbm, offset_hbm, dict_ref,
    grad_ref, small_ref,
    inputs_ref, center_ref, offset_ref,
    weights, gx, ge, pre, dacc, acts, tmat, gacc,
    raw, raw_in, cen, cen_in, sm, sm_in, sums, sums_in,
    part, b0_out, b0_in, a0_out, a0_in, z_out, z_in,
    side, y_out, y_in, c1_out, c1_in, c2_out, c2_in,
    g_out, g_in,
    vx, vx_in, vz, vz_in,
    load_sem, pair_send, pair_recv,
    gx_send, gx_recv, ge_send, ge_recv, rs_send, rs_recv,
    g_send, g_recv, v_send, v_recv,
):
    h = lax.axis_index("dp")
    i = lax.axis_index("latent")
    core = lax.rem(i, 2)
    y = lax.rem(i // 2, 4)
    x = lax.rem(i // 8, 4)
    zl = i // 32
    z = 2 * h + zl

    def dev(xx, yy, zz, cc):
        return (zz // 2, ((lax.rem(zz, 2) * 4 + xx) * 4 + yy) * 2 + cc)

    coord = {"x": x, "y": y, "z": z}
    place = {(a, s): mod4(coord[a] + s) for a in coord for s in range(4)}
    near = {}
    for s in range(1, 4):
        near["x", s] = dev(place["x", s], y, z, core)
        near["y", s] = dev(x, place["y", s], z, core)
        near["z", s] = dev(x, y, place["z", s], core)

    def along(axis, step):
        return near[axis, step % 4]

    sibling = dev(x, y, z, 1 - core)
    far_z = 2 * h + 1 - zl
    other_z = dev(x, y, far_z, core)

    def rcopy(src, dst, ssem, rsem, device):
        return pltpu.make_async_remote_copy(
            src_ref=src, dst_ref=dst, send_sem=ssem, recv_sem=rsem,
            device_id=device, device_id_type=MESH,
        )

    def load(j):
        return pltpu.make_async_copy(
            dict_ref.at[:, pl.ds(512 * j, 512)], gacc.at[j], load_sem.at[j]
        )

    first_loads = [
        pltpu.make_async_copy(src, dst, load_sem.at[8 + k])
        for k, (src, dst) in enumerate(
            ((inputs_hbm, inputs_ref), (center_hbm, center_ref), (offset_hbm, offset_ref))
        )
    ]
    for c in first_loads:
        c.start()
    for j in range(8):
        load(j).start()

    plane = [
        dev(place["x", a], place["y", b], z, core) for a in range(4) for b in range(4) if a + b
    ]
    column = [
        dev(x, y, place["z", a], c)
        for a in range(4) for b, c in enumerate((core, 1 - core)) if a + b
    ]
    across = {
        axis: [near[axis, a] for a in range(1, 4)]
        + [
            dev(place["x", a], y, far_z, core) if axis == "x" else dev(x, place["y", a], far_z, core)
            for a in range(4)
        ]
        for axis in ("x", "y")
    }
    barrier = pltpu.get_barrier_semaphore()
    partners = plane + column + across["x"][4:] + across["y"][4:]
    for partner in partners:
        pl.semaphore_signal(barrier, inc=1, device_id=partner, device_id_type=MESH)

    for c in first_loads:
        c.wait()
    lane = lax.broadcasted_iota(jnp.int32, (1, 128), 1)
    mine = (lane // 64) == core
    both = inputs_ref[...].astype(F32)
    both = jnp.concatenate([both, both], axis=0).T
    raw[...] = jnp.where(mine, both, 0.0).astype(BF16).reshape(2, ROWS, 128)
    cboth = jnp.concatenate([center_ref[...], center_ref[...]], axis=1)
    cen[...] = jnp.broadcast_to(jnp.where(mine, cboth, 0.0), (8, 128))
    pl.semaphore_wait(barrier, len(partners))

    pair = [
        rcopy(raw.at[1 - core], raw_in, pair_send.at[0], pair_recv.at[0], sibling),
        rcopy(cen, cen_in, pair_send.at[1], pair_recv.at[1], sibling),
    ]
    for c in pair:
        c.start()
    for c in pair:
        c.wait_recv()
    center = cen[0:1, :] + cen_in[0:1, :]

    def own_rows(t):
        rows = pl.ds(CHUNK * t, CHUNK)
        return raw[core, rows].astype(F32) + raw_in[rows].astype(F32)

    sent = []

    def flush(log):
        for c in log:
            c.wait_send()
        log.clear()

    orders = (("y", "x", "z"), ("x", "z", "y"), ("z", "y", "x"))
    dirs = ((0, 1), (1, -1))

    def gather(buf, t, block, ssem, rsem, log):
        at = [tuple(coord[a] for a in reversed(o)) for o in orders]
        for p in range(3):
            buf[(t, p) + at[p]] = block[PART * p : PART * (p + 1)]

        def chunk(p, f, step):
            q = place[orders[p][f], step % 4]
            return (t, p) + at[p][: 2 - f] + (q,)

        def move(p, f, idx, k, step):
            ref = buf.at[idx]
            return rcopy(
                ref, ref, ssem.at[t, p, f, k], rsem.at[t, p, f, k], along(orders[p][f], step)
            )

        for f in range(2):
            for p in range(3):
                for k in range(3):
                    c = move(p, f, chunk(p, f, 0), k, k + 1)
                    c.start()
                    log.append(c)
            yield
            for p in range(3):
                for k in range(3):
                    move(p, f, chunk(p, f, -k - 1), k, k + 1).wait_recv()
        for p in range(3):
            for k, step in dirs:
                c = move(p, 2, chunk(p, 2, 0), k, step)
                c.start()
                log.append(c)
        yield
        for p in range(3):
            for k, step in dirs:
                move(p, 2, chunk(p, 2, -step), k, step).wait_recv()
                c = move(p, 2, chunk(p, 2, -step) + (pl.ds(2 * k, 2),), 2 + k, step)
                c.start()
                log.append(c)
        yield
        for p in range(3):
            for k, step in dirs:
                move(p, 2, chunk(p, 2, 2) + (pl.ds(2 * k, 2),), 2 + k, step).wait_recv()

    def weight_copy(j):
        return rcopy(
            weights.at[0, j], weights.at[1, j], pair_send.at[2 + j], pair_recv.at[2 + j], sibling
        )

    small_copy = rcopy(sm, sm_in, pair_send.at[10], pair_recv.at[10], sibling)

    def prepare():
        sq = jnp.zeros((LAT, 1), F32)
        for j in range(8):
            load(j).wait()
            block = gacc[j]
            weights[0, j] = block.astype(BF16)
            weight_copy(j).start()
            sq = sq + jnp.sum(block * block, axis=1, keepdims=True)
        norm = jnp.sqrt(sq + norm_eps)
        sm[...] = jnp.zeros((8, LAT), F32)
        sm[0:1, :] = offset_ref[...]
        sm[1:2, :] = jnp.broadcast_to(norm, (LAT, 128)).T[0:1, :]
        small_copy.start()

    def slab(buf, t, j):
        jz, jx = j // 4, lax.rem(j, 4)
        rows = []
        for r in range(2):
            zz = 2 * (h if r == 0 else 1 - h) + jz
            for p in range(3):
                cols = []
                for yy in range(4):
                    idx = ((zz, jx, yy), (yy, zz, jx), (jx, yy, zz))[p]
                    cols.append(buf[(t, p) + idx])
                rows.append(jnp.concatenate(cols, axis=1))
        return jnp.concatenate(rows, axis=0)

    def all_weights(j):
        return jnp.concatenate([weights[0, j], weights[1, j]], axis=0)

    def project(buf, t, acc, first, last):
        if first == 0:
            acc[t] = jnp.zeros((2 * CHUNK, 512), F32)

        @pl.loop(first, last, unroll=2)
        def _(j):
            acc[t] += dot_nt(slab(buf, t, j), all_weights(j))

    def ring_first(src, lead, axis, b_out, b_in, sems, log):
        q = place[axis, 2]
        for k, step in dirs:
            b_out[k][...] = src[lead + (q, pl.ds(2 * k, 2))].astype(BF16)
            c = rcopy(b_out[k], b_in[k], sems[0][k], sems[1][k], along(axis, step))
            c.start()
            log.append(c)

    def ring_second(src, lead, axis, b_out, b_in, a_out, a_in, sems, log):
        for k, step in dirs:
            q = place[axis, step % 4]
            mix, rest = pl.ds(2 * k, 2), pl.ds(2 - 2 * k, 2)
            a_out[k][rest] = src[lead + (q, rest)].astype(BF16)
            rcopy(b_out[k], b_in[k], sems[0][k], sems[1][k], along(axis, step)).wait_recv()
            a_out[k][mix] = (src[lead + (q, mix)] + b_in[k][...].astype(F32)).astype(BF16)
            c = rcopy(a_out[k], a_in[k], sems[0][2 + k], sems[1][2 + k], along(axis, step))
            c.start()
            log.append(c)

    def ring_last(src, lead, axis, a_out, a_in, sems):
        for k, step in dirs:
            rcopy(a_out[k], a_in[k], sems[0][2 + k], sems[1][2 + k], along(axis, step)).wait_recv()
        return src[lead + (coord[axis],)] + a_in[0][...].astype(F32) + a_in[1][...].astype(F32)

    def direct_first(value, axis, out, into, sems, log):
        for k in range(3):
            out[k][...] = value(place[axis, k + 1]).astype(BF16)
            c = rcopy(out[k], into[k], sems[0][k], sems[1][k], along(axis, k + 1))
            c.start()
            log.append(c)

    def direct_last(value, axis, out, into, sems):
        for k in range(3):
            rcopy(out[k], into[k], sems[0][k], sems[1][k], along(axis, k + 1)).wait_recv()
        total = value(coord[axis])
        for k in range(3):
            total = total + into[k][...].astype(F32)
        return total

    def scatter(t, log):
        side_axes = ("x", "y") if t == 0 else ("y", "x")
        axes = (("x", "y"), ("y", "x"), side_axes)

        def some(ref, *lead):
            return [ref.at[lead + (k,)] for k in range(ref.shape[len(lead)])]

        def sems(p, s):
            return (
                [rs_send.at[t, p, 4 * s + e] for e in range(4)],
                [rs_recv.at[t, p, 4 * s + e] for e in range(4)],
            )

        def line_copy(p, e):
            return rcopy(
                z_out.at[t, p, e], z_in.at[t, p, e], rs_send.at[t, p, 4 + e], rs_recv.at[t, p, 4 + e],
                across[axes[p][1]][e],
            )

        pair_copy = rcopy(
            y_out.at[t], y_in.at[t], rs_send.at[t, 2, 10], rs_recv.at[t, 2, 10], other_z
        )
        y_out[t] = side[t, 1 - zl].astype(BF16)
        pair_copy.start()
        ring = [
            (part, (t, p), axes[p][0], some(b0_out, t, p), some(b0_in, t, p), some(a0_out, t, p), some(a0_in, t, p), sems(p, 0))
            for p in range(2)
        ]
        for a in ring:
            ring_first(*a[:5], a[7], log)
        yield
        pair_copy.wait_recv()
        side[t, zl] = side[t, zl] + y_in[t].astype(F32)
        wide = (lambda q: side[t, zl, q], axes[2][0], some(c1_out, t), some(c1_in, t), sems(2, 0))
        direct_first(*wide, log)
        for a in ring:
            ring_second(*a, log)
        yield
        here = coord[axes[2][0]]
        side[t, zl, here] = direct_last(*wide)
        thin = (lambda q: side[t, zl, here, q], axes[2][1], some(c2_out, t), some(c2_in, t), sems(2, 1))
        direct_first(*thin, log)
        for p in range(2):
            first = coord[axes[p][0]]
            part[t, p, first] = ring_last(*ring[p][:3], *ring[p][5:])
            for e in range(7):
                a, w = (e + 1, zl) if e < 3 else (e - 3, 1 - zl)
                z_out[t, p, e] = part[t, p, first, place[axes[p][1], a], w].astype(BF16)
                c = line_copy(p, e)
                c.start()
                log.append(c)
        yield
        out = []
        for p in range(2):
            total = part[t, p, coord[axes[p][0]], coord[axes[p][1]], zl]
            for e in range(7):
                line_copy(p, e).wait_recv()
                total = total + z_in[t, p, e].astype(F32)
            out.append(total)
        out.append(direct_last(*thin))
        log.append(pair_copy)
        result[t] = jnp.concatenate(out, axis=0)

    result, sq, err_sum, act_own, act_all, off_own, off_all = {}, {}, {}, {}, {}, {}, {}
    shared = {}

    def g_copy(j):
        return rcopy(g_out.at[j], g_in.at[j], g_send.at[j], g_recv.at[j], sibling)

    def gradient(t, first, last):
        @pl.loop(first, last)
        def _(j):
            both = jnp.concatenate([slab(gx, t, j), slab(ge, t, j)], axis=0)
            out = dot(tmat[t], both)
            cols = pl.ds(pl.multiple_of(512 * j, 512), 512)
            if t == 0:
                gacc[j] = out[LAT:]
                grad_ref[:, cols] = out[:LAT]
            else:
                g_out[j] = (gacc[j] + out[LAT:]).astype(BF16)
                g_copy(j).start()
                grad_ref[:, cols] = grad_ref[:, cols] + out[:LAT]

    def steps(t):
        centered = (own_rows(t) - center).astype(BF16)
        log_x, log_r, log_e = [], [], []
        yield from gather(gx, t, centered, gx_send, gx_recv, log_x)
        if t == 0:
            for j in range(8):
                weight_copy(j).wait_recv()
            small_copy.wait_recv()
            shared["bias"] = jnp.concatenate([sm[0:1, :], sm_in[0:1, :]], axis=1)
            shared["norms"] = jnp.concatenate([sm[1:2, :], sm_in[1:2, :]], axis=1)
        norms = shared["norms"]
        project(gx, t, pre, 0, 4)
        yield
        project(gx, t, pre, 4, 8)
        yield
        pre[t] = pre[t] + shared["bias"]
        acts[t] = jnp.maximum(pre[t], 0.0).astype(BF16)

        @pl.loop(0, 8, unroll=2)
        def _(j):
            jz, jx = j // 4, lax.rem(j, 4)
            out = dot(acts[t, :CHUNK], all_weights(j))
            for yy in range(4):
                cols = slice(128 * yy, 128 * (yy + 1))
                part[t, 0, jx, yy, jz] = out[:PART, cols]
                part[t, 1, yy, jx, jz] = out[PART : 2 * PART, cols]
                if t == 0:
                    side[t, jz, jx, yy] = out[2 * PART :, cols]
                else:
                    side[t, jz, yy, jx] = out[2 * PART :, cols]

        ready = scatter(t, log_r)
        next(ready)
        flush(log_x)
        yield
        yield from ready
        err = result[t] + center - own_rows(t)
        sq[t] = jnp.sum(err * err)
        err_sum[t] = jnp.sum(err, axis=0, keepdims=True)
        derr = (2.0 / TOK * err).astype(BF16)
        ready = gather(ge, t, derr, ge_send, ge_recv, log_e)
        next(ready)
        flush(log_r)
        yield
        yield from ready
        sent.extend(log_e)
        project(ge, t, dacc, 0, 4)
        yield
        project(ge, t, dacc, 4, 8)
        yield
        dacts = dacc[t] + sparsity_coeff / TOK * norms
        dpre = jnp.where(pre[t] > 0, dacts, 0.0).astype(BF16)
        act = acts[t]
        tmat[t] = jnp.concatenate([dpre, act], axis=0).T
        off_own[t] = jnp.sum(dpre[:CHUNK].astype(F32), axis=0, keepdims=True)
        off_all[t] = off_own[t] + jnp.sum(dpre[CHUNK:].astype(F32), axis=0, keepdims=True)
        act_own[t] = jnp.sum(act[:CHUNK].astype(F32), axis=0, keepdims=True)
        act_all[t] = act_own[t] + jnp.sum(act[CHUNK:].astype(F32), axis=0, keepdims=True)
        yield
        if t == 0:
            gradient(0, 0, 4)
            yield
            gradient(0, 4, 8)
            yield

    run = [steps(0), steps(1)]
    plan = ["01" * 2, "0w0", "1", "00", "1", "01" * 5, "1", "01" * 2, "00", "1", "000", "111"]
    for who in "".join(plan):
        if who == "w":
            prepare()
        else:
            next(run[int(who)])
    for one in run:
        assert next(one, one) is one
    off = off_own[0] + off_own[1]
    offs = off_all[0] + off_all[1]
    act_tot = act_all[0] + act_all[1]
    spars = jnp.sum((act_own[0] + act_own[1]) * shared["norms"])

    sums[...] = jnp.zeros((2, 8, LAT), F32)
    for k in range(2):
        sums[k, 0:1, :] = offs[:, LAT * k : LAT * (k + 1)]
        sums[k, 1:2, :] = act_tot[:, LAT * k : LAT * (k + 1)]
    sums_copy = rcopy(sums.at[1], sums_in, pair_send.at[11], pair_recv.at[11], sibling)
    sums_copy.start()

    hi = off.astype(BF16)
    rest = off - hi.astype(F32)
    mid = rest.astype(BF16)
    low = (rest - mid.astype(F32)).astype(BF16)
    row = lax.broadcasted_iota(jnp.int32, (16, 512), 0)
    terms = jnp.where(
        row == 0, hi.astype(F32),
        jnp.where(row == 1, mid.astype(F32), jnp.where(row == 2, low.astype(F32), 0.0)),
    ).astype(BF16)
    for j in range(8):
        enc = jnp.sum(dot(terms, all_weights(j)), axis=0, keepdims=True)
        for yy in range(4):
            vx[(j % 4) * 4 + yy, j // 4 : j // 4 + 1, :] = -enc[:, 128 * yy : 128 * (yy + 1)]
    scalars = jnp.where(lane == 0, sq[0] + sq[1], jnp.where(lane == 1, spars, 0.0))
    for k in range(16):
        vx[k, 2:8, :] = jnp.broadcast_to(scalars, (6, 128))
    here = x * 4 + y
    sub = lax.broadcasted_iota(jnp.int32, (8, 128), 0)
    vx[here] = vx[here] + jnp.where(sub == zl, 2.0 / TOK * (err_sum[0] + err_sum[1]), 0.0)

    def v_plane(e):
        a, b = (e + 1) // 4, (e + 1) % 4
        return rcopy(
            vx.at[place["x", a] * 4 + place["y", b]], vx_in.at[e], v_send.at[e], v_recv.at[e], plane[e]
        )

    def v_column(e):
        return rcopy(vz, vz_in.at[e], v_send.at[15 + e], v_recv.at[15 + e], column[e])

    for e in range(15):
        v_plane(e).start()
    gradient(1, 0, 4)
    total = vx[here]
    for e in range(15):
        v_plane(e).wait_recv()
        total = total + vx_in[e]
    vz[...] = total
    for e in range(7):
        v_column(e).start()
    gradient(1, 4, 8)
    for e in range(7):
        v_column(e).wait_recv()
        total = total + vz_in[e]
    sums_copy.wait_recv()

    small_ref[...] = jnp.zeros((8, LAT), F32)
    small_ref[0:1, :] = sums[0, 0:1, :] + sums_in[0:1, :]
    small_ref[1:2, :] = sparsity_coeff / TOK * (sums[0, 1:2, :] + sums_in[1:2, :]) / sm[1:2, :]
    slot = jnp.where(zl == 0, total[0:1], total[1:2])
    small_ref[2:3, 0:64] = jnp.where(core == 0, slot[:, :64], slot[:, 64:])
    small_ref[3:4, 0:128] = total[2:3]

    flush(sent)
    for j in range(8):
        weight_copy(j).wait_send()
    for c in pair + [small_copy, sums_copy]:
        c.wait_send()
    for e in range(15):
        v_plane(e).wait_send()
    for e in range(7):
        v_column(e).wait_send()
    for j in range(8):
        cols = slice(512 * j, 512 * (j + 1))
        g_copy(j).wait_recv()
        grad_ref[:, cols] = grad_ref[:, cols] + g_in[j].astype(F32)
    for j in range(8):
        g_copy(j).wait_send()


def step_kernel(inputs, center, offset, dictionary):
    vm = pltpu.VMEM
    dma = pltpu.SemaphoreType.DMA
    block = (PART, 128)
    return pl.pallas_call(
        kernel,
        out_shape=[
            jax.ShapeDtypeStruct((LAT, WIDTH), F32),
            jax.ShapeDtypeStruct((8, LAT), F32),
        ],
        in_specs=[pl.BlockSpec(memory_space=pltpu.HBM)] * 4,
        out_specs=[pl.BlockSpec(memory_space=pltpu.VMEM)] * 2,
        scratch_shapes=[
            vm((64, 2 * ROWS), BF16),
            vm((1, 64), F32),
            vm((1, LAT), F32),
            vm((2, 8, LAT, 512), BF16),
            vm((2, 3, 4, 4, 4) + block, BF16),
            vm((2, 3, 4, 4, 4) + block, BF16),
            vm((2, 2 * CHUNK, 512), F32),
            vm((2, 2 * CHUNK, 512), F32),
            vm((2, 2 * CHUNK, 512), BF16),
            vm((2, 512, 4 * CHUNK), BF16),
            vm((8, LAT, 512), F32),
            vm((2, ROWS, 128), BF16),
            vm((ROWS, 128), BF16),
            vm((8, 128), F32),
            vm((8, 128), F32),
            vm((8, LAT), F32),
            vm((8, LAT), F32),
            vm((2, 8, LAT), F32),
            vm((8, LAT), F32),
            vm((2, 2, 4, 4, 2) + block, F32),
            vm((2, 2, 2, 2, 2) + block, BF16),
            vm((2, 2, 2, 2, 2) + block, BF16),
            vm((2, 2, 2, 4, 2) + block, BF16),
            vm((2, 2, 2, 4, 2) + block, BF16),
            vm((2, 2, 7) + block, BF16),
            vm((2, 2, 7) + block, BF16),
            vm((2, 2, 4, 4) + block, F32),
            vm((2, 4, 4) + block, BF16),
            vm((2, 4, 4) + block, BF16),
            vm((2, 3, 4) + block, BF16),
            vm((2, 3, 4) + block, BF16),
            vm((2, 3) + block, BF16),
            vm((2, 3) + block, BF16),
            vm((8, LAT, 512), BF16),
            vm((8, LAT, 512), BF16),
            vm((16, 8, 128), F32),
            vm((15, 8, 128), F32),
            vm((8, 128), F32),
            vm((7, 8, 128), F32),
            dma((11,)),
            dma((12,)),
            dma((12,)),
            dma((2, 3, 3, 4)),
            dma((2, 3, 3, 4)),
            dma((2, 3, 3, 4)),
            dma((2, 3, 3, 4)),
            dma((2, 3, 11)),
            dma((2, 3, 11)),
            dma((8,)),
            dma((8,)),
            dma((22,)),
            dma((22,)),
        ],
        compiler_params=pltpu.CompilerParams(
            collective_id=0, has_side_effects=True, vmem_limit_bytes=VMEM_LIMIT
        ),
        cost_estimate=pl.CostEstimate(
            flops=12 * 2**30, bytes_accessed=160 * 2**20, transcendentals=0
        ),
        name="step",
    )(*[pltpu.with_memory_space_constraint(v, pltpu.HBM) for v in (inputs, center, offset, dictionary)])


def small_kernel(small, offset, offset_mean, offset_var, center, center_mean, center_var, *outs):
    rows = (
        (offset, small[0:1, :], offset_mean, offset_var),
        (center, small[2:3, 0:64], center_mean, center_var),
    )
    for k, (param, grad, mean, var) in enumerate(rows):
        new = adam_update(param[...], grad, mean[...], var[...])
        for n in range(3):
            outs[3 * k + n][...] = new[n]
    scalars = small[3:4, 0:128]
    lane = lax.broadcasted_iota(jnp.int32, (1, 128), 1)
    weight = jnp.where(lane == 0, 1.0, jnp.where(lane == 1, sparsity_coeff, 0.0))
    outs[6][...] = jnp.sum(scalars * weight, axis=1, keepdims=True) / (TOK * WIDTH)


def small_step(small, *rows):
    shapes = [(1, LAT)] * 3 + [(1, 64)] * 3 + [(1, 1)]
    return pl.pallas_call(
        small_kernel,
        out_shape=[jax.ShapeDtypeStruct(s, F32) for s in shapes],
        in_specs=[pl.BlockSpec(memory_space=pltpu.VMEM)] * 7,
        out_specs=[pl.BlockSpec(memory_space=pltpu.VMEM)] * 7,
        compiler_params=pltpu.CompilerParams(vmem_limit_bytes=2**20),
        name="small",
    )(small, *[r.reshape(1, -1) for r in rows])


def body(
    inputs,
    dictionary,
    offset,
    center,
    dict_mean,
    dict_var,
    offset_mean,
    offset_var,
    center_mean,
    center_var,
):
    grad, small = step_kernel(
        inputs.T, center.reshape(1, -1), offset.reshape(1, -1), dictionary
    )
    g_dict = grad + small[1][:, None] * dictionary
    fresh_dict, mean_dict, var_dict = adam_update(dictionary, g_dict, dict_mean, dict_var)
    *rows, loss = small_step(
        small, offset, offset_mean, offset_var, center, center_mean, center_var
    )
    fresh_offset, mean_offset, var_offset, fresh_center, mean_center, var_center = [
        r.reshape(-1) for r in rows
    ]
    loss_value = loss.reshape(())
    return (
        fresh_dict,
        fresh_offset,
        fresh_center,
        mean_dict,
        var_dict,
        mean_offset,
        var_offset,
        mean_center,
        var_center,
        loss_value,
    )


def solution(mesh):
    return jax.shard_map(
        body,
        mesh=mesh,
        in_specs=(
            P("dp", "latent"),
            P("latent", None),
            P("latent"),
            P("latent"),
            P("latent", None),
            P("latent", None),
            P("latent"),
            P("latent"),
            P("latent"),
            P("latent"),
        ),
        out_specs=(
            P("latent", None),
            P("latent"),
            P("latent"),
            P("latent", None),
            P("latent", None),
            P("latent"),
            P("latent"),
            P("latent"),
            P("latent"),
            P(),
        ),
        check_vma=False,
    )
```

```python
import jax
import jax.numpy as jnp
from jax import lax
from jax.experimental import pallas as pl
from jax.experimental.pallas import tpu as pltpu
from jax.sharding import PartitionSpec as P

STEP = 1000
sparsity_coeff = 5.0
beta_one = 0.9
beta_two = 0.999
learn_rate = 0.001
adam_eps = 1e-08
norm_eps = 1e-06

TOK = 1152
WIDTH = 4096
ROWS = 288
CHUNK = 144
PART = 48
MAIN, SIDE = 64, 16
LAT = 256
VMEM_LIMIT = 42 * 1024 * 1024
F32 = jnp.float32
BF16 = jnp.bfloat16
MESH = pl.DeviceIdType.MESH


def adam_update(param, grad, mean, var):
    mean_new = beta_one * mean + (1.0 - beta_one) * grad
    var_new = beta_two * var + (1.0 - beta_two) * grad * grad
    corr_one = 1.0 - beta_one**STEP
    corr_two = 1.0 - beta_two**STEP
    param_new = param - learn_rate * (mean_new / corr_one) / (
        jnp.sqrt(var_new / corr_two) + adam_eps
    )
    return (param_new, mean_new, var_new)


def mod4(v):
    return lax.rem(v + 4, 4)


def dot(a, b):
    return jnp.dot(a, b, preferred_element_type=F32)


def dot_nt(a, b):
    return lax.dot_general(a, b, (((1,), (1,)), ((), ())), preferred_element_type=F32)


def kernel(
    inputs_hbm, center_hbm, offset_hbm, dict_ref,
    grad_ref, small_ref,
    inputs_ref, center_ref, offset_ref,
    weights, gx, ge, pre, dacc, acts, tmat, gacc,
    raw, raw_in, cen, cen_in, sm, sm_in, sums, sums_in,
    part, b0_out, b0_in, a0_out, a0_in, z_out, z_in,
    side, y_out, y_in, c1_out, c1_in, c2_out, c2_in,
    g_out, g_in,
    vx, vx_in, vz, vz_in,
    load_sem, pair_send, pair_recv,
    gx_send, gx_recv, ge_send, ge_recv, rs_send, rs_recv,
    g_send, g_recv, v_send, v_recv,
):
    h = lax.axis_index("dp")
    i = lax.axis_index("latent")
    core = lax.rem(i, 2)
    y = lax.rem(i // 2, 4)
    x = lax.rem(i // 8, 4)
    zl = i // 32
    z = 2 * h + zl

    def dev(xx, yy, zz, cc):
        return (zz // 2, ((lax.rem(zz, 2) * 4 + xx) * 4 + yy) * 2 + cc)

    coord = {"x": x, "y": y, "z": z}
    place = {(a, s): mod4(coord[a] + s) for a in coord for s in range(4)}
    near = {}
    for s in range(1, 4):
        near["x", s] = dev(place["x", s], y, z, core)
        near["y", s] = dev(x, place["y", s], z, core)
        near["z", s] = dev(x, y, place["z", s], core)

    def along(axis, step):
        return near[axis, step % 4]

    sibling = dev(x, y, z, 1 - core)
    far_z = 2 * h + 1 - zl
    other_z = dev(x, y, far_z, core)

    def rcopy(src, dst, ssem, rsem, device):
        return pltpu.make_async_remote_copy(
            src_ref=src, dst_ref=dst, send_sem=ssem, recv_sem=rsem,
            device_id=device, device_id_type=MESH,
        )

    def load(j):
        return pltpu.make_async_copy(
            dict_ref.at[:, pl.ds(512 * j, 512)], gacc.at[j], load_sem.at[j]
        )

    first_loads = [
        pltpu.make_async_copy(src, dst, load_sem.at[8 + k])
        for k, (src, dst) in enumerate(
            ((inputs_hbm, inputs_ref), (center_hbm, center_ref), (offset_hbm, offset_ref))
        )
    ]
    for c in first_loads:
        c.start()
    for j in range(8):
        load(j).start()

    plane = [
        dev(place["x", a], place["y", b], z, core) for a in range(4) for b in range(4) if a + b
    ]
    column = [
        dev(x, y, place["z", a], c)
        for a in range(4) for b, c in enumerate((core, 1 - core)) if a + b
    ]
    across = {
        axis: [near[axis, a] for a in range(1, 4)]
        + [
            dev(place["x", a], y, far_z, core) if axis == "x" else dev(x, place["y", a], far_z, core)
            for a in range(4)
        ]
        for axis in ("x", "y")
    }
    barrier = pltpu.get_barrier_semaphore()
    partners = plane + column + across["x"][4:] + across["y"][4:]
    for partner in partners:
        pl.semaphore_signal(barrier, inc=1, device_id=partner, device_id_type=MESH)

    for c in first_loads:
        c.wait()
    lane = lax.broadcasted_iota(jnp.int32, (1, 128), 1)
    mine = (lane // 64) == core
    both = inputs_ref[...].astype(F32)
    both = jnp.concatenate([both, both], axis=0).T
    raw[...] = jnp.where(mine, both, 0.0).astype(BF16).reshape(2, ROWS, 128)
    cboth = jnp.concatenate([center_ref[...], center_ref[...]], axis=1)
    cen[...] = jnp.broadcast_to(jnp.where(mine, cboth, 0.0), (8, 128))
    pl.semaphore_wait(barrier, len(partners))

    pair = [
        rcopy(raw.at[1 - core], raw_in, pair_send.at[0], pair_recv.at[0], sibling),
        rcopy(cen, cen_in, pair_send.at[1], pair_recv.at[1], sibling),
    ]
    for c in pair:
        c.start()
    for c in pair:
        c.wait_recv()
    center = cen[0:1, :] + cen_in[0:1, :]

    def own_rows(t):
        rows = pl.ds(CHUNK * t, CHUNK)
        return raw[core, rows].astype(F32) + raw_in[rows].astype(F32)

    sent = []

    def flush(log):
        for c in log:
            c.wait_send()
        log.clear()

    orders = (("y", "x", "z"), ("x", "z", "y"), ("z", "y", "x"))
    dirs = ((0, 1), (1, -1))

    def gather(buf, t, block, ssem, rsem, log):
        at = [tuple(coord[a] for a in reversed(o)) for o in orders]
        for p in range(3):
            buf[(t, p) + at[p]] = block[PART * p : PART * (p + 1)]

        def chunk(p, f, step):
            q = place[orders[p][f], step % 4]
            return (t, p) + at[p][: 2 - f] + (q,)

        def send(p, f, e, idx, step):
            ref = buf.at[idx]
            rcopy(
                ref, ref, ssem.at[t, p, f], rsem.at[t, p, e], along(orders[p][f], step)
            ).start()

        def whole(p, f, e, idx):
            ref = buf.at[idx]
            return rcopy(ref, ref, ssem.at[t, p, f], rsem.at[t, p, e], sibling)

        def triple(p, f):
            return (t, p) + at[p][: 2 - f] + (pl.ds(0, 3),)

        def double(p, f):
            return (t, p) + at[p][: 2 - f] + (pl.ds(0, 2),)

        def single(p, f):
            return (t, p) + at[p][: 2 - f] + (0,)

        for p in range(3):
            for step in (1, 3, 2):
                send(p, 0, 0, chunk(p, 0, 0), step)
            log.append(whole(p, 0, 0, triple(p, 0)))
        yield
        for p in range(3):
            whole(p, 0, 0, triple(p, 0)).wait_recv()
            for k, step in dirs:
                send(p, 1, 1, chunk(p, 1, 0), step)
            log.append(whole(p, 1, 1, triple(p, 1)))
        yield
        for p in range(3):
            whole(p, 1, 1, double(p, 1)).wait_recv()
            for k, step in dirs:
                send(p, 1, 2, chunk(p, 1, -step) + (pl.ds(2 * k, 2),), step)
        yield
        for p in range(3):
            whole(p, 1, 2, single(p, 1)).wait_recv()
            for k, step in dirs:
                send(p, 2, 3, chunk(p, 2, 0) + (pl.ds(2 * k, 2),), step)
            log.append(whole(p, 2, 3, triple(p, 2)))
        for p in range(3):
            for k, step in dirs:
                send(p, 2, 4, chunk(p, 2, 0) + (pl.ds(2 - 2 * k, 2),), step)
        yield
        for p in range(3):
            whole(p, 2, 3, single(p, 2)).wait_recv()
            for k, step in dirs:
                send(p, 2, 5, chunk(p, 2, -step) + (pl.ds(2 * k, 2),), step)
        yield
        for e in (4, 5):
            for p in range(3):
                whole(p, 2, e, single(p, 2)).wait_recv()

    def weight_copy(j):
        return rcopy(
            weights.at[0, j], weights.at[1, j], pair_send.at[2 + j], pair_recv.at[2 + j], sibling
        )

    small_copy = rcopy(sm, sm_in, pair_send.at[10], pair_recv.at[10], sibling)

    def prepare():
        sq = jnp.zeros((LAT, 1), F32)
        for j in range(8):
            load(j).wait()
            block = gacc[j]
            weights[0, j] = block.astype(BF16)
            weight_copy(j).start()
            sq = sq + jnp.sum(block * block, axis=1, keepdims=True)
        norm = jnp.sqrt(sq + norm_eps)
        sm[...] = jnp.zeros((8, LAT), F32)
        sm[0:1, :] = offset_ref[...]
        sm[1:2, :] = jnp.broadcast_to(norm, (LAT, 128)).T[0:1, :]
        small_copy.start()

    def slab(buf, t, j):
        jz, jx = j // 4, lax.rem(j, 4)
        rows = []
        for r in range(2):
            zz = 2 * (h if r == 0 else 1 - h) + jz
            for p in range(3):
                cols = []
                for yy in range(4):
                    idx = ((zz, jx, yy), (yy, zz, jx), (jx, yy, zz))[p]
                    cols.append(buf[(t, p) + idx])
                rows.append(jnp.concatenate(cols, axis=1))
        return jnp.concatenate(rows, axis=0)

    def all_weights(j):
        return jnp.concatenate([weights[0, j], weights[1, j]], axis=0)

    def project(buf, t, acc, first, last):
        if first == 0:
            acc[t] = jnp.zeros((2 * CHUNK, 512), F32)

        @pl.loop(first, last, unroll=2)
        def _(j):
            acc[t] += dot_nt(slab(buf, t, j), all_weights(j))

    def ring_first(src, lead, axis, b_out, b_in, sems, log):
        q = place[axis, 2]
        for k, step in dirs:
            b_out[k][...] = src[lead + (q, pl.ds(2 * k, 2))].astype(BF16)
            c = rcopy(b_out[k], b_in[k], sems[0][k], sems[1][k], along(axis, step))
            c.start()
            log.append(c)

    def ring_second(src, lead, axis, b_out, b_in, a_out, a_in, sems, log):
        for k, step in dirs:
            q = place[axis, step % 4]
            mix, rest = pl.ds(2 * k, 2), pl.ds(2 - 2 * k, 2)
            a_out[k][rest] = src[lead + (q, rest)].astype(BF16)
            rcopy(b_out[k], b_in[k], sems[0][k], sems[1][k], along(axis, step)).wait_recv()
            a_out[k][mix] = (src[lead + (q, mix)] + b_in[k][...].astype(F32)).astype(BF16)
            c = rcopy(a_out[k], a_in[k], sems[0][2 + k], sems[1][2 + k], along(axis, step))
            c.start()
            log.append(c)

    def ring_last(src, lead, axis, a_out, a_in, sems):
        for k, step in dirs:
            rcopy(a_out[k], a_in[k], sems[0][2 + k], sems[1][2 + k], along(axis, step)).wait_recv()
        return src[lead + (coord[axis],)] + a_in[0][...].astype(F32) + a_in[1][...].astype(F32)

    def direct_first(value, axis, out, into, sems, log):
        for k in range(3):
            out[k] = value(place[axis, k + 1]).astype(BF16)
            rcopy(out.at[k], into.at[k], sems[0][0], sems[1][0], along(axis, k + 1)).start()
        log.append(rcopy(out, into, sems[0][0], sems[1][0], sibling))

    def direct_last(value, axis, out, into, sems):
        rcopy(out, into, sems[0][0], sems[1][0], sibling).wait_recv()
        total = value(coord[axis])
        for k in range(3):
            total = total + into[k].astype(F32)
        return total

    def scatter(t, log):
        side_axes = ("x", "y") if t == 0 else ("y", "x")
        axes = (("x", "y"), ("y", "x"), side_axes)

        def some(ref, *lead):
            return [ref.at[lead + (k,)] for k in range(ref.shape[len(lead)])]

        def sems(p, s):
            return (
                [rs_send.at[t, p, 4 * s + e] for e in range(4)],
                [rs_recv.at[t, p, 4 * s + e] for e in range(4)],
            )

        def line_copy(p, e):
            src, dst = (z_out.at[t, p], z_in.at[t, p]) if e is None else (z_out.at[t, p, e], z_in.at[t, p, e])
            device = sibling if e is None else across[axes[p][1]][e]
            return rcopy(src, dst, rs_send.at[t, p, 4], rs_recv.at[t, p, 4], device)

        pair_copy = rcopy(
            y_out.at[t], y_in.at[t], rs_send.at[t, 2, 8], rs_recv.at[t, 2, 8], other_z
        )
        y_out[t] = side[t, 1 - zl].astype(BF16)
        pair_copy.start()
        ring = [
            (part, (t, p), axes[p][0], some(b0_out, t, p), some(b0_in, t, p), some(a0_out, t, p), some(a0_in, t, p), sems(p, 0))
            for p in range(2)
        ]
        for a in ring:
            ring_first(*a[:5], a[7], log)
        yield
        pair_copy.wait_recv()
        side[t, zl] = side[t, zl] + y_in[t].astype(F32)
        wide = (lambda q: side[t, zl, q], axes[2][0], c1_out.at[t], c1_in.at[t], sems(2, 0))
        direct_first(*wide, log)
        for a in ring:
            ring_second(*a, log)
        yield
        here = coord[axes[2][0]]
        side[t, zl, here] = direct_last(*wide)
        thin = (lambda q: side[t, zl, here, q], axes[2][1], c2_out.at[t], c2_in.at[t], sems(2, 1))
        direct_first(*thin, log)
        for p in range(2):
            first = coord[axes[p][0]]
            part[t, p, first] = ring_last(*ring[p][:3], *ring[p][5:])
            for e in range(7):
                a, w = (e + 1, zl) if e < 3 else (e - 3, 1 - zl)
                z_out[t, p, e] = part[t, p, first, place[axes[p][1], a], w].astype(BF16)
                line_copy(p, e).start()
            log.append(line_copy(p, None))
        yield
        out = []
        for p in range(2):
            total = part[t, p, coord[axes[p][0]], coord[axes[p][1]], zl]
            line_copy(p, None).wait_recv()
            for e in range(7):
                total = total + z_in[t, p, e].astype(F32)
            out.append(total)
        out.append(direct_last(*thin))
        log.append(pair_copy)
        result[t] = jnp.concatenate(out, axis=0)

    result, sq, err_sum, act_own, act_all, off_own, off_all = {}, {}, {}, {}, {}, {}, {}
    shared = {}

    def g_copy(j):
        return rcopy(g_out.at[j], g_in.at[j], g_send.at[j], g_recv.at[j], sibling)

    def gradient(t, first, last):
        @pl.loop(first, last)
        def _(j):
            both = jnp.concatenate([slab(gx, t, j), slab(ge, t, j)], axis=0)
            out = dot(tmat[t], both)
            cols = pl.ds(pl.multiple_of(512 * j, 512), 512)
            if t == 0:
                gacc[j] = out[LAT:]
                grad_ref[:, cols] = out[:LAT]
            else:
                g_out[j] = (gacc[j] + out[LAT:]).astype(BF16)
                g_copy(j).start()
                grad_ref[:, cols] = grad_ref[:, cols] + out[:LAT]

    def steps(t):
        centered = (own_rows(t) - center).astype(BF16)
        log_x, log_r, log_e = [], [], []
        yield from gather(gx, t, centered, gx_send, gx_recv, log_x)
        if t == 0:
            for j in range(8):
                weight_copy(j).wait_recv()
            small_copy.wait_recv()
            shared["bias"] = jnp.concatenate([sm[0:1, :], sm_in[0:1, :]], axis=1)
            shared["norms"] = jnp.concatenate([sm[1:2, :], sm_in[1:2, :]], axis=1)
        norms = shared["norms"]
        project(gx, t, pre, 0, 4)
        yield
        project(gx, t, pre, 4, 8)
        yield
        pre[t] = pre[t] + shared["bias"]
        acts[t] = jnp.maximum(pre[t], 0.0).astype(BF16)

        @pl.loop(0, 8, unroll=2)
        def _(j):
            jz, jx = j // 4, lax.rem(j, 4)
            out = dot(acts[t, :CHUNK], all_weights(j))
            for yy in range(4):
                cols = slice(128 * yy, 128 * (yy + 1))
                part[t, 0, jx, yy, jz] = out[:MAIN, cols]
                part[t, 1, yy, jx, jz] = out[MAIN : 2 * MAIN, cols]
                if t == 0:
                    side[t, jz, jx, yy] = out[2 * MAIN :, cols]
                else:
                    side[t, jz, yy, jx] = out[2 * MAIN :, cols]

        ready = scatter(t, log_r)
        next(ready)
        flush(log_x)
        yield
        yield from ready
        err = result[t] + center - own_rows(t)
        sq[t] = jnp.sum(err * err)
        err_sum[t] = jnp.sum(err, axis=0, keepdims=True)
        derr = (2.0 / TOK * err).astype(BF16)
        ready = gather(ge, t, derr, ge_send, ge_recv, log_e)
        next(ready)
        flush(log_r)
        yield
        yield from ready
        sent.extend(log_e)
        project(ge, t, dacc, 0, 4)
        yield
        project(ge, t, dacc, 4, 8)
        yield
        dacts = dacc[t] + sparsity_coeff / TOK * norms
        dpre = jnp.where(pre[t] > 0, dacts, 0.0).astype(BF16)
        act = acts[t]
        tmat[t] = jnp.concatenate([dpre, act], axis=0).T
        off_own[t] = jnp.sum(dpre[:CHUNK].astype(F32), axis=0, keepdims=True)
        off_all[t] = off_own[t] + jnp.sum(dpre[CHUNK:].astype(F32), axis=0, keepdims=True)
        act_own[t] = jnp.sum(act[:CHUNK].astype(F32), axis=0, keepdims=True)
        act_all[t] = act_own[t] + jnp.sum(act[CHUNK:].astype(F32), axis=0, keepdims=True)
        yield
        if t == 0:
            gradient(0, 0, 4)
            yield
            gradient(0, 4, 8)
            yield

    run = [steps(0), steps(1)]
    plan = "0101010w0100101011010101010101000100111"
    for who in plan:
        if who == "w":
            prepare()
        else:
            next(run[int(who)])
    for one in run:
        assert next(one, one) is one
    off = off_own[0] + off_own[1]
    offs = off_all[0] + off_all[1]
    act_tot = act_all[0] + act_all[1]
    spars = jnp.sum((act_own[0] + act_own[1]) * shared["norms"])

    sums[...] = jnp.zeros((2, 8, LAT), F32)
    for k in range(2):
        sums[k, 0:1, :] = offs[:, LAT * k : LAT * (k + 1)]
        sums[k, 1:2, :] = act_tot[:, LAT * k : LAT * (k + 1)]
    sums_copy = rcopy(sums.at[1], sums_in, pair_send.at[11], pair_recv.at[11], sibling)
    sums_copy.start()

    hi = off.astype(BF16)
    rest = off - hi.astype(F32)
    mid = rest.astype(BF16)
    low = (rest - mid.astype(F32)).astype(BF16)
    row = lax.broadcasted_iota(jnp.int32, (16, 512), 0)
    terms = jnp.where(
        row == 0, hi.astype(F32),
        jnp.where(row == 1, mid.astype(F32), jnp.where(row == 2, low.astype(F32), 0.0)),
    ).astype(BF16)
    for j in range(8):
        enc = jnp.sum(dot(terms, all_weights(j)), axis=0, keepdims=True)
        for yy in range(4):
            vx[(j % 4) * 4 + yy, j // 4 : j // 4 + 1, :] = -enc[:, 128 * yy : 128 * (yy + 1)]
    scalars = jnp.where(lane == 0, sq[0] + sq[1], jnp.where(lane == 1, spars, 0.0))
    for k in range(16):
        vx[k, 2:8, :] = jnp.broadcast_to(scalars, (6, 128))
    here = x * 4 + y
    sub = lax.broadcasted_iota(jnp.int32, (8, 128), 0)
    vx[here] = vx[here] + jnp.where(sub == zl, 2.0 / TOK * (err_sum[0] + err_sum[1]), 0.0)

    def v_plane(e):
        a, b = (e + 1) // 4, (e + 1) % 4
        return rcopy(
            vx.at[place["x", a] * 4 + place["y", b]], vx_in.at[e], v_send.at[0], v_recv.at[0], plane[e]
        )

    def v_column(e):
        return rcopy(vz, vz_in.at[e], v_send.at[1], v_recv.at[1], column[e])

    v_planes = rcopy(vx_in, vx_in, v_send.at[0], v_recv.at[0], sibling)
    v_columns = rcopy(vz_in, vz_in, v_send.at[1], v_recv.at[1], sibling)

    for e in range(15):
        v_plane(e).start()
    gradient(1, 0, 4)
    total = vx[here]
    v_planes.wait_recv()
    for e in range(15):
        total = total + vx_in[e]
    vz[...] = total
    for e in range(7):
        v_column(e).start()
    gradient(1, 4, 8)
    v_columns.wait_recv()
    for e in range(7):
        total = total + vz_in[e]
    sums_copy.wait_recv()

    small_ref[...] = jnp.zeros((8, LAT), F32)
    small_ref[0:1, :] = sums[0, 0:1, :] + sums_in[0:1, :]
    small_ref[1:2, :] = sparsity_coeff / TOK * (sums[0, 1:2, :] + sums_in[1:2, :]) / sm[1:2, :]
    slot = jnp.where(zl == 0, total[0:1], total[1:2])
    small_ref[2:3, 0:64] = jnp.where(core == 0, slot[:, :64], slot[:, 64:])
    small_ref[3:4, 0:128] = total[2:3]

    flush(sent)
    for j in range(8):
        weight_copy(j).wait_send()
    for c in pair + [small_copy, sums_copy]:
        c.wait_send()
    v_planes.wait_send()
    v_columns.wait_send()
    for j in range(8):
        cols = slice(512 * j, 512 * (j + 1))
        g_copy(j).wait_recv()
        grad_ref[:, cols] = grad_ref[:, cols] + g_in[j].astype(F32)
    for j in range(8):
        g_copy(j).wait_send()


def step_kernel(inputs, center, offset, dictionary):
    vm = pltpu.VMEM
    dma = pltpu.SemaphoreType.DMA
    block = (PART, 128)
    main, side = (MAIN, 128), (SIDE, 128)
    return pl.pallas_call(
        kernel,
        out_shape=[
            jax.ShapeDtypeStruct((LAT, WIDTH), F32),
            jax.ShapeDtypeStruct((8, LAT), F32),
        ],
        in_specs=[pl.BlockSpec(memory_space=pltpu.HBM)] * 4,
        out_specs=[pl.BlockSpec(memory_space=pltpu.VMEM)] * 2,
        scratch_shapes=[
            vm((64, 2 * ROWS), BF16),
            vm((1, 64), F32),
            vm((1, LAT), F32),
            vm((2, 8, LAT, 512), BF16),
            vm((2, 3, 4, 4, 4) + block, BF16),
            vm((2, 3, 4, 4, 4) + block, BF16),
            vm((2, 2 * CHUNK, 512), F32),
            vm((2, 2 * CHUNK, 512), F32),
            vm((2, 2 * CHUNK, 512), BF16),
            vm((2, 512, 4 * CHUNK), BF16),
            vm((8, LAT, 512), F32),
            vm((2, ROWS, 128), BF16),
            vm((ROWS, 128), BF16),
            vm((8, 128), F32),
            vm((8, 128), F32),
            vm((8, LAT), F32),
            vm((8, LAT), F32),
            vm((2, 8, LAT), F32),
            vm((8, LAT), F32),
            vm((2, 2, 4, 4, 2) + main, F32),
            vm((2, 2, 2, 2, 2) + main, BF16),
            vm((2, 2, 2, 2, 2) + main, BF16),
            vm((2, 2, 2, 4, 2) + main, BF16),
            vm((2, 2, 2, 4, 2) + main, BF16),
            vm((2, 2, 7) + main, BF16),
            vm((2, 2, 7) + main, BF16),
            vm((2, 2, 4, 4) + side, F32),
            vm((2, 4, 4) + side, BF16),
            vm((2, 4, 4) + side, BF16),
            vm((2, 3, 4) + side, BF16),
            vm((2, 3, 4) + side, BF16),
            vm((2, 3) + side, BF16),
            vm((2, 3) + side, BF16),
            vm((8, LAT, 512), BF16),
            vm((8, LAT, 512), BF16),
            vm((16, 8, 128), F32),
            vm((15, 8, 128), F32),
            vm((8, 128), F32),
            vm((7, 8, 128), F32),
            dma((11,)),
            dma((12,)),
            dma((12,)),
            dma((2, 3, 3)),
            dma((2, 3, 6)),
            dma((2, 3, 3)),
            dma((2, 3, 6)),
            dma((2, 3, 9)),
            dma((2, 3, 9)),
            dma((8,)),
            dma((8,)),
            dma((2,)),
            dma((2,)),
        ],
        compiler_params=pltpu.CompilerParams(
            collective_id=0, has_side_effects=True, vmem_limit_bytes=VMEM_LIMIT
        ),
        cost_estimate=pl.CostEstimate(
            flops=12 * 2**30, bytes_accessed=160 * 2**20, transcendentals=0
        ),
        name="step",
    )(*[pltpu.with_memory_space_constraint(v, pltpu.HBM) for v in (inputs, center, offset, dictionary)])


def small_kernel(small, offset, offset_mean, offset_var, center, center_mean, center_var, *outs):
    rows = (
        (offset, small[0:1, :], offset_mean, offset_var),
        (center, small[2:3, 0:64], center_mean, center_var),
    )
    for k, (param, grad, mean, var) in enumerate(rows):
        new = adam_update(param[...], grad, mean[...], var[...])
        for n in range(3):
            outs[3 * k + n][...] = new[n]
    scalars = small[3:4, 0:128]
    lane = lax.broadcasted_iota(jnp.int32, (1, 128), 1)
    weight = jnp.where(lane == 0, 1.0, jnp.where(lane == 1, sparsity_coeff, 0.0))
    outs[6][...] = jnp.sum(scalars * weight, axis=1, keepdims=True) / (TOK * WIDTH)


def small_step(small, *rows):
    shapes = [(1, LAT)] * 3 + [(1, 64)] * 3 + [(1, 1)]
    return pl.pallas_call(
        small_kernel,
        out_shape=[jax.ShapeDtypeStruct(s, F32) for s in shapes],
        in_specs=[pl.BlockSpec(memory_space=pltpu.VMEM)] * 7,
        out_specs=[pl.BlockSpec(memory_space=pltpu.VMEM)] * 7,
        compiler_params=pltpu.CompilerParams(vmem_limit_bytes=2**20),
        name="small",
    )(small, *[r.reshape(1, -1) for r in rows])


def body(
    inputs,
    dictionary,
    offset,
    center,
    dict_mean,
    dict_var,
    offset_mean,
    offset_var,
    center_mean,
    center_var,
):
    grad, small = step_kernel(
        inputs.T, center.reshape(1, -1), offset.reshape(1, -1), dictionary
    )
    g_dict = grad + small[1][:, None] * dictionary
    fresh_dict, mean_dict, var_dict = adam_update(dictionary, g_dict, dict_mean, dict_var)
    *rows, loss = small_step(
        small, offset, offset_mean, offset_var, center, center_mean, center_var
    )
    fresh_offset, mean_offset, var_offset, fresh_center, mean_center, var_center = [
        r.reshape(-1) for r in rows
    ]
    loss_value = loss.reshape(())
    return (
        fresh_dict,
        fresh_offset,
        fresh_center,
        mean_dict,
        var_dict,
        mean_offset,
        var_offset,
        mean_center,
        var_center,
        loss_value,
    )


def solution(mesh):
    return jax.shard_map(
        body,
        mesh=mesh,
        in_specs=(
            P("dp", "latent"),
            P("latent", None),
            P("latent"),
            P("latent"),
            P("latent", None),
            P("latent", None),
            P("latent"),
            P("latent"),
            P("latent"),
            P("latent"),
        ),
        out_specs=(
            P("latent", None),
            P("latent"),
            P("latent"),
            P("latent", None),
            P("latent", None),
            P("latent"),
            P("latent"),
            P("latent"),
            P("latent"),
            P(),
        ),
        check_vma=False,
    )
```

```python
import jax
import jax.numpy as jnp
from jax import lax
from jax.experimental import pallas as pl
from jax.experimental.pallas import tpu as pltpu
from jax.sharding import PartitionSpec as P

STEP = 1000
sparsity_coeff = 5.0
beta_one = 0.9
beta_two = 0.999
learn_rate = 0.001
adam_eps = 1e-08
norm_eps = 1e-06

TOK = 1152
WIDTH = 4096
ROWS = 288
CHUNK = 144
PART = 48
MAIN, SIDE = 64, 16
LAT = 256
VMEM_LIMIT = 42 * 1024 * 1024
F32 = jnp.float32
BF16 = jnp.bfloat16
MESH = pl.DeviceIdType.MESH


def adam_update(param, grad, mean, var):
    mean_new = beta_one * mean + (1.0 - beta_one) * grad
    var_new = beta_two * var + (1.0 - beta_two) * grad * grad
    corr_one = 1.0 - beta_one**STEP
    corr_two = 1.0 - beta_two**STEP
    param_new = param - learn_rate * (mean_new / corr_one) / (
        jnp.sqrt(var_new / corr_two) + adam_eps
    )
    return (param_new, mean_new, var_new)


def mod4(v):
    return lax.rem(v + 4, 4)


def dot(a, b):
    return jnp.dot(a, b, preferred_element_type=F32)


def dot_nt(a, b):
    return lax.dot_general(a, b, (((1,), (1,)), ((), ())), preferred_element_type=F32)


def kernel(
    inputs_hbm, center_hbm, offset_hbm, dict_ref,
    grad_ref, small_ref,
    inputs_ref, center_ref, offset_ref,
    weights, gx, ge, pre, dacc, acts, tmat, gacc,
    raw, raw_in, cen, cen_in, sm, sm_in, sums, sums_in,
    part, b0_out, b0_in, a0_out, a0_in, z_out, z_in,
    side, y_out, y_in, c1_out, c1_in, c2_out, c2_in,
    g_out, g_in,
    vx, vx_in, vz, vz_in,
    load_sem, pair_send, pair_recv,
    gx_send, gx_recv, ge_send, ge_recv, rs_send, rs_recv,
    g_send, g_recv, v_send, v_recv,
):
    h = lax.axis_index("dp")
    i = lax.axis_index("latent")
    core = lax.rem(i, 2)
    y = lax.rem(i // 2, 4)
    x = lax.rem(i // 8, 4)
    zl = i // 32
    z = 2 * h + zl

    def dev(xx, yy, zz, cc):
        return (zz // 2, ((lax.rem(zz, 2) * 4 + xx) * 4 + yy) * 2 + cc)

    coord = {"x": x, "y": y, "z": z}
    place = {(a, s): mod4(coord[a] + s) for a in coord for s in range(4)}
    near = {}
    for s in range(1, 4):
        near["x", s] = dev(place["x", s], y, z, core)
        near["y", s] = dev(x, place["y", s], z, core)
        near["z", s] = dev(x, y, place["z", s], core)

    def along(axis, step):
        return near[axis, step % 4]

    sibling = dev(x, y, z, 1 - core)
    far_z = 2 * h + 1 - zl
    other_z = dev(x, y, far_z, core)

    def rcopy(src, dst, ssem, rsem, device):
        return pltpu.make_async_remote_copy(
            src_ref=src, dst_ref=dst, send_sem=ssem, recv_sem=rsem,
            device_id=device, device_id_type=MESH,
        )

    def load(j):
        return pltpu.make_async_copy(
            dict_ref.at[:, pl.ds(512 * j, 512)], gacc.at[j], load_sem.at[j]
        )

    first_loads = [
        pltpu.make_async_copy(src, dst, load_sem.at[8 + k])
        for k, (src, dst) in enumerate(
            ((inputs_hbm, inputs_ref), (center_hbm, center_ref), (offset_hbm, offset_ref))
        )
    ]
    for c in first_loads:
        c.start()
    for j in range(8):
        load(j).start()

    plane = [
        dev(place["x", a], place["y", b], z, core) for a in range(4) for b in range(4) if a + b
    ]
    column = [
        dev(x, y, place["z", a], c)
        for a in range(4) for b, c in enumerate((core, 1 - core)) if a + b
    ]
    across = {
        axis: [near[axis, a] for a in range(1, 4)]
        + [
            dev(place["x", a], y, far_z, core) if axis == "x" else dev(x, place["y", a], far_z, core)
            for a in range(4)
        ]
        for axis in ("x", "y")
    }
    barrier = pltpu.get_barrier_semaphore()
    partners = plane + column + across["x"][4:] + across["y"][4:]
    for partner in partners:
        pl.semaphore_signal(barrier, inc=1, device_id=partner, device_id_type=MESH)

    for c in first_loads:
        c.wait()
    lane = lax.broadcasted_iota(jnp.int32, (1, 128), 1)
    mine = (lane // 64) == core
    both = inputs_ref[...].astype(F32)
    both = jnp.concatenate([both, both], axis=0).T
    raw[...] = jnp.where(mine, both, 0.0).astype(BF16).reshape(2, ROWS, 128)
    cboth = jnp.concatenate([center_ref[...], center_ref[...]], axis=1)
    cen[...] = jnp.broadcast_to(jnp.where(mine, cboth, 0.0), (8, 128))
    pl.semaphore_wait(barrier, len(partners))

    pair = [
        rcopy(raw.at[1 - core], raw_in, pair_send.at[0], pair_recv.at[0], sibling),
        rcopy(cen, cen_in, pair_send.at[1], pair_recv.at[1], sibling),
    ]
    for c in pair:
        c.start()
    for c in pair:
        c.wait_recv()
    center = cen[0:1, :] + cen_in[0:1, :]

    def own_rows(t):
        rows = pl.ds(CHUNK * t, CHUNK)
        return raw[core, rows].astype(F32) + raw_in[rows].astype(F32)

    sent = []

    def flush(log):
        for c in log:
            c.wait_send()
        log.clear()

    orders = (("y", "x", "z"), ("x", "z", "y"), ("z", "y", "x"))
    dirs = ((0, 1), (1, -1))

    def gather(buf, t, block, ssem, rsem, log):
        at = [tuple(coord[a] for a in reversed(o)) for o in orders]
        for p in range(3):
            buf[(t, p) + at[p]] = block[PART * p : PART * (p + 1)]

        def chunk(p, f, step):
            q = place[orders[p][f], step % 4]
            return (t, p) + at[p][: 2 - f] + (q,)

        def send(p, f, e, idx, step):
            ref = buf.at[idx]
            rcopy(
                ref, ref, ssem.at[t, p, f], rsem.at[t, p, e], along(orders[p][f], step)
            ).start()

        def whole(p, f, e, idx):
            ref = buf.at[idx]
            return rcopy(ref, ref, ssem.at[t, p, f], rsem.at[t, p, e], sibling)

        def triple(p, f):
            return (t, p) + at[p][: 2 - f] + (pl.ds(0, 3),)

        def double(p, f):
            return (t, p) + at[p][: 2 - f] + (pl.ds(0, 2),)

        def single(p, f):
            return (t, p) + at[p][: 2 - f] + (0,)

        for p in range(3):
            for step in (1, 3, 2):
                send(p, 0, 0, chunk(p, 0, 0), step)
            log.append(whole(p, 0, 0, triple(p, 0)))
        yield
        for p in range(3):
            whole(p, 0, 0, triple(p, 0)).wait_recv()
            for k, step in dirs:
                send(p, 1, 1, chunk(p, 1, 0), step)
            log.append(whole(p, 1, 1, triple(p, 1)))
        yield
        for p in range(3):
            whole(p, 1, 1, double(p, 1)).wait_recv()
            for k, step in dirs:
                send(p, 1, 2, chunk(p, 1, -step) + (pl.ds(2 * k, 2),), step)
        yield
        for p in range(3):
            whole(p, 1, 2, single(p, 1)).wait_recv()
            for k, step in dirs:
                send(p, 2, 3, chunk(p, 2, 0) + (pl.ds(2 * k, 2),), step)
            log.append(whole(p, 2, 3, triple(p, 2)))
        for p in range(3):
            for k, step in dirs:
                send(p, 2, 4, chunk(p, 2, 0) + (pl.ds(2 - 2 * k, 2),), step)
        yield
        for p in range(3):
            whole(p, 2, 3, single(p, 2)).wait_recv()
            for k, step in dirs:
                send(p, 2, 5, chunk(p, 2, -step) + (pl.ds(2 * k, 2),), step)
        yield
        for e in (4, 5):
            for p in range(3):
                whole(p, 2, e, single(p, 2)).wait_recv()

    def weight_copy(j):
        return rcopy(
            weights.at[0, j], weights.at[1, j], pair_send.at[2 + j], pair_recv.at[2 + j], sibling
        )

    small_copy = rcopy(sm, sm_in, pair_send.at[10], pair_recv.at[10], sibling)

    def prepare():
        sq = jnp.zeros((LAT, 1), F32)
        for j in range(8):
            load(j).wait()
            block = gacc[j]
            weights[0, j] = block.astype(BF16)
            weight_copy(j).start()
            sq = sq + jnp.sum(block * block, axis=1, keepdims=True)
        norm = jnp.sqrt(sq + norm_eps)
        sm[...] = jnp.zeros((8, LAT), F32)
        sm[0:1, :] = offset_ref[...]
        sm[1:2, :] = jnp.broadcast_to(norm, (LAT, 128)).T[0:1, :]
        small_copy.start()

    def slab(buf, t, j):
        jz, jx = j // 4, j % 4
        rows = []
        for r in range(2):
            zz = 2 * (h if r == 0 else 1 - h) + jz
            for p in range(3):
                cols = []
                for yy in range(4):
                    idx = ((zz, jx, yy), (yy, zz, jx), (jx, yy, zz))[p]
                    cols.append(buf[(t, p) + idx])
                rows.append(jnp.concatenate(cols, axis=1))
        return jnp.concatenate(rows, axis=0)

    def all_weights(j):
        return jnp.concatenate([weights[0, j], weights[1, j]], axis=0)

    def project(buf, t, acc, half):
        rows = jnp.concatenate([slab(buf, t, 4 * half + jx) for jx in range(4)], axis=1)
        cols = jnp.concatenate([all_weights(4 * half + jx) for jx in range(4)], axis=1)
        out = dot_nt(rows, cols)
        acc[t] = out if half == 0 else acc[t] + out

    def ring_first(src, lead, axis, b_out, b_in, sems, log):
        q = place[axis, 2]
        for k, step in dirs:
            b_out[k][...] = src[lead + (q, pl.ds(2 * k, 2))].astype(BF16)
            c = rcopy(b_out[k], b_in[k], sems[0][k], sems[1][k], along(axis, step))
            c.start()
            log.append(c)

    def ring_second(src, lead, axis, b_out, b_in, a_out, a_in, sems, log):
        for k, step in dirs:
            q = place[axis, step % 4]
            mix, rest = pl.ds(2 * k, 2), pl.ds(2 - 2 * k, 2)
            a_out[k][rest] = src[lead + (q, rest)].astype(BF16)
            rcopy(b_out[k], b_in[k], sems[0][k], sems[1][k], along(axis, step)).wait_recv()
            a_out[k][mix] = (src[lead + (q, mix)] + b_in[k][...].astype(F32)).astype(BF16)
            c = rcopy(a_out[k], a_in[k], sems[0][2 + k], sems[1][2 + k], along(axis, step))
            c.start()
            log.append(c)

    def ring_last(src, lead, axis, a_out, a_in, sems):
        for k, step in dirs:
            rcopy(a_out[k], a_in[k], sems[0][2 + k], sems[1][2 + k], along(axis, step)).wait_recv()
        return src[lead + (coord[axis],)] + a_in[0][...].astype(F32) + a_in[1][...].astype(F32)

    def direct_first(value, axis, out, into, sems, log):
        for k in range(3):
            out[k] = value(place[axis, k + 1]).astype(BF16)
            rcopy(out.at[k], into.at[k], sems[0][0], sems[1][0], along(axis, k + 1)).start()
        log.append(rcopy(out, into, sems[0][0], sems[1][0], sibling))

    def direct_last(value, axis, out, into, sems):
        rcopy(out, into, sems[0][0], sems[1][0], sibling).wait_recv()
        total = value(coord[axis])
        for k in range(3):
            total = total + into[k].astype(F32)
        return total

    def scatter(t, log):
        side_axes = ("x", "y") if t == 0 else ("y", "x")
        axes = (("x", "y"), ("y", "x"), side_axes)

        def some(ref, *lead):
            return [ref.at[lead + (k,)] for k in range(ref.shape[len(lead)])]

        def sems(p, s):
            return (
                [rs_send.at[t, p, 4 * s + e] for e in range(4)],
                [rs_recv.at[t, p, 4 * s + e] for e in range(4)],
            )

        def line_copy(p, e):
            src, dst = (z_out.at[t, p], z_in.at[t, p]) if e is None else (z_out.at[t, p, e], z_in.at[t, p, e])
            device = sibling if e is None else across[axes[p][1]][e]
            return rcopy(src, dst, rs_send.at[t, p, 4], rs_recv.at[t, p, 4], device)

        pair_copy = rcopy(
            y_out.at[t], y_in.at[t], rs_send.at[t, 2, 8], rs_recv.at[t, 2, 8], other_z
        )
        y_out[t] = side[t, 1 - zl].astype(BF16)
        pair_copy.start()
        ring = [
            (part, (t, p), axes[p][0], some(b0_out, t, p), some(b0_in, t, p), some(a0_out, t, p), some(a0_in, t, p), sems(p, 0))
            for p in range(2)
        ]
        for a in ring:
            ring_first(*a[:5], a[7], log)
        yield
        pair_copy.wait_recv()
        side[t, zl] = side[t, zl] + y_in[t].astype(F32)
        wide = (lambda q: side[t, zl, q], axes[2][0], c1_out.at[t], c1_in.at[t], sems(2, 0))
        direct_first(*wide, log)
        for a in ring:
            ring_second(*a, log)
        yield
        here = coord[axes[2][0]]
        side[t, zl, here] = direct_last(*wide)
        thin = (lambda q: side[t, zl, here, q], axes[2][1], c2_out.at[t], c2_in.at[t], sems(2, 1))
        direct_first(*thin, log)
        for p in range(2):
            first = coord[axes[p][0]]
            part[t, p, first] = ring_last(*ring[p][:3], *ring[p][5:])
            for e in range(7):
                a, w = (e + 1, zl) if e < 3 else (e - 3, 1 - zl)
                z_out[t, p, e] = part[t, p, first, place[axes[p][1], a], w].astype(BF16)
                line_copy(p, e).start()
            log.append(line_copy(p, None))
        yield
        out = []
        for p in range(2):
            total = part[t, p, coord[axes[p][0]], coord[axes[p][1]], zl]
            line_copy(p, None).wait_recv()
            for e in range(7):
                total = total + z_in[t, p, e].astype(F32)
            out.append(total)
        out.append(direct_last(*thin))
        log.append(pair_copy)
        result[t] = jnp.concatenate(out, axis=0)

    result, sq, err_sum, act_own, act_all, off_own, off_all = {}, {}, {}, {}, {}, {}, {}
    shared = {}

    def g_copy(j):
        return rcopy(g_out.at[j], g_in.at[j], g_send.at[j], g_recv.at[j], sibling)

    def gradient(t, first, last):
        @pl.loop(first, last, unroll=2)
        def _(j):
            both = jnp.concatenate([slab(gx, t, j), slab(ge, t, j)], axis=0)
            out = dot(tmat[t], both)
            cols = pl.ds(pl.multiple_of(512 * j, 512), 512)
            if t == 0:
                gacc[j] = out[LAT:]
                grad_ref[:, cols] = out[:LAT]
            else:
                g_out[j] = (gacc[j] + out[LAT:]).astype(BF16)
                g_copy(j).start()
                grad_ref[:, cols] = grad_ref[:, cols] + out[:LAT]

    def steps(t):
        centered = (own_rows(t) - center).astype(BF16)
        log_x, log_r, log_e = [], [], []
        yield from gather(gx, t, centered, gx_send, gx_recv, log_x)
        if t == 0:
            for j in range(8):
                weight_copy(j).wait_recv()
            small_copy.wait_recv()
            shared["bias"] = jnp.concatenate([sm[0:1, :], sm_in[0:1, :]], axis=1)
            shared["norms"] = jnp.concatenate([sm[1:2, :], sm_in[1:2, :]], axis=1)
        norms = shared["norms"]
        project(gx, t, pre, 0)
        yield
        project(gx, t, pre, 1)
        yield
        pre[t] = pre[t] + shared["bias"]
        acts[t] = jnp.maximum(pre[t], 0.0).astype(BF16)

        @pl.loop(0, 8, unroll=4)
        def _(j):
            jz, jx = j // 4, lax.rem(j, 4)
            out = dot(acts[t, :CHUNK], all_weights(j))
            for yy in range(4):
                cols = slice(128 * yy, 128 * (yy + 1))
                part[t, 0, jx, yy, jz] = out[:MAIN, cols]
                part[t, 1, yy, jx, jz] = out[MAIN : 2 * MAIN, cols]
                if t == 0:
                    side[t, jz, jx, yy] = out[2 * MAIN :, cols]
                else:
                    side[t, jz, yy, jx] = out[2 * MAIN :, cols]

        ready = scatter(t, log_r)
        next(ready)
        flush(log_x)
        yield
        yield from ready
        err = result[t] + center - own_rows(t)
        sq[t] = jnp.sum(err * err)
        err_sum[t] = jnp.sum(err, axis=0, keepdims=True)
        derr = (2.0 / TOK * err).astype(BF16)
        ready = gather(ge, t, derr, ge_send, ge_recv, log_e)
        next(ready)
        flush(log_r)
        yield
        yield from ready
        sent.extend(log_e)
        project(ge, t, dacc, 0)
        yield
        project(ge, t, dacc, 1)
        yield
        dacts = dacc[t] + sparsity_coeff / TOK * norms
        dpre = jnp.where(pre[t] > 0, dacts, 0.0).astype(BF16)
        act = acts[t]
        tmat[t] = jnp.concatenate([dpre, act], axis=0).T
        off_own[t] = jnp.sum(dpre[:CHUNK].astype(F32), axis=0, keepdims=True)
        off_all[t] = off_own[t] + jnp.sum(dpre[CHUNK:].astype(F32), axis=0, keepdims=True)
        act_own[t] = jnp.sum(act[:CHUNK].astype(F32), axis=0, keepdims=True)
        act_all[t] = act_own[t] + jnp.sum(act[CHUNK:].astype(F32), axis=0, keepdims=True)
        yield
        if t == 0:
            gradient(0, 0, 4)
            yield
            gradient(0, 4, 8)
            yield

    run = [steps(0), steps(1)]
    plan = "0101010w0100101011010101010101000100111"
    for who in plan:
        if who == "w":
            prepare()
        else:
            next(run[int(who)])
    for one in run:
        assert next(one, one) is one
    off = off_own[0] + off_own[1]
    offs = off_all[0] + off_all[1]
    act_tot = act_all[0] + act_all[1]
    spars = jnp.sum((act_own[0] + act_own[1]) * shared["norms"])

    sums[...] = jnp.zeros((2, 8, LAT), F32)
    for k in range(2):
        sums[k, 0:1, :] = offs[:, LAT * k : LAT * (k + 1)]
        sums[k, 1:2, :] = act_tot[:, LAT * k : LAT * (k + 1)]
    sums_copy = rcopy(sums.at[1], sums_in, pair_send.at[11], pair_recv.at[11], sibling)
    sums_copy.start()

    hi = off.astype(BF16)
    rest = off - hi.astype(F32)
    mid = rest.astype(BF16)
    low = (rest - mid.astype(F32)).astype(BF16)
    row = lax.broadcasted_iota(jnp.int32, (16, 512), 0)
    terms = jnp.where(
        row == 0, hi.astype(F32),
        jnp.where(row == 1, mid.astype(F32), jnp.where(row == 2, low.astype(F32), 0.0)),
    ).astype(BF16)
    for j in range(8):
        enc = jnp.sum(dot(terms, all_weights(j)), axis=0, keepdims=True)
        for yy in range(4):
            vx[(j % 4) * 4 + yy, j // 4 : j // 4 + 1, :] = -enc[:, 128 * yy : 128 * (yy + 1)]
    scalars = jnp.where(lane == 0, sq[0] + sq[1], jnp.where(lane == 1, spars, 0.0))
    for k in range(16):
        vx[k, 2:8, :] = jnp.broadcast_to(scalars, (6, 128))
    here = x * 4 + y
    sub = lax.broadcasted_iota(jnp.int32, (8, 128), 0)
    vx[here] = vx[here] + jnp.where(sub == zl, 2.0 / TOK * (err_sum[0] + err_sum[1]), 0.0)

    def v_plane(e):
        a, b = (e + 1) // 4, (e + 1) % 4
        return rcopy(
            vx.at[place["x", a] * 4 + place["y", b]], vx_in.at[e], v_send.at[0], v_recv.at[0], plane[e]
        )

    def v_column(e):
        return rcopy(vz, vz_in.at[e], v_send.at[1], v_recv.at[1], column[e])

    v_planes = rcopy(vx_in, vx_in, v_send.at[0], v_recv.at[0], sibling)
    v_columns = rcopy(vz_in, vz_in, v_send.at[1], v_recv.at[1], sibling)

    for e in range(15):
        v_plane(e).start()
    gradient(1, 0, 4)
    total = vx[here]
    v_planes.wait_recv()
    for e in range(15):
        total = total + vx_in[e]
    vz[...] = total
    for e in range(7):
        v_column(e).start()
    gradient(1, 4, 8)
    v_columns.wait_recv()
    for e in range(7):
        total = total + vz_in[e]
    sums_copy.wait_recv()

    small_ref[...] = jnp.zeros((8, LAT), F32)
    small_ref[0:1, :] = sums[0, 0:1, :] + sums_in[0:1, :]
    small_ref[1:2, :] = sparsity_coeff / TOK * (sums[0, 1:2, :] + sums_in[1:2, :]) / sm[1:2, :]
    slot = jnp.where(zl == 0, total[0:1], total[1:2])
    small_ref[2:3, 0:64] = jnp.where(core == 0, slot[:, :64], slot[:, 64:])
    small_ref[3:4, 0:128] = total[2:3]

    flush(sent)
    for j in range(8):
        weight_copy(j).wait_send()
    for c in pair + [small_copy, sums_copy]:
        c.wait_send()
    v_planes.wait_send()
    v_columns.wait_send()
    for j in range(8):
        cols = slice(512 * j, 512 * (j + 1))
        g_copy(j).wait_recv()
        grad_ref[:, cols] = grad_ref[:, cols] + g_in[j].astype(F32)
    for j in range(8):
        g_copy(j).wait_send()


def step_kernel(inputs, center, offset, dictionary):
    vm = pltpu.VMEM
    dma = pltpu.SemaphoreType.DMA
    block = (PART, 128)
    main, side = (MAIN, 128), (SIDE, 128)
    return pl.pallas_call(
        kernel,
        out_shape=[
            jax.ShapeDtypeStruct((LAT, WIDTH), F32),
            jax.ShapeDtypeStruct((8, LAT), F32),
        ],
        in_specs=[pl.BlockSpec(memory_space=pltpu.HBM)] * 4,
        out_specs=[pl.BlockSpec(memory_space=pltpu.VMEM)] * 2,
        scratch_shapes=[
            vm((64, 2 * ROWS), BF16),
            vm((1, 64), F32),
            vm((1, LAT), F32),
            vm((2, 8, LAT, 512), BF16),
            vm((2, 3, 4, 4, 4) + block, BF16),
            vm((2, 3, 4, 4, 4) + block, BF16),
            vm((2, 2 * CHUNK, 512), F32),
            vm((2, 2 * CHUNK, 512), F32),
            vm((2, 2 * CHUNK, 512), BF16),
            vm((2, 512, 4 * CHUNK), BF16),
            vm((8, LAT, 512), F32),
            vm((2, ROWS, 128), BF16),
            vm((ROWS, 128), BF16),
            vm((8, 128), F32),
            vm((8, 128), F32),
            vm((8, LAT), F32),
            vm((8, LAT), F32),
            vm((2, 8, LAT), F32),
            vm((8, LAT), F32),
            vm((2, 2, 4, 4, 2) + main, F32),
            vm((2, 2, 2, 2, 2) + main, BF16),
            vm((2, 2, 2, 2, 2) + main, BF16),
            vm((2, 2, 2, 4, 2) + main, BF16),
            vm((2, 2, 2, 4, 2) + main, BF16),
            vm((2, 2, 7) + main, BF16),
            vm((2, 2, 7) + main, BF16),
            vm((2, 2, 4, 4) + side, F32),
            vm((2, 4, 4) + side, BF16),
            vm((2, 4, 4) + side, BF16),
            vm((2, 3, 4) + side, BF16),
            vm((2, 3, 4) + side, BF16),
            vm((2, 3) + side, BF16),
            vm((2, 3) + side, BF16),
            vm((8, LAT, 512), BF16),
            vm((8, LAT, 512), BF16),
            vm((16, 8, 128), F32),
            vm((15, 8, 128), F32),
            vm((8, 128), F32),
            vm((7, 8, 128), F32),
            dma((11,)),
            dma((12,)),
            dma((12,)),
            dma((2, 3, 3)),
            dma((2, 3, 6)),
            dma((2, 3, 3)),
            dma((2, 3, 6)),
            dma((2, 3, 9)),
            dma((2, 3, 9)),
            dma((8,)),
            dma((8,)),
            dma((2,)),
            dma((2,)),
        ],
        compiler_params=pltpu.CompilerParams(
            collective_id=0, has_side_effects=True, vmem_limit_bytes=VMEM_LIMIT
        ),
        cost_estimate=pl.CostEstimate(
            flops=12 * 2**30, bytes_accessed=160 * 2**20, transcendentals=0
        ),
        name="step",
    )(*[pltpu.with_memory_space_constraint(v, pltpu.HBM) for v in (inputs, center, offset, dictionary)])


def small_kernel(small, offset, offset_mean, offset_var, center, center_mean, center_var, *outs):
    rows = (
        (offset, small[0:1, :], offset_mean, offset_var),
        (center, small[2:3, 0:64], center_mean, center_var),
    )
    for k, (param, grad, mean, var) in enumerate(rows):
        new = adam_update(param[...], grad, mean[...], var[...])
        for n in range(3):
            outs[3 * k + n][...] = new[n]
    scalars = small[3:4, 0:128]
    lane = lax.broadcasted_iota(jnp.int32, (1, 128), 1)
    weight = jnp.where(lane == 0, 1.0, jnp.where(lane == 1, sparsity_coeff, 0.0))
    outs[6][...] = jnp.sum(scalars * weight, axis=1, keepdims=True) / (TOK * WIDTH)


def small_step(small, *rows):
    shapes = [(1, LAT)] * 3 + [(1, 64)] * 3 + [(1, 1)]
    return pl.pallas_call(
        small_kernel,
        out_shape=[jax.ShapeDtypeStruct(s, F32) for s in shapes],
        in_specs=[pl.BlockSpec(memory_space=pltpu.VMEM)] * 7,
        out_specs=[pl.BlockSpec(memory_space=pltpu.VMEM)] * 7,
        compiler_params=pltpu.CompilerParams(vmem_limit_bytes=2**20),
        name="small",
    )(small, *[r.reshape(1, -1) for r in rows])


def body(
    inputs,
    dictionary,
    offset,
    center,
    dict_mean,
    dict_var,
    offset_mean,
    offset_var,
    center_mean,
    center_var,
):
    grad, small = step_kernel(
        inputs.T, center.reshape(1, -1), offset.reshape(1, -1), dictionary
    )
    g_dict = grad + small[1][:, None] * dictionary
    fresh_dict, mean_dict, var_dict = adam_update(dictionary, g_dict, dict_mean, dict_var)
    *rows, loss = small_step(
        small, offset, offset_mean, offset_var, center, center_mean, center_var
    )
    fresh_offset, mean_offset, var_offset, fresh_center, mean_center, var_center = [
        r.reshape(-1) for r in rows
    ]
    loss_value = loss.reshape(())
    return (
        fresh_dict,
        fresh_offset,
        fresh_center,
        mean_dict,
        var_dict,
        mean_offset,
        var_offset,
        mean_center,
        var_center,
        loss_value,
    )


def solution(mesh):
    return jax.shard_map(
        body,
        mesh=mesh,
        in_specs=(
            P("dp", "latent"),
            P("latent", None),
            P("latent"),
            P("latent"),
            P("latent", None),
            P("latent", None),
            P("latent"),
            P("latent"),
            P("latent"),
            P("latent"),
        ),
        out_specs=(
            P("latent", None),
            P("latent"),
            P("latent"),
            P("latent", None),
            P("latent", None),
            P("latent"),
            P("latent"),
            P("latent"),
            P("latent"),
            P(),
        ),
        check_vma=False,
    )
```

```python
import jax
import jax.numpy as jnp
from jax import lax
from jax.experimental import pallas as pl
from jax.experimental.pallas import tpu as pltpu
from jax.sharding import PartitionSpec as P

STEP = 1000
sparsity_coeff = 5.0
beta_one = 0.9
beta_two = 0.999
learn_rate = 0.001
adam_eps = 1e-08
norm_eps = 1e-06

TOK = 1152
WIDTH = 4096
ROWS = 288
CHUNKS = 3
CHUNK = 96
PART = 32
MAIN = 48
LAT = 256
BLOCK = 16
VMEM_LIMIT = 42 * 1024 * 1024
F32 = jnp.float32
BF16 = jnp.bfloat16
MESH = pl.DeviceIdType.MESH


def adam_update(param, grad, mean, var):
    mean_new = beta_one * mean + (1.0 - beta_one) * grad
    var_new = beta_two * var + (1.0 - beta_two) * grad * grad
    rate = learn_rate / (1.0 - beta_one**STEP)
    corr_two = 1.0 / (1.0 - beta_two**STEP)
    param_new = param - rate * mean_new / (jnp.sqrt(var_new * corr_two) + adam_eps)
    return (param_new, mean_new, var_new)


def mod4(v):
    return lax.rem(v + 4, 4)


def dot(a, b):
    return jnp.dot(a, b, preferred_element_type=F32)


def dot_nt(a, b):
    return lax.dot_general(a, b, (((1,), (1,)), ((), ())), preferred_element_type=F32)


def kernel(
    inputs_hbm, center_hbm, offset_hbm, dict_ref,
    grad_ref, small_ref,
    inputs_ref, center_ref, offset_ref,
    weights, gx, ge, pre, dacc, acts, tmat, gacc,
    raw, raw_in, cen, cen_in, sm, sm_in, sums, sums_in,
    part, b0_out, b0_in, a0_out, a0_in, z_out, z_in,
    g_out, g_in,
    vx, vx_in, vz, vz_in,
    load_sem, pair_send, pair_recv,
    gx_send, gx_recv, ge_send, ge_recv, rs_send, rs_recv,
    g_send, g_recv, v_send, v_recv,
):
    h = lax.axis_index("dp")
    i = lax.axis_index("latent")
    core = lax.rem(i, 2)
    y = lax.rem(i // 2, 4)
    x = lax.rem(i // 8, 4)
    zl = i // 32
    z = 2 * h + zl

    def dev(xx, yy, zz, cc):
        return (zz // 2, ((lax.rem(zz, 2) * 4 + xx) * 4 + yy) * 2 + cc)

    coord = {"x": x, "y": y, "z": z}
    place = {(a, s): mod4(coord[a] + s) for a in coord for s in range(4)}
    near = {}
    for s in range(1, 4):
        near["x", s] = dev(place["x", s], y, z, core)
        near["y", s] = dev(x, place["y", s], z, core)
        near["z", s] = dev(x, y, place["z", s], core)

    def along(axis, step):
        return near[axis, step % 4]

    sibling = dev(x, y, z, 1 - core)
    far_z = 2 * h + 1 - zl
    other_z = dev(x, y, far_z, core)

    def rcopy(src, dst, ssem, rsem, device):
        return pltpu.make_async_remote_copy(
            src_ref=src, dst_ref=dst, send_sem=ssem, recv_sem=rsem,
            device_id=device, device_id_type=MESH,
        )

    def load(j):
        return pltpu.make_async_copy(
            dict_ref.at[:, pl.ds(512 * j, 512)], gacc.at[j], load_sem.at[j]
        )

    first_loads = [
        pltpu.make_async_copy(src, dst, load_sem.at[8 + k])
        for k, (src, dst) in enumerate(
            ((inputs_hbm, inputs_ref), (center_hbm, center_ref), (offset_hbm, offset_ref))
        )
    ]
    for c in first_loads:
        c.start()
    for j in range(8):
        load(j).start()

    plane = [
        dev(place["x", a], place["y", b], z, core) for a in range(4) for b in range(4) if a + b
    ]
    column = [
        dev(x, y, place["z", a], c)
        for a in range(4) for b, c in enumerate((core, 1 - core)) if a + b
    ]
    across = {
        axis: [near[axis, a] for a in range(1, 4)]
        + [
            dev(place["x", a], y, far_z, core) if axis == "x" else dev(x, place["y", a], far_z, core)
            for a in range(4)
        ]
        for axis in ("x", "y")
    }
    barrier = pltpu.get_barrier_semaphore()
    partners = plane + column + across["x"][4:] + across["y"][4:]
    for partner in partners:
        pl.semaphore_signal(barrier, inc=1, device_id=partner, device_id_type=MESH)

    for c in first_loads:
        c.wait()
    lane = lax.broadcasted_iota(jnp.int32, (1, 128), 1)
    mine = (lane // 64) == core
    both = inputs_ref[...].astype(F32)
    both = jnp.concatenate([both, both], axis=0).T
    raw[...] = jnp.where(mine, both, 0.0).astype(BF16).reshape(2, ROWS, 128)
    cboth = jnp.concatenate([center_ref[...], center_ref[...]], axis=1)
    cen[...] = jnp.broadcast_to(jnp.where(mine, cboth, 0.0), (8, 128))
    pl.semaphore_wait(barrier, len(partners))

    pair = [
        rcopy(raw.at[1 - core], raw_in, pair_send.at[0], pair_recv.at[0], sibling),
        rcopy(cen, cen_in, pair_send.at[1], pair_recv.at[1], sibling),
    ]
    for c in pair:
        c.start()
    for c in pair:
        c.wait_recv()
    center = cen[0:1, :] + cen_in[0:1, :]

    def own_rows(t):
        rows = pl.ds(CHUNK * t, CHUNK)
        return raw[core, rows].astype(F32) + raw_in[rows].astype(F32)

    sent = []

    def flush(log):
        for c in log:
            c.wait_send()
        log.clear()

    orders = (("y", "x", "z"), ("x", "z", "y"), ("z", "y", "x"))
    dirs = ((0, 1), (1, -1))

    def gather(buf, t, block, ssem, rsem, log):
        at = [tuple(coord[a] for a in reversed(o)) for o in orders]
        for p in range(3):
            buf[(t, p) + at[p]] = block[PART * p : PART * (p + 1)]

        def chunk(p, f, step):
            q = place[orders[p][f], step % 4]
            return (t, p) + at[p][: 2 - f] + (q,)

        def send(p, f, e, idx, step):
            ref = buf.at[idx]
            rcopy(
                ref, ref, ssem.at[t, p, f], rsem.at[t, p, e], along(orders[p][f], step)
            ).start()

        def whole(p, f, e, idx):
            ref = buf.at[idx]
            return rcopy(ref, ref, ssem.at[t, p, f], rsem.at[t, p, e], sibling)

        def triple(p, f):
            return (t, p) + at[p][: 2 - f] + (pl.ds(0, 3),)

        def double(p, f):
            return (t, p) + at[p][: 2 - f] + (pl.ds(0, 2),)

        def single(p, f):
            return (t, p) + at[p][: 2 - f] + (0,)

        for p in range(3):
            for step in (1, 3, 2):
                send(p, 0, 0, chunk(p, 0, 0), step)
            log.append(whole(p, 0, 0, triple(p, 0)))
        yield
        for p in range(3):
            whole(p, 0, 0, triple(p, 0)).wait_recv()
            for k, step in dirs:
                send(p, 1, 1, chunk(p, 1, 0), step)
            log.append(whole(p, 1, 1, triple(p, 1)))
        yield
        for p in range(3):
            whole(p, 1, 1, double(p, 1)).wait_recv()
            for k, step in dirs:
                send(p, 1, 2, chunk(p, 1, -step) + (pl.ds(2 * k, 2),), step)
        yield
        for p in range(3):
            whole(p, 1, 2, single(p, 1)).wait_recv()
            for k, step in dirs:
                send(p, 2, 3, chunk(p, 2, 0) + (pl.ds(2 * k, 2),), step)
            log.append(whole(p, 2, 3, triple(p, 2)))
        for p in range(3):
            for k, step in dirs:
                send(p, 2, 4, chunk(p, 2, 0) + (pl.ds(2 - 2 * k, 2),), step)
        yield
        for p in range(3):
            whole(p, 2, 3, single(p, 2)).wait_recv()
            for k, step in dirs:
                send(p, 2, 5, chunk(p, 2, -step) + (pl.ds(2 * k, 2),), step)
        yield
        for e in (4, 5):
            for p in range(3):
                whole(p, 2, e, single(p, 2)).wait_recv()

    def weight_copy(j):
        return rcopy(
            weights.at[0, j], weights.at[1, j], pair_send.at[2 + j], pair_recv.at[2 + j], sibling
        )

    small_copy = rcopy(sm, sm_in, pair_send.at[10], pair_recv.at[10], sibling)

    def prepare():
        sq = jnp.zeros((LAT, 1), F32)
        for j in range(8):
            load(j).wait()
            block = gacc[j]
            weights[0, j] = block.astype(BF16)
            weight_copy(j).start()
            sq = sq + jnp.sum(block * block, axis=1, keepdims=True)
        norm = jnp.sqrt(sq + norm_eps)
        sm[...] = jnp.zeros((8, LAT), F32)
        sm[0:1, :] = offset_ref[...]
        sm[1:2, :] = jnp.broadcast_to(norm, (LAT, 128)).T[0:1, :]
        small_copy.start()

    def slab(buf, t, j):
        jz, jx = j // 4, j % 4
        rows = []
        for r in range(2):
            zz = 2 * (h if r == 0 else 1 - h) + jz
            for p in range(3):
                cols = []
                for yy in range(4):
                    idx = ((zz, jx, yy), (yy, zz, jx), (jx, yy, zz))[p]
                    cols.append(buf[(t, p) + idx])
                rows.append(jnp.concatenate(cols, axis=1))
        return jnp.concatenate(rows, axis=0)

    def all_weights(j):
        return jnp.concatenate([weights[0, j], weights[1, j]], axis=0)

    def project(buf, t, acc, half):
        rows = jnp.concatenate([slab(buf, t, 4 * half + jx) for jx in range(4)], axis=1)
        cols = jnp.concatenate([all_weights(4 * half + jx) for jx in range(4)], axis=1)
        out = dot_nt(rows, cols)
        acc[t] = out if half == 0 else acc[t] + out

    def ring_first(src, lead, axis, b_out, b_in, sems, log):
        q = place[axis, 2]
        for k, step in dirs:
            b_out[k][...] = src[lead + (q, pl.ds(2 * k, 2))].astype(BF16)
            c = rcopy(b_out[k], b_in[k], sems[0][k], sems[1][k], along(axis, step))
            c.start()
            log.append(c)

    def ring_second(src, lead, axis, b_out, b_in, a_out, a_in, sems, log):
        for k, step in dirs:
            q = place[axis, step % 4]
            mix, rest = pl.ds(2 * k, 2), pl.ds(2 - 2 * k, 2)
            a_out[k][rest] = src[lead + (q, rest)].astype(BF16)
            rcopy(b_out[k], b_in[k], sems[0][k], sems[1][k], along(axis, step)).wait_recv()
            a_out[k][mix] = (src[lead + (q, mix)] + b_in[k][...].astype(F32)).astype(BF16)
            c = rcopy(a_out[k], a_in[k], sems[0][2 + k], sems[1][2 + k], along(axis, step))
            c.start()
            log.append(c)

    def ring_last(src, lead, axis, a_out, a_in, sems):
        for k, step in dirs:
            rcopy(a_out[k], a_in[k], sems[0][2 + k], sems[1][2 + k], along(axis, step)).wait_recv()
        return src[lead + (coord[axis],)] + a_in[0][...].astype(F32) + a_in[1][...].astype(F32)

    def scatter(t, log):
        axes = (("x", "y"), ("y", "x"))

        def some(ref, *lead):
            return [ref.at[lead + (k,)] for k in range(ref.shape[len(lead)])]

        def sems(p, s):
            return (
                [rs_send.at[t, p, 4 * s + e] for e in range(4)],
                [rs_recv.at[t, p, 4 * s + e] for e in range(4)],
            )

        def line_copy(p, e):
            src, dst = (z_out.at[t, p], z_in.at[t, p]) if e is None else (z_out.at[t, p, e], z_in.at[t, p, e])
            device = sibling if e is None else across[axes[p][1]][e]
            return rcopy(src, dst, rs_send.at[t, p, 4], rs_recv.at[t, p, 4], device)

        ring = [
            (part, (t, p), axes[p][0], some(b0_out, t, p), some(b0_in, t, p), some(a0_out, t, p), some(a0_in, t, p), sems(p, 0))
            for p in range(2)
        ]
        for a in ring:
            ring_first(*a[:5], a[7], log)
        yield
        for a in ring:
            ring_second(*a, log)
        yield
        for p in range(2):
            first = coord[axes[p][0]]
            part[t, p, first] = ring_last(*ring[p][:3], *ring[p][5:])
            for e in range(7):
                a, w = (e + 1, zl) if e < 3 else (e - 3, 1 - zl)
                z_out[t, p, e] = part[t, p, first, place[axes[p][1], a], w].astype(BF16)
                line_copy(p, e).start()
            log.append(line_copy(p, None))
        yield
        out = []
        for p in range(2):
            total = part[t, p, coord[axes[p][0]], coord[axes[p][1]], zl]
            line_copy(p, None).wait_recv()
            for e in range(7):
                total = total + z_in[t, p, e].astype(F32)
            out.append(total)
        result[t] = jnp.concatenate(out, axis=0)

    result, sq, err_sum, act_own, act_all, off_own, off_all = {}, {}, {}, {}, {}, {}, {}
    shared = {}

    def g_copy(j):
        return rcopy(g_out.at[j], g_in.at[j], g_send.at[j], g_recv.at[j], sibling)

    def gradient(t, first, last):
        @pl.loop(first, last, unroll=2)
        def _(j):
            both = jnp.concatenate([slab(gx, t, j), slab(ge, t, j)], axis=0)
            out = dot(tmat[t], both)
            cols = pl.ds(pl.multiple_of(512 * j, 512), 512)
            if t < CHUNKS - 1:
                gacc[j] = out[LAT:] if t == 0 else gacc[j] + out[LAT:]
            else:
                g_out[j] = (gacc[j] + out[LAT:]).astype(BF16)
                g_copy(j).start()
            grad_ref[:, cols] = out[:LAT] if t == 0 else grad_ref[:, cols] + out[:LAT]

    def steps(t):
        centered = (own_rows(t) - center).astype(BF16)
        log_x, log_r, log_e = [], [], []
        yield from gather(gx, t, centered, gx_send, gx_recv, log_x)
        if t == 0:
            for j in range(8):
                weight_copy(j).wait_recv()
            small_copy.wait_recv()
            shared["bias"] = jnp.concatenate([sm[0:1, :], sm_in[0:1, :]], axis=1)
            shared["norms"] = jnp.concatenate([sm[1:2, :], sm_in[1:2, :]], axis=1)
        norms = shared["norms"]
        project(gx, t, pre, 0)
        yield
        project(gx, t, pre, 1)
        yield
        pre[t] = pre[t] + shared["bias"]
        acts[t] = jnp.maximum(pre[t], 0.0).astype(BF16)

        @pl.loop(0, 8, unroll=4)
        def _(j):
            jz, jx = j // 4, lax.rem(j, 4)
            out = dot(acts[t, :CHUNK], all_weights(j))
            for yy in range(4):
                cols = slice(128 * yy, 128 * (yy + 1))
                part[t, 0, jx, yy, jz] = out[:MAIN, cols]
                part[t, 1, yy, jx, jz] = out[MAIN : 2 * MAIN, cols]

        ready = scatter(t, log_r)
        next(ready)
        flush(log_x)
        yield
        yield from ready
        err = result[t] + center - own_rows(t)
        sq[t] = jnp.sum(err * err)
        err_sum[t] = jnp.sum(err, axis=0, keepdims=True)
        derr = (2.0 / TOK * err).astype(BF16)
        ready = gather(ge, t, derr, ge_send, ge_recv, log_e)
        next(ready)
        flush(log_r)
        yield
        yield from ready
        sent.extend(log_e)
        project(ge, t, dacc, 0)
        yield
        project(ge, t, dacc, 1)
        yield
        dacts = dacc[t] + sparsity_coeff / TOK * norms
        dpre = jnp.where(pre[t] > 0, dacts, 0.0).astype(BF16)
        act = acts[t]
        tmat[t] = jnp.concatenate([dpre, act], axis=0).T
        off_own[t] = jnp.sum(dpre[:CHUNK].astype(F32), axis=0, keepdims=True)
        off_all[t] = off_own[t] + jnp.sum(dpre[CHUNK:].astype(F32), axis=0, keepdims=True)
        act_own[t] = jnp.sum(act[:CHUNK].astype(F32), axis=0, keepdims=True)
        act_all[t] = act_own[t] + jnp.sum(act[CHUNK:].astype(F32), axis=0, keepdims=True)
        yield
        if t < CHUNKS - 1:
            gradient(t, 0, 4)
            yield
            gradient(t, 4, 8)
            yield

    run = [steps(t) for t in range(CHUNKS)]
    plan = "0210w021010120010210121022120102102101021002100211201211222"
    for who in plan:
        if who == "w":
            prepare()
        else:
            next(run[int(who)])
    for one in run:
        assert next(one, one) is one
    off = sum(off_own.values())
    offs = sum(off_all.values())
    act_tot = sum(act_all.values())
    spars = jnp.sum(sum(act_own.values()) * shared["norms"])

    sums[...] = jnp.zeros((2, 8, LAT), F32)
    for k in range(2):
        sums[k, 0:1, :] = offs[:, LAT * k : LAT * (k + 1)]
        sums[k, 1:2, :] = act_tot[:, LAT * k : LAT * (k + 1)]
    sums_copy = rcopy(sums.at[1], sums_in, pair_send.at[11], pair_recv.at[11], sibling)
    sums_copy.start()

    hi = off.astype(BF16)
    rest = off - hi.astype(F32)
    mid = rest.astype(BF16)
    low = (rest - mid.astype(F32)).astype(BF16)
    row = lax.broadcasted_iota(jnp.int32, (16, 512), 0)
    terms = jnp.where(
        row == 0, hi.astype(F32),
        jnp.where(row == 1, mid.astype(F32), jnp.where(row == 2, low.astype(F32), 0.0)),
    ).astype(BF16)
    for j in range(8):
        enc = jnp.sum(dot(terms, all_weights(j)), axis=0, keepdims=True)
        for yy in range(4):
            vx[(j % 4) * 4 + yy, j // 4 : j // 4 + 1, :] = -enc[:, 128 * yy : 128 * (yy + 1)]
    scalars = jnp.where(lane == 0, sum(sq.values()), jnp.where(lane == 1, spars, 0.0))
    for k in range(16):
        vx[k, 2:8, :] = jnp.broadcast_to(scalars, (6, 128))
    here = x * 4 + y
    sub = lax.broadcasted_iota(jnp.int32, (8, 128), 0)
    vx[here] = vx[here] + jnp.where(sub == zl, 2.0 / TOK * sum(err_sum.values()), 0.0)

    def v_plane(e):
        a, b = (e + 1) // 4, (e + 1) % 4
        return rcopy(
            vx.at[place["x", a] * 4 + place["y", b]], vx_in.at[e], v_send.at[0], v_recv.at[0], plane[e]
        )

    def v_column(e):
        return rcopy(vz, vz_in.at[e], v_send.at[1], v_recv.at[1], column[e])

    v_planes = rcopy(vx_in, vx_in, v_send.at[0], v_recv.at[0], sibling)
    v_columns = rcopy(vz_in, vz_in, v_send.at[1], v_recv.at[1], sibling)

    for e in range(15):
        v_plane(e).start()
    gradient(CHUNKS - 1, 0, 4)
    total = vx[here]
    v_planes.wait_recv()
    for e in range(15):
        total = total + vx_in[e]
    vz[...] = total
    for e in range(7):
        v_column(e).start()
    gradient(CHUNKS - 1, 4, 8)
    v_columns.wait_recv()
    for e in range(7):
        total = total + vz_in[e]
    sums_copy.wait_recv()

    small_ref[...] = jnp.zeros((8, LAT), F32)
    small_ref[0:1, :] = sums[0, 0:1, :] + sums_in[0:1, :]
    small_ref[1:2, :] = sparsity_coeff / TOK * (sums[0, 1:2, :] + sums_in[1:2, :]) / sm[1:2, :]
    slot = jnp.where(zl == 0, total[0:1], total[1:2])
    small_ref[2:3, 0:64] = jnp.where(core == 0, slot[:, :64], slot[:, 64:])
    small_ref[3:4, 0:128] = total[2:3]

    flush(sent)
    for j in range(8):
        weight_copy(j).wait_send()
    for c in pair + [small_copy, sums_copy]:
        c.wait_send()
    v_planes.wait_send()
    v_columns.wait_send()
    for j in range(8):
        cols = slice(512 * j, 512 * (j + 1))
        g_copy(j).wait_recv()
        grad_ref[:, cols] = grad_ref[:, cols] + g_in[j].astype(F32)
    for j in range(8):
        g_copy(j).wait_send()


def step_kernel(inputs, center, offset, dictionary):
    vm = pltpu.VMEM
    dma = pltpu.SemaphoreType.DMA
    block = (PART, 128)
    main = (MAIN, 128)
    return pl.pallas_call(
        kernel,
        out_shape=[
            jax.ShapeDtypeStruct((LAT, WIDTH), F32),
            jax.ShapeDtypeStruct((8, LAT), F32),
        ],
        in_specs=[pl.BlockSpec(memory_space=pltpu.HBM)] * 4,
        out_specs=[pl.BlockSpec(memory_space=pltpu.VMEM)] * 2,
        scratch_shapes=[
            vm((64, 2 * ROWS), BF16),
            vm((1, 64), F32),
            vm((1, LAT), F32),
            vm((2, 8, LAT, 512), BF16),
            vm((CHUNKS, 3, 4, 4, 4) + block, BF16),
            vm((CHUNKS, 3, 4, 4, 4) + block, BF16),
            vm((CHUNKS, 2 * CHUNK, 512), F32),
            vm((CHUNKS, 2 * CHUNK, 512), F32),
            vm((CHUNKS, 2 * CHUNK, 512), BF16),
            vm((CHUNKS, 512, 4 * CHUNK), BF16),
            vm((8, LAT, 512), F32),
            vm((2, ROWS, 128), BF16),
            vm((ROWS, 128), BF16),
            vm((8, 128), F32),
            vm((8, 128), F32),
            vm((8, LAT), F32),
            vm((8, LAT), F32),
            vm((2, 8, LAT), F32),
            vm((8, LAT), F32),
            vm((CHUNKS, 2, 4, 4, 2) + main, F32),
            vm((CHUNKS, 2, 2, 2, 2) + main, BF16),
            vm((CHUNKS, 2, 2, 2, 2) + main, BF16),
            vm((CHUNKS, 2, 2, 4, 2) + main, BF16),
            vm((CHUNKS, 2, 2, 4, 2) + main, BF16),
            vm((CHUNKS, 2, 7) + main, BF16),
            vm((CHUNKS, 2, 7) + main, BF16),
            vm((8, LAT, 512), BF16),
            vm((8, LAT, 512), BF16),
            vm((16, 8, 128), F32),
            vm((15, 8, 128), F32),
            vm((8, 128), F32),
            vm((7, 8, 128), F32),
            dma((11,)),
            dma((12,)),
            dma((12,)),
            dma((CHUNKS, 3, 3)),
            dma((CHUNKS, 3, 6)),
            dma((CHUNKS, 3, 3)),
            dma((CHUNKS, 3, 6)),
            dma((CHUNKS, 2, 5)),
            dma((CHUNKS, 2, 5)),
            dma((8,)),
            dma((8,)),
            dma((2,)),
            dma((2,)),
        ],
        compiler_params=pltpu.CompilerParams(
            collective_id=0, has_side_effects=True, vmem_limit_bytes=VMEM_LIMIT
        ),
        cost_estimate=pl.CostEstimate(
            flops=12 * 2**30, bytes_accessed=160 * 2**20, transcendentals=0
        ),
        name="step",
    )(*[pltpu.with_memory_space_constraint(v, pltpu.HBM) for v in (inputs, center, offset, dictionary)])


def adam_kernel(
    grad, dictionary, dict_mean, dict_var, small,
    offset, offset_mean, offset_var, center, center_mean, center_var,
    fresh_out, mean_out, var_out, *rest,
):
    outs, (fresh, mean, var, coef, sem) = rest[:7], rest[7:]
    coef[...] = jnp.broadcast_to(small[1:2, :], (128, LAT)).T

    def store(k, i):
        rows = pl.ds(pl.multiple_of(BLOCK * i, BLOCK), BLOCK)
        src, dst = ((fresh, fresh_out), (mean, mean_out), (var, var_out))[k]
        return pltpu.make_async_copy(src.at[rows], dst.at[rows], sem.at[k, i])

    @pl.loop(0, LAT // BLOCK)
    def _(i):
        rows = pl.ds(pl.multiple_of(BLOCK * i, BLOCK), BLOCK)
        param = dictionary[rows, :]
        g = grad[rows, :] + coef[rows, 0:1] * param
        fresh[rows, :], mean[rows, :], var[rows, :] = adam_update(
            param, g, dict_mean[rows, :], dict_var[rows, :]
        )
        for k in range(3):
            store(k, i).start()

    sets = (
        (offset, small[0:1, :], offset_mean, offset_var),
        (center, small[2:3, 0:64], center_mean, center_var),
    )
    for k, (param, g, m, v) in enumerate(sets):
        new = adam_update(param[...], g, m[...], v[...])
        for n in range(3):
            outs[3 * k + n][...] = new[n]
    lane = lax.broadcasted_iota(jnp.int32, (1, 128), 1)
    weight = jnp.where(lane == 0, 1.0, jnp.where(lane == 1, sparsity_coeff, 0.0))
    outs[6][...] = jnp.sum(small[3:4, 0:128] * weight, axis=1, keepdims=True) / (TOK * WIDTH)

    @pl.loop(0, LAT // BLOCK)
    def _(i):
        for k in range(3):
            store(k, i).wait()


def adam_step(grad, dictionary, dict_mean, dict_var, small, *rows):
    big = jax.ShapeDtypeStruct((LAT, WIDTH), F32)
    shapes = [(1, LAT)] * 3 + [(1, 64)] * 3 + [(1, 1)]
    return pl.pallas_call(
        adam_kernel,
        out_shape=[big] * 3 + [jax.ShapeDtypeStruct(s, F32) for s in shapes],
        in_specs=[pl.BlockSpec(memory_space=pltpu.VMEM)] * 11,
        out_specs=[pl.BlockSpec(memory_space=pl.ANY)] * 3
        + [pl.BlockSpec(memory_space=pltpu.VMEM)] * 7,
        scratch_shapes=[pltpu.VMEM((LAT, WIDTH), F32)] * 3
        + [pltpu.VMEM((LAT, 128), F32), pltpu.SemaphoreType.DMA((3, LAT // BLOCK))],
        compiler_params=pltpu.CompilerParams(vmem_limit_bytes=16 * 2**20),
        cost_estimate=pl.CostEstimate(
            flops=16 * 2**20, bytes_accessed=28 * 2**20, transcendentals=2**21
        ),
        name="adam",
    )(grad, dictionary, dict_mean, dict_var, small, *[r.reshape(1, -1) for r in rows])


def body(
    inputs,
    dictionary,
    offset,
    center,
    dict_mean,
    dict_var,
    offset_mean,
    offset_var,
    center_mean,
    center_var,
):
    grad, small = step_kernel(
        inputs.T, center.reshape(1, -1), offset.reshape(1, -1), dictionary
    )
    fresh_dict, mean_dict, var_dict, *rows, loss = adam_step(
        grad, dictionary, dict_mean, dict_var, small,
        offset, offset_mean, offset_var, center, center_mean, center_var,
    )
    fresh_offset, mean_offset, var_offset, fresh_center, mean_center, var_center = [
        r.reshape(-1) for r in rows
    ]
    loss_value = loss.reshape(())
    return (
        fresh_dict,
        fresh_offset,
        fresh_center,
        mean_dict,
        var_dict,
        mean_offset,
        var_offset,
        mean_center,
        var_center,
        loss_value,
    )


def solution(mesh):
    return jax.shard_map(
        body,
        mesh=mesh,
        in_specs=(
            P("dp", "latent"),
            P("latent", None),
            P("latent"),
            P("latent"),
            P("latent", None),
            P("latent", None),
            P("latent"),
            P("latent"),
            P("latent"),
            P("latent"),
        ),
        out_specs=(
            P("latent", None),
            P("latent"),
            P("latent"),
            P("latent", None),
            P("latent", None),
            P("latent"),
            P("latent"),
            P("latent"),
            P("latent"),
            P(),
        ),
        check_vma=False,
    )
```

```python
import jax
import jax.numpy as jnp
from jax import lax
from jax.experimental import pallas as pl
from jax.experimental.pallas import tpu as pltpu
from jax.sharding import PartitionSpec as P

STEP = 1000
sparsity_coeff = 5.0
beta_one = 0.9
beta_two = 0.999
learn_rate = 0.001
adam_eps = 1e-08
norm_eps = 1e-06

TOK = 1152
WIDTH = 4096
ROWS = 288
CHUNK = 144
PART = 48
MAIN, SIDE = 64, 16
LAT = 256
EARLY = 512 - 2 * CHUNK
VMEM_LIMIT = 42 * 1024 * 1024
F32 = jnp.float32
BF16 = jnp.bfloat16
MESH = pl.DeviceIdType.MESH


def adam_update(param, grad, mean, var):
    mean_new = beta_one * mean + (1.0 - beta_one) * grad
    var_new = beta_two * var + (1.0 - beta_two) * grad * grad
    rate = learn_rate / (1.0 - beta_one**STEP)
    scaled = var_new * (1.0 / (1.0 - beta_two**STEP))
    param_new = param - rate * mean_new / (scaled * lax.rsqrt(scaled) + adam_eps)
    return (param_new, mean_new, var_new)


def mod4(v):
    return lax.rem(v + 4, 4)


def dot(a, b):
    return jnp.dot(a, b, preferred_element_type=F32)


def dot_nt(a, b):
    return lax.dot_general(a, b, (((1,), (1,)), ((), ())), preferred_element_type=F32)


def kernel(
    inputs_hbm, center_hbm, offset_hbm, dict_ref,
    grad_ref, small_ref,
    inputs_ref, center_ref, offset_ref,
    weights, gx, ge, pre, dacc, acts, tmat0, tmat1, gacc,
    raw, raw_in, cen, cen_in, sm, sm_in, sums, sums_in,
    part, b0_out, b0_in, a0_out, a0_in, z_out, z_in,
    side, y_out, y_in, c1_out, c1_in, c2_out, c2_in,
    g_out, g_in,
    vx, vx_in, vy, vy_in, vz, vz_in,
    load_sem, pair_send, pair_recv,
    gx_send, gx_recv, ge_send, ge_recv, rs_send, rs_recv,
    g_send, g_recv, v_send, v_recv,
):
    h = lax.axis_index("dp")
    i = lax.axis_index("latent")
    core = lax.rem(i, 2)
    y = lax.rem(i // 2, 4)
    x = lax.rem(i // 8, 4)
    zl = i // 32
    z = 2 * h + zl

    def dev(xx, yy, zz, cc):
        return (zz // 2, ((lax.rem(zz, 2) * 4 + xx) * 4 + yy) * 2 + cc)

    coord = {"x": x, "y": y, "z": z}
    place = {(a, s): mod4(coord[a] + s) for a in coord for s in range(4)}
    near = {}
    for s in range(1, 4):
        near["x", s] = dev(place["x", s], y, z, core)
        near["y", s] = dev(x, place["y", s], z, core)
        near["z", s] = dev(x, y, place["z", s], core)

    def along(axis, step):
        return near[axis, step % 4]

    sibling = dev(x, y, z, 1 - core)
    far_z = 2 * h + 1 - zl
    other_z = dev(x, y, far_z, core)

    def rcopy(src, dst, ssem, rsem, device):
        return pltpu.make_async_remote_copy(
            src_ref=src, dst_ref=dst, send_sem=ssem, recv_sem=rsem,
            device_id=device, device_id_type=MESH,
        )

    def load(j):
        return pltpu.make_async_copy(
            dict_ref.at[:, pl.ds(512 * j, 512)], gacc.at[j], load_sem.at[j]
        )

    first_loads = [
        pltpu.make_async_copy(src, dst, load_sem.at[8 + k])
        for k, (src, dst) in enumerate(
            ((inputs_hbm, inputs_ref), (center_hbm, center_ref), (offset_hbm, offset_ref))
        )
    ]
    for c in first_loads:
        c.start()
    for j in range(8):
        load(j).start()

    column = [
        dev(x, y, place["z", a], c)
        for a in range(4) for b, c in enumerate((core, 1 - core)) if a + b
    ]
    across = {
        axis: [near[axis, a] for a in range(1, 4)]
        + [
            dev(place["x", a], y, far_z, core) if axis == "x" else dev(x, place["y", a], far_z, core)
            for a in range(4)
        ]
        for axis in ("x", "y")
    }
    barrier = pltpu.get_barrier_semaphore()
    partners = column + [d for a in ("x", "y") for d in across[a][:3] + across[a][4:]]
    for partner in partners:
        pl.semaphore_signal(barrier, inc=1, device_id=partner, device_id_type=MESH)

    for c in first_loads:
        c.wait()
    lane = lax.broadcasted_iota(jnp.int32, (1, 128), 1)
    mine = (lane // 64) == core
    both = inputs_ref[...].astype(F32)
    both = jnp.concatenate([both, both], axis=0).T
    raw[...] = jnp.where(mine, both, 0.0).astype(BF16).reshape(2, ROWS, 128)
    cboth = jnp.concatenate([center_ref[...], center_ref[...]], axis=1)
    cen[...] = jnp.broadcast_to(jnp.where(mine, cboth, 0.0), (8, 128))
    pl.semaphore_wait(barrier, len(partners))

    pair = [
        rcopy(raw.at[1 - core], raw_in, pair_send.at[0], pair_recv.at[0], sibling),
        rcopy(cen, cen_in, pair_send.at[1], pair_recv.at[1], sibling),
    ]
    for c in pair:
        c.start()
    for c in pair:
        c.wait_recv()
    center = cen[0:1, :] + cen_in[0:1, :]

    def own_rows(t):
        rows = pl.ds(CHUNK * t, CHUNK)
        return raw[core, rows].astype(F32) + raw_in[rows].astype(F32)

    sent = []

    def flush(log):
        for c in log:
            c.wait_send()
        log.clear()

    orders = (("y", "x", "z"), ("x", "z", "y"), ("z", "y", "x"))
    dirs = ((0, 1), (1, -1))

    def gather(buf, t, block, ssem, rsem, log):
        at = [tuple(coord[a] for a in reversed(o)) for o in orders]
        for p in range(3):
            buf[(t, p) + at[p]] = block[PART * p : PART * (p + 1)]

        def chunk(p, f, step):
            q = place[orders[p][f], step % 4]
            return (t, p) + at[p][: 2 - f] + (q,)

        def send(p, f, e, idx, step):
            ref = buf.at[idx]
            rcopy(
                ref, ref, ssem.at[t, p, f], rsem.at[t, p, e], along(orders[p][f], step)
            ).start()

        def whole(p, f, e, idx):
            ref = buf.at[idx]
            return rcopy(ref, ref, ssem.at[t, p, f], rsem.at[t, p, e], sibling)

        def triple(p, f):
            return (t, p) + at[p][: 2 - f] + (pl.ds(0, 3),)

        def single(p, f):
            return (t, p) + at[p][: 2 - f] + (0,)

        for f in range(2):
            for p in range(3):
                if f == 1:
                    whole(p, 0, 0, triple(p, 0)).wait_recv()
                for step in (1, 3, 2):
                    send(p, f, f, chunk(p, f, 0), step)
                log.append(whole(p, f, f, triple(p, f)))
            yield
        for p in range(3):
            whole(p, 1, 1, triple(p, 1)).wait_recv()
            for k, step in dirs:
                send(p, 2, 3, chunk(p, 2, 0) + (pl.ds(2 * k, 2),), step)
            log.append(whole(p, 2, 3, triple(p, 2)))
        for p in range(3):
            for k, step in dirs:
                send(p, 2, 4, chunk(p, 2, 0) + (pl.ds(2 - 2 * k, 2),), step)
        yield
        for p in range(3):
            whole(p, 2, 3, single(p, 2)).wait_recv()
            for k, step in dirs:
                send(p, 2, 5, chunk(p, 2, -step) + (pl.ds(2 * k, 2),), step)
        yield
        for e in (4, 5):
            for p in range(3):
                whole(p, 2, e, single(p, 2)).wait_recv()

    def weight_copy(j):
        return rcopy(
            weights.at[0, j], weights.at[1, j], pair_send.at[2 + j], pair_recv.at[2 + j], sibling
        )

    small_copy = rcopy(sm, sm_in, pair_send.at[10], pair_recv.at[10], sibling)

    def prepare():
        sq = jnp.zeros((LAT, 1), F32)
        for j in range(8):
            load(j).wait()
            block = gacc[j]
            weights[0, j] = block.astype(BF16)
            weight_copy(j).start()
            sq = sq + jnp.sum(block * block, axis=1, keepdims=True)
        norm = jnp.sqrt(sq + norm_eps)
        sm[...] = jnp.zeros((8, LAT), F32)
        sm[0:1, :] = offset_ref[...]
        sm[1:2, :] = jnp.broadcast_to(norm, (LAT, 128)).T[0:1, :]
        small_copy.start()

    def slab(buf, t, j):
        jz, jx = j // 4, j % 4
        rows = []
        for r in range(2):
            zz = 2 * (h if r == 0 else 1 - h) + jz
            for p in range(3):
                cols = []
                for yy in range(4):
                    idx = ((zz, jx, yy), (yy, zz, jx), (jx, yy, zz))[p]
                    cols.append(buf[(t, p) + idx])
                rows.append(jnp.concatenate(cols, axis=1))
        return jnp.concatenate(rows, axis=0)

    def all_weights(j):
        return jnp.concatenate([weights[0, j], weights[1, j]], axis=0)

    def project(buf, t, acc, half):
        rows = jnp.concatenate([slab(buf, t, 4 * half + jx) for jx in range(4)], axis=1)
        cols = jnp.concatenate([all_weights(4 * half + jx) for jx in range(4)], axis=1)
        out = dot_nt(rows, cols)
        acc[t] = out if half == 0 else acc[t] + out

    def ring_first(src, lead, axis, b_out, b_in, sems, log):
        q = place[axis, 2]
        for k, step in dirs:
            b_out[k][...] = src[lead + (q, pl.ds(2 * k, 2))].astype(BF16)
            c = rcopy(b_out[k], b_in[k], sems[0][k], sems[1][k], along(axis, step))
            c.start()
            log.append(c)

    def ring_second(src, lead, axis, b_out, b_in, a_out, a_in, sems, log):
        for k, step in dirs:
            q = place[axis, step % 4]
            mix, rest = pl.ds(2 * k, 2), pl.ds(2 - 2 * k, 2)
            a_out[k][rest] = src[lead + (q, rest)].astype(BF16)
            rcopy(b_out[k], b_in[k], sems[0][k], sems[1][k], along(axis, step)).wait_recv()
            a_out[k][mix] = (src[lead + (q, mix)] + b_in[k][...].astype(F32)).astype(BF16)
            c = rcopy(a_out[k], a_in[k], sems[0][2 + k], sems[1][2 + k], along(axis, step))
            c.start()
            log.append(c)

    def ring_last(src, lead, axis, a_out, a_in, sems):
        for k, step in dirs:
            rcopy(a_out[k], a_in[k], sems[0][2 + k], sems[1][2 + k], along(axis, step)).wait_recv()
        return src[lead + (coord[axis],)] + a_in[0][...].astype(F32) + a_in[1][...].astype(F32)

    def direct_first(value, axis, out, into, sems, log):
        for k in range(3):
            out[k] = value(place[axis, k + 1]).astype(BF16)
            rcopy(out.at[k], into.at[k], sems[0][0], sems[1][0], along(axis, k + 1)).start()
        log.append(rcopy(out, into, sems[0][0], sems[1][0], sibling))

    def direct_last(value, axis, out, into, sems):
        rcopy(out, into, sems[0][0], sems[1][0], sibling).wait_recv()
        total = value(coord[axis])
        for k in range(3):
            total = total + into[k].astype(F32)
        return total

    def scatter(t, log):
        side_axes = ("x", "y") if t == 0 else ("y", "x")
        axes = (("x", "y"), ("y", "x"), side_axes)

        def some(ref, *lead):
            return [ref.at[lead + (k,)] for k in range(ref.shape[len(lead)])]

        def sems(p, s):
            return (
                [rs_send.at[t, p, 4 * s + e] for e in range(4)],
                [rs_recv.at[t, p, 4 * s + e] for e in range(4)],
            )

        def line_copy(p, e):
            src, dst = (z_out.at[t, p], z_in.at[t, p]) if e is None else (z_out.at[t, p, e], z_in.at[t, p, e])
            device = sibling if e is None else across[axes[p][1]][e]
            return rcopy(src, dst, rs_send.at[t, p, 4], rs_recv.at[t, p, 4], device)

        pair_copy = rcopy(
            y_out.at[t], y_in.at[t], rs_send.at[t, 2, 8], rs_recv.at[t, 2, 8], other_z
        )
        y_out[t] = side[t, 1 - zl].astype(BF16)
        pair_copy.start()
        ring = [
            (part, (t, p), axes[p][0], some(b0_out, t, p), some(b0_in, t, p), some(a0_out, t, p), some(a0_in, t, p), sems(p, 0))
            for p in range(2)
        ]
        for a in ring:
            ring_first(*a[:5], a[7], log)
        yield
        pair_copy.wait_recv()
        side[t, zl] = side[t, zl] + y_in[t].astype(F32)
        wide = (lambda q: side[t, zl, q], axes[2][0], c1_out.at[t], c1_in.at[t], sems(2, 0))
        direct_first(*wide, log)
        for a in ring:
            ring_second(*a, log)
        yield
        here = coord[axes[2][0]]
        side[t, zl, here] = direct_last(*wide)
        thin = (lambda q: side[t, zl, here, q], axes[2][1], c2_out.at[t], c2_in.at[t], sems(2, 1))
        direct_first(*thin, log)
        for p in range(2):
            first = coord[axes[p][0]]
            part[t, p, first] = ring_last(*ring[p][:3], *ring[p][5:])
            for e in range(7):
                a, w = (e + 1, zl) if e < 3 else (e - 3, 1 - zl)
                z_out[t, p, e] = part[t, p, first, place[axes[p][1], a], w].astype(BF16)
                line_copy(p, e).start()
            log.append(line_copy(p, None))
        yield
        out = []
        for p in range(2):
            total = part[t, p, coord[axes[p][0]], coord[axes[p][1]], zl]
            line_copy(p, None).wait_recv()
            for e in range(7):
                total = total + z_in[t, p, e].astype(F32)
            out.append(total)
        out.append(direct_last(*thin))
        log.append(pair_copy)
        result[t] = jnp.concatenate(out, axis=0)

    result, sq, err_sum, act_own, act_all, off_own, off_all = {}, {}, {}, {}, {}, {}, {}
    shared = {}

    def g_copy(j):
        return rcopy(g_out.at[j], g_in.at[j], g_send.at[j], g_recv.at[j], sibling)

    def gradient(t, first, last):
        @pl.loop(first, last, unroll=2)
        def _(j):
            errs = slab(ge, 0, j)
            if t == 0:
                out = dot(tmat0[...], jnp.concatenate([slab(gx, 0, j), errs[:EARLY]], axis=0))
            else:
                rows = [slab(gx, 1, j), slab(ge, 1, j), errs[EARLY:]]
                out = dot(tmat1[...], jnp.concatenate(rows, axis=0))
            cols = pl.ds(pl.multiple_of(512 * j, 512), 512)
            if t == 0:
                gacc[j] = out[LAT:]
                grad_ref[:, cols] = out[:LAT]
            else:
                g_out[j] = (gacc[j] + out[LAT:]).astype(BF16)
                g_copy(j).start()
                grad_ref[:, cols] = grad_ref[:, cols] + out[:LAT]

    def steps(t):
        centered = (own_rows(t) - center).astype(BF16)
        log_x, log_r, log_e = [], [], []
        yield from gather(gx, t, centered, gx_send, gx_recv, log_x)
        if t == 0:
            for j in range(8):
                weight_copy(j).wait_recv()
            small_copy.wait_recv()
            shared["bias"] = jnp.concatenate([sm[0:1, :], sm_in[0:1, :]], axis=1)
            shared["norms"] = jnp.concatenate([sm[1:2, :], sm_in[1:2, :]], axis=1)
        norms = shared["norms"]
        project(gx, t, pre, 0)
        yield
        project(gx, t, pre, 1)
        yield
        pre[t] = pre[t] + shared["bias"]
        acts[t] = jnp.maximum(pre[t], 0.0).astype(BF16)

        @pl.loop(0, 8, unroll=4)
        def _(j):
            jz, jx = j // 4, lax.rem(j, 4)
            out = dot(acts[t, :CHUNK], all_weights(j))
            for yy in range(4):
                cols = slice(128 * yy, 128 * (yy + 1))
                part[t, 0, jx, yy, jz] = out[:MAIN, cols]
                part[t, 1, yy, jx, jz] = out[MAIN : 2 * MAIN, cols]
                if t == 0:
                    side[t, jz, jx, yy] = out[2 * MAIN :, cols]
                else:
                    side[t, jz, yy, jx] = out[2 * MAIN :, cols]

        ready = scatter(t, log_r)
        next(ready)
        flush(log_x)
        yield
        yield from ready
        err = result[t] + center - own_rows(t)
        sq[t] = jnp.sum(err * err)
        err_sum[t] = jnp.sum(err, axis=0, keepdims=True)
        derr = (2.0 / TOK * err).astype(BF16)
        ready = gather(ge, t, derr, ge_send, ge_recv, log_e)
        next(ready)
        flush(log_r)
        yield
        yield from ready
        sent.extend(log_e)
        project(ge, t, dacc, 0)
        yield
        project(ge, t, dacc, 1)
        yield
        dacts = dacc[t] + sparsity_coeff / TOK * norms
        dpre = jnp.where(pre[t] > 0, dacts, 0.0).astype(BF16)
        act = acts[t]
        if t == 0:
            tmat0[...] = jnp.concatenate([dpre, act[:EARLY]], axis=0).T
        else:
            tmat1[...] = jnp.concatenate([dpre, act, acts[0, EARLY:]], axis=0).T
        off_own[t] = jnp.sum(dpre[:CHUNK].astype(F32), axis=0, keepdims=True)
        off_all[t] = off_own[t] + jnp.sum(dpre[CHUNK:].astype(F32), axis=0, keepdims=True)
        act_own[t] = jnp.sum(act[:CHUNK].astype(F32), axis=0, keepdims=True)
        act_all[t] = act_own[t] + jnp.sum(act[CHUNK:].astype(F32), axis=0, keepdims=True)
        yield
        if t == 0:
            gradient(0, 0, 4)
            yield
            gradient(0, 4, 8)
            yield

    run = [steps(0), steps(1)]
    plan = "0101w001001010101010101010010100111"
    for who in plan:
        if who == "w":
            prepare()
        else:
            next(run[int(who)])
    for one in run:
        assert next(one, one) is one
    off = off_own[0] + off_own[1]
    offs = off_all[0] + off_all[1]
    act_tot = act_all[0] + act_all[1]
    spars = jnp.sum((act_own[0] + act_own[1]) * shared["norms"])

    sums[...] = jnp.zeros((2, 8, LAT), F32)
    for k in range(2):
        sums[k, 0:1, :] = offs[:, LAT * k : LAT * (k + 1)]
        sums[k, 1:2, :] = act_tot[:, LAT * k : LAT * (k + 1)]
    sums_copy = rcopy(sums.at[1], sums_in, pair_send.at[11], pair_recv.at[11], sibling)
    sums_copy.start()

    hi = off.astype(BF16)
    rest = off - hi.astype(F32)
    mid = rest.astype(BF16)
    low = (rest - mid.astype(F32)).astype(BF16)
    row = lax.broadcasted_iota(jnp.int32, (16, 512), 0)
    terms = jnp.where(
        row == 0, hi.astype(F32),
        jnp.where(row == 1, mid.astype(F32), jnp.where(row == 2, low.astype(F32), 0.0)),
    ).astype(BF16)
    for j in range(8):
        enc = jnp.sum(dot(terms, all_weights(j)), axis=0, keepdims=True)
        for yy in range(4):
            vx[j % 4, (j // 4) * 4 + yy : (j // 4) * 4 + yy + 1, :] = -enc[:, 128 * yy : 128 * (yy + 1)]
    scalars = jnp.where(lane == 0, sq[0] + sq[1], jnp.where(lane == 1, spars, 0.0))
    for k in range(4):
        vx[k, 8:16, :] = jnp.broadcast_to(scalars, (8, 128))
    sub = lax.broadcasted_iota(jnp.int32, (16, 128), 0)
    vx[x] = vx[x] + jnp.where(sub == zl * 4 + y, 2.0 / TOK * (err_sum[0] + err_sum[1]), 0.0)

    def v_start(k, src, dst, devices):
        for e, device in enumerate(devices):
            rcopy(src(e), dst.at[e], v_send.at[k], v_recv.at[k], device).start()

    def v_done(k, dst):
        return rcopy(dst, dst, v_send.at[k], v_recv.at[k], sibling)

    v_start(0, lambda e: vx.at[place["x", e + 1]], vx_in, across["x"][:3])
    gradient(1, 0, 3)
    v_done(0, vx_in).wait_recv()
    total = vx[x] + vx_in[0] + vx_in[1] + vx_in[2]
    for k in range(4):
        vy[k, 0:1, :] = total[k : k + 1]
        vy[k, 1:2, :] = total[4 + k : 5 + k]
        vy[k, 2:8, :] = total[8:14]
    v_start(1, lambda e: vy.at[place["y", e + 1]], vy_in, across["y"][:3])
    gradient(1, 3, 5)
    v_done(1, vy_in).wait_recv()
    total = vy[y] + vy_in[0] + vy_in[1] + vy_in[2]
    vz[...] = total
    v_start(2, lambda e: vz, vz_in, column)
    gradient(1, 5, 8)
    v_done(2, vz_in).wait_recv()
    for e in range(7):
        total = total + vz_in[e]
    sums_copy.wait_recv()

    small_ref[...] = jnp.zeros((8, LAT), F32)
    small_ref[0:1, :] = sums[0, 0:1, :] + sums_in[0:1, :]
    small_ref[1:2, :] = sparsity_coeff / TOK * (sums[0, 1:2, :] + sums_in[1:2, :]) / sm[1:2, :]
    slot = jnp.where(zl == 0, total[0:1], total[1:2])
    small_ref[2:3, 0:64] = jnp.where(core == 0, slot[:, :64], slot[:, 64:])
    small_ref[3:4, 0:128] = total[2:3]

    flush(sent)
    for j in range(8):
        weight_copy(j).wait_send()
    for c in pair + [small_copy, sums_copy]:
        c.wait_send()
    for k, dst in enumerate((vx_in, vy_in, vz_in)):
        v_done(k, dst).wait_send()
    for j in range(8):
        cols = slice(512 * j, 512 * (j + 1))
        g_copy(j).wait_recv()
        grad_ref[:, cols] = grad_ref[:, cols] + g_in[j].astype(F32)
    for j in range(8):
        g_copy(j).wait_send()


def step_kernel(inputs, center, offset, dictionary):
    vm = pltpu.VMEM
    dma = pltpu.SemaphoreType.DMA
    block = (PART, 128)
    main, side = (MAIN, 128), (SIDE, 128)
    return pl.pallas_call(
        kernel,
        out_shape=[
            jax.ShapeDtypeStruct((LAT, WIDTH), F32),
            jax.ShapeDtypeStruct((8, LAT), F32),
        ],
        in_specs=[pl.BlockSpec(memory_space=pltpu.HBM)] * 4,
        out_specs=[pl.BlockSpec(memory_space=pltpu.VMEM)] * 2,
        scratch_shapes=[
            vm((64, 2 * ROWS), BF16),
            vm((1, 64), F32),
            vm((1, LAT), F32),
            vm((2, 8, LAT, 512), BF16),
            vm((2, 3, 4, 4, 4) + block, BF16),
            vm((2, 3, 4, 4, 4) + block, BF16),
            vm((2, 2 * CHUNK, 512), F32),
            vm((2, 2 * CHUNK, 512), F32),
            vm((2, 2 * CHUNK, 512), BF16),
            vm((512, 512), BF16),
            vm((512, 640), BF16),
            vm((8, LAT, 512), F32),
            vm((2, ROWS, 128), BF16),
            vm((ROWS, 128), BF16),
            vm((8, 128), F32),
            vm((8, 128), F32),
            vm((8, LAT), F32),
            vm((8, LAT), F32),
            vm((2, 8, LAT), F32),
            vm((8, LAT), F32),
            vm((2, 2, 4, 4, 2) + main, F32),
            vm((2, 2, 2, 2, 2) + main, BF16),
            vm((2, 2, 2, 2, 2) + main, BF16),
            vm((2, 2, 2, 4, 2) + main, BF16),
            vm((2, 2, 2, 4, 2) + main, BF16),
            vm((2, 2, 7) + main, BF16),
            vm((2, 2, 7) + main, BF16),
            vm((2, 2, 4, 4) + side, F32),
            vm((2, 4, 4) + side, BF16),
            vm((2, 4, 4) + side, BF16),
            vm((2, 3, 4) + side, BF16),
            vm((2, 3, 4) + side, BF16),
            vm((2, 3) + side, BF16),
            vm((2, 3) + side, BF16),
            vm((8, LAT, 512), BF16),
            vm((8, LAT, 512), BF16),
            vm((4, 16, 128), F32),
            vm((3, 16, 128), F32),
            vm((4, 8, 128), F32),
            vm((3, 8, 128), F32),
            vm((8, 128), F32),
            vm((7, 8, 128), F32),
            dma((11,)),
            dma((12,)),
            dma((12,)),
            dma((2, 3, 3)),
            dma((2, 3, 6)),
            dma((2, 3, 3)),
            dma((2, 3, 6)),
            dma((2, 3, 9)),
            dma((2, 3, 9)),
            dma((8,)),
            dma((8,)),
            dma((3,)),
            dma((3,)),
        ],
        compiler_params=pltpu.CompilerParams(
            collective_id=0, has_side_effects=True, vmem_limit_bytes=VMEM_LIMIT
        ),
        cost_estimate=pl.CostEstimate(
            flops=12 * 2**30, bytes_accessed=160 * 2**20, transcendentals=0
        ),
        name="step",
    )(*[pltpu.with_memory_space_constraint(v, pltpu.HBM) for v in (inputs, center, offset, dictionary)])


def small_kernel(small, offset, offset_mean, offset_var, center, center_mean, center_var, *outs):
    rows = (
        (offset, small[0:1, :], offset_mean, offset_var),
        (center, small[2:3, 0:64], center_mean, center_var),
    )
    for k, (param, grad, mean, var) in enumerate(rows):
        new = adam_update(param[...], grad, mean[...], var[...])
        for n in range(3):
            outs[3 * k + n][...] = new[n]
    scalars = small[3:4, 0:128]
    lane = lax.broadcasted_iota(jnp.int32, (1, 128), 1)
    weight = jnp.where(lane == 0, 1.0, jnp.where(lane == 1, sparsity_coeff, 0.0))
    outs[6][...] = jnp.sum(scalars * weight, axis=1, keepdims=True) / (TOK * WIDTH)


def small_step(small, *rows):
    shapes = [(1, LAT)] * 3 + [(1, 64)] * 3 + [(1, 1)]
    return pl.pallas_call(
        small_kernel,
        out_shape=[jax.ShapeDtypeStruct(s, F32) for s in shapes],
        in_specs=[pl.BlockSpec(memory_space=pltpu.VMEM)] * 7,
        out_specs=[pl.BlockSpec(memory_space=pltpu.VMEM)] * 7,
        compiler_params=pltpu.CompilerParams(vmem_limit_bytes=2**20),
        name="small",
    )(small, *[r.reshape(1, -1) for r in rows])


def body(
    inputs,
    dictionary,
    offset,
    center,
    dict_mean,
    dict_var,
    offset_mean,
    offset_var,
    center_mean,
    center_var,
):
    grad, small = step_kernel(
        inputs.T, center.reshape(1, -1), offset.reshape(1, -1), dictionary
    )
    g_dict = grad + small[1][:, None] * dictionary
    fresh_dict, mean_dict, var_dict = adam_update(dictionary, g_dict, dict_mean, dict_var)
    *rows, loss = small_step(
        small, offset, offset_mean, offset_var, center, center_mean, center_var
    )
    fresh_offset, mean_offset, var_offset, fresh_center, mean_center, var_center = [
        r.reshape(-1) for r in rows
    ]
    loss_value = loss.reshape(())
    return (
        fresh_dict,
        fresh_offset,
        fresh_center,
        mean_dict,
        var_dict,
        mean_offset,
        var_offset,
        mean_center,
        var_center,
        loss_value,
    )


def solution(mesh):
    return jax.shard_map(
        body,
        mesh=mesh,
        in_specs=(
            P("dp", "latent"),
            P("latent", None),
            P("latent"),
            P("latent"),
            P("latent", None),
            P("latent", None),
            P("latent"),
            P("latent"),
            P("latent"),
            P("latent"),
        ),
        out_specs=(
            P("latent", None),
            P("latent"),
            P("latent"),
            P("latent", None),
            P("latent", None),
            P("latent"),
            P("latent"),
            P("latent"),
            P("latent"),
            P(),
        ),
        check_vma=False,
    )
```

```python
import jax
import jax.numpy as jnp
from jax import lax
from jax.experimental import pallas as pl
from jax.experimental.pallas import tpu as pltpu
from jax.sharding import PartitionSpec as P

STEP = 1000
sparsity_coeff = 5.0
beta_one = 0.9
beta_two = 0.999
learn_rate = 0.001
adam_eps = 1e-08
norm_eps = 1e-06

TOK = 1152
WIDTH = 4096
ROWS = 288
CHUNK = 144
PART = 48
MAIN, SIDE = 64, 16
LAT = 256
EARLY = 192
LATE = 384
VMEM_LIMIT = 40 * 1024 * 1024
F32 = jnp.float32
BF16 = jnp.bfloat16
MESH = pl.DeviceIdType.MESH


def adam_update(param, grad, mean, var):
    mean_new = beta_one * mean + (1.0 - beta_one) * grad
    var_new = beta_two * var + (1.0 - beta_two) * grad * grad
    rate = learn_rate / (1.0 - beta_one**STEP)
    scaled = var_new * (1.0 / (1.0 - beta_two**STEP))
    param_new = param - rate * mean_new / (scaled * lax.rsqrt(scaled) + adam_eps)
    return (param_new, mean_new, var_new)


def mod4(v):
    return lax.rem(v + 4, 4)


def dot(a, b):
    return jnp.dot(a, b, preferred_element_type=F32)


def dot_nt(a, b):
    return lax.dot_general(a, b, (((1,), (1,)), ((), ())), preferred_element_type=F32)


def kernel(
    inputs_hbm, center_hbm, offset_hbm, dict_ref,
    grad_ref, g_in, small_ref,
    inputs_ref, center_ref, offset_ref,
    weights, gx, ge, pre, dacc, acts, tmat0, tmat1, gacc,
    raw, raw_in, cen, cen_in, sm, sm_in, sums, sums_in,
    part, b0_out, b0_in, a0_out, a0_in, z_out, z_in,
    side, y_out, y_in, c1_out, c1_in, c2_out, c2_in,
    g_out,
    vx, vx_in, vy, vy_in, vz, vz_in,
    load_sem, pair_send, pair_recv,
    gx_send, gx_recv, ge_send, ge_recv, rs_send, rs_recv,
    g_send, g_recv, v_send, v_recv,
):
    h = lax.axis_index("dp")
    i = lax.axis_index("latent")
    core = lax.rem(i, 2)
    y = lax.rem(i // 2, 4)
    x = lax.rem(i // 8, 4)
    zl = i // 32
    z = 2 * h + zl

    def dev(xx, yy, zz, cc):
        return (zz // 2, ((lax.rem(zz, 2) * 4 + xx) * 4 + yy) * 2 + cc)

    coord = {"x": x, "y": y, "z": z}
    place = {(a, s): mod4(coord[a] + s) for a in coord for s in range(4)}
    near = {}
    for s in range(1, 4):
        near["x", s] = dev(place["x", s], y, z, core)
        near["y", s] = dev(x, place["y", s], z, core)
        near["z", s] = dev(x, y, place["z", s], core)

    def along(axis, step):
        return near[axis, step % 4]

    sibling = dev(x, y, z, 1 - core)
    far_z = 2 * h + 1 - zl
    other_z = dev(x, y, far_z, core)

    def rcopy(src, dst, ssem, rsem, device):
        return pltpu.make_async_remote_copy(
            src_ref=src, dst_ref=dst, send_sem=ssem, recv_sem=rsem,
            device_id=device, device_id_type=MESH,
        )

    def load(j):
        return pltpu.make_async_copy(
            dict_ref.at[:, pl.ds(512 * j, 512)], gacc.at[j], load_sem.at[j]
        )

    first_loads = [
        pltpu.make_async_copy(src, dst, load_sem.at[8 + k])
        for k, (src, dst) in enumerate(
            ((inputs_hbm, inputs_ref), (center_hbm, center_ref), (offset_hbm, offset_ref))
        )
    ]
    for c in first_loads:
        c.start()
    for j in range(8):
        load(j).start()

    column = [
        dev(x, y, place["z", a], c)
        for a in range(4) for b, c in enumerate((core, 1 - core)) if a + b
    ]
    across = {
        axis: [near[axis, a] for a in range(1, 4)]
        + [
            dev(place["x", a], y, far_z, core) if axis == "x" else dev(x, place["y", a], far_z, core)
            for a in range(4)
        ]
        for axis in ("x", "y")
    }
    barrier = pltpu.get_barrier_semaphore()
    partners = column + [d for a in ("x", "y") for d in across[a][:3] + across[a][4:]]
    for partner in partners:
        pl.semaphore_signal(barrier, inc=1, device_id=partner, device_id_type=MESH)

    for c in first_loads:
        c.wait()
    lane = lax.broadcasted_iota(jnp.int32, (1, 128), 1)
    mine = (lane // 64) == core
    both = inputs_ref[...].astype(F32)
    both = jnp.concatenate([both, both], axis=0).T
    raw[...] = jnp.where(mine, both, 0.0).astype(BF16).reshape(2, ROWS, 128)
    cboth = jnp.concatenate([center_ref[...], center_ref[...]], axis=1)
    cen[...] = jnp.broadcast_to(jnp.where(mine, cboth, 0.0), (8, 128))
    pl.semaphore_wait(barrier, len(partners))

    pair = [
        rcopy(raw.at[1 - core], raw_in, pair_send.at[0], pair_recv.at[0], sibling),
        rcopy(cen, cen_in, pair_send.at[1], pair_recv.at[1], sibling),
    ]
    for c in pair:
        c.start()
    for c in pair:
        c.wait_recv()
    center = cen[0:1, :] + cen_in[0:1, :]

    def own_rows(t):
        rows = pl.ds(CHUNK * t, CHUNK)
        return raw[core, rows].astype(F32) + raw_in[rows].astype(F32)

    sent = []

    def flush(log):
        for c in log:
            c.wait_send()
        log.clear()

    orders = (("y", "x", "z"), ("x", "z", "y"), ("z", "y", "x"))
    dirs = ((0, 1), (1, -1))

    def gather(buf, t, block, ssem, rsem, log):
        at = [tuple(coord[a] for a in reversed(o)) for o in orders]
        for p in range(3):
            buf[(t, p) + at[p]] = block[PART * p : PART * (p + 1)]

        def chunk(p, f, step):
            q = place[orders[p][f], step % 4]
            return (t, p) + at[p][: 2 - f] + (q,)

        def send(p, f, e, idx, step):
            ref = buf.at[idx]
            rcopy(
                ref, ref, ssem.at[t, p, f], rsem.at[t, p, e], along(orders[p][f], step)
            ).start()

        def whole(p, f, e, idx):
            ref = buf.at[idx]
            return rcopy(ref, ref, ssem.at[t, p, f], rsem.at[t, p, e], sibling)

        def triple(p, f):
            return (t, p) + at[p][: 2 - f] + (pl.ds(0, 3),)

        def double(p, f):
            return (t, p) + at[p][: 2 - f] + (pl.ds(0, 2),)

        def single(p, f):
            return (t, p) + at[p][: 2 - f] + (0,)

        for p in range(3):
            for step in (1, 3, 2):
                send(p, 0, 0, chunk(p, 0, 0), step)
            log.append(whole(p, 0, 0, triple(p, 0)))
        yield
        for p in range(3):
            whole(p, 0, 0, triple(p, 0)).wait_recv()
            for k, step in dirs:
                send(p, 1, 1, chunk(p, 1, 0), step)
            log.append(whole(p, 1, 1, triple(p, 1)))
        yield
        for p in range(3):
            whole(p, 1, 1, double(p, 1)).wait_recv()
            for k, step in dirs:
                send(p, 1, 2, chunk(p, 1, -step) + (pl.ds(2 * k, 2),), step)
        yield
        for p in range(3):
            whole(p, 1, 2, single(p, 1)).wait_recv()
            for k, step in dirs:
                send(p, 2, 3, chunk(p, 2, 0) + (pl.ds(2 * k, 2),), step)
            log.append(whole(p, 2, 3, triple(p, 2)))
        for p in range(3):
            for k, step in dirs:
                send(p, 2, 4, chunk(p, 2, 0) + (pl.ds(2 - 2 * k, 2),), step)
        yield
        for p in range(3):
            whole(p, 2, 3, single(p, 2)).wait_recv()
            for k, step in dirs:
                send(p, 2, 5, chunk(p, 2, -step) + (pl.ds(2 * k, 2),), step)
        yield
        for e in (4, 5):
            for p in range(3):
                whole(p, 2, e, single(p, 2)).wait_recv()

    def weight_copy(j):
        return rcopy(
            weights.at[0, j], weights.at[1, j], pair_send.at[2], pair_recv.at[2], sibling
        )

    all_weight_copies = rcopy(
        weights.at[0], weights.at[1], pair_send.at[2], pair_recv.at[2], sibling
    )

    small_copy = rcopy(sm, sm_in, pair_send.at[3], pair_recv.at[3], sibling)

    def prepare():
        sq = jnp.zeros((LAT, 1), F32)
        for j in range(8):
            load(j).wait()
            block = gacc[j]
            weights[0, j] = block.astype(BF16)
            weight_copy(j).start()
            sq = sq + jnp.sum(block * block, axis=1, keepdims=True)
        norm = jnp.sqrt(sq + norm_eps)
        sm[...] = jnp.zeros((8, LAT), F32)
        sm[0:1, :] = offset_ref[...]
        sm[1:2, :] = jnp.broadcast_to(norm, (LAT, 128)).T[0:1, :]
        small_copy.start()

    def slab(buf, t, j):
        jz, jx = j // 4, j % 4
        rows = []
        for r in range(2):
            zz = 2 * (h if r == 0 else 1 - h) + jz
            for p in range(3):
                cols = []
                for yy in range(4):
                    idx = ((zz, jx, yy), (yy, zz, jx), (jx, yy, zz))[p]
                    cols.append(buf[(t, p) + idx])
                rows.append(jnp.concatenate(cols, axis=1))
        return jnp.concatenate(rows, axis=0)

    def all_weights(j):
        return jnp.concatenate([weights[0, j], weights[1, j]], axis=0)

    def project(buf, t, half):
        rows = jnp.concatenate([slab(buf, t, 4 * half + jx) for jx in range(4)], axis=1)
        cols = jnp.concatenate([all_weights(4 * half + jx) for jx in range(4)], axis=1)
        return dot_nt(rows, cols)

    def ring_first(src, lead, axis, b_out, b_in, sems, log):
        q = place[axis, 2]
        for k, step in dirs:
            b_out[k][...] = src[lead + (q, pl.ds(2 * k, 2))].astype(BF16)
            c = rcopy(b_out[k], b_in[k], sems[0][k], sems[1][k], along(axis, step))
            c.start()
            log.append(c)

    def ring_second(src, lead, axis, b_out, b_in, a_out, a_in, sems, log):
        for k, step in dirs:
            q = place[axis, step % 4]
            mix, rest = pl.ds(2 * k, 2), pl.ds(2 - 2 * k, 2)
            a_out[k][rest] = src[lead + (q, rest)].astype(BF16)
            rcopy(b_out[k], b_in[k], sems[0][k], sems[1][k], along(axis, step)).wait_recv()
            a_out[k][mix] = (src[lead + (q, mix)] + b_in[k][...].astype(F32)).astype(BF16)
            c = rcopy(a_out[k], a_in[k], sems[0][2 + k], sems[1][2 + k], along(axis, step))
            c.start()
            log.append(c)

    def ring_last(src, lead, axis, a_out, a_in, sems):
        for k, step in dirs:
            rcopy(a_out[k], a_in[k], sems[0][2 + k], sems[1][2 + k], along(axis, step)).wait_recv()
        return src[lead + (coord[axis],)] + a_in[0][...].astype(F32) + a_in[1][...].astype(F32)

    def direct_first(value, axis, out, into, sems, log):
        for k in range(3):
            out[k] = value(place[axis, k + 1]).astype(BF16)
            rcopy(out.at[k], into.at[k], sems[0][0], sems[1][0], along(axis, k + 1)).start()
        log.append(rcopy(out, into, sems[0][0], sems[1][0], sibling))

    def direct_last(value, axis, out, into, sems):
        rcopy(out, into, sems[0][0], sems[1][0], sibling).wait_recv()
        total = value(coord[axis])
        for k in range(3):
            total = total + into[k].astype(F32)
        return total

    def scatter(t, log):
        side_axes = ("x", "y") if t == 0 else ("y", "x")
        axes = (("x", "y"), ("y", "x"), side_axes)

        def some(ref, *lead):
            return [ref.at[lead + (k,)] for k in range(ref.shape[len(lead)])]

        def sems(p, s):
            return (
                [rs_send.at[t, p, 4 * s + e] for e in range(4)],
                [rs_recv.at[t, p, 4 * s + e] for e in range(4)],
            )

        def line_copy(p, e):
            src, dst = (z_out.at[t, p], z_in.at[t, p]) if e is None else (z_out.at[t, p, e], z_in.at[t, p, e])
            device = sibling if e is None else across[axes[p][1]][e]
            return rcopy(src, dst, rs_send.at[t, p, 4], rs_recv.at[t, p, 4], device)

        pair_copy = rcopy(
            y_out.at[t], y_in.at[t], rs_send.at[t, 2, 8], rs_recv.at[t, 2, 8], other_z
        )
        y_out[t] = side[t, 1 - zl].astype(BF16)
        pair_copy.start()
        ring = [
            (part, (t, p), axes[p][0], some(b0_out, t, p), some(b0_in, t, p), some(a0_out, t, p), some(a0_in, t, p), sems(p, 0))
            for p in range(2)
        ]
        for a in ring:
            ring_first(*a[:5], a[7], log)
        yield
        pair_copy.wait_recv()
        side[t, zl] = side[t, zl] + y_in[t].astype(F32)
        wide = (lambda q: side[t, zl, q], axes[2][0], c1_out.at[t], c1_in.at[t], sems(2, 0))
        direct_first(*wide, log)
        for a in ring:
            ring_second(*a, log)
        yield
        here = coord[axes[2][0]]
        side[t, zl, here] = direct_last(*wide)
        thin = (lambda q: side[t, zl, here, q], axes[2][1], c2_out.at[t], c2_in.at[t], sems(2, 1))
        direct_first(*thin, log)
        for p in range(2):
            first = coord[axes[p][0]]
            part[t, p, first] = ring_last(*ring[p][:3], *ring[p][5:])
            for e in range(7):
                a, w = (e + 1, zl) if e < 3 else (e - 3, 1 - zl)
                z_out[t, p, e] = part[t, p, first, place[axes[p][1], a], w].astype(BF16)
                line_copy(p, e).start()
            log.append(line_copy(p, None))
        yield
        out = []
        for p in range(2):
            total = part[t, p, coord[axes[p][0]], coord[axes[p][1]], zl]
            line_copy(p, None).wait_recv()
            for e in range(7):
                total = total + z_in[t, p, e].astype(F32)
            out.append(total)
        out.append(direct_last(*thin))
        log.append(pair_copy)
        result[t] = jnp.concatenate(out, axis=0)

    result, sq, err_sum, act_own, act_all, off_own, off_all = {}, {}, {}, {}, {}, {}, {}
    shared = {}

    def g_copy(j):
        cols = pl.ds(pl.multiple_of(512 * j, 512), 512)
        return rcopy(g_out.at[:, cols], g_in.at[:, cols], g_send.at[0], g_recv.at[0], sibling)

    def gradient(t, first, last):
        @pl.loop(first, last, unroll=2)
        def _(j):
            errs = slab(ge, 0, j)
            if t == 0:
                out = dot(tmat0[...], jnp.concatenate([slab(gx, 0, j), errs[:EARLY]], axis=0))
            else:
                rows = [slab(ge, 1, j), errs[EARLY:], slab(gx, 1, j)]
                out = dot(tmat1[...], jnp.concatenate(rows, axis=0))
            cols = pl.ds(pl.multiple_of(512 * j, 512), 512)
            if t == 0:
                gacc[j] = out[LAT:]
                grad_ref[:, cols] = out[:LAT]
            else:
                g_out[:, cols] = (gacc[j] + out[LAT:]).astype(BF16)
                g_copy(j).start()
                grad_ref[:, cols] = grad_ref[:, cols] + out[:LAT]

    def steps(t):
        centered = (own_rows(t) - center).astype(BF16)
        log_x, log_r, log_e = [], [], []
        yield from gather(gx, t, centered, gx_send, gx_recv, log_x)
        if t == 0:
            all_weight_copies.wait_recv()
            small_copy.wait_recv()
            shared["bias"] = jnp.concatenate([sm[0:1, :], sm_in[0:1, :]], axis=1)
            shared["norms"] = jnp.concatenate([sm[1:2, :], sm_in[1:2, :]], axis=1)
        norms = shared["norms"]
        pre[t] = project(gx, t, 0) + shared["bias"]
        yield
        pre[t] = pre[t] + project(gx, t, 1)
        yield
        acts[t] = jnp.maximum(pre[t], 0.0).astype(BF16)

        @pl.loop(0, 8, unroll=4)
        def _(j):
            jz, jx = j // 4, lax.rem(j, 4)
            out = dot(acts[t, :CHUNK], all_weights(j))
            for yy in range(4):
                cols = slice(128 * yy, 128 * (yy + 1))
                part[t, 0, jx, yy, jz] = out[:MAIN, cols]
                part[t, 1, yy, jx, jz] = out[MAIN : 2 * MAIN, cols]
                if t == 0:
                    side[t, jz, jx, yy] = out[2 * MAIN :, cols]
                else:
                    side[t, jz, yy, jx] = out[2 * MAIN :, cols]

        ready = scatter(t, log_r)
        next(ready)
        flush(log_x)
        act = acts[t]
        act_own[t] = jnp.sum(act[:CHUNK].astype(F32), axis=0, keepdims=True)
        act_all[t] = act_own[t] + jnp.sum(act[CHUNK:].astype(F32), axis=0, keepdims=True)
        if t == 1:
            tmat1[:, :LATE] = jnp.concatenate([act, acts[0, EARLY:]], axis=0).T
        yield
        yield from ready
        err = result[t] + center - own_rows(t)
        sq[t] = jnp.sum(err * err)
        err_sum[t] = jnp.sum(err, axis=0, keepdims=True)
        derr = (2.0 / TOK * err).astype(BF16)
        ready = gather(ge, t, derr, ge_send, ge_recv, log_e)
        next(ready)
        flush(log_r)
        yield
        yield from ready
        sent.extend(log_e)
        dacc[t] = project(ge, t, 0) + sparsity_coeff / TOK * norms
        yield
        dacts = dacc[t] + project(ge, t, 1)
        dpre = jnp.where(pre[t] > 0, dacts, 0.0).astype(BF16)
        if t == 0:
            tmat0[...] = jnp.concatenate([dpre, acts[0, :EARLY]], axis=0).T
        else:
            tmat1[:, LATE:] = dpre.T
        off_own[t] = jnp.sum(dpre[:CHUNK].astype(F32), axis=0, keepdims=True)
        off_all[t] = off_own[t] + jnp.sum(dpre[CHUNK:].astype(F32), axis=0, keepdims=True)
        yield
        if t == 0:
            gradient(0, 0, 4)
            yield
            gradient(0, 4, 8)
            yield

    run = [steps(0), steps(1)]
    plan = "0101010w01001010110101010101010010011"
    for who in plan:
        if who == "w":
            prepare()
        else:
            next(run[int(who)])
    for one in run:
        assert next(one, one) is one
    off = off_own[0] + off_own[1]
    offs = off_all[0] + off_all[1]
    act_tot = act_all[0] + act_all[1]
    spars = jnp.sum((act_own[0] + act_own[1]) * shared["norms"])

    sums[...] = jnp.zeros((2, 8, LAT), F32)
    for k in range(2):
        sums[k, 0:1, :] = offs[:, LAT * k : LAT * (k + 1)]
        sums[k, 1:2, :] = act_tot[:, LAT * k : LAT * (k + 1)]
    sums_copy = rcopy(sums.at[1], sums_in, pair_send.at[4], pair_recv.at[4], sibling)
    sums_copy.start()

    hi = off.astype(BF16)
    rest = off - hi.astype(F32)
    mid = rest.astype(BF16)
    low = (rest - mid.astype(F32)).astype(BF16)
    row = lax.broadcasted_iota(jnp.int32, (16, 512), 0)
    terms = jnp.where(
        row == 0, hi.astype(F32),
        jnp.where(row == 1, mid.astype(F32), jnp.where(row == 2, low.astype(F32), 0.0)),
    ).astype(BF16)
    for j in range(8):
        enc = jnp.sum(dot(terms, all_weights(j)), axis=0, keepdims=True)
        for yy in range(4):
            vx[j % 4, (j // 4) * 4 + yy : (j // 4) * 4 + yy + 1, :] = -enc[:, 128 * yy : 128 * (yy + 1)]
    scalars = jnp.where(lane == 0, sq[0] + sq[1], jnp.where(lane == 1, spars, 0.0))
    for k in range(4):
        vx[k, 8:16, :] = jnp.broadcast_to(scalars, (8, 128))
    sub = lax.broadcasted_iota(jnp.int32, (16, 128), 0)
    vx[x] = vx[x] + jnp.where(sub == zl * 4 + y, 2.0 / TOK * (err_sum[0] + err_sum[1]), 0.0)

    def v_start(k, src, dst, devices):
        for e, device in enumerate(devices):
            rcopy(src(e), dst.at[e], v_send.at[k], v_recv.at[k], device).start()

    def v_done(k, dst):
        return rcopy(dst, dst, v_send.at[k], v_recv.at[k], sibling)

    v_start(0, lambda e: vx.at[place["x", e + 1]], vx_in, across["x"][:3])
    gradient(1, 0, 3)
    v_done(0, vx_in).wait_recv()
    total = vx[x] + vx_in[0] + vx_in[1] + vx_in[2]
    for k in range(4):
        vy[k, 0:1, :] = total[k : k + 1]
        vy[k, 1:2, :] = total[4 + k : 5 + k]
        vy[k, 2:8, :] = total[8:14]
    v_start(1, lambda e: vy.at[place["y", e + 1]], vy_in, across["y"][:3])
    gradient(1, 3, 5)
    v_done(1, vy_in).wait_recv()
    total = vy[y] + vy_in[0] + vy_in[1] + vy_in[2]
    vz[...] = total
    v_start(2, lambda e: vz, vz_in, column)
    gradient(1, 5, 8)
    v_done(2, vz_in).wait_recv()
    for e in range(7):
        total = total + vz_in[e]
    sums_copy.wait_recv()

    small_ref[...] = jnp.zeros((8, LAT), F32)
    small_ref[0:1, :] = sums[0, 0:1, :] + sums_in[0:1, :]
    small_ref[1:2, :] = sparsity_coeff / TOK * (sums[0, 1:2, :] + sums_in[1:2, :]) / sm[1:2, :]
    slot = jnp.where(zl == 0, total[0:1], total[1:2])
    small_ref[2:3, 0:64] = jnp.where(core == 0, slot[:, :64], slot[:, 64:])
    small_ref[3:4, 0:128] = total[2:3]

    flush(sent)
    for c in pair + [all_weight_copies, small_copy, sums_copy]:
        c.wait_send()
    for k, dst in enumerate((vx_in, vy_in, vz_in)):
        v_done(k, dst).wait_send()
    all_g_copies = rcopy(g_out, g_in, g_send.at[0], g_recv.at[0], sibling)
    all_g_copies.wait_recv()
    all_g_copies.wait_send()


def step_kernel(inputs, center, offset, dictionary):
    vm = pltpu.VMEM
    dma = pltpu.SemaphoreType.DMA
    block = (PART, 128)
    main, side = (MAIN, 128), (SIDE, 128)
    return pl.pallas_call(
        kernel,
        out_shape=[
            jax.ShapeDtypeStruct((LAT, WIDTH), F32),
            jax.ShapeDtypeStruct((LAT, WIDTH), BF16),
            jax.ShapeDtypeStruct((8, LAT), F32),
        ],
        in_specs=[pl.BlockSpec(memory_space=pltpu.HBM)] * 4,
        out_specs=[pl.BlockSpec(memory_space=pltpu.VMEM)] * 3,
        scratch_shapes=[
            vm((64, 2 * ROWS), BF16),
            vm((1, 64), F32),
            vm((1, LAT), F32),
            vm((2, 8, LAT, 512), BF16),
            vm((2, 3, 4, 4, 4) + block, BF16),
            vm((2, 3, 4, 4, 4) + block, BF16),
            vm((2, 2 * CHUNK, 512), F32),
            vm((2, 2 * CHUNK, 512), F32),
            vm((2, 2 * CHUNK, 512), BF16),
            vm((512, 480), BF16),
            vm((512, 672), BF16),
            vm((8, LAT, 512), F32),
            vm((2, ROWS, 128), BF16),
            vm((ROWS, 128), BF16),
            vm((8, 128), F32),
            vm((8, 128), F32),
            vm((8, LAT), F32),
            vm((8, LAT), F32),
            vm((2, 8, LAT), F32),
            vm((8, LAT), F32),
            vm((2, 2, 4, 4, 2) + main, F32),
            vm((2, 2, 2, 2, 2) + main, BF16),
            vm((2, 2, 2, 2, 2) + main, BF16),
            vm((2, 2, 2, 4, 2) + main, BF16),
            vm((2, 2, 2, 4, 2) + main, BF16),
            vm((2, 2, 7) + main, BF16),
            vm((2, 2, 7) + main, BF16),
            vm((2, 2, 4, 4) + side, F32),
            vm((2, 4, 4) + side, BF16),
            vm((2, 4, 4) + side, BF16),
            vm((2, 3, 4) + side, BF16),
            vm((2, 3, 4) + side, BF16),
            vm((2, 3) + side, BF16),
            vm((2, 3) + side, BF16),
            vm((LAT, WIDTH), BF16),
            vm((4, 16, 128), F32),
            vm((3, 16, 128), F32),
            vm((4, 8, 128), F32),
            vm((3, 8, 128), F32),
            vm((8, 128), F32),
            vm((7, 8, 128), F32),
            dma((11,)),
            dma((5,)),
            dma((5,)),
            dma((2, 3, 3)),
            dma((2, 3, 6)),
            dma((2, 3, 3)),
            dma((2, 3, 6)),
            dma((2, 3, 9)),
            dma((2, 3, 9)),
            dma((1,)),
            dma((1,)),
            dma((3,)),
            dma((3,)),
        ],
        compiler_params=pltpu.CompilerParams(
            collective_id=0, has_side_effects=True, vmem_limit_bytes=VMEM_LIMIT
        ),
        cost_estimate=pl.CostEstimate(
            flops=12 * 2**30, bytes_accessed=160 * 2**20, transcendentals=0
        ),
        name="step",
    )(*[pltpu.with_memory_space_constraint(v, pltpu.HBM) for v in (inputs, center, offset, dictionary)])


def small_kernel(small, offset, offset_mean, offset_var, center, center_mean, center_var, *outs):
    rows = (
        (offset, small[0:1, :], offset_mean, offset_var),
        (center, small[2:3, 0:64], center_mean, center_var),
    )
    for k, (param, grad, mean, var) in enumerate(rows):
        new = adam_update(param[...], grad, mean[...], var[...])
        for n in range(3):
            outs[3 * k + n][...] = new[n]
    scalars = small[3:4, 0:128]
    lane = lax.broadcasted_iota(jnp.int32, (1, 128), 1)
    weight = jnp.where(lane == 0, 1.0, jnp.where(lane == 1, sparsity_coeff, 0.0))
    outs[6][...] = jnp.sum(scalars * weight, axis=1, keepdims=True) / (TOK * WIDTH)


def small_step(small, *rows):
    shapes = [(1, LAT)] * 3 + [(1, 64)] * 3 + [(1, 1)]
    return pl.pallas_call(
        small_kernel,
        out_shape=[jax.ShapeDtypeStruct(s, F32) for s in shapes],
        in_specs=[pl.BlockSpec(memory_space=pltpu.VMEM)] * 7,
        out_specs=[pl.BlockSpec(memory_space=pltpu.VMEM)] * 7,
        compiler_params=pltpu.CompilerParams(vmem_limit_bytes=2**20),
        name="small",
    )(small, *[r.reshape(1, -1) for r in rows])


def body(
    inputs,
    dictionary,
    offset,
    center,
    dict_mean,
    dict_var,
    offset_mean,
    offset_var,
    center_mean,
    center_var,
):
    grad, shared, small = step_kernel(
        inputs.T, center.reshape(1, -1), offset.reshape(1, -1), dictionary
    )
    g_dict = grad + shared.astype(F32) + small[1][:, None] * dictionary
    fresh_dict, mean_dict, var_dict = adam_update(dictionary, g_dict, dict_mean, dict_var)
    *rows, loss = small_step(
        small, offset, offset_mean, offset_var, center, center_mean, center_var
    )
    fresh_offset, mean_offset, var_offset, fresh_center, mean_center, var_center = [
        r.reshape(-1) for r in rows
    ]
    loss_value = loss.reshape(())
    return (
        fresh_dict,
        fresh_offset,
        fresh_center,
        mean_dict,
        var_dict,
        mean_offset,
        var_offset,
        mean_center,
        var_center,
        loss_value,
    )


def solution(mesh):
    return jax.shard_map(
        body,
        mesh=mesh,
        in_specs=(
            P("dp", "latent"),
            P("latent", None),
            P("latent"),
            P("latent"),
            P("latent", None),
            P("latent", None),
            P("latent"),
            P("latent"),
            P("latent"),
            P("latent"),
        ),
        out_specs=(
            P("latent", None),
            P("latent"),
            P("latent"),
            P("latent", None),
            P("latent", None),
            P("latent"),
            P("latent"),
            P("latent"),
            P("latent"),
            P(),
        ),
        check_vma=False,
    )
```

```python
import jax
import jax.numpy as jnp
from jax import lax
from jax.experimental import pallas as pl
from jax.experimental.pallas import tpu as pltpu
from jax.sharding import PartitionSpec as P

STEP = 1000
sparsity_coeff = 5.0
beta_one = 0.9
beta_two = 0.999
learn_rate = 0.001
adam_eps = 1e-08
norm_eps = 1e-06

TOK = 1152
WIDTH = 4096
ROWS = 288
CHUNK = 144
PART = 48
MAIN, SIDE = 64, 16
LAT = 256
EARLY = 192
LATE = 384
VMEM_LIMIT = 40 * 1024 * 1024
F32 = jnp.float32
BF16 = jnp.bfloat16
MESH = pl.DeviceIdType.MESH


def adam_update(param, grad, mean, var):
    mean_new = beta_one * mean + (1.0 - beta_one) * grad
    var_new = beta_two * var + (1.0 - beta_two) * grad * grad
    rate = learn_rate / (1.0 - beta_one**STEP)
    scaled = var_new * (1.0 / (1.0 - beta_two**STEP))
    param_new = param - rate * mean_new / (scaled * lax.rsqrt(scaled) + adam_eps)
    return (param_new, mean_new, var_new)


def mod4(v):
    return lax.rem(v + 4, 4)


def dot(a, b):
    return jnp.dot(a, b, preferred_element_type=F32)


def dot_nt(a, b):
    return lax.dot_general(a, b, (((1,), (1,)), ((), ())), preferred_element_type=F32)


def kernel(
    inputs_hbm, center_hbm, offset_hbm, dict_ref,
    grad_ref, g_in, small_ref,
    inputs_ref, center_ref, offset_ref,
    weights, gx, ge, pre, dpre_own, acts, tmat0, tmat1, gacc,
    raw, raw_in, cen, cen_in, sm, sm_in, sums, sums_in,
    part, b0_out, b0_in, a0_out, a0_in, z_out, z_in,
    side, y_out, y_in, c1_out, c1_in, c2_out, c2_in,
    g_out,
    vx, vx_in, vz, vz_in,
    load_sem, pair_send, pair_recv,
    gx_send, gx_recv, ge_send, ge_recv, rs_send, rs_recv,
    g_send, g_recv, v_send, v_recv,
):
    h = lax.axis_index("dp")
    i = lax.axis_index("latent")
    core = lax.rem(i, 2)
    y = lax.rem(i // 2, 4)
    x = lax.rem(i // 8, 4)
    zl = i // 32
    z = 2 * h + zl

    def dev(xx, yy, zz, cc):
        return (zz // 2, ((lax.rem(zz, 2) * 4 + xx) * 4 + yy) * 2 + cc)

    coord = {"x": x, "y": y, "z": z}
    place = {(a, s): mod4(coord[a] + s) for a in coord for s in range(4)}
    near = {}
    for s in range(1, 4):
        near["x", s] = dev(place["x", s], y, z, core)
        near["y", s] = dev(x, place["y", s], z, core)
        near["z", s] = dev(x, y, place["z", s], core)

    def along(axis, step):
        return near[axis, step % 4]

    sibling = dev(x, y, z, 1 - core)
    far_z = 2 * h + 1 - zl
    other_z = dev(x, y, far_z, core)

    def rcopy(src, dst, ssem, rsem, device):
        return pltpu.make_async_remote_copy(
            src_ref=src, dst_ref=dst, send_sem=ssem, recv_sem=rsem,
            device_id=device, device_id_type=MESH,
        )

    def load(j):
        return pltpu.make_async_copy(
            dict_ref.at[:, pl.ds(512 * j, 512)], gacc.at[j], load_sem.at[j]
        )

    first_loads = [
        pltpu.make_async_copy(src, dst, load_sem.at[8 + k])
        for k, (src, dst) in enumerate(
            ((inputs_hbm, inputs_ref), (center_hbm, center_ref), (offset_hbm, offset_ref))
        )
    ]
    for c in first_loads:
        c.start()
    for j in range(8):
        load(j).start()

    plane = [
        dev(place["x", a], place["y", b], z, core) for a in range(4) for b in range(4) if a + b
    ]
    column = [
        dev(x, y, place["z", a], c)
        for a in range(4) for b, c in enumerate((core, 1 - core)) if a + b
    ]
    across = {
        axis: [near[axis, a] for a in range(1, 4)]
        + [
            dev(place["x", a], y, far_z, core) if axis == "x" else dev(x, place["y", a], far_z, core)
            for a in range(4)
        ]
        for axis in ("x", "y")
    }
    barrier = pltpu.get_barrier_semaphore()
    partners = plane + column + across["x"][4:] + across["y"][4:]
    for partner in partners:
        pl.semaphore_signal(barrier, inc=1, device_id=partner, device_id_type=MESH)

    for c in first_loads:
        c.wait()
    lane = lax.broadcasted_iota(jnp.int32, (1, 128), 1)
    mine = (lane // 64) == core
    both = inputs_ref[...].astype(F32)
    both = jnp.concatenate([both, both], axis=0).T
    raw[...] = jnp.where(mine, both, 0.0).astype(BF16).reshape(2, ROWS, 128)
    cboth = jnp.concatenate([center_ref[...], center_ref[...]], axis=1)
    cen[...] = jnp.broadcast_to(jnp.where(mine, cboth, 0.0), (8, 128))
    pl.semaphore_wait(barrier, len(partners))

    pair = [
        rcopy(raw.at[1 - core], raw_in, pair_send.at[0], pair_recv.at[0], sibling),
        rcopy(cen, cen_in, pair_send.at[1], pair_recv.at[1], sibling),
    ]
    for c in pair:
        c.start()
    for c in pair:
        c.wait_recv()
    center = cen[0:1, :] + cen_in[0:1, :]

    def own_rows(t):
        rows = pl.ds(CHUNK * t, CHUNK)
        return raw[core, rows].astype(F32) + raw_in[rows].astype(F32)

    sent = []

    def flush(log):
        for c in log:
            c.wait_send()
        log.clear()

    orders = (("y", "x", "z"), ("x", "z", "y"), ("z", "y", "x"))
    dirs = ((0, 1), (1, -1))

    def gather(buf, t, block, ssem, rsem, log):
        at = [tuple(coord[a] for a in reversed(o)) for o in orders]
        for p in range(3):
            buf[(t, p) + at[p]] = block[PART * p : PART * (p + 1)]

        def chunk(p, f, step):
            q = place[orders[p][f], step % 4]
            return (t, p) + at[p][: 2 - f] + (q,)

        def send(p, f, e, idx, step):
            ref = buf.at[idx]
            rcopy(
                ref, ref, ssem.at[t, p, f], rsem.at[t, p, e], along(orders[p][f], step)
            ).start()

        def whole(p, f, e, idx):
            ref = buf.at[idx]
            return rcopy(ref, ref, ssem.at[t, p, f], rsem.at[t, p, e], sibling)

        def triple(p, f):
            return (t, p) + at[p][: 2 - f] + (pl.ds(0, 3),)

        def double(p, f):
            return (t, p) + at[p][: 2 - f] + (pl.ds(0, 2),)

        def single(p, f):
            return (t, p) + at[p][: 2 - f] + (0,)

        for p in range(3):
            for step in (1, 3, 2):
                send(p, 0, 0, chunk(p, 0, 0), step)
            log.append(whole(p, 0, 0, triple(p, 0)))
        yield
        for p in range(3):
            whole(p, 0, 0, triple(p, 0)).wait_recv()
            for k, step in dirs:
                send(p, 1, 1, chunk(p, 1, 0), step)
            log.append(whole(p, 1, 1, triple(p, 1)))
        yield
        for p in range(3):
            whole(p, 1, 1, double(p, 1)).wait_recv()
            for k, step in dirs:
                send(p, 1, 2, chunk(p, 1, -step) + (pl.ds(2 * k, 2),), step)
        yield
        for p in range(3):
            whole(p, 1, 2, single(p, 1)).wait_recv()
            for k, step in dirs:
                send(p, 2, 3, chunk(p, 2, 0) + (pl.ds(2 * k, 2),), step)
            log.append(whole(p, 2, 3, triple(p, 2)))
        for p in range(3):
            for k, step in dirs:
                send(p, 2, 4, chunk(p, 2, 0) + (pl.ds(2 - 2 * k, 2),), step)
        yield
        for p in range(3):
            whole(p, 2, 3, single(p, 2)).wait_recv()
            for k, step in dirs:
                send(p, 2, 5, chunk(p, 2, -step) + (pl.ds(2 * k, 2),), step)
        yield
        for e in (4, 5):
            for p in range(3):
                whole(p, 2, e, single(p, 2)).wait_recv()

    def weight_copy(j):
        return rcopy(
            weights.at[0, j], weights.at[1, j], pair_send.at[2], pair_recv.at[2], sibling
        )

    all_weight_copies = rcopy(
        weights.at[0], weights.at[1], pair_send.at[2], pair_recv.at[2], sibling
    )

    small_copy = rcopy(sm, sm_in, pair_send.at[3], pair_recv.at[3], sibling)

    def prepare(part):
        sq = jnp.zeros((LAT, 128), F32)
        for j in range(4 * part, 4 * part + 4):
            load(j).wait()
            block = gacc[j]
            weights[0, j] = block.astype(BF16)
            weight_copy(j).start()
            for k in range(4):
                piece = block[:, 128 * k : 128 * (k + 1)]
                sq = sq + piece * piece
        squares.append(sq)
        if part == 0:
            return
        norm = jnp.sqrt(jnp.sum(squares[0] + squares[1], axis=1, keepdims=True) + norm_eps)
        sm[...] = jnp.zeros((8, LAT), F32)
        sm[0:1, :] = offset_ref[...]
        sm[1:2, :] = jnp.broadcast_to(norm, (LAT, 128)).T[0:1, :]
        small_copy.start()

    squares = []

    def slab(buf, t, j):
        jz, jx = j // 4, j % 4
        rows = []
        for r in range(2):
            zz = 2 * (h if r == 0 else 1 - h) + jz
            for p in range(3):
                cols = []
                for yy in range(4):
                    idx = ((zz, jx, yy), (yy, zz, jx), (jx, yy, zz))[p]
                    cols.append(buf[(t, p) + idx])
                rows.append(jnp.concatenate(cols, axis=1))
        return jnp.concatenate(rows, axis=0)

    def all_weights(j):
        return jnp.concatenate([weights[0, j], weights[1, j]], axis=0)

    def project(buf, t, which):
        rows = jnp.concatenate([slab(buf, t, j) for j in range(8)], axis=1)
        return dot_nt(rows, jnp.concatenate([weights[which, j] for j in range(8)], axis=1))

    def ring_first(src, lead, axis, b_out, b_in, sems, log):
        q = place[axis, 2]
        for k, step in dirs:
            b_out[k][...] = src[lead + (q, pl.ds(2 * k, 2))].astype(BF16)
            c = rcopy(b_out[k], b_in[k], sems[0][k], sems[1][k], along(axis, step))
            c.start()
            log.append(c)

    def ring_second(src, lead, axis, b_out, b_in, a_out, a_in, sems, log):
        for k, step in dirs:
            q = place[axis, step % 4]
            mix, rest = pl.ds(2 * k, 2), pl.ds(2 - 2 * k, 2)
            a_out[k][rest] = src[lead + (q, rest)].astype(BF16)
            rcopy(b_out[k], b_in[k], sems[0][k], sems[1][k], along(axis, step)).wait_recv()
            a_out[k][mix] = (src[lead + (q, mix)] + b_in[k][...].astype(F32)).astype(BF16)
            c = rcopy(a_out[k], a_in[k], sems[0][2 + k], sems[1][2 + k], along(axis, step))
            c.start()
            log.append(c)

    def ring_last(src, lead, axis, a_out, a_in, sems):
        for k, step in dirs:
            rcopy(a_out[k], a_in[k], sems[0][2 + k], sems[1][2 + k], along(axis, step)).wait_recv()
        return src[lead + (coord[axis],)] + a_in[0][...].astype(F32) + a_in[1][...].astype(F32)

    def direct_first(value, axis, out, into, sems, log):
        for k in range(3):
            out[k] = value(place[axis, k + 1]).astype(BF16)
            rcopy(out.at[k], into.at[k], sems[0][0], sems[1][0], along(axis, k + 1)).start()
        log.append(rcopy(out, into, sems[0][0], sems[1][0], sibling))

    def direct_last(value, axis, out, into, sems):
        rcopy(out, into, sems[0][0], sems[1][0], sibling).wait_recv()
        total = value(coord[axis])
        for k in range(3):
            total = total + into[k].astype(F32)
        return total

    def scatter(t, log):
        side_axes = ("x", "y") if t == 0 else ("y", "x")
        axes = (("x", "y"), ("y", "x"), side_axes)

        def some(ref, *lead):
            return [ref.at[lead + (k,)] for k in range(ref.shape[len(lead)])]

        def sems(p, s):
            return (
                [rs_send.at[t, p, 4 * s + e] for e in range(4)],
                [rs_recv.at[t, p, 4 * s + e] for e in range(4)],
            )

        def line_copy(p, e):
            src, dst = (z_out.at[t, p], z_in.at[t, p]) if e is None else (z_out.at[t, p, e], z_in.at[t, p, e])
            device = sibling if e is None else across[axes[p][1]][e]
            return rcopy(src, dst, rs_send.at[t, p, 4], rs_recv.at[t, p, 4], device)

        pair_copy = rcopy(
            y_out.at[t], y_in.at[t], rs_send.at[t, 2, 8], rs_recv.at[t, 2, 8], other_z
        )
        y_out[t] = side[t, 1 - zl].astype(BF16)
        pair_copy.start()
        ring = [
            (part, (t, p), axes[p][0], some(b0_out, t, p), some(b0_in, t, p), some(a0_out, t, p), some(a0_in, t, p), sems(p, 0))
            for p in range(2)
        ]
        for a in ring:
            ring_first(*a[:5], a[7], log)
        yield
        pair_copy.wait_recv()
        side[t, zl] = side[t, zl] + y_in[t].astype(F32)
        wide = (lambda q: side[t, zl, q], axes[2][0], c1_out.at[t], c1_in.at[t], sems(2, 0))
        direct_first(*wide, log)
        for a in ring:
            ring_second(*a, log)
        yield
        here = coord[axes[2][0]]
        side[t, zl, here] = direct_last(*wide)
        thin = (lambda q: side[t, zl, here, q], axes[2][1], c2_out.at[t], c2_in.at[t], sems(2, 1))
        direct_first(*thin, log)
        for p in range(2):
            first = coord[axes[p][0]]
            part[t, p, first] = ring_last(*ring[p][:3], *ring[p][5:])
            for e in range(7):
                a, w = (e + 1, zl) if e < 3 else (e - 3, 1 - zl)
                z_out[t, p, e] = part[t, p, first, place[axes[p][1], a], w].astype(BF16)
                line_copy(p, e).start()
            log.append(line_copy(p, None))
        yield
        out = []
        for p in range(2):
            total = part[t, p, coord[axes[p][0]], coord[axes[p][1]], zl]
            line_copy(p, None).wait_recv()
            for e in range(7):
                total = total + z_in[t, p, e].astype(F32)
            out.append(total)
        out.append(direct_last(*thin))
        log.append(pair_copy)
        result[t] = jnp.concatenate(out, axis=0)

    result, sq, err_sum, act_own, act_all, off_own, off_all = {}, {}, {}, {}, {}, {}, {}

    def g_copy(j):
        cols = pl.ds(pl.multiple_of(512 * j, 512), 512)
        return rcopy(g_out.at[:, cols], g_in.at[:, cols], g_send.at[0], g_recv.at[0], sibling)

    def gradient(t, first, last):
        @pl.loop(first, last, unroll=2)
        def _(j):
            errs = slab(ge, 0, j)
            if t == 0:
                out = dot(tmat0[...], jnp.concatenate([slab(gx, 0, j), errs[:EARLY]], axis=0))
            else:
                rows = [slab(ge, 1, j), errs[EARLY:], slab(gx, 1, j)]
                out = dot(tmat1[...], jnp.concatenate(rows, axis=0))
            cols = pl.ds(pl.multiple_of(512 * j, 512), 512)
            if t == 0:
                gacc[j] = out[LAT:]
                grad_ref[:, cols] = out[:LAT]
            else:
                g_out[:, cols] = (gacc[j] + out[LAT:]).astype(BF16)
                g_copy(j).start()
                grad_ref[:, cols] = grad_ref[:, cols] + out[:LAT]

    def steps(t):
        centered = (own_rows(t) - center).astype(BF16)
        log_x, log_r, log_e = [], [], []
        yield from gather(gx, t, centered, gx_send, gx_recv, log_x)
        pre[t, :, :LAT] = project(gx, t, 0) + sm[0:1, :]
        yield
        if t == 0:
            all_weight_copies.wait_recv()
            small_copy.wait_recv()
        pre[t, :, LAT:] = project(gx, t, 1) + sm_in[0:1, :]
        yield
        acts[t] = jnp.maximum(pre[t], 0.0).astype(BF16)

        @pl.loop(0, 8, unroll=4)
        def _(j):
            jz, jx = j // 4, lax.rem(j, 4)
            out = dot(acts[t, :CHUNK], all_weights(j))
            for yy in range(4):
                cols = slice(128 * yy, 128 * (yy + 1))
                part[t, 0, jx, yy, jz] = out[:MAIN, cols]
                part[t, 1, yy, jx, jz] = out[MAIN : 2 * MAIN, cols]
                if t == 0:
                    side[t, jz, jx, yy] = out[2 * MAIN :, cols]
                else:
                    side[t, jz, yy, jx] = out[2 * MAIN :, cols]

        ready = scatter(t, log_r)
        next(ready)
        flush(log_x)
        act = acts[t]
        act_own[t] = jnp.sum(act[:CHUNK].astype(F32), axis=0, keepdims=True)
        act_all[t] = act_own[t] + jnp.sum(act[CHUNK:].astype(F32), axis=0, keepdims=True)
        if t == 1:
            tmat1[:, :LATE] = jnp.concatenate([act, acts[0, EARLY:]], axis=0).T
        yield
        yield from ready
        err = result[t] + center - own_rows(t)
        sq[t] = jnp.sum(err * err)
        err_sum[t] = jnp.sum(err, axis=0, keepdims=True)
        derr = (2.0 / TOK * err).astype(BF16)
        ready = gather(ge, t, derr, ge_send, ge_recv, log_e)
        next(ready)
        flush(log_r)
        yield
        yield from ready
        sent.extend(log_e)

        def backward(which, norm):
            dacts = project(ge, t, which) + sparsity_coeff / TOK * norm
            kept = pre[t, :, LAT * which : LAT * (which + 1)] > 0
            return jnp.where(kept, dacts, 0.0).astype(BF16)

        dpre_own[t] = backward(0, sm[1:2, :])
        yield
        dpre = jnp.concatenate([dpre_own[t], backward(1, sm_in[1:2, :])], axis=1)
        if t == 0:
            tmat0[...] = jnp.concatenate([dpre, acts[0, :EARLY]], axis=0).T
        else:
            tmat1[:, LATE:] = dpre.T
        off_own[t] = jnp.sum(dpre[:CHUNK].astype(F32), axis=0, keepdims=True)
        off_all[t] = off_own[t] + jnp.sum(dpre[CHUNK:].astype(F32), axis=0, keepdims=True)
        yield
        if t == 0:
            gradient(0, 0, 4)
            yield
            gradient(0, 4, 8)
            yield

    run = [steps(0), steps(1)]
    plan = "0101u010w01001010110101010101010010011"
    for who in plan:
        if who in "uw":
            prepare("uw".index(who))
        else:
            next(run[int(who)])
    for one in run:
        assert next(one, one) is one
    off = off_own[0] + off_own[1]
    offs = off_all[0] + off_all[1]
    act_tot = act_all[0] + act_all[1]
    norms = jnp.concatenate([sm[1:2, :], sm_in[1:2, :]], axis=1)
    spars = jnp.sum((act_own[0] + act_own[1]) * norms)

    sums[...] = jnp.zeros((2, 8, LAT), F32)
    for k in range(2):
        sums[k, 0:1, :] = offs[:, LAT * k : LAT * (k + 1)]
        sums[k, 1:2, :] = act_tot[:, LAT * k : LAT * (k + 1)]
    sums_copy = rcopy(sums.at[1], sums_in, pair_send.at[4], pair_recv.at[4], sibling)
    sums_copy.start()

    hi = off.astype(BF16)
    rest = off - hi.astype(F32)
    mid = rest.astype(BF16)
    low = (rest - mid.astype(F32)).astype(BF16)
    row = lax.broadcasted_iota(jnp.int32, (16, 512), 0)
    terms = jnp.where(
        row == 0, hi.astype(F32),
        jnp.where(row == 1, mid.astype(F32), jnp.where(row == 2, low.astype(F32), 0.0)),
    ).astype(BF16)
    for j in range(8):
        enc = jnp.sum(dot(terms, all_weights(j)), axis=0, keepdims=True)
        for yy in range(4):
            vx[(j % 4) * 4 + yy, j // 4 : j // 4 + 1, :] = -enc[:, 128 * yy : 128 * (yy + 1)]
    scalars = jnp.where(lane == 0, sq[0] + sq[1], jnp.where(lane == 1, spars, 0.0))
    for k in range(16):
        vx[k, 2:8, :] = jnp.broadcast_to(scalars, (6, 128))
    here = x * 4 + y
    sub = lax.broadcasted_iota(jnp.int32, (8, 128), 0)
    vx[here] = vx[here] + jnp.where(sub == zl, 2.0 / TOK * (err_sum[0] + err_sum[1]), 0.0)

    def v_plane(e):
        a, b = (e + 1) // 4, (e + 1) % 4
        return rcopy(
            vx.at[place["x", a] * 4 + place["y", b]], vx_in.at[e], v_send.at[0], v_recv.at[0], plane[e]
        )

    def v_column(e):
        return rcopy(vz, vz_in.at[e], v_send.at[1], v_recv.at[1], column[e])

    v_planes = rcopy(vx_in, vx_in, v_send.at[0], v_recv.at[0], sibling)
    v_columns = rcopy(vz_in, vz_in, v_send.at[1], v_recv.at[1], sibling)

    for e in range(15):
        v_plane(e).start()
    gradient(1, 0, 4)
    total = vx[here]
    v_planes.wait_recv()
    for e in range(15):
        total = total + vx_in[e]
    vz[...] = total
    for e in range(7):
        v_column(e).start()
    gradient(1, 4, 8)
    v_columns.wait_recv()
    for e in range(7):
        total = total + vz_in[e]
    sums_copy.wait_recv()

    small_ref[...] = jnp.zeros((8, LAT), F32)
    small_ref[0:1, :] = sums[0, 0:1, :] + sums_in[0:1, :]
    small_ref[1:2, :] = sparsity_coeff / TOK * (sums[0, 1:2, :] + sums_in[1:2, :]) / sm[1:2, :]
    slot = jnp.where(zl == 0, total[0:1], total[1:2])
    small_ref[2:3, 0:64] = jnp.where(core == 0, slot[:, :64], slot[:, 64:])
    small_ref[3:4, 0:128] = total[2:3]

    flush(sent)
    for c in pair + [all_weight_copies, small_copy, sums_copy]:
        c.wait_send()
    v_planes.wait_send()
    v_columns.wait_send()
    all_g_copies = rcopy(g_out, g_in, g_send.at[0], g_recv.at[0], sibling)
    all_g_copies.wait_recv()
    all_g_copies.wait_send()


def step_kernel(inputs, center, offset, dictionary):
    vm = pltpu.VMEM
    dma = pltpu.SemaphoreType.DMA
    block = (PART, 128)
    main, side = (MAIN, 128), (SIDE, 128)
    return pl.pallas_call(
        kernel,
        out_shape=[
            jax.ShapeDtypeStruct((LAT, WIDTH), F32),
            jax.ShapeDtypeStruct((LAT, WIDTH), BF16),
            jax.ShapeDtypeStruct((8, LAT), F32),
        ],
        in_specs=[pl.BlockSpec(memory_space=pltpu.HBM)] * 4,
        out_specs=[pl.BlockSpec(memory_space=pltpu.VMEM)] * 3,
        scratch_shapes=[
            vm((64, 2 * ROWS), BF16),
            vm((1, 64), F32),
            vm((1, LAT), F32),
            vm((2, 8, LAT, 512), BF16),
            vm((2, 3, 4, 4, 4) + block, BF16),
            vm((2, 3, 4, 4, 4) + block, BF16),
            vm((2, 2 * CHUNK, 512), F32),
            vm((2, 2 * CHUNK, LAT), BF16),
            vm((2, 2 * CHUNK, 512), BF16),
            vm((512, 480), BF16),
            vm((512, 672), BF16),
            vm((8, LAT, 512), F32),
            vm((2, ROWS, 128), BF16),
            vm((ROWS, 128), BF16),
            vm((8, 128), F32),
            vm((8, 128), F32),
            vm((8, LAT), F32),
            vm((8, LAT), F32),
            vm((2, 8, LAT), F32),
            vm((8, LAT), F32),
            vm((2, 2, 4, 4, 2) + main, F32),
            vm((2, 2, 2, 2, 2) + main, BF16),
            vm((2, 2, 2, 2, 2) + main, BF16),
            vm((2, 2, 2, 4, 2) + main, BF16),
            vm((2, 2, 2, 4, 2) + main, BF16),
            vm((2, 2, 7) + main, BF16),
            vm((2, 2, 7) + main, BF16),
            vm((2, 2, 4, 4) + side, F32),
            vm((2, 4, 4) + side, BF16),
            vm((2, 4, 4) + side, BF16),
            vm((2, 3, 4) + side, BF16),
            vm((2, 3, 4) + side, BF16),
            vm((2, 3) + side, BF16),
            vm((2, 3) + side, BF16),
            vm((LAT, WIDTH), BF16),
            vm((16, 8, 128), F32),
            vm((15, 8, 128), F32),
            vm((8, 128), F32),
            vm((7, 8, 128), F32),
            dma((11,)),
            dma((5,)),
            dma((5,)),
            dma((2, 3, 3)),
            dma((2, 3, 6)),
            dma((2, 3, 3)),
            dma((2, 3, 6)),
            dma((2, 3, 9)),
            dma((2, 3, 9)),
            dma((1,)),
            dma((1,)),
            dma((2,)),
            dma((2,)),
        ],
        compiler_params=pltpu.CompilerParams(
            collective_id=0, has_side_effects=True, vmem_limit_bytes=VMEM_LIMIT
        ),
        cost_estimate=pl.CostEstimate(
            flops=12 * 2**30, bytes_accessed=160 * 2**20, transcendentals=0
        ),
        name="step",
    )(*[pltpu.with_memory_space_constraint(v, pltpu.HBM) for v in (inputs, center, offset, dictionary)])


def small_kernel(small, offset, offset_mean, offset_var, center, center_mean, center_var, *outs):
    rows = (
        (offset, small[0:1, :], offset_mean, offset_var),
        (center, small[2:3, 0:64], center_mean, center_var),
    )
    for k, (param, grad, mean, var) in enumerate(rows):
        new = adam_update(param[...], grad, mean[...], var[...])
        for n in range(3):
            outs[3 * k + n][...] = new[n]
    scalars = small[3:4, 0:128]
    lane = lax.broadcasted_iota(jnp.int32, (1, 128), 1)
    weight = jnp.where(lane == 0, 1.0, jnp.where(lane == 1, sparsity_coeff, 0.0))
    outs[6][...] = jnp.sum(scalars * weight, axis=1, keepdims=True) / (TOK * WIDTH)


def small_step(small, *rows):
    shapes = [(1, LAT)] * 3 + [(1, 64)] * 3 + [(1, 1)]
    return pl.pallas_call(
        small_kernel,
        out_shape=[jax.ShapeDtypeStruct(s, F32) for s in shapes],
        in_specs=[pl.BlockSpec(memory_space=pltpu.VMEM)] * 7,
        out_specs=[pl.BlockSpec(memory_space=pltpu.VMEM)] * 7,
        compiler_params=pltpu.CompilerParams(vmem_limit_bytes=2**20),
        name="small",
    )(small, *[r.reshape(1, -1) for r in rows])


def body(
    inputs,
    dictionary,
    offset,
    center,
    dict_mean,
    dict_var,
    offset_mean,
    offset_var,
    center_mean,
    center_var,
):
    grad, shared, small = step_kernel(
        inputs.T, center.reshape(1, -1), offset.reshape(1, -1), dictionary
    )
    g_dict = grad + shared.astype(F32) + small[1][:, None] * dictionary
    fresh_dict, mean_dict, var_dict = adam_update(dictionary, g_dict, dict_mean, dict_var)
    *rows, loss = small_step(
        small, offset, offset_mean, offset_var, center, center_mean, center_var
    )
    fresh_offset, mean_offset, var_offset, fresh_center, mean_center, var_center = [
        r.reshape(-1) for r in rows
    ]
    loss_value = loss.reshape(())
    return (
        fresh_dict,
        fresh_offset,
        fresh_center,
        mean_dict,
        var_dict,
        mean_offset,
        var_offset,
        mean_center,
        var_center,
        loss_value,
    )


def solution(mesh):
    return jax.shard_map(
        body,
        mesh=mesh,
        in_specs=(
            P("dp", "latent"),
            P("latent", None),
            P("latent"),
            P("latent"),
            P("latent", None),
            P("latent", None),
            P("latent"),
            P("latent"),
            P("latent"),
            P("latent"),
        ),
        out_specs=(
            P("latent", None),
            P("latent"),
            P("latent"),
            P("latent", None),
            P("latent", None),
            P("latent"),
            P("latent"),
            P("latent"),
            P("latent"),
            P(),
        ),
        check_vma=False,
    )
```

```python
import jax
import jax.numpy as jnp
from jax import lax
from jax.experimental import pallas as pl
from jax.experimental.pallas import tpu as pltpu
from jax.sharding import PartitionSpec as P

STEP = 1000
sparsity_coeff = 5.0
beta_one = 0.9
beta_two = 0.999
learn_rate = 0.001
adam_eps = 1e-08
norm_eps = 1e-06

TOK = 1152
WIDTH = 4096
ROWS = 288
CHUNK = 144
PART = 48
MAIN, SIDE = 64, 16
LAT = 256
VMEM_LIMIT = 40 * 1024 * 1024
F32 = jnp.float32
BF16 = jnp.bfloat16
MESH = pl.DeviceIdType.MESH


def adam_update(param, grad, mean, var):
    mean_new = beta_one * mean + (1.0 - beta_one) * grad
    var_new = beta_two * var + (1.0 - beta_two) * grad * grad
    rate = learn_rate / (1.0 - beta_one**STEP)
    scaled = var_new * (1.0 / (1.0 - beta_two**STEP))
    param_new = param - rate * mean_new / (scaled * lax.rsqrt(scaled) + adam_eps)
    return (param_new, mean_new, var_new)


def mod4(v):
    return lax.rem(v + 4, 4)


def dot(a, b):
    return jnp.dot(a, b, preferred_element_type=F32)


def dot_nt(a, b):
    return lax.dot_general(a, b, (((1,), (1,)), ((), ())), preferred_element_type=F32)


def kernel(
    inputs_hbm, center_hbm, offset_hbm, dict_ref,
    grad_ref, g_in, small_ref,
    inputs_ref, center_ref, offset_ref,
    weights, gx, ge, pre, dpre_own, acts, tmat, gacc,
    raw, raw_in, cen, cen_in, sm, sm_in, sums, sums_in,
    part, b0_out, b0_in, a0_out, a0_in, z_out, z_in,
    side, y_out, y_in, c1_out, c1_in, c2_out, c2_in,
    g_out,
    vx, vx_in, vz, vz_in,
    load_sem, pair_send, pair_recv,
    gx_send, gx_recv, ge_send, ge_recv, rs_send, rs_recv,
    g_send, g_recv, v_send, v_recv,
):
    h = lax.axis_index("dp")
    i = lax.axis_index("latent")
    core = lax.rem(i, 2)
    y = lax.rem(i // 2, 4)
    x = lax.rem(i // 8, 4)
    zl = i // 32
    z = 2 * h + zl

    def dev(xx, yy, zz, cc):
        return (zz // 2, ((lax.rem(zz, 2) * 4 + xx) * 4 + yy) * 2 + cc)

    coord = {"x": x, "y": y, "z": z}
    place = {(a, s): mod4(coord[a] + s) for a in coord for s in range(4)}
    near = {}
    for s in range(1, 4):
        near["x", s] = dev(place["x", s], y, z, core)
        near["y", s] = dev(x, place["y", s], z, core)
        near["z", s] = dev(x, y, place["z", s], core)

    def along(axis, step):
        return near[axis, step % 4]

    sibling = dev(x, y, z, 1 - core)
    far_z = 2 * h + 1 - zl
    other_z = dev(x, y, far_z, core)

    def rcopy(src, dst, ssem, rsem, device):
        return pltpu.make_async_remote_copy(
            src_ref=src, dst_ref=dst, send_sem=ssem, recv_sem=rsem,
            device_id=device, device_id_type=MESH,
        )

    def load(j):
        return pltpu.make_async_copy(
            dict_ref.at[:, pl.ds(512 * j, 512)], gacc.at[j], load_sem.at[j]
        )

    first_loads = [
        pltpu.make_async_copy(src, dst, load_sem.at[8 + k])
        for k, (src, dst) in enumerate(
            ((inputs_hbm, inputs_ref), (center_hbm, center_ref), (offset_hbm, offset_ref))
        )
    ]
    for c in first_loads:
        c.start()
    for j in range(8):
        load(j).start()

    plane = [
        dev(place["x", a], place["y", b], z, core) for a in range(4) for b in range(4) if a + b
    ]
    column = [
        dev(x, y, place["z", a], c)
        for a in range(4) for b, c in enumerate((core, 1 - core)) if a + b
    ]
    across = {
        axis: [near[axis, a] for a in range(1, 4)]
        + [
            dev(place["x", a], y, far_z, core) if axis == "x" else dev(x, place["y", a], far_z, core)
            for a in range(4)
        ]
        for axis in ("x", "y")
    }
    barrier = pltpu.get_barrier_semaphore()
    partners = plane + column + across["x"][4:] + across["y"][4:]
    for partner in partners:
        pl.semaphore_signal(barrier, inc=1, device_id=partner, device_id_type=MESH)

    for c in first_loads:
        c.wait()
    lane = lax.broadcasted_iota(jnp.int32, (1, 128), 1)
    mine = (lane // 64) == core
    both = inputs_ref[...].astype(F32)
    both = jnp.concatenate([both, both], axis=0).T
    raw[...] = jnp.where(mine, both, 0.0).astype(BF16).reshape(2, ROWS, 128)
    cboth = jnp.concatenate([center_ref[...], center_ref[...]], axis=1)
    cen[...] = jnp.broadcast_to(jnp.where(mine, cboth, 0.0), (8, 128))
    pl.semaphore_wait(barrier, len(partners))

    pair = [
        rcopy(raw.at[1 - core], raw_in, pair_send.at[0], pair_recv.at[0], sibling),
        rcopy(cen, cen_in, pair_send.at[1], pair_recv.at[1], sibling),
    ]
    for c in pair:
        c.start()
    for c in pair:
        c.wait_recv()
    center = cen[0:1, :] + cen_in[0:1, :]

    def own_rows(t):
        rows = pl.ds(CHUNK * t, CHUNK)
        return raw[core, rows].astype(F32) + raw_in[rows].astype(F32)

    sent = []

    def flush(log):
        for c in log:
            c.wait_send()
        log.clear()

    orders = (("y", "x", "z"), ("x", "z", "y"), ("z", "y", "x"))
    dirs = ((0, 1), (1, -1))

    def gather(buf, t, block, ssem, rsem, log):
        at = [tuple(coord[a] for a in reversed(o)) for o in orders]
        for p in range(3):
            buf[(t, p) + at[p]] = block[PART * p : PART * (p + 1)]

        def chunk(p, f, step):
            q = place[orders[p][f], step % 4]
            return (t, p) + at[p][: 2 - f] + (q,)

        def send(p, f, e, idx, step):
            ref = buf.at[idx]
            rcopy(
                ref, ref, ssem.at[t, p, f], rsem.at[t, p, e], along(orders[p][f], step)
            ).start()

        def whole(p, f, e, idx):
            ref = buf.at[idx]
            return rcopy(ref, ref, ssem.at[t, p, f], rsem.at[t, p, e], sibling)

        def triple(p, f):
            return (t, p) + at[p][: 2 - f] + (pl.ds(0, 3),)

        def double(p, f):
            return (t, p) + at[p][: 2 - f] + (pl.ds(0, 2),)

        def single(p, f):
            return (t, p) + at[p][: 2 - f] + (0,)

        for p in range(3):
            for step in (1, 3, 2):
                send(p, 0, 0, chunk(p, 0, 0), step)
            log.append(whole(p, 0, 0, triple(p, 0)))
        yield
        for p in range(3):
            whole(p, 0, 0, triple(p, 0)).wait_recv()
            for k, step in dirs:
                send(p, 1, 1, chunk(p, 1, 0), step)
            log.append(whole(p, 1, 1, triple(p, 1)))
        yield
        for p in range(3):
            whole(p, 1, 1, double(p, 1)).wait_recv()
            for k, step in dirs:
                send(p, 1, 2, chunk(p, 1, -step) + (pl.ds(2 * k, 2),), step)
        yield
        for p in range(3):
            whole(p, 1, 2, single(p, 1)).wait_recv()
            for k, step in dirs:
                send(p, 2, 3, chunk(p, 2, 0) + (pl.ds(2 * k, 2),), step)
            log.append(whole(p, 2, 3, triple(p, 2)))
        for p in range(3):
            for k, step in dirs:
                send(p, 2, 4, chunk(p, 2, 0) + (pl.ds(2 - 2 * k, 2),), step)
        yield
        for p in range(3):
            whole(p, 2, 3, single(p, 2)).wait_recv()
            for k, step in dirs:
                send(p, 2, 5, chunk(p, 2, -step) + (pl.ds(2 * k, 2),), step)
        yield
        for e in (4, 5):
            for p in range(3):
                whole(p, 2, e, single(p, 2)).wait_recv()

    def weight_copy(j):
        return rcopy(
            weights.at[0, j], weights.at[1, j], pair_send.at[2], pair_recv.at[2], sibling
        )

    all_weight_copies = rcopy(
        weights.at[0], weights.at[1], pair_send.at[2], pair_recv.at[2], sibling
    )

    small_copy = rcopy(sm, sm_in, pair_send.at[3], pair_recv.at[3], sibling)

    def prepare(part):
        sq = jnp.zeros((LAT, 128), F32)
        for j in range(4 * part, 4 * part + 4):
            load(j).wait()
            block = gacc[j]
            weights[0, j] = block.astype(BF16)
            weight_copy(j).start()
            for k in range(4):
                piece = block[:, 128 * k : 128 * (k + 1)]
                sq = sq + piece * piece
        squares.append(sq)
        if part == 0:
            return
        norm = jnp.sqrt(jnp.sum(squares[0] + squares[1], axis=1, keepdims=True) + norm_eps)
        sm[...] = jnp.zeros((8, LAT), F32)
        sm[0:1, :] = offset_ref[...]
        sm[1:2, :] = jnp.broadcast_to(norm, (LAT, 128)).T[0:1, :]
        small_copy.start()

    squares = []

    def slab(buf, t, j):
        jz, jx = j // 4, j % 4
        rows = []
        for r in range(2):
            zz = 2 * (h if r == 0 else 1 - h) + jz
            for p in range(3):
                cols = []
                for yy in range(4):
                    idx = ((zz, jx, yy), (yy, zz, jx), (jx, yy, zz))[p]
                    cols.append(buf[(t, p) + idx])
                rows.append(jnp.concatenate(cols, axis=1))
        return jnp.concatenate(rows, axis=0)

    def all_weights(j):
        return jnp.concatenate([weights[0, j], weights[1, j]], axis=0)

    def project(buf, t, which):
        rows = jnp.concatenate([slab(buf, t, j) for j in range(8)], axis=1)
        return dot_nt(rows, jnp.concatenate([weights[which, j] for j in range(8)], axis=1))

    def ring_first(src, lead, axis, b_out, b_in, sems, log):
        q = place[axis, 2]
        for k, step in dirs:
            b_out[k][...] = src[lead + (q, pl.ds(2 * k, 2))].astype(BF16)
            c = rcopy(b_out[k], b_in[k], sems[0][k], sems[1][k], along(axis, step))
            c.start()
            log.append(c)

    def ring_second(src, lead, axis, b_out, b_in, a_out, a_in, sems, log):
        for k, step in dirs:
            q = place[axis, step % 4]
            mix, rest = pl.ds(2 * k, 2), pl.ds(2 - 2 * k, 2)
            a_out[k][rest] = src[lead + (q, rest)].astype(BF16)
            rcopy(b_out[k], b_in[k], sems[0][k], sems[1][k], along(axis, step)).wait_recv()
            a_out[k][mix] = (src[lead + (q, mix)] + b_in[k][...].astype(F32)).astype(BF16)
            c = rcopy(a_out[k], a_in[k], sems[0][2 + k], sems[1][2 + k], along(axis, step))
            c.start()
            log.append(c)

    def ring_last(src, lead, axis, a_out, a_in, sems):
        for k, step in dirs:
            rcopy(a_out[k], a_in[k], sems[0][2 + k], sems[1][2 + k], along(axis, step)).wait_recv()
        return src[lead + (coord[axis],)] + a_in[0][...].astype(F32) + a_in[1][...].astype(F32)

    def direct_first(value, axis, out, into, sems, log):
        for k in range(3):
            out[k] = value(place[axis, k + 1]).astype(BF16)
            rcopy(out.at[k], into.at[k], sems[0][0], sems[1][0], along(axis, k + 1)).start()
        log.append(rcopy(out, into, sems[0][0], sems[1][0], sibling))

    def direct_last(value, axis, out, into, sems):
        rcopy(out, into, sems[0][0], sems[1][0], sibling).wait_recv()
        total = value(coord[axis])
        for k in range(3):
            total = total + into[k].astype(F32)
        return total

    def scatter(t, log):
        side_axes = ("x", "y") if t == 0 else ("y", "x")
        axes = (("x", "y"), ("y", "x"), side_axes)

        def some(ref, *lead):
            return [ref.at[lead + (k,)] for k in range(ref.shape[len(lead)])]

        def sems(p, s):
            return (
                [rs_send.at[t, p, 4 * s + e] for e in range(4)],
                [rs_recv.at[t, p, 4 * s + e] for e in range(4)],
            )

        def line_copy(p, e):
            src, dst = (z_out.at[t, p], z_in.at[t, p]) if e is None else (z_out.at[t, p, e], z_in.at[t, p, e])
            device = sibling if e is None else across[axes[p][1]][e]
            return rcopy(src, dst, rs_send.at[t, p, 4], rs_recv.at[t, p, 4], device)

        pair_copy = rcopy(
            y_out.at[t], y_in.at[t], rs_send.at[t, 2, 8], rs_recv.at[t, 2, 8], other_z
        )
        y_out[t] = side[t, 1 - zl].astype(BF16)
        pair_copy.start()
        ring = [
            (part, (t, p), axes[p][0], some(b0_out, t, p), some(b0_in, t, p), some(a0_out, t, p), some(a0_in, t, p), sems(p, 0))
            for p in range(2)
        ]
        for a in ring:
            ring_first(*a[:5], a[7], log)
        yield
        pair_copy.wait_recv()
        side[t, zl] = side[t, zl] + y_in[t].astype(F32)
        wide = (lambda q: side[t, zl, q], axes[2][0], c1_out.at[t], c1_in.at[t], sems(2, 0))
        direct_first(*wide, log)
        for a in ring:
            ring_second(*a, log)
        yield
        here = coord[axes[2][0]]
        side[t, zl, here] = direct_last(*wide)
        thin = (lambda q: side[t, zl, here, q], axes[2][1], c2_out.at[t], c2_in.at[t], sems(2, 1))
        direct_first(*thin, log)
        for p in range(2):
            first = coord[axes[p][0]]
            part[t, p, first] = ring_last(*ring[p][:3], *ring[p][5:])
            for e in range(7):
                a, w = (e + 1, zl) if e < 3 else (e - 3, 1 - zl)
                z_out[t, p, e] = part[t, p, first, place[axes[p][1], a], w].astype(BF16)
                line_copy(p, e).start()
            log.append(line_copy(p, None))
        yield
        out = []
        for p in range(2):
            total = part[t, p, coord[axes[p][0]], coord[axes[p][1]], zl]
            line_copy(p, None).wait_recv()
            for e in range(7):
                total = total + z_in[t, p, e].astype(F32)
            out.append(total)
        out.append(direct_last(*thin))
        log.append(pair_copy)
        result[t] = jnp.concatenate(out, axis=0)

    result, sq, err_sum, act_own, act_all, off_own, off_all = {}, {}, {}, {}, {}, {}, {}

    def g_copy(j):
        cols = pl.ds(pl.multiple_of(512 * j, 512), 512)
        return rcopy(g_out.at[:, cols], g_in.at[:, cols], g_send.at[0], g_recv.at[0], sibling)

    def gradient(t, first, last, parts=(1, 0)):
        @pl.loop(first, last, unroll=2)
        def _(j):
            both = jnp.concatenate([slab(gx, t, j), slab(ge, t, j)], axis=0)
            cols = pl.ds(pl.multiple_of(512 * j, 512), 512)
            for which in parts:
                out = dot(tmat[t, LAT * which : LAT * (which + 1), :], both)
                if which == 0:
                    grad_ref[:, cols] = out if t == 0 else grad_ref[:, cols] + out
                elif t == 0:
                    gacc[j] = out
                else:
                    g_out[:, cols] = (gacc[j] + out).astype(BF16)
                    g_copy(j).start()

    def steps(t):
        centered = (own_rows(t) - center).astype(BF16)
        log_x, log_r, log_e = [], [], []
        yield from gather(gx, t, centered, gx_send, gx_recv, log_x)
        pre[t, :, :LAT] = project(gx, t, 0) + sm[0:1, :]
        yield
        if t == 0:
            all_weight_copies.wait_recv()
            small_copy.wait_recv()
        pre[t, :, LAT:] = project(gx, t, 1) + sm_in[0:1, :]
        yield
        acts[t] = jnp.maximum(pre[t], 0.0).astype(BF16)

        @pl.loop(0, 8, unroll=4)
        def _(j):
            jz, jx = j // 4, lax.rem(j, 4)
            out = dot(acts[t, :CHUNK], all_weights(j))
            for yy in range(4):
                cols = slice(128 * yy, 128 * (yy + 1))
                part[t, 0, jx, yy, jz] = out[:MAIN, cols]
                part[t, 1, yy, jx, jz] = out[MAIN : 2 * MAIN, cols]
                if t == 0:
                    side[t, jz, jx, yy] = out[2 * MAIN :, cols]
                else:
                    side[t, jz, yy, jx] = out[2 * MAIN :, cols]

        ready = scatter(t, log_r)
        next(ready)
        flush(log_x)
        act = acts[t]
        act_own[t] = jnp.sum(act[:CHUNK].astype(F32), axis=0, keepdims=True)
        act_all[t] = act_own[t] + jnp.sum(act[CHUNK:].astype(F32), axis=0, keepdims=True)
        yield
        yield from ready
        err = result[t] + center - own_rows(t)
        sq[t] = jnp.sum(err * err)
        err_sum[t] = jnp.sum(err, axis=0, keepdims=True)
        derr = (2.0 / TOK * err).astype(BF16)
        ready = gather(ge, t, derr, ge_send, ge_recv, log_e)
        next(ready)
        flush(log_r)
        yield
        yield from ready
        sent.extend(log_e)

        def backward(which, norm):
            dacts = project(ge, t, which) + sparsity_coeff / TOK * norm
            kept = pre[t, :, LAT * which : LAT * (which + 1)] > 0
            return jnp.where(kept, dacts, 0.0).astype(BF16)

        dpre_own[t] = backward(0, sm[1:2, :])
        yield
        dpre = jnp.concatenate([dpre_own[t], backward(1, sm_in[1:2, :])], axis=1)
        tmat[t] = jnp.concatenate([dpre, acts[t]], axis=0).T
        off_own[t] = jnp.sum(dpre[:CHUNK].astype(F32), axis=0, keepdims=True)
        off_all[t] = off_own[t] + jnp.sum(dpre[CHUNK:].astype(F32), axis=0, keepdims=True)
        yield
        if t == 0:
            gradient(0, 0, 4)
            yield
            gradient(0, 4, 8)
            yield

    run = [steps(0), steps(1)]
    plan = "010u0101w01001010101010100101010101011"
    for who in plan:
        if who in "uw":
            prepare("uw".index(who))
        else:
            next(run[int(who)])
    for one in run:
        assert next(one, one) is one
    off = off_own[0] + off_own[1]
    offs = off_all[0] + off_all[1]
    act_tot = act_all[0] + act_all[1]
    norms = jnp.concatenate([sm[1:2, :], sm_in[1:2, :]], axis=1)
    spars = jnp.sum((act_own[0] + act_own[1]) * norms)

    sums[...] = jnp.zeros((2, 8, LAT), F32)
    for k in range(2):
        sums[k, 0:1, :] = offs[:, LAT * k : LAT * (k + 1)]
        sums[k, 1:2, :] = act_tot[:, LAT * k : LAT * (k + 1)]
    sums_copy = rcopy(sums.at[1], sums_in, pair_send.at[4], pair_recv.at[4], sibling)
    sums_copy.start()

    hi = off.astype(BF16)
    rest = off - hi.astype(F32)
    mid = rest.astype(BF16)
    low = (rest - mid.astype(F32)).astype(BF16)
    row = lax.broadcasted_iota(jnp.int32, (16, 512), 0)
    terms = jnp.where(
        row == 0, hi.astype(F32),
        jnp.where(row == 1, mid.astype(F32), jnp.where(row == 2, low.astype(F32), 0.0)),
    ).astype(BF16)
    for j in range(8):
        enc = jnp.sum(dot(terms, all_weights(j)), axis=0, keepdims=True)
        for yy in range(4):
            vx[(j % 4) * 4 + yy, j // 4 : j // 4 + 1, :] = -enc[:, 128 * yy : 128 * (yy + 1)]
    scalars = jnp.where(lane == 0, sq[0] + sq[1], jnp.where(lane == 1, spars, 0.0))
    for k in range(16):
        vx[k, 2:8, :] = jnp.broadcast_to(scalars, (6, 128))
    here = x * 4 + y
    sub = lax.broadcasted_iota(jnp.int32, (8, 128), 0)
    vx[here] = vx[here] + jnp.where(sub == zl, 2.0 / TOK * (err_sum[0] + err_sum[1]), 0.0)

    def v_plane(e):
        a, b = (e + 1) // 4, (e + 1) % 4
        return rcopy(
            vx.at[place["x", a] * 4 + place["y", b]], vx_in.at[e], v_send.at[0], v_recv.at[0], plane[e]
        )

    def v_column(e):
        return rcopy(vz, vz_in.at[e], v_send.at[1], v_recv.at[1], column[e])

    v_planes = rcopy(vx_in, vx_in, v_send.at[0], v_recv.at[0], sibling)
    v_columns = rcopy(vz_in, vz_in, v_send.at[1], v_recv.at[1], sibling)

    for e in range(15):
        v_plane(e).start()
    gradient(1, 0, 8, (1,))
    total = vx[here]
    v_planes.wait_recv()
    for e in range(15):
        total = total + vx_in[e]
    vz[...] = total
    for e in range(7):
        v_column(e).start()
    gradient(1, 0, 8, (0,))
    v_columns.wait_recv()
    for e in range(7):
        total = total + vz_in[e]
    sums_copy.wait_recv()

    small_ref[...] = jnp.zeros((8, LAT), F32)
    small_ref[0:1, :] = sums[0, 0:1, :] + sums_in[0:1, :]
    small_ref[1:2, :] = sparsity_coeff / TOK * (sums[0, 1:2, :] + sums_in[1:2, :]) / sm[1:2, :]
    slot = jnp.where(zl == 0, total[0:1], total[1:2])
    small_ref[2:3, 0:64] = jnp.where(core == 0, slot[:, :64], slot[:, 64:])
    small_ref[3:4, 0:128] = total[2:3]

    flush(sent)
    for c in pair + [all_weight_copies, small_copy, sums_copy]:
        c.wait_send()
    v_planes.wait_send()
    v_columns.wait_send()
    all_g_copies = rcopy(g_out, g_in, g_send.at[0], g_recv.at[0], sibling)
    all_g_copies.wait_recv()
    all_g_copies.wait_send()


def step_kernel(inputs, center, offset, dictionary):
    vm = pltpu.VMEM
    dma = pltpu.SemaphoreType.DMA
    block = (PART, 128)
    main, side = (MAIN, 128), (SIDE, 128)
    return pl.pallas_call(
        kernel,
        out_shape=[
            jax.ShapeDtypeStruct((LAT, WIDTH), F32),
            jax.ShapeDtypeStruct((LAT, WIDTH), BF16),
            jax.ShapeDtypeStruct((8, LAT), F32),
        ],
        in_specs=[pl.BlockSpec(memory_space=pltpu.HBM)] * 4,
        out_specs=[pl.BlockSpec(memory_space=pltpu.VMEM)] * 3,
        scratch_shapes=[
            vm((64, 2 * ROWS), BF16),
            vm((1, 64), F32),
            vm((1, LAT), F32),
            vm((2, 8, LAT, 512), BF16),
            vm((2, 3, 4, 4, 4) + block, BF16),
            vm((2, 3, 4, 4, 4) + block, BF16),
            vm((2, 2 * CHUNK, 512), F32),
            vm((2, 2 * CHUNK, LAT), BF16),
            vm((2, 2 * CHUNK, 512), BF16),
            vm((2, 512, 4 * CHUNK), BF16),
            vm((8, LAT, 512), F32),
            vm((2, ROWS, 128), BF16),
            vm((ROWS, 128), BF16),
            vm((8, 128), F32),
            vm((8, 128), F32),
            vm((8, LAT), F32),
            vm((8, LAT), F32),
            vm((2, 8, LAT), F32),
            vm((8, LAT), F32),
            vm((2, 2, 4, 4, 2) + main, F32),
            vm((2, 2, 2, 2, 2) + main, BF16),
            vm((2, 2, 2, 2, 2) + main, BF16),
            vm((2, 2, 2, 4, 2) + main, BF16),
            vm((2, 2, 2, 4, 2) + main, BF16),
            vm((2, 2, 7) + main, BF16),
            vm((2, 2, 7) + main, BF16),
            vm((2, 2, 4, 4) + side, F32),
            vm((2, 4, 4) + side, BF16),
            vm((2, 4, 4) + side, BF16),
            vm((2, 3, 4) + side, BF16),
            vm((2, 3, 4) + side, BF16),
            vm((2, 3) + side, BF16),
            vm((2, 3) + side, BF16),
            vm((LAT, WIDTH), BF16),
            vm((16, 8, 128), F32),
            vm((15, 8, 128), F32),
            vm((8, 128), F32),
            vm((7, 8, 128), F32),
            dma((11,)),
            dma((5,)),
            dma((5,)),
            dma((2, 3, 3)),
            dma((2, 3, 6)),
            dma((2, 3, 3)),
            dma((2, 3, 6)),
            dma((2, 3, 9)),
            dma((2, 3, 9)),
            dma((1,)),
            dma((1,)),
            dma((2,)),
            dma((2,)),
        ],
        compiler_params=pltpu.CompilerParams(
            collective_id=0, has_side_effects=True, vmem_limit_bytes=VMEM_LIMIT
        ),
        cost_estimate=pl.CostEstimate(
            flops=12 * 2**30, bytes_accessed=160 * 2**20, transcendentals=0
        ),
        name="step",
    )(*[pltpu.with_memory_space_constraint(v, pltpu.HBM) for v in (inputs, center, offset, dictionary)])


def small_kernel(small, offset, offset_mean, offset_var, center, center_mean, center_var, *outs):
    rows = (
        (offset, small[0:1, :], offset_mean, offset_var),
        (center, small[2:3, 0:64], center_mean, center_var),
    )
    for k, (param, grad, mean, var) in enumerate(rows):
        new = adam_update(param[...], grad, mean[...], var[...])
        for n in range(3):
            outs[3 * k + n][...] = new[n]
    scalars = small[3:4, 0:128]
    lane = lax.broadcasted_iota(jnp.int32, (1, 128), 1)
    weight = jnp.where(lane == 0, 1.0, jnp.where(lane == 1, sparsity_coeff, 0.0))
    outs[6][...] = jnp.sum(scalars * weight, axis=1, keepdims=True) / (TOK * WIDTH)


def small_step(small, *rows):
    shapes = [(1, LAT)] * 3 + [(1, 64)] * 3 + [(1, 1)]
    return pl.pallas_call(
        small_kernel,
        out_shape=[jax.ShapeDtypeStruct(s, F32) for s in shapes],
        in_specs=[pl.BlockSpec(memory_space=pltpu.VMEM)] * 7,
        out_specs=[pl.BlockSpec(memory_space=pltpu.VMEM)] * 7,
        compiler_params=pltpu.CompilerParams(vmem_limit_bytes=2**20),
        name="small",
    )(small, *[r.reshape(1, -1) for r in rows])


def body(
    inputs,
    dictionary,
    offset,
    center,
    dict_mean,
    dict_var,
    offset_mean,
    offset_var,
    center_mean,
    center_var,
):
    grad, shared, small = step_kernel(
        inputs.T, center.reshape(1, -1), offset.reshape(1, -1), dictionary
    )
    g_dict = grad + shared.astype(F32) + small[1][:, None] * dictionary
    fresh_dict, mean_dict, var_dict = adam_update(dictionary, g_dict, dict_mean, dict_var)
    *rows, loss = small_step(
        small, offset, offset_mean, offset_var, center, center_mean, center_var
    )
    fresh_offset, mean_offset, var_offset, fresh_center, mean_center, var_center = [
        r.reshape(-1) for r in rows
    ]
    loss_value = loss.reshape(())
    return (
        fresh_dict,
        fresh_offset,
        fresh_center,
        mean_dict,
        var_dict,
        mean_offset,
        var_offset,
        mean_center,
        var_center,
        loss_value,
    )


def solution(mesh):
    return jax.shard_map(
        body,
        mesh=mesh,
        in_specs=(
            P("dp", "latent"),
            P("latent", None),
            P("latent"),
            P("latent"),
            P("latent", None),
            P("latent", None),
            P("latent"),
            P("latent"),
            P("latent"),
            P("latent"),
        ),
        out_specs=(
            P("latent", None),
            P("latent"),
            P("latent"),
            P("latent", None),
            P("latent", None),
            P("latent"),
            P("latent"),
            P("latent"),
            P("latent"),
            P(),
        ),
        check_vma=False,
    )
```

```python
import jax
import jax.numpy as jnp
from jax import lax
from jax.experimental import pallas as pl
from jax.experimental.pallas import tpu as pltpu
from jax.sharding import PartitionSpec as P

STEP = 1000
sparsity_coeff = 5.0
beta_one = 0.9
beta_two = 0.999
learn_rate = 0.001
adam_eps = 1e-08
norm_eps = 1e-06

TOK = 1152
WIDTH = 4096
ROWS = 288
CHUNK = 144
PART = 48
MAIN, SIDE = 64, 16
LAT = 256
VMEM_LIMIT = 40 * 1024 * 1024
F32 = jnp.float32
BF16 = jnp.bfloat16
MESH = pl.DeviceIdType.MESH


def adam_update(param, grad, mean, var):
    mean_new = beta_one * mean + (1.0 - beta_one) * grad
    var_new = beta_two * var + (1.0 - beta_two) * grad * grad
    rate = learn_rate / (1.0 - beta_one**STEP)
    scaled = var_new * (1.0 / (1.0 - beta_two**STEP))
    param_new = param - rate * mean_new / (scaled * lax.rsqrt(scaled) + adam_eps)
    return (param_new, mean_new, var_new)


def mod4(v):
    return lax.rem(v + 4, 4)


def dot(a, b):
    return jnp.dot(a, b, preferred_element_type=F32)


def dot_nt(a, b):
    return lax.dot_general(a, b, (((1,), (1,)), ((), ())), preferred_element_type=F32)


def kernel(
    inputs_hbm, center_hbm, offset_hbm, dict_ref,
    grad_ref, g_in, small_ref,
    inputs_ref, center_ref, offset_ref,
    weights, gx, ge, pre, dacc, acts, tmat, gacc,
    raw, raw_in, cen, cen_in, sm, sm_in, sums, sums_in,
    part, b0_out, b0_in, a0_out, a0_in, z_out, z_in,
    side, y_out, y_in, c1_out, c1_in, c2_out, c2_in,
    g_out,
    vx, vx_in, vz, vz_in,
    load_sem, pair_send, pair_recv,
    gx_send, gx_recv, ge_send, ge_recv, rs_send, rs_recv,
    g_send, g_recv, v_send, v_recv,
):
    h = lax.axis_index("dp")
    i = lax.axis_index("latent")
    core = lax.rem(i, 2)
    y = lax.rem(i // 2, 4)
    x = lax.rem(i // 8, 4)
    zl = i // 32
    z = 2 * h + zl

    def dev(xx, yy, zz, cc):
        return (zz // 2, ((lax.rem(zz, 2) * 4 + xx) * 4 + yy) * 2 + cc)

    coord = {"x": x, "y": y, "z": z}
    place = {(a, s): mod4(coord[a] + s) for a in coord for s in range(4)}
    near = {}
    for s in range(1, 4):
        near["x", s] = dev(place["x", s], y, z, core)
        near["y", s] = dev(x, place["y", s], z, core)
        near["z", s] = dev(x, y, place["z", s], core)

    def along(axis, step):
        return near[axis, step % 4]

    sibling = dev(x, y, z, 1 - core)
    far_z = 2 * h + 1 - zl
    other_z = dev(x, y, far_z, core)

    def rcopy(src, dst, ssem, rsem, device):
        return pltpu.make_async_remote_copy(
            src_ref=src, dst_ref=dst, send_sem=ssem, recv_sem=rsem,
            device_id=device, device_id_type=MESH,
        )

    def load(j):
        return pltpu.make_async_copy(
            dict_ref.at[:, pl.ds(512 * j, 512)], gacc.at[j], load_sem.at[j]
        )

    first_loads = [
        pltpu.make_async_copy(src, dst, load_sem.at[8 + k])
        for k, (src, dst) in enumerate(
            ((inputs_hbm, inputs_ref), (center_hbm, center_ref), (offset_hbm, offset_ref))
        )
    ]
    for c in first_loads:
        c.start()
    for j in range(8):
        load(j).start()

    plane = [
        dev(place["x", a], place["y", b], z, core) for a in range(4) for b in range(4) if a + b
    ]
    column = [
        dev(x, y, place["z", a], c)
        for a in range(4) for b, c in enumerate((core, 1 - core)) if a + b
    ]
    across = {
        axis: [near[axis, a] for a in range(1, 4)]
        + [
            dev(place["x", a], y, far_z, core) if axis == "x" else dev(x, place["y", a], far_z, core)
            for a in range(4)
        ]
        for axis in ("x", "y")
    }
    barrier = pltpu.get_barrier_semaphore()
    partners = plane + column + across["x"][4:] + across["y"][4:]
    for partner in partners:
        pl.semaphore_signal(barrier, inc=1, device_id=partner, device_id_type=MESH)

    for c in first_loads:
        c.wait()
    lane = lax.broadcasted_iota(jnp.int32, (1, 128), 1)
    mine = (lane // 64) == core
    both = inputs_ref[...].astype(F32)
    both = jnp.concatenate([both, both], axis=0).T
    raw[...] = jnp.where(mine, both, 0.0).astype(BF16).reshape(2, ROWS, 128)
    cboth = jnp.concatenate([center_ref[...], center_ref[...]], axis=1)
    cen[...] = jnp.broadcast_to(jnp.where(mine, cboth, 0.0), (8, 128))
    pl.semaphore_wait(barrier, len(partners))

    pair = [
        rcopy(raw.at[1 - core], raw_in, pair_send.at[0], pair_recv.at[0], sibling),
        rcopy(cen, cen_in, pair_send.at[1], pair_recv.at[1], sibling),
    ]
    for c in pair:
        c.start()
    for c in pair:
        c.wait_recv()
    center = cen[0:1, :] + cen_in[0:1, :]

    def own_rows(t):
        rows = pl.ds(CHUNK * t, CHUNK)
        return raw[core, rows].astype(F32) + raw_in[rows].astype(F32)

    sent = []

    def flush(log):
        for c in log:
            c.wait_send()
        log.clear()

    orders = (("y", "x", "z"), ("x", "z", "y"), ("z", "y", "x"))
    dirs = ((0, 1), (1, -1))

    def gather(buf, t, block, ssem, rsem, log):
        at = [tuple(coord[a] for a in reversed(o)) for o in orders]
        for p in range(3):
            buf[(t, p) + at[p]] = block[PART * p : PART * (p + 1)]

        def chunk(p, f, step):
            q = place[orders[p][f], step % 4]
            return (t, p) + at[p][: 2 - f] + (q,)

        def send(p, f, e, idx, step):
            ref = buf.at[idx]
            rcopy(
                ref, ref, ssem.at[t, p, f], rsem.at[t, p, e], along(orders[p][f], step)
            ).start()

        def whole(p, f, e, idx):
            ref = buf.at[idx]
            return rcopy(ref, ref, ssem.at[t, p, f], rsem.at[t, p, e], sibling)

        def triple(p, f):
            return (t, p) + at[p][: 2 - f] + (pl.ds(0, 3),)

        def double(p, f):
            return (t, p) + at[p][: 2 - f] + (pl.ds(0, 2),)

        def single(p, f):
            return (t, p) + at[p][: 2 - f] + (0,)

        for p in range(3):
            for step in (1, 3, 2):
                send(p, 0, 0, chunk(p, 0, 0), step)
            log.append(whole(p, 0, 0, triple(p, 0)))
        yield
        for p in range(3):
            whole(p, 0, 0, triple(p, 0)).wait_recv()
            for k, step in dirs:
                send(p, 1, 1, chunk(p, 1, 0), step)
            log.append(whole(p, 1, 1, triple(p, 1)))
        yield
        for p in range(3):
            whole(p, 1, 1, double(p, 1)).wait_recv()
            for k, step in dirs:
                send(p, 1, 2, chunk(p, 1, -step) + (pl.ds(2 * k, 2),), step)
        yield
        for p in range(3):
            whole(p, 1, 2, single(p, 1)).wait_recv()
            for k, step in dirs:
                send(p, 2, 3, chunk(p, 2, 0) + (pl.ds(2 * k, 2),), step)
            log.append(whole(p, 2, 3, triple(p, 2)))
        for p in range(3):
            for k, step in dirs:
                send(p, 2, 4, chunk(p, 2, 0) + (pl.ds(2 - 2 * k, 2),), step)
        yield
        for p in range(3):
            whole(p, 2, 3, single(p, 2)).wait_recv()
            for k, step in dirs:
                send(p, 2, 5, chunk(p, 2, -step) + (pl.ds(2 * k, 2),), step)
        yield
        for e in (4, 5):
            for p in range(3):
                whole(p, 2, e, single(p, 2)).wait_recv()

    def weight_copy(j):
        return rcopy(
            weights.at[0, j], weights.at[1, j], pair_send.at[2], pair_recv.at[2], sibling
        )

    all_weight_copies = rcopy(
        weights.at[0], weights.at[1], pair_send.at[2], pair_recv.at[2], sibling
    )

    small_copy = rcopy(sm, sm_in, pair_send.at[3], pair_recv.at[3], sibling)

    def prepare():
        sq = jnp.zeros((LAT, 1), F32)
        for j in range(8):
            load(j).wait()
            block = gacc[j]
            weights[0, j] = block.astype(BF16)
            weight_copy(j).start()
            sq = sq + jnp.sum(block * block, axis=1, keepdims=True)
        norm = jnp.sqrt(sq + norm_eps)
        sm[...] = jnp.zeros((8, LAT), F32)
        sm[0:1, :] = offset_ref[...]
        sm[1:2, :] = jnp.broadcast_to(norm, (LAT, 128)).T[0:1, :]
        small_copy.start()

    def slab(buf, t, j):
        jz, jx = j // 4, j % 4
        rows = []
        for r in range(2):
            zz = 2 * (h if r == 0 else 1 - h) + jz
            for p in range(3):
                cols = []
                for yy in range(4):
                    idx = ((zz, jx, yy), (yy, zz, jx), (jx, yy, zz))[p]
                    cols.append(buf[(t, p) + idx])
                rows.append(jnp.concatenate(cols, axis=1))
        return jnp.concatenate(rows, axis=0)

    def all_weights(j):
        return jnp.concatenate([weights[0, j], weights[1, j]], axis=0)

    def project(buf, t, half):
        rows = jnp.concatenate([slab(buf, t, 4 * half + jx) for jx in range(4)], axis=1)
        cols = jnp.concatenate([all_weights(4 * half + jx) for jx in range(4)], axis=1)
        return dot_nt(rows, cols)

    def ring_first(src, lead, axis, b_out, b_in, sems, log):
        q = place[axis, 2]
        for k, step in dirs:
            b_out[k][...] = src[lead + (q, pl.ds(2 * k, 2))].astype(BF16)
            c = rcopy(b_out[k], b_in[k], sems[0][k], sems[1][k], along(axis, step))
            c.start()
            log.append(c)

    def ring_second(src, lead, axis, b_out, b_in, a_out, a_in, sems, log):
        for k, step in dirs:
            q = place[axis, step % 4]
            mix, rest = pl.ds(2 * k, 2), pl.ds(2 - 2 * k, 2)
            a_out[k][rest] = src[lead + (q, rest)].astype(BF16)
            rcopy(b_out[k], b_in[k], sems[0][k], sems[1][k], along(axis, step)).wait_recv()
            a_out[k][mix] = (src[lead + (q, mix)] + b_in[k][...].astype(F32)).astype(BF16)
            c = rcopy(a_out[k], a_in[k], sems[0][2 + k], sems[1][2 + k], along(axis, step))
            c.start()
            log.append(c)

    def ring_last(src, lead, axis, a_out, a_in, sems):
        for k, step in dirs:
            rcopy(a_out[k], a_in[k], sems[0][2 + k], sems[1][2 + k], along(axis, step)).wait_recv()
        return src[lead + (coord[axis],)] + a_in[0][...].astype(F32) + a_in[1][...].astype(F32)

    def direct_first(value, axis, out, into, sems, log):
        for k in range(3):
            out[k] = value(place[axis, k + 1]).astype(BF16)
            rcopy(out.at[k], into.at[k], sems[0][0], sems[1][0], along(axis, k + 1)).start()
        log.append(rcopy(out, into, sems[0][0], sems[1][0], sibling))

    def direct_last(value, axis, out, into, sems):
        rcopy(out, into, sems[0][0], sems[1][0], sibling).wait_recv()
        total = value(coord[axis])
        for k in range(3):
            total = total + into[k].astype(F32)
        return total

    def scatter(t, log):
        side_axes = ("x", "y") if t == 0 else ("y", "x")
        axes = (("x", "y"), ("y", "x"), side_axes)

        def some(ref, *lead):
            return [ref.at[lead + (k,)] for k in range(ref.shape[len(lead)])]

        def sems(p, s):
            return (
                [rs_send.at[t, p, 4 * s + e] for e in range(4)],
                [rs_recv.at[t, p, 4 * s + e] for e in range(4)],
            )

        def line_copy(p, e):
            src, dst = (z_out.at[t, p], z_in.at[t, p]) if e is None else (z_out.at[t, p, e], z_in.at[t, p, e])
            device = sibling if e is None else across[axes[p][1]][e]
            return rcopy(src, dst, rs_send.at[t, p, 4], rs_recv.at[t, p, 4], device)

        pair_copy = rcopy(
            y_out.at[t], y_in.at[t], rs_send.at[t, 2, 8], rs_recv.at[t, 2, 8], other_z
        )
        y_out[t] = side[t, 1 - zl].astype(BF16)
        pair_copy.start()
        ring = [
            (part, (t, p), axes[p][0], some(b0_out, t, p), some(b0_in, t, p), some(a0_out, t, p), some(a0_in, t, p), sems(p, 0))
            for p in range(2)
        ]
        for a in ring:
            ring_first(*a[:5], a[7], log)
        yield
        pair_copy.wait_recv()
        side[t, zl] = side[t, zl] + y_in[t].astype(F32)
        wide = (lambda q: side[t, zl, q], axes[2][0], c1_out.at[t], c1_in.at[t], sems(2, 0))
        direct_first(*wide, log)
        for a in ring:
            ring_second(*a, log)
        yield
        here = coord[axes[2][0]]
        side[t, zl, here] = direct_last(*wide)
        thin = (lambda q: side[t, zl, here, q], axes[2][1], c2_out.at[t], c2_in.at[t], sems(2, 1))
        direct_first(*thin, log)
        for p in range(2):
            first = coord[axes[p][0]]
            part[t, p, first] = ring_last(*ring[p][:3], *ring[p][5:])
            for e in range(7):
                a, w = (e + 1, zl) if e < 3 else (e - 3, 1 - zl)
                z_out[t, p, e] = part[t, p, first, place[axes[p][1], a], w].astype(BF16)
                line_copy(p, e).start()
            log.append(line_copy(p, None))
        yield
        out = []
        for p in range(2):
            total = part[t, p, coord[axes[p][0]], coord[axes[p][1]], zl]
            line_copy(p, None).wait_recv()
            for e in range(7):
                total = total + z_in[t, p, e].astype(F32)
            out.append(total)
        out.append(direct_last(*thin))
        log.append(pair_copy)
        result[t] = jnp.concatenate(out, axis=0)

    result, sq, err_sum, act_own, act_all, off_own, off_all = {}, {}, {}, {}, {}, {}, {}
    shared = {}

    def g_copy(j):
        cols = pl.ds(pl.multiple_of(512 * j, 512), 512)
        return rcopy(g_out.at[:, cols], g_in.at[:, cols], g_send.at[0], g_recv.at[0], sibling)

    def gradient(t, first, last):
        @pl.loop(first, last, unroll=2)
        def _(j):
            out = dot(tmat[t], jnp.concatenate([slab(gx, t, j), slab(ge, t, j)], axis=0))
            cols = pl.ds(pl.multiple_of(512 * j, 512), 512)
            if t == 0:
                gacc[j] = out[LAT:]
                grad_ref[:, cols] = out[:LAT]
            else:
                g_out[:, cols] = (gacc[j] + out[LAT:]).astype(BF16)
                g_copy(j).start()
                grad_ref[:, cols] = grad_ref[:, cols] + out[:LAT]

    def steps(t):
        centered = (own_rows(t) - center).astype(BF16)
        log_x, log_r, log_e = [], [], []
        yield from gather(gx, t, centered, gx_send, gx_recv, log_x)
        if t == 0:
            all_weight_copies.wait_recv()
            small_copy.wait_recv()
            shared["bias"] = jnp.concatenate([sm[0:1, :], sm_in[0:1, :]], axis=1)
            shared["norms"] = jnp.concatenate([sm[1:2, :], sm_in[1:2, :]], axis=1)
        norms = shared["norms"]
        pre[t] = project(gx, t, 0) + shared["bias"]
        yield
        pre[t] = pre[t] + project(gx, t, 1)
        yield
        acts[t] = jnp.maximum(pre[t], 0.0).astype(BF16)

        @pl.loop(0, 8, unroll=4)
        def _(j):
            jz, jx = j // 4, lax.rem(j, 4)
            out = dot(acts[t, :CHUNK], all_weights(j))
            for yy in range(4):
                cols = slice(128 * yy, 128 * (yy + 1))
                part[t, 0, jx, yy, jz] = out[:MAIN, cols]
                part[t, 1, yy, jx, jz] = out[MAIN : 2 * MAIN, cols]
                if t == 0:
                    side[t, jz, jx, yy] = out[2 * MAIN :, cols]
                else:
                    side[t, jz, yy, jx] = out[2 * MAIN :, cols]

        ready = scatter(t, log_r)
        next(ready)
        flush(log_x)
        act = acts[t]
        act_own[t] = jnp.sum(act[:CHUNK].astype(F32), axis=0, keepdims=True)
        act_all[t] = act_own[t] + jnp.sum(act[CHUNK:].astype(F32), axis=0, keepdims=True)
        yield
        yield from ready
        err = result[t] + center - own_rows(t)
        sq[t] = jnp.sum(err * err)
        err_sum[t] = jnp.sum(err, axis=0, keepdims=True)
        derr = (2.0 / TOK * err).astype(BF16)
        ready = gather(ge, t, derr, ge_send, ge_recv, log_e)
        next(ready)
        flush(log_r)
        yield
        yield from ready
        sent.extend(log_e)
        dacc[t] = project(ge, t, 0) + sparsity_coeff / TOK * norms
        yield
        dacts = dacc[t] + project(ge, t, 1)
        dpre = jnp.where(pre[t] > 0, dacts, 0.0).astype(BF16)
        tmat[t] = jnp.concatenate([dpre, acts[t]], axis=0).T
        off_own[t] = jnp.sum(dpre[:CHUNK].astype(F32), axis=0, keepdims=True)
        off_all[t] = off_own[t] + jnp.sum(dpre[CHUNK:].astype(F32), axis=0, keepdims=True)
        yield
        if t == 0:
            gradient(0, 0, 4)
            yield
            gradient(0, 4, 8)
            yield

    run = [steps(0), steps(1)]
    plan = "0101010w01001010110101010101010010011"
    for who in plan:
        if who == "w":
            prepare()
        else:
            next(run[int(who)])
    for one in run:
        assert next(one, one) is one
    off = off_own[0] + off_own[1]
    offs = off_all[0] + off_all[1]
    act_tot = act_all[0] + act_all[1]
    spars = jnp.sum((act_own[0] + act_own[1]) * shared["norms"])

    sums[...] = jnp.zeros((2, 8, LAT), F32)
    for k in range(2):
        sums[k, 0:1, :] = offs[:, LAT * k : LAT * (k + 1)]
        sums[k, 1:2, :] = act_tot[:, LAT * k : LAT * (k + 1)]
    sums_copy = rcopy(sums.at[1], sums_in, pair_send.at[4], pair_recv.at[4], sibling)
    sums_copy.start()

    hi = off.astype(BF16)
    rest = off - hi.astype(F32)
    mid = rest.astype(BF16)
    low = (rest - mid.astype(F32)).astype(BF16)
    row = lax.broadcasted_iota(jnp.int32, (16, 512), 0)
    terms = jnp.where(
        row == 0, hi.astype(F32),
        jnp.where(row == 1, mid.astype(F32), jnp.where(row == 2, low.astype(F32), 0.0)),
    ).astype(BF16)
    for j in range(8):
        enc = jnp.sum(dot(terms, all_weights(j)), axis=0, keepdims=True)
        for yy in range(4):
            vx[(j % 4) * 4 + yy, j // 4 : j // 4 + 1, :] = -enc[:, 128 * yy : 128 * (yy + 1)]
    scalars = jnp.where(lane == 0, sq[0] + sq[1], jnp.where(lane == 1, spars, 0.0))
    for k in range(16):
        vx[k, 2:8, :] = jnp.broadcast_to(scalars, (6, 128))
    here = x * 4 + y
    sub = lax.broadcasted_iota(jnp.int32, (8, 128), 0)
    vx[here] = vx[here] + jnp.where(sub == zl, 2.0 / TOK * (err_sum[0] + err_sum[1]), 0.0)

    def v_plane(e):
        a, b = (e + 1) // 4, (e + 1) % 4
        return rcopy(
            vx.at[place["x", a] * 4 + place["y", b]], vx_in.at[e], v_send.at[0], v_recv.at[0], plane[e]
        )

    def v_column(e):
        return rcopy(vz, vz_in.at[e], v_send.at[1], v_recv.at[1], column[e])

    v_planes = rcopy(vx_in, vx_in, v_send.at[0], v_recv.at[0], sibling)
    v_columns = rcopy(vz_in, vz_in, v_send.at[1], v_recv.at[1], sibling)

    for e in range(15):
        v_plane(e).start()
    gradient(1, 0, 4)
    total = vx[here]
    v_planes.wait_recv()
    for e in range(15):
        total = total + vx_in[e]
    vz[...] = total
    for e in range(7):
        v_column(e).start()
    gradient(1, 4, 8)
    v_columns.wait_recv()
    for e in range(7):
        total = total + vz_in[e]
    sums_copy.wait_recv()

    small_ref[...] = jnp.zeros((8, LAT), F32)
    small_ref[0:1, :] = sums[0, 0:1, :] + sums_in[0:1, :]
    small_ref[1:2, :] = sparsity_coeff / TOK * (sums[0, 1:2, :] + sums_in[1:2, :]) / sm[1:2, :]
    slot = jnp.where(zl == 0, total[0:1], total[1:2])
    small_ref[2:3, 0:64] = jnp.where(core == 0, slot[:, :64], slot[:, 64:])
    small_ref[3:4, 0:128] = total[2:3]

    flush(sent)
    for c in pair + [all_weight_copies, small_copy, sums_copy]:
        c.wait_send()
    v_planes.wait_send()
    v_columns.wait_send()
    all_g_copies = rcopy(g_out, g_in, g_send.at[0], g_recv.at[0], sibling)
    all_g_copies.wait_recv()
    all_g_copies.wait_send()


def step_kernel(inputs, center, offset, dictionary):
    vm = pltpu.VMEM
    dma = pltpu.SemaphoreType.DMA
    block = (PART, 128)
    main, side = (MAIN, 128), (SIDE, 128)
    return pl.pallas_call(
        kernel,
        out_shape=[
            jax.ShapeDtypeStruct((LAT, WIDTH), F32),
            jax.ShapeDtypeStruct((LAT, WIDTH), BF16),
            jax.ShapeDtypeStruct((8, LAT), F32),
        ],
        in_specs=[pl.BlockSpec(memory_space=pltpu.HBM)] * 4,
        out_specs=[pl.BlockSpec(memory_space=pltpu.VMEM)] * 3,
        scratch_shapes=[
            vm((64, 2 * ROWS), BF16),
            vm((1, 64), F32),
            vm((1, LAT), F32),
            vm((2, 8, LAT, 512), BF16),
            vm((2, 3, 4, 4, 4) + block, BF16),
            vm((2, 3, 4, 4, 4) + block, BF16),
            vm((2, 2 * CHUNK, 512), F32),
            vm((2, 2 * CHUNK, 512), F32),
            vm((2, 2 * CHUNK, 512), BF16),
            vm((2, 512, 4 * CHUNK), BF16),
            vm((8, LAT, 512), F32),
            vm((2, ROWS, 128), BF16),
            vm((ROWS, 128), BF16),
            vm((8, 128), F32),
            vm((8, 128), F32),
            vm((8, LAT), F32),
            vm((8, LAT), F32),
            vm((2, 8, LAT), F32),
            vm((8, LAT), F32),
            vm((2, 2, 4, 4, 2) + main, F32),
            vm((2, 2, 2, 2, 2) + main, BF16),
            vm((2, 2, 2, 2, 2) + main, BF16),
            vm((2, 2, 2, 4, 2) + main, BF16),
            vm((2, 2, 2, 4, 2) + main, BF16),
            vm((2, 2, 7) + main, BF16),
            vm((2, 2, 7) + main, BF16),
            vm((2, 2, 4, 4) + side, F32),
            vm((2, 4, 4) + side, BF16),
            vm((2, 4, 4) + side, BF16),
            vm((2, 3, 4) + side, BF16),
            vm((2, 3, 4) + side, BF16),
            vm((2, 3) + side, BF16),
            vm((2, 3) + side, BF16),
            vm((LAT, WIDTH), BF16),
            vm((16, 8, 128), F32),
            vm((15, 8, 128), F32),
            vm((8, 128), F32),
            vm((7, 8, 128), F32),
            dma((11,)),
            dma((5,)),
            dma((5,)),
            dma((2, 3, 3)),
            dma((2, 3, 6)),
            dma((2, 3, 3)),
            dma((2, 3, 6)),
            dma((2, 3, 9)),
            dma((2, 3, 9)),
            dma((1,)),
            dma((1,)),
            dma((2,)),
            dma((2,)),
        ],
        compiler_params=pltpu.CompilerParams(
            collective_id=0, has_side_effects=True, vmem_limit_bytes=VMEM_LIMIT
        ),
        cost_estimate=pl.CostEstimate(
            flops=12 * 2**30, bytes_accessed=160 * 2**20, transcendentals=0
        ),
        name="step",
    )(*[pltpu.with_memory_space_constraint(v, pltpu.HBM) for v in (inputs, center, offset, dictionary)])


def small_kernel(small, offset, offset_mean, offset_var, center, center_mean, center_var, *outs):
    rows = (
        (offset, small[0:1, :], offset_mean, offset_var),
        (center, small[2:3, 0:64], center_mean, center_var),
    )
    for k, (param, grad, mean, var) in enumerate(rows):
        new = adam_update(param[...], grad, mean[...], var[...])
        for n in range(3):
            outs[3 * k + n][...] = new[n]
    scalars = small[3:4, 0:128]
    lane = lax.broadcasted_iota(jnp.int32, (1, 128), 1)
    weight = jnp.where(lane == 0, 1.0, jnp.where(lane == 1, sparsity_coeff, 0.0))
    outs[6][...] = jnp.sum(scalars * weight, axis=1, keepdims=True) / (TOK * WIDTH)


def small_step(small, *rows):
    shapes = [(1, LAT)] * 3 + [(1, 64)] * 3 + [(1, 1)]
    return pl.pallas_call(
        small_kernel,
        out_shape=[jax.ShapeDtypeStruct(s, F32) for s in shapes],
        in_specs=[pl.BlockSpec(memory_space=pltpu.VMEM)] * 7,
        out_specs=[pl.BlockSpec(memory_space=pltpu.VMEM)] * 7,
        compiler_params=pltpu.CompilerParams(vmem_limit_bytes=2**20),
        name="small",
    )(small, *[r.reshape(1, -1) for r in rows])


def body(
    inputs,
    dictionary,
    offset,
    center,
    dict_mean,
    dict_var,
    offset_mean,
    offset_var,
    center_mean,
    center_var,
):
    grad, shared, small = step_kernel(
        inputs.T, center.reshape(1, -1), offset.reshape(1, -1), dictionary
    )
    g_dict = grad + shared.astype(F32) + small[1][:, None] * dictionary
    fresh_dict, mean_dict, var_dict = adam_update(dictionary, g_dict, dict_mean, dict_var)
    *rows, loss = small_step(
        small, offset, offset_mean, offset_var, center, center_mean, center_var
    )
    fresh_offset, mean_offset, var_offset, fresh_center, mean_center, var_center = [
        r.reshape(-1) for r in rows
    ]
    loss_value = loss.reshape(())
    return (
        fresh_dict,
        fresh_offset,
        fresh_center,
        mean_dict,
        var_dict,
        mean_offset,
        var_offset,
        mean_center,
        var_center,
        loss_value,
    )


def solution(mesh):
    return jax.shard_map(
        body,
        mesh=mesh,
        in_specs=(
            P("dp", "latent"),
            P("latent", None),
            P("latent"),
            P("latent"),
            P("latent", None),
            P("latent", None),
            P("latent"),
            P("latent"),
            P("latent"),
            P("latent"),
        ),
        out_specs=(
            P("latent", None),
            P("latent"),
            P("latent"),
            P("latent", None),
            P("latent", None),
            P("latent"),
            P("latent"),
            P("latent"),
            P("latent"),
            P(),
        ),
        check_vma=False,
    )
```

```python
import jax
import jax.numpy as jnp
from jax import lax
from jax.experimental import pallas as pl
from jax.experimental.pallas import tpu as pltpu
from jax.sharding import PartitionSpec as P

STEP = 1000
sparsity_coeff = 5.0
beta_one = 0.9
beta_two = 0.999
learn_rate = 0.001
adam_eps = 1e-08
norm_eps = 1e-06

TOK = 1152
WIDTH = 4096
ROWS = 288
CHUNK = 144
PART = 48
MAIN, SIDE = 64, 16
LAT = 256
VMEM_LIMIT = 40 * 1024 * 1024
F32 = jnp.float32
BF16 = jnp.bfloat16
MESH = pl.DeviceIdType.MESH


def adam_update(param, grad, mean, var):
    mean_new = beta_one * mean + (1.0 - beta_one) * grad
    var_new = beta_two * var + (1.0 - beta_two) * grad * grad
    rate = learn_rate / (1.0 - beta_one**STEP)
    scaled = var_new * (1.0 / (1.0 - beta_two**STEP))
    param_new = param - rate * mean_new / (scaled * lax.rsqrt(scaled) + adam_eps)
    return (param_new, mean_new, var_new)


def mod4(v):
    return lax.rem(v + 4, 4)


def dot(a, b):
    return jnp.dot(a, b, preferred_element_type=F32)


def dot_nt(a, b):
    return lax.dot_general(a, b, (((1,), (1,)), ((), ())), preferred_element_type=F32)


def kernel(
    inputs_hbm, center_hbm, offset_hbm, dict_ref,
    grad_ref, g_in, small_ref,
    inputs_ref, center_ref, offset_ref,
    weights, gx, ge, pre, dacc, acts, tmat, gacc,
    raw, raw_in, cen, cen_in, sm, sm_in, sums, sums_in,
    part, b0_out, b0_in, a0_out, a0_in, z_out, z_in,
    side, y_out, y_in, c1_out, c1_in, c2_out, c2_in,
    g_out,
    vx, vx_in, vz, vz_in,
    load_sem, pair_send, pair_recv,
    gx_send, gx_recv, ge_send, ge_recv, rs_send, rs_recv,
    g_send, g_recv, v_send, v_recv,
):
    h = lax.axis_index("dp")
    i = lax.axis_index("latent")
    core = lax.rem(i, 2)
    y = lax.rem(i // 2, 4)
    x = lax.rem(i // 8, 4)
    zl = i // 32
    z = 2 * h + zl

    def dev(xx, yy, zz, cc):
        return (zz // 2, ((lax.rem(zz, 2) * 4 + xx) * 4 + yy) * 2 + cc)

    coord = {"x": x, "y": y, "z": z}
    place = {(a, s): mod4(coord[a] + s) for a in coord for s in range(4)}
    near = {}
    for s in range(1, 4):
        near["x", s] = dev(place["x", s], y, z, core)
        near["y", s] = dev(x, place["y", s], z, core)
        near["z", s] = dev(x, y, place["z", s], core)

    def along(axis, step):
        return near[axis, step % 4]

    sibling = dev(x, y, z, 1 - core)
    far_z = 2 * h + 1 - zl
    other_z = dev(x, y, far_z, core)

    def rcopy(src, dst, ssem, rsem, device):
        return pltpu.make_async_remote_copy(
            src_ref=src, dst_ref=dst, send_sem=ssem, recv_sem=rsem,
            device_id=device, device_id_type=MESH,
        )

    def load(j):
        return pltpu.make_async_copy(
            dict_ref.at[:, pl.ds(512 * j, 512)], gacc.at[j], load_sem.at[j]
        )

    first_loads = [
        pltpu.make_async_copy(src, dst, load_sem.at[8 + k])
        for k, (src, dst) in enumerate(
            ((inputs_hbm, inputs_ref), (center_hbm, center_ref), (offset_hbm, offset_ref))
        )
    ]
    for c in first_loads:
        c.start()
    for j in range(8):
        load(j).start()

    plane = [
        dev(place["x", a], place["y", b], z, core) for a in range(4) for b in range(4) if a + b
    ]
    column = [
        dev(x, y, place["z", a], c)
        for a in range(4) for b, c in enumerate((core, 1 - core)) if a + b
    ]
    across = {
        axis: [near[axis, a] for a in range(1, 4)]
        + [
            dev(place["x", a], y, far_z, core) if axis == "x" else dev(x, place["y", a], far_z, core)
            for a in range(4)
        ]
        for axis in ("x", "y")
    }
    barrier = pltpu.get_barrier_semaphore()
    partners = plane + column + across["x"][4:] + across["y"][4:]
    for partner in partners:
        pl.semaphore_signal(barrier, inc=1, device_id=partner, device_id_type=MESH)

    for c in first_loads:
        c.wait()
    lane = lax.broadcasted_iota(jnp.int32, (1, 128), 1)
    mine = (lane // 64) == core
    both = inputs_ref[...].astype(F32)
    both = jnp.concatenate([both, both], axis=0).T
    raw[...] = jnp.where(mine, both, 0.0).astype(BF16).reshape(2, ROWS, 128)
    cboth = jnp.concatenate([center_ref[...], center_ref[...]], axis=1)
    cen[...] = jnp.broadcast_to(jnp.where(mine, cboth, 0.0), (8, 128))
    pl.semaphore_wait(barrier, len(partners))

    pair = [
        rcopy(raw.at[1 - core], raw_in, pair_send.at[0], pair_recv.at[0], sibling),
        rcopy(cen, cen_in, pair_send.at[1], pair_recv.at[1], sibling),
    ]
    for c in pair:
        c.start()
    for c in pair:
        c.wait_recv()
    center = cen[0:1, :] + cen_in[0:1, :]

    def own_rows(t):
        rows = pl.ds(CHUNK * t, CHUNK)
        return raw[core, rows].astype(F32) + raw_in[rows].astype(F32)

    sent = []

    def flush(log):
        for c in log:
            c.wait_send()
        log.clear()

    orders = (("y", "x", "z"), ("x", "z", "y"), ("z", "y", "x"))
    dirs = ((0, 1), (1, -1))

    def gather(buf, t, block, ssem, rsem, log):
        at = [tuple(coord[a] for a in reversed(o)) for o in orders]
        for p in range(3):
            buf[(t, p) + at[p]] = block[PART * p : PART * (p + 1)]

        def chunk(p, f, step):
            q = place[orders[p][f], step % 4]
            return (t, p) + at[p][: 2 - f] + (q,)

        def send(p, f, e, idx, step):
            ref = buf.at[idx]
            rcopy(
                ref, ref, ssem.at[t, p, f], rsem.at[t, p, e], along(orders[p][f], step)
            ).start()

        def whole(p, f, e, idx):
            ref = buf.at[idx]
            return rcopy(ref, ref, ssem.at[t, p, f], rsem.at[t, p, e], sibling)

        def triple(p, f):
            return (t, p) + at[p][: 2 - f] + (pl.ds(0, 3),)

        def double(p, f):
            return (t, p) + at[p][: 2 - f] + (pl.ds(0, 2),)

        def single(p, f):
            return (t, p) + at[p][: 2 - f] + (0,)

        for p in range(3):
            for step in (1, 3, 2):
                send(p, 0, 0, chunk(p, 0, 0), step)
            log.append(whole(p, 0, 0, triple(p, 0)))
        yield
        for p in range(3):
            whole(p, 0, 0, triple(p, 0)).wait_recv()
            for k, step in dirs:
                send(p, 1, 1, chunk(p, 1, 0), step)
            log.append(whole(p, 1, 1, triple(p, 1)))
        yield
        for p in range(3):
            whole(p, 1, 1, double(p, 1)).wait_recv()
            for k, step in dirs:
                send(p, 1, 2, chunk(p, 1, -step) + (pl.ds(2 * k, 2),), step)
        yield
        for p in range(3):
            whole(p, 1, 2, single(p, 1)).wait_recv()
            for k, step in dirs:
                send(p, 2, 3, chunk(p, 2, 0) + (pl.ds(2 * k, 2),), step)
            log.append(whole(p, 2, 3, triple(p, 2)))
        for p in range(3):
            for k, step in dirs:
                send(p, 2, 4, chunk(p, 2, 0) + (pl.ds(2 - 2 * k, 2),), step)
        yield
        for p in range(3):
            whole(p, 2, 3, single(p, 2)).wait_recv()
            for k, step in dirs:
                send(p, 2, 5, chunk(p, 2, -step) + (pl.ds(2 * k, 2),), step)
        yield
        for e in (4, 5):
            for p in range(3):
                whole(p, 2, e, single(p, 2)).wait_recv()

    def weight_copy(j):
        return rcopy(
            weights.at[0, j], weights.at[1, j], pair_send.at[2], pair_recv.at[2], sibling
        )

    all_weight_copies = rcopy(
        weights.at[0], weights.at[1], pair_send.at[2], pair_recv.at[2], sibling
    )

    small_copy = rcopy(sm, sm_in, pair_send.at[3], pair_recv.at[3], sibling)

    def prepare():
        sq = jnp.zeros((LAT, 1), F32)
        for j in range(8):
            load(j).wait()
            block = gacc[j]
            weights[0, j] = block.astype(BF16)
            weight_copy(j).start()
            sq = sq + jnp.sum(block * block, axis=1, keepdims=True)
        norm = jnp.sqrt(sq + norm_eps)
        sm[...] = jnp.zeros((8, LAT), F32)
        sm[0:1, :] = offset_ref[...]
        sm[1:2, :] = jnp.broadcast_to(norm, (LAT, 128)).T[0:1, :]
        small_copy.start()

    def slab(buf, t, j, blocks=(0, 1, 2, 3)):
        jz, jx = j // 4, j % 4
        rows = []
        for r in range(2):
            zz = 2 * (h if r == 0 else 1 - h) + jz
            for p in range(3):
                cols = []
                for yy in blocks:
                    idx = ((zz, jx, yy), (yy, zz, jx), (jx, yy, zz))[p]
                    cols.append(buf[(t, p) + idx])
                rows.append(jnp.concatenate(cols, axis=1))
        return jnp.concatenate(rows, axis=0)

    def all_weights(j):
        return jnp.concatenate([weights[0, j], weights[1, j]], axis=0)

    def project(buf, t, half):
        rows = jnp.concatenate([slab(buf, t, 4 * half + jx) for jx in range(4)], axis=1)
        cols = jnp.concatenate([all_weights(4 * half + jx) for jx in range(4)], axis=1)
        return dot_nt(rows, cols)

    def ring_first(src, lead, axis, b_out, b_in, sems, log):
        q = place[axis, 2]
        for k, step in dirs:
            b_out[k][...] = src[lead + (q, pl.ds(2 * k, 2))].astype(BF16)
            c = rcopy(b_out[k], b_in[k], sems[0][k], sems[1][k], along(axis, step))
            c.start()
            log.append(c)

    def ring_second(src, lead, axis, b_out, b_in, a_out, a_in, sems, log):
        for k, step in dirs:
            q = place[axis, step % 4]
            mix, rest = pl.ds(2 * k, 2), pl.ds(2 - 2 * k, 2)
            a_out[k][rest] = src[lead + (q, rest)].astype(BF16)
            rcopy(b_out[k], b_in[k], sems[0][k], sems[1][k], along(axis, step)).wait_recv()
            a_out[k][mix] = (src[lead + (q, mix)] + b_in[k][...].astype(F32)).astype(BF16)
            c = rcopy(a_out[k], a_in[k], sems[0][2 + k], sems[1][2 + k], along(axis, step))
            c.start()
            log.append(c)

    def ring_last(src, lead, axis, a_out, a_in, sems):
        for k, step in dirs:
            rcopy(a_out[k], a_in[k], sems[0][2 + k], sems[1][2 + k], along(axis, step)).wait_recv()
        return src[lead + (coord[axis],)] + a_in[0][...].astype(F32) + a_in[1][...].astype(F32)

    def direct_first(value, axis, out, into, sems, log):
        for k in range(3):
            out[k] = value(place[axis, k + 1]).astype(BF16)
            rcopy(out.at[k], into.at[k], sems[0][0], sems[1][0], along(axis, k + 1)).start()
        log.append(rcopy(out, into, sems[0][0], sems[1][0], sibling))

    def direct_last(value, axis, out, into, sems):
        rcopy(out, into, sems[0][0], sems[1][0], sibling).wait_recv()
        total = value(coord[axis])
        for k in range(3):
            total = total + into[k].astype(F32)
        return total

    def scatter(t, log):
        side_axes = ("x", "y") if t == 0 else ("y", "x")
        axes = (("x", "y"), ("y", "x"), side_axes)

        def some(ref, *lead):
            return [ref.at[lead + (k,)] for k in range(ref.shape[len(lead)])]

        def sems(p, s):
            return (
                [rs_send.at[t, p, 4 * s + e] for e in range(4)],
                [rs_recv.at[t, p, 4 * s + e] for e in range(4)],
            )

        def line_copy(p, e):
            src, dst = (z_out.at[t, p], z_in.at[t, p]) if e is None else (z_out.at[t, p, e], z_in.at[t, p, e])
            device = sibling if e is None else across[axes[p][1]][e]
            return rcopy(src, dst, rs_send.at[t, p, 4], rs_recv.at[t, p, 4], device)

        pair_copy = rcopy(
            y_out.at[t], y_in.at[t], rs_send.at[t, 2, 8], rs_recv.at[t, 2, 8], other_z
        )
        y_out[t] = side[t, 1 - zl].astype(BF16)
        pair_copy.start()
        ring = [
            (part, (t, p), axes[p][0], some(b0_out, t, p), some(b0_in, t, p), some(a0_out, t, p), some(a0_in, t, p), sems(p, 0))
            for p in range(2)
        ]
        for a in ring:
            ring_first(*a[:5], a[7], log)
        yield
        pair_copy.wait_recv()
        side[t, zl] = side[t, zl] + y_in[t].astype(F32)
        wide = (lambda q: side[t, zl, q], axes[2][0], c1_out.at[t], c1_in.at[t], sems(2, 0))
        direct_first(*wide, log)
        for a in ring:
            ring_second(*a, log)
        yield
        here = coord[axes[2][0]]
        side[t, zl, here] = direct_last(*wide)
        thin = (lambda q: side[t, zl, here, q], axes[2][1], c2_out.at[t], c2_in.at[t], sems(2, 1))
        direct_first(*thin, log)
        for p in range(2):
            first = coord[axes[p][0]]
            part[t, p, first] = ring_last(*ring[p][:3], *ring[p][5:])
            for e in range(7):
                a, w = (e + 1, zl) if e < 3 else (e - 3, 1 - zl)
                z_out[t, p, e] = part[t, p, first, place[axes[p][1], a], w].astype(BF16)
                line_copy(p, e).start()
            log.append(line_copy(p, None))
        yield
        out = []
        for p in range(2):
            total = part[t, p, coord[axes[p][0]], coord[axes[p][1]], zl]
            line_copy(p, None).wait_recv()
            for e in range(7):
                total = total + z_in[t, p, e].astype(F32)
            out.append(total)
        out.append(direct_last(*thin))
        log.append(pair_copy)
        result[t] = jnp.concatenate(out, axis=0)

    result, sq, err_sum, act_own, act_all, off_own, off_all = {}, {}, {}, {}, {}, {}, {}
    shared = {}

    def g_copy(j):
        cols = pl.ds(pl.multiple_of(512 * j, 512), 512)
        return rcopy(g_out.at[:, cols], g_in.at[:, cols], g_send.at[0], g_recv.at[0], sibling)

    def gradient(t, first, last):
        @pl.loop(first, last)
        def _(j):
            for k in range(2):
                blocks = (2 * k, 2 * k + 1)
                both = jnp.concatenate([slab(gx, t, j, blocks), slab(ge, t, j, blocks)], axis=0)
                out = dot(tmat[t], both)
                half = slice(256 * k, 256 * (k + 1))
                cols = pl.ds(pl.multiple_of(512 * j + 256 * k, 256), 256)
                if t == 0:
                    gacc[j, :, half] = out[LAT:]
                    grad_ref[:, cols] = out[:LAT]
                else:
                    g_out[:, cols] = (gacc[j, :, half] + out[LAT:]).astype(BF16)
                    grad_ref[:, cols] = grad_ref[:, cols] + out[:LAT]
            if t == 1:
                g_copy(j).start()

    def steps(t):
        centered = (own_rows(t) - center).astype(BF16)
        log_x, log_r, log_e = [], [], []
        yield from gather(gx, t, centered, gx_send, gx_recv, log_x)
        if t == 0:
            all_weight_copies.wait_recv()
            small_copy.wait_recv()
            shared["bias"] = jnp.concatenate([sm[0:1, :], sm_in[0:1, :]], axis=1)
            shared["norms"] = jnp.concatenate([sm[1:2, :], sm_in[1:2, :]], axis=1)
        norms = shared["norms"]
        pre[t] = project(gx, t, 0) + shared["bias"]
        yield
        pre[t] = pre[t] + project(gx, t, 1)
        yield
        acts[t] = jnp.maximum(pre[t], 0.0).astype(BF16)

        @pl.loop(0, 8, unroll=4)
        def _(j):
            jz, jx = j // 4, lax.rem(j, 4)
            out = dot(acts[t, :CHUNK], all_weights(j))
            for yy in range(4):
                cols = slice(128 * yy, 128 * (yy + 1))
                part[t, 0, jx, yy, jz] = out[:MAIN, cols]
                part[t, 1, yy, jx, jz] = out[MAIN : 2 * MAIN, cols]
                if t == 0:
                    side[t, jz, jx, yy] = out[2 * MAIN :, cols]
                else:
                    side[t, jz, yy, jx] = out[2 * MAIN :, cols]

        ready = scatter(t, log_r)
        next(ready)
        flush(log_x)
        act = acts[t]
        act_own[t] = jnp.sum(act[:CHUNK].astype(F32), axis=0, keepdims=True)
        act_all[t] = act_own[t] + jnp.sum(act[CHUNK:].astype(F32), axis=0, keepdims=True)
        yield
        yield from ready
        err = result[t] + center - own_rows(t)
        sq[t] = jnp.sum(err * err)
        err_sum[t] = jnp.sum(err, axis=0, keepdims=True)
        derr = (2.0 / TOK * err).astype(BF16)
        ready = gather(ge, t, derr, ge_send, ge_recv, log_e)
        next(ready)
        flush(log_r)
        yield
        yield from ready
        sent.extend(log_e)
        dacc[t] = project(ge, t, 0) + sparsity_coeff / TOK * norms
        yield
        dacts = dacc[t] + project(ge, t, 1)
        dpre = jnp.where(pre[t] > 0, dacts, 0.0).astype(BF16)
        tmat[t] = jnp.concatenate([dpre, acts[t]], axis=0).T
        off_own[t] = jnp.sum(dpre[:CHUNK].astype(F32), axis=0, keepdims=True)
        off_all[t] = off_own[t] + jnp.sum(dpre[CHUNK:].astype(F32), axis=0, keepdims=True)
        yield
        if t == 0:
            gradient(0, 0, 4)
            yield
            gradient(0, 4, 8)
            yield

    run = [steps(0), steps(1)]
    plan = "0101010w01001010110101010101010010011"
    for who in plan:
        if who == "w":
            prepare()
        else:
            next(run[int(who)])
    for one in run:
        assert next(one, one) is one
    off = off_own[0] + off_own[1]
    offs = off_all[0] + off_all[1]
    act_tot = act_all[0] + act_all[1]
    spars = jnp.sum((act_own[0] + act_own[1]) * shared["norms"])

    sums[...] = jnp.zeros((2, 8, LAT), F32)
    for k in range(2):
        sums[k, 0:1, :] = offs[:, LAT * k : LAT * (k + 1)]
        sums[k, 1:2, :] = act_tot[:, LAT * k : LAT * (k + 1)]
    sums_copy = rcopy(sums.at[1], sums_in, pair_send.at[4], pair_recv.at[4], sibling)
    sums_copy.start()

    hi = off.astype(BF16)
    rest = off - hi.astype(F32)
    mid = rest.astype(BF16)
    low = (rest - mid.astype(F32)).astype(BF16)
    row = lax.broadcasted_iota(jnp.int32, (16, 512), 0)
    terms = jnp.where(
        row == 0, hi.astype(F32),
        jnp.where(row == 1, mid.astype(F32), jnp.where(row == 2, low.astype(F32), 0.0)),
    ).astype(BF16)
    for j in range(8):
        enc = jnp.sum(dot(terms, all_weights(j)), axis=0, keepdims=True)
        for yy in range(4):
            vx[(j % 4) * 4 + yy, j // 4 : j // 4 + 1, :] = -enc[:, 128 * yy : 128 * (yy + 1)]
    scalars = jnp.where(lane == 0, sq[0] + sq[1], jnp.where(lane == 1, spars, 0.0))
    for k in range(16):
        vx[k, 2:8, :] = jnp.broadcast_to(scalars, (6, 128))
    here = x * 4 + y
    sub = lax.broadcasted_iota(jnp.int32, (8, 128), 0)
    vx[here] = vx[here] + jnp.where(sub == zl, 2.0 / TOK * (err_sum[0] + err_sum[1]), 0.0)

    def v_plane(e):
        a, b = (e + 1) // 4, (e + 1) % 4
        return rcopy(
            vx.at[place["x", a] * 4 + place["y", b]], vx_in.at[e], v_send.at[0], v_recv.at[0], plane[e]
        )

    def v_column(e):
        return rcopy(vz, vz_in.at[e], v_send.at[1], v_recv.at[1], column[e])

    v_planes = rcopy(vx_in, vx_in, v_send.at[0], v_recv.at[0], sibling)
    v_columns = rcopy(vz_in, vz_in, v_send.at[1], v_recv.at[1], sibling)

    for e in range(15):
        v_plane(e).start()
    gradient(1, 0, 4)
    total = vx[here]
    v_planes.wait_recv()
    for e in range(15):
        total = total + vx_in[e]
    vz[...] = total
    for e in range(7):
        v_column(e).start()
    gradient(1, 4, 8)
    v_columns.wait_recv()
    for e in range(7):
        total = total + vz_in[e]
    sums_copy.wait_recv()

    small_ref[...] = jnp.zeros((8, LAT), F32)
    small_ref[0:1, :] = sums[0, 0:1, :] + sums_in[0:1, :]
    small_ref[1:2, :] = sparsity_coeff / TOK * (sums[0, 1:2, :] + sums_in[1:2, :]) / sm[1:2, :]
    slot = jnp.where(zl == 0, total[0:1], total[1:2])
    small_ref[2:3, 0:64] = jnp.where(core == 0, slot[:, :64], slot[:, 64:])
    small_ref[3:4, 0:128] = total[2:3]

    flush(sent)
    for c in pair + [all_weight_copies, small_copy, sums_copy]:
        c.wait_send()
    v_planes.wait_send()
    v_columns.wait_send()
    all_g_copies = rcopy(g_out, g_in, g_send.at[0], g_recv.at[0], sibling)
    all_g_copies.wait_recv()
    all_g_copies.wait_send()


def step_kernel(inputs, center, offset, dictionary):
    vm = pltpu.VMEM
    dma = pltpu.SemaphoreType.DMA
    block = (PART, 128)
    main, side = (MAIN, 128), (SIDE, 128)
    return pl.pallas_call(
        kernel,
        out_shape=[
            jax.ShapeDtypeStruct((LAT, WIDTH), F32),
            jax.ShapeDtypeStruct((LAT, WIDTH), BF16),
            jax.ShapeDtypeStruct((8, LAT), F32),
        ],
        in_specs=[pl.BlockSpec(memory_space=pltpu.HBM)] * 4,
        out_specs=[pl.BlockSpec(memory_space=pltpu.VMEM)] * 3,
        scratch_shapes=[
            vm((64, 2 * ROWS), BF16),
            vm((1, 64), F32),
            vm((1, LAT), F32),
            vm((2, 8, LAT, 512), BF16),
            vm((2, 3, 4, 4, 4) + block, BF16),
            vm((2, 3, 4, 4, 4) + block, BF16),
            vm((2, 2 * CHUNK, 512), F32),
            vm((2, 2 * CHUNK, 512), F32),
            vm((2, 2 * CHUNK, 512), BF16),
            vm((2, 512, 4 * CHUNK), BF16),
            vm((8, LAT, 512), F32),
            vm((2, ROWS, 128), BF16),
            vm((ROWS, 128), BF16),
            vm((8, 128), F32),
            vm((8, 128), F32),
            vm((8, LAT), F32),
            vm((8, LAT), F32),
            vm((2, 8, LAT), F32),
            vm((8, LAT), F32),
            vm((2, 2, 4, 4, 2) + main, F32),
            vm((2, 2, 2, 2, 2) + main, BF16),
            vm((2, 2, 2, 2, 2) + main, BF16),
            vm((2, 2, 2, 4, 2) + main, BF16),
            vm((2, 2, 2, 4, 2) + main, BF16),
            vm((2, 2, 7) + main, BF16),
            vm((2, 2, 7) + main, BF16),
            vm((2, 2, 4, 4) + side, F32),
            vm((2, 4, 4) + side, BF16),
            vm((2, 4, 4) + side, BF16),
            vm((2, 3, 4) + side, BF16),
            vm((2, 3, 4) + side, BF16),
            vm((2, 3) + side, BF16),
            vm((2, 3) + side, BF16),
            vm((LAT, WIDTH), BF16),
            vm((16, 8, 128), F32),
            vm((15, 8, 128), F32),
            vm((8, 128), F32),
            vm((7, 8, 128), F32),
            dma((11,)),
            dma((5,)),
            dma((5,)),
            dma((2, 3, 3)),
            dma((2, 3, 6)),
            dma((2, 3, 3)),
            dma((2, 3, 6)),
            dma((2, 3, 9)),
            dma((2, 3, 9)),
            dma((1,)),
            dma((1,)),
            dma((2,)),
            dma((2,)),
        ],
        compiler_params=pltpu.CompilerParams(
            collective_id=0, has_side_effects=True, vmem_limit_bytes=VMEM_LIMIT
        ),
        cost_estimate=pl.CostEstimate(
            flops=12 * 2**30, bytes_accessed=160 * 2**20, transcendentals=0
        ),
        name="step",
    )(*[pltpu.with_memory_space_constraint(v, pltpu.HBM) for v in (inputs, center, offset, dictionary)])


def small_kernel(small, offset, offset_mean, offset_var, center, center_mean, center_var, *outs):
    rows = (
        (offset, small[0:1, :], offset_mean, offset_var),
        (center, small[2:3, 0:64], center_mean, center_var),
    )
    for k, (param, grad, mean, var) in enumerate(rows):
        new = adam_update(param[...], grad, mean[...], var[...])
        for n in range(3):
            outs[3 * k + n][...] = new[n]
    scalars = small[3:4, 0:128]
    lane = lax.broadcasted_iota(jnp.int32, (1, 128), 1)
    weight = jnp.where(lane == 0, 1.0, jnp.where(lane == 1, sparsity_coeff, 0.0))
    outs[6][...] = jnp.sum(scalars * weight, axis=1, keepdims=True) / (TOK * WIDTH)


def small_step(small, *rows):
    shapes = [(1, LAT)] * 3 + [(1, 64)] * 3 + [(1, 1)]
    return pl.pallas_call(
        small_kernel,
        out_shape=[jax.ShapeDtypeStruct(s, F32) for s in shapes],
        in_specs=[pl.BlockSpec(memory_space=pltpu.VMEM)] * 7,
        out_specs=[pl.BlockSpec(memory_space=pltpu.VMEM)] * 7,
        compiler_params=pltpu.CompilerParams(vmem_limit_bytes=2**20),
        name="small",
    )(small, *[r.reshape(1, -1) for r in rows])


def body(
    inputs,
    dictionary,
    offset,
    center,
    dict_mean,
    dict_var,
    offset_mean,
    offset_var,
    center_mean,
    center_var,
):
    grad, shared, small = step_kernel(
        inputs.T, center.reshape(1, -1), offset.reshape(1, -1), dictionary
    )
    g_dict = grad + shared.astype(F32) + small[1][:, None] * dictionary
    fresh_dict, mean_dict, var_dict = adam_update(dictionary, g_dict, dict_mean, dict_var)
    *rows, loss = small_step(
        small, offset, offset_mean, offset_var, center, center_mean, center_var
    )
    fresh_offset, mean_offset, var_offset, fresh_center, mean_center, var_center = [
        r.reshape(-1) for r in rows
    ]
    loss_value = loss.reshape(())
    return (
        fresh_dict,
        fresh_offset,
        fresh_center,
        mean_dict,
        var_dict,
        mean_offset,
        var_offset,
        mean_center,
        var_center,
        loss_value,
    )


def solution(mesh):
    return jax.shard_map(
        body,
        mesh=mesh,
        in_specs=(
            P("dp", "latent"),
            P("latent", None),
            P("latent"),
            P("latent"),
            P("latent", None),
            P("latent", None),
            P("latent"),
            P("latent"),
            P("latent"),
            P("latent"),
        ),
        out_specs=(
            P("latent", None),
            P("latent"),
            P("latent"),
            P("latent", None),
            P("latent", None),
            P("latent"),
            P("latent"),
            P("latent"),
            P("latent"),
            P(),
        ),
        check_vma=False,
    )
```

```python
import jax
import jax.numpy as jnp
from jax import lax
from jax.experimental import pallas as pl
from jax.experimental.pallas import tpu as pltpu
from jax.sharding import PartitionSpec as P

STEP = 1000
sparsity_coeff = 5.0
beta_one = 0.9
beta_two = 0.999
learn_rate = 0.001
adam_eps = 1e-08
norm_eps = 1e-06

TOK = 1152
WIDTH = 4096
ROWS = 288
CHUNK = 144
PART = 48
MAIN, SIDE = 64, 16
LAT = 256
VMEM_LIMIT = 40 * 1024 * 1024
F32 = jnp.float32
BF16 = jnp.bfloat16
MESH = pl.DeviceIdType.MESH


def adam_update(param, grad, mean, var):
    mean_new = beta_one * mean + (1.0 - beta_one) * grad
    var_new = beta_two * var + (1.0 - beta_two) * grad * grad
    rate = learn_rate / (1.0 - beta_one**STEP)
    scaled = var_new * (1.0 / (1.0 - beta_two**STEP))
    param_new = param - rate * mean_new / (scaled * lax.rsqrt(scaled) + adam_eps)
    return (param_new, mean_new, var_new)


def mod4(v):
    return lax.rem(v + 4, 4)


def dot(a, b):
    return jnp.dot(a, b, preferred_element_type=F32)


def dot_nt(a, b):
    return lax.dot_general(a, b, (((1,), (1,)), ((), ())), preferred_element_type=F32)


def kernel(
    inputs_hbm, center_hbm, offset_hbm, dict_ref,
    grad_ref, g_in, small_ref,
    inputs_ref, center_ref, offset_ref,
    weights, gx, ge, pre, dacc, acts, act_t, dpre_t, gacc,
    raw, raw_in, cen, cen_in, sm, sm_in, stat, sums, sums_in,
    part, b0_out, b0_in, a0_out, a0_in, z_out, z_in,
    side, y_out, y_in, c1_out, c1_in, c2_out, c2_in,
    g_out,
    vx, vx_in, vz, vz_in,
    load_sem, pair_send, pair_recv,
    gx_send, gx_recv, ge_send, ge_recv, rs_send, rs_recv,
    g_send, g_recv, v_send, v_recv,
):
    h = lax.axis_index("dp")
    i = lax.axis_index("latent")
    core = lax.rem(i, 2)
    y = lax.rem(i // 2, 4)
    x = lax.rem(i // 8, 4)
    zl = i // 32
    z = 2 * h + zl

    def dev(xx, yy, zz, cc):
        return (zz // 2, ((lax.rem(zz, 2) * 4 + xx) * 4 + yy) * 2 + cc)

    coord = {"x": x, "y": y, "z": z}
    place = {(a, s): mod4(coord[a] + s) for a in coord for s in range(4)}
    near = {}
    for s in range(1, 4):
        near["x", s] = dev(place["x", s], y, z, core)
        near["y", s] = dev(x, place["y", s], z, core)
        near["z", s] = dev(x, y, place["z", s], core)

    def along(axis, step):
        return near[axis, step % 4]

    sibling = dev(x, y, z, 1 - core)
    far_z = 2 * h + 1 - zl
    other_z = dev(x, y, far_z, core)

    def rcopy(src, dst, ssem, rsem, device):
        return pltpu.make_async_remote_copy(
            src_ref=src, dst_ref=dst, send_sem=ssem, recv_sem=rsem,
            device_id=device, device_id_type=MESH,
        )

    def load(j):
        return pltpu.make_async_copy(
            dict_ref.at[:, pl.ds(512 * j, 512)], gacc.at[j], load_sem.at[j]
        )

    first_loads = [
        pltpu.make_async_copy(src, dst, load_sem.at[8 + k])
        for k, (src, dst) in enumerate(
            ((inputs_hbm, inputs_ref), (center_hbm, center_ref), (offset_hbm, offset_ref))
        )
    ]
    for c in first_loads:
        c.start()
    for j in range(8):
        load(j).start()

    plane = [
        dev(place["x", a], place["y", b], z, core) for a in range(4) for b in range(4) if a + b
    ]
    column = [
        dev(x, y, place["z", a], c)
        for a in range(4) for b, c in enumerate((core, 1 - core)) if a + b
    ]
    across = {
        axis: [near[axis, a] for a in range(1, 4)]
        + [
            dev(place["x", a], y, far_z, core) if axis == "x" else dev(x, place["y", a], far_z, core)
            for a in range(4)
        ]
        for axis in ("x", "y")
    }
    barrier = pltpu.get_barrier_semaphore()
    partners = plane + column + across["x"][4:] + across["y"][4:]
    for partner in partners:
        pl.semaphore_signal(barrier, inc=1, device_id=partner, device_id_type=MESH)

    for c in first_loads:
        c.wait()
    lane = lax.broadcasted_iota(jnp.int32, (1, 128), 1)
    mine = (lane // 64) == core
    both = inputs_ref[...].astype(F32)
    both = jnp.concatenate([both, both], axis=0).T
    raw[...] = jnp.where(mine, both, 0.0).astype(BF16).reshape(2, ROWS, 128)
    cboth = jnp.concatenate([center_ref[...], center_ref[...]], axis=1)
    cen[...] = jnp.broadcast_to(jnp.where(mine, cboth, 0.0), (8, 128))
    pl.semaphore_wait(barrier, len(partners))

    pair = [
        rcopy(raw.at[1 - core], raw_in, pair_send.at[0], pair_recv.at[0], sibling),
        rcopy(cen, cen_in, pair_send.at[1], pair_recv.at[1], sibling),
    ]
    for c in pair:
        c.start()
    for c in pair:
        c.wait_recv()
    center = cen[0:1, :] + cen_in[0:1, :]

    def own_rows(t):
        rows = pl.ds(CHUNK * t, CHUNK)
        return raw[core, rows].astype(F32) + raw_in[rows].astype(F32)

    sent = []

    def flush(log):
        for c in log:
            c.wait_send()
        log.clear()

    orders = (("y", "x", "z"), ("x", "z", "y"), ("z", "y", "x"))
    dirs = ((0, 1), (1, -1))

    def gather(buf, t, block, ssem, rsem, log):
        at = [tuple(coord[a] for a in reversed(o)) for o in orders]
        for p in range(3):
            buf[(t, p) + at[p]] = block[PART * p : PART * (p + 1)]

        def chunk(p, f, step):
            q = place[orders[p][f], step % 4]
            return (t, p) + at[p][: 2 - f] + (q,)

        def send(p, f, e, idx, step):
            ref = buf.at[idx]
            rcopy(
                ref, ref, ssem.at[t, p, f], rsem.at[t, p, e], along(orders[p][f], step)
            ).start()

        def whole(p, f, e, idx):
            ref = buf.at[idx]
            return rcopy(ref, ref, ssem.at[t, p, f], rsem.at[t, p, e], sibling)

        def triple(p, f):
            return (t, p) + at[p][: 2 - f] + (pl.ds(0, 3),)

        def double(p, f):
            return (t, p) + at[p][: 2 - f] + (pl.ds(0, 2),)

        def single(p, f):
            return (t, p) + at[p][: 2 - f] + (0,)

        for p in range(3):
            for step in (1, 3, 2):
                send(p, 0, 0, chunk(p, 0, 0), step)
            log.append(whole(p, 0, 0, triple(p, 0)))
        yield
        for p in range(3):
            whole(p, 0, 0, triple(p, 0)).wait_recv()
            for k, step in dirs:
                send(p, 1, 1, chunk(p, 1, 0), step)
            log.append(whole(p, 1, 1, triple(p, 1)))
        yield
        for p in range(3):
            whole(p, 1, 1, double(p, 1)).wait_recv()
            for k, step in dirs:
                send(p, 1, 2, chunk(p, 1, -step) + (pl.ds(2 * k, 2),), step)
        yield
        for p in range(3):
            whole(p, 1, 2, single(p, 1)).wait_recv()
            for k, step in dirs:
                send(p, 2, 3, chunk(p, 2, 0) + (pl.ds(2 * k, 2),), step)
            log.append(whole(p, 2, 3, triple(p, 2)))
        for p in range(3):
            for k, step in dirs:
                send(p, 2, 4, chunk(p, 2, 0) + (pl.ds(2 - 2 * k, 2),), step)
        yield
        for p in range(3):
            whole(p, 2, 3, single(p, 2)).wait_recv()
            for k, step in dirs:
                send(p, 2, 5, chunk(p, 2, -step) + (pl.ds(2 * k, 2),), step)
        yield
        for e in (4, 5):
            for p in range(3):
                whole(p, 2, e, single(p, 2)).wait_recv()

    def weight_copy(j):
        return rcopy(
            weights.at[0, j], weights.at[1, j], pair_send.at[2], pair_recv.at[2], sibling
        )

    all_weight_copies = rcopy(
        weights.at[0], weights.at[1], pair_send.at[2], pair_recv.at[2], sibling
    )

    small_copy = rcopy(sm, sm_in, pair_send.at[3], pair_recv.at[3], sibling)

    def prepare():
        sq = jnp.zeros((LAT, 1), F32)
        for j in range(8):
            load(j).wait()
            block = gacc[j]
            weights[0, j] = block.astype(BF16)
            weight_copy(j).start()
            sq = sq + jnp.sum(block * block, axis=1, keepdims=True)
        norm = jnp.sqrt(sq + norm_eps)
        offset = jnp.broadcast_to(offset_ref[...], (128, LAT)).T
        sm[...] = jnp.where(lane == 0, offset, jnp.where(lane == 1, norm, 0.0))
        small_copy.start()

    def slab(buf, t, j, blocks=(0, 1, 2, 3)):
        jz, jx = j // 4, j % 4
        rows = []
        for r in range(2):
            zz = 2 * (h if r == 0 else 1 - h) + jz
            for p in range(3):
                cols = []
                for yy in blocks:
                    idx = ((zz, jx, yy), (yy, zz, jx), (jx, yy, zz))[p]
                    cols.append(buf[(t, p) + idx])
                rows.append(jnp.concatenate(cols, axis=1))
        return jnp.concatenate(rows, axis=0)

    def all_weights(j):
        return jnp.concatenate([weights[0, j], weights[1, j]], axis=0)

    def project(buf, t, half):
        rows = jnp.concatenate([slab(buf, t, 4 * half + jx) for jx in range(4)], axis=1)
        cols = jnp.concatenate([all_weights(4 * half + jx) for jx in range(4)], axis=1)
        return dot_nt(cols, rows)

    def ring_first(src, lead, axis, b_out, b_in, sems, log):
        q = place[axis, 2]
        for k, step in dirs:
            b_out[k][...] = src[lead + (q, pl.ds(2 * k, 2))].astype(BF16)
            c = rcopy(b_out[k], b_in[k], sems[0][k], sems[1][k], along(axis, step))
            c.start()
            log.append(c)

    def ring_second(src, lead, axis, b_out, b_in, a_out, a_in, sems, log):
        for k, step in dirs:
            q = place[axis, step % 4]
            mix, rest = pl.ds(2 * k, 2), pl.ds(2 - 2 * k, 2)
            a_out[k][rest] = src[lead + (q, rest)].astype(BF16)
            rcopy(b_out[k], b_in[k], sems[0][k], sems[1][k], along(axis, step)).wait_recv()
            a_out[k][mix] = (src[lead + (q, mix)] + b_in[k][...].astype(F32)).astype(BF16)
            c = rcopy(a_out[k], a_in[k], sems[0][2 + k], sems[1][2 + k], along(axis, step))
            c.start()
            log.append(c)

    def ring_last(src, lead, axis, a_out, a_in, sems):
        for k, step in dirs:
            rcopy(a_out[k], a_in[k], sems[0][2 + k], sems[1][2 + k], along(axis, step)).wait_recv()
        return src[lead + (coord[axis],)] + a_in[0][...].astype(F32) + a_in[1][...].astype(F32)

    def direct_first(value, axis, out, into, sems, log):
        for k in range(3):
            out[k] = value(place[axis, k + 1]).astype(BF16)
            rcopy(out.at[k], into.at[k], sems[0][0], sems[1][0], along(axis, k + 1)).start()
        log.append(rcopy(out, into, sems[0][0], sems[1][0], sibling))

    def direct_last(value, axis, out, into, sems):
        rcopy(out, into, sems[0][0], sems[1][0], sibling).wait_recv()
        total = value(coord[axis])
        for k in range(3):
            total = total + into[k].astype(F32)
        return total

    def scatter(t, log):
        side_axes = ("x", "y") if t == 0 else ("y", "x")
        axes = (("x", "y"), ("y", "x"), side_axes)

        def some(ref, *lead):
            return [ref.at[lead + (k,)] for k in range(ref.shape[len(lead)])]

        def sems(p, s):
            return (
                [rs_send.at[t, p, 4 * s + e] for e in range(4)],
                [rs_recv.at[t, p, 4 * s + e] for e in range(4)],
            )

        def line_copy(p, e):
            src, dst = (z_out.at[t, p], z_in.at[t, p]) if e is None else (z_out.at[t, p, e], z_in.at[t, p, e])
            device = sibling if e is None else across[axes[p][1]][e]
            return rcopy(src, dst, rs_send.at[t, p, 4], rs_recv.at[t, p, 4], device)

        pair_copy = rcopy(
            y_out.at[t], y_in.at[t], rs_send.at[t, 2, 8], rs_recv.at[t, 2, 8], other_z
        )
        y_out[t] = side[t, 1 - zl].astype(BF16)
        pair_copy.start()
        ring = [
            (part, (t, p), axes[p][0], some(b0_out, t, p), some(b0_in, t, p), some(a0_out, t, p), some(a0_in, t, p), sems(p, 0))
            for p in range(2)
        ]
        for a in ring:
            ring_first(*a[:5], a[7], log)
        yield
        pair_copy.wait_recv()
        side[t, zl] = side[t, zl] + y_in[t].astype(F32)
        wide = (lambda q: side[t, zl, q], axes[2][0], c1_out.at[t], c1_in.at[t], sems(2, 0))
        direct_first(*wide, log)
        for a in ring:
            ring_second(*a, log)
        yield
        here = coord[axes[2][0]]
        side[t, zl, here] = direct_last(*wide)
        thin = (lambda q: side[t, zl, here, q], axes[2][1], c2_out.at[t], c2_in.at[t], sems(2, 1))
        direct_first(*thin, log)
        for p in range(2):
            first = coord[axes[p][0]]
            part[t, p, first] = ring_last(*ring[p][:3], *ring[p][5:])
            for e in range(7):
                a, w = (e + 1, zl) if e < 3 else (e - 3, 1 - zl)
                z_out[t, p, e] = part[t, p, first, place[axes[p][1], a], w].astype(BF16)
                line_copy(p, e).start()
            log.append(line_copy(p, None))
        yield
        out = []
        for p in range(2):
            total = part[t, p, coord[axes[p][0]], coord[axes[p][1]], zl]
            line_copy(p, None).wait_recv()
            for e in range(7):
                total = total + z_in[t, p, e].astype(F32)
            out.append(total)
        out.append(direct_last(*thin))
        log.append(pair_copy)
        result[t] = jnp.concatenate(out, axis=0)

    result, sq, err_sum = {}, {}, {}
    own_lane = lax.broadcasted_iota(jnp.int32, (1, 2 * CHUNK), 1) < CHUNK
    def column_of(k):
        return jnp.concatenate([sm[:, k : k + 1], sm_in[:, k : k + 1]], axis=0)


    def g_copy(j):
        cols = pl.ds(pl.multiple_of(512 * j, 512), 512)
        return rcopy(g_out.at[:, cols], g_in.at[:, cols], g_send.at[0], g_recv.at[0], sibling)

    def gradient(t, first, last):
        @pl.loop(first, last)
        def _(j):
            for k in range(2):
                blocks = (2 * k, 2 * k + 1)
                out = dot(dpre_t[t], slab(gx, t, j, blocks)) + dot(act_t[t], slab(ge, t, j, blocks))
                half = slice(256 * k, 256 * (k + 1))
                cols = pl.ds(pl.multiple_of(512 * j + 256 * k, 256), 256)
                if t == 0:
                    gacc[j, :, half] = out[LAT:]
                    grad_ref[:, cols] = out[:LAT]
                else:
                    g_out[:, cols] = (gacc[j, :, half] + out[LAT:]).astype(BF16)
                    grad_ref[:, cols] = grad_ref[:, cols] + out[:LAT]
            if t == 1:
                g_copy(j).start()

    def steps(t):
        centered = (own_rows(t) - center).astype(BF16)
        log_x, log_r, log_e = [], [], []
        yield from gather(gx, t, centered, gx_send, gx_recv, log_x)
        if t == 0:
            all_weight_copies.wait_recv()
            small_copy.wait_recv()
        pre[t] = project(gx, t, 0) + column_of(0)
        yield
        pre[t] = pre[t] + project(gx, t, 1)
        yield
        act = jnp.maximum(pre[t], 0.0).astype(BF16)
        act_t[t] = act
        acts[t] = act.T[:CHUNK]

        @pl.loop(0, 8, unroll=4)
        def _(j):
            jz, jx = j // 4, lax.rem(j, 4)
            out = dot(acts[t], all_weights(j))
            for yy in range(4):
                cols = slice(128 * yy, 128 * (yy + 1))
                part[t, 0, jx, yy, jz] = out[:MAIN, cols]
                part[t, 1, yy, jx, jz] = out[MAIN : 2 * MAIN, cols]
                if t == 0:
                    side[t, jz, jx, yy] = out[2 * MAIN :, cols]
                else:
                    side[t, jz, yy, jx] = out[2 * MAIN :, cols]

        ready = scatter(t, log_r)
        next(ready)
        flush(log_x)
        wide = act_t[t].astype(F32)
        act_own = jnp.sum(jnp.where(own_lane, wide, 0.0), axis=1, keepdims=True)
        act_all = jnp.sum(wide, axis=1, keepdims=True)
        stat[t] = jnp.where(lane == 0, act_own, jnp.where(lane == 1, act_all, 0.0))
        yield
        yield from ready
        err = result[t] + center - own_rows(t)
        sq[t] = jnp.sum(err * err)
        err_sum[t] = jnp.sum(err, axis=0, keepdims=True)
        derr = (2.0 / TOK * err).astype(BF16)
        ready = gather(ge, t, derr, ge_send, ge_recv, log_e)
        next(ready)
        flush(log_r)
        yield
        yield from ready
        sent.extend(log_e)
        dacc[t] = project(ge, t, 0) + sparsity_coeff / TOK * column_of(1)
        yield
        dacts = dacc[t] + project(ge, t, 1)
        dpre = jnp.where(pre[t] > 0, dacts, 0.0).astype(BF16)
        dpre_t[t] = dpre
        wide = dpre.astype(F32)
        off_own = jnp.sum(jnp.where(own_lane, wide, 0.0), axis=1, keepdims=True)
        off_all = jnp.sum(wide, axis=1, keepdims=True)
        stat[t] = stat[t] + jnp.where(lane == 2, off_own, jnp.where(lane == 3, off_all, 0.0))
        yield
        if t == 0:
            gradient(0, 0, 4)
            yield
            gradient(0, 4, 8)
            yield

    run = [steps(0), steps(1)]
    plan = "0101010w01001010110101010101010010011"
    for who in plan:
        if who == "w":
            prepare()
        else:
            next(run[int(who)])
    for one in run:
        assert next(one, one) is one
    rows = (stat[0] + stat[1]).T
    act_row, act_tot, off, offs = [rows[k : k + 1] for k in range(4)]
    norms = jnp.concatenate([sm[...].T[1:2], sm_in[...].T[1:2]], axis=1)
    spars = jnp.sum(act_row * norms)

    sums[...] = jnp.zeros((2, 8, LAT), F32)
    for k in range(2):
        sums[k, 0:1, :] = offs[:, LAT * k : LAT * (k + 1)]
        sums[k, 1:2, :] = act_tot[:, LAT * k : LAT * (k + 1)]
    sums_copy = rcopy(sums.at[1], sums_in, pair_send.at[4], pair_recv.at[4], sibling)
    sums_copy.start()

    hi = off.astype(BF16)
    rest = off - hi.astype(F32)
    mid = rest.astype(BF16)
    low = (rest - mid.astype(F32)).astype(BF16)
    row = lax.broadcasted_iota(jnp.int32, (16, 512), 0)
    terms = jnp.where(
        row == 0, hi.astype(F32),
        jnp.where(row == 1, mid.astype(F32), jnp.where(row == 2, low.astype(F32), 0.0)),
    ).astype(BF16)
    for j in range(8):
        enc = jnp.sum(dot(terms, all_weights(j)), axis=0, keepdims=True)
        for yy in range(4):
            vx[(j % 4) * 4 + yy, j // 4 : j // 4 + 1, :] = -enc[:, 128 * yy : 128 * (yy + 1)]
    scalars = jnp.where(lane == 0, sq[0] + sq[1], jnp.where(lane == 1, spars, 0.0))
    for k in range(16):
        vx[k, 2:8, :] = jnp.broadcast_to(scalars, (6, 128))
    here = x * 4 + y
    sub = lax.broadcasted_iota(jnp.int32, (8, 128), 0)
    vx[here] = vx[here] + jnp.where(sub == zl, 2.0 / TOK * (err_sum[0] + err_sum[1]), 0.0)

    def v_plane(e):
        a, b = (e + 1) // 4, (e + 1) % 4
        return rcopy(
            vx.at[place["x", a] * 4 + place["y", b]], vx_in.at[e], v_send.at[0], v_recv.at[0], plane[e]
        )

    def v_column(e):
        return rcopy(vz, vz_in.at[e], v_send.at[1], v_recv.at[1], column[e])

    v_planes = rcopy(vx_in, vx_in, v_send.at[0], v_recv.at[0], sibling)
    v_columns = rcopy(vz_in, vz_in, v_send.at[1], v_recv.at[1], sibling)

    for e in range(15):
        v_plane(e).start()
    gradient(1, 0, 4)
    total = vx[here]
    v_planes.wait_recv()
    for e in range(15):
        total = total + vx_in[e]
    vz[...] = total
    for e in range(7):
        v_column(e).start()
    gradient(1, 4, 8)
    v_columns.wait_recv()
    for e in range(7):
        total = total + vz_in[e]
    sums_copy.wait_recv()

    small_ref[...] = jnp.zeros((8, LAT), F32)
    small_ref[0:1, :] = sums[0, 0:1, :] + sums_in[0:1, :]
    small_ref[1:2, :] = sparsity_coeff / TOK * (sums[0, 1:2, :] + sums_in[1:2, :]) / norms[:, :LAT]
    slot = jnp.where(zl == 0, total[0:1], total[1:2])
    small_ref[2:3, 0:64] = jnp.where(core == 0, slot[:, :64], slot[:, 64:])
    small_ref[3:4, 0:128] = total[2:3]

    flush(sent)
    for c in pair + [all_weight_copies, small_copy, sums_copy]:
        c.wait_send()
    v_planes.wait_send()
    v_columns.wait_send()
    all_g_copies = rcopy(g_out, g_in, g_send.at[0], g_recv.at[0], sibling)
    all_g_copies.wait_recv()
    all_g_copies.wait_send()


def step_kernel(inputs, center, offset, dictionary):
    vm = pltpu.VMEM
    dma = pltpu.SemaphoreType.DMA
    block = (PART, 128)
    main, side = (MAIN, 128), (SIDE, 128)
    return pl.pallas_call(
        kernel,
        out_shape=[
            jax.ShapeDtypeStruct((LAT, WIDTH), F32),
            jax.ShapeDtypeStruct((LAT, WIDTH), BF16),
            jax.ShapeDtypeStruct((8, LAT), F32),
        ],
        in_specs=[pl.BlockSpec(memory_space=pltpu.HBM)] * 4,
        out_specs=[pl.BlockSpec(memory_space=pltpu.VMEM)] * 3,
        scratch_shapes=[
            vm((64, 2 * ROWS), BF16),
            vm((1, 64), F32),
            vm((1, LAT), F32),
            vm((2, 8, LAT, 512), BF16),
            vm((2, 3, 4, 4, 4) + block, BF16),
            vm((2, 3, 4, 4, 4) + block, BF16),
            vm((2, 512, 2 * CHUNK), F32),
            vm((2, 512, 2 * CHUNK), F32),
            vm((2, CHUNK, 512), BF16),
            vm((2, 512, 2 * CHUNK), BF16),
            vm((2, 512, 2 * CHUNK), BF16),
            vm((8, LAT, 512), F32),
            vm((2, ROWS, 128), BF16),
            vm((ROWS, 128), BF16),
            vm((8, 128), F32),
            vm((8, 128), F32),
            vm((LAT, 128), F32),
            vm((LAT, 128), F32),
            vm((2, 2 * LAT, 128), F32),
            vm((2, 8, LAT), F32),
            vm((8, LAT), F32),
            vm((2, 2, 4, 4, 2) + main, F32),
            vm((2, 2, 2, 2, 2) + main, BF16),
            vm((2, 2, 2, 2, 2) + main, BF16),
            vm((2, 2, 2, 4, 2) + main, BF16),
            vm((2, 2, 2, 4, 2) + main, BF16),
            vm((2, 2, 7) + main, BF16),
            vm((2, 2, 7) + main, BF16),
            vm((2, 2, 4, 4) + side, F32),
            vm((2, 4, 4) + side, BF16),
            vm((2, 4, 4) + side, BF16),
            vm((2, 3, 4) + side, BF16),
            vm((2, 3, 4) + side, BF16),
            vm((2, 3) + side, BF16),
            vm((2, 3) + side, BF16),
            vm((LAT, WIDTH), BF16),
            vm((16, 8, 128), F32),
            vm((15, 8, 128), F32),
            vm((8, 128), F32),
            vm((7, 8, 128), F32),
            dma((11,)),
            dma((5,)),
            dma((5,)),
            dma((2, 3, 3)),
            dma((2, 3, 6)),
            dma((2, 3, 3)),
            dma((2, 3, 6)),
            dma((2, 3, 9)),
            dma((2, 3, 9)),
            dma((1,)),
            dma((1,)),
            dma((2,)),
            dma((2,)),
        ],
        compiler_params=pltpu.CompilerParams(
            collective_id=0, has_side_effects=True, vmem_limit_bytes=VMEM_LIMIT
        ),
        cost_estimate=pl.CostEstimate(
            flops=12 * 2**30, bytes_accessed=160 * 2**20, transcendentals=0
        ),
        name="step",
    )(*[pltpu.with_memory_space_constraint(v, pltpu.HBM) for v in (inputs, center, offset, dictionary)])


def small_kernel(small, offset, offset_mean, offset_var, center, center_mean, center_var, *outs):
    rows = (
        (offset, small[0:1, :], offset_mean, offset_var),
        (center, small[2:3, 0:64], center_mean, center_var),
    )
    for k, (param, grad, mean, var) in enumerate(rows):
        new = adam_update(param[...], grad, mean[...], var[...])
        for n in range(3):
            outs[3 * k + n][...] = new[n]
    scalars = small[3:4, 0:128]
    lane = lax.broadcasted_iota(jnp.int32, (1, 128), 1)
    weight = jnp.where(lane == 0, 1.0, jnp.where(lane == 1, sparsity_coeff, 0.0))
    outs[6][...] = jnp.sum(scalars * weight, axis=1, keepdims=True) / (TOK * WIDTH)


def small_step(small, *rows):
    shapes = [(1, LAT)] * 3 + [(1, 64)] * 3 + [(1, 1)]
    return pl.pallas_call(
        small_kernel,
        out_shape=[jax.ShapeDtypeStruct(s, F32) for s in shapes],
        in_specs=[pl.BlockSpec(memory_space=pltpu.VMEM)] * 7,
        out_specs=[pl.BlockSpec(memory_space=pltpu.VMEM)] * 7,
        compiler_params=pltpu.CompilerParams(vmem_limit_bytes=2**20),
        name="small",
    )(small, *[r.reshape(1, -1) for r in rows])


def body(
    inputs,
    dictionary,
    offset,
    center,
    dict_mean,
    dict_var,
    offset_mean,
    offset_var,
    center_mean,
    center_var,
):
    grad, shared, small = step_kernel(
        inputs.T, center.reshape(1, -1), offset.reshape(1, -1), dictionary
    )
    g_dict = grad + shared.astype(F32) + small[1][:, None] * dictionary
    fresh_dict, mean_dict, var_dict = adam_update(dictionary, g_dict, dict_mean, dict_var)
    *rows, loss = small_step(
        small, offset, offset_mean, offset_var, center, center_mean, center_var
    )
    fresh_offset, mean_offset, var_offset, fresh_center, mean_center, var_center = [
        r.reshape(-1) for r in rows
    ]
    loss_value = loss.reshape(())
    return (
        fresh_dict,
        fresh_offset,
        fresh_center,
        mean_dict,
        var_dict,
        mean_offset,
        var_offset,
        mean_center,
        var_center,
        loss_value,
    )


def solution(mesh):
    return jax.shard_map(
        body,
        mesh=mesh,
        in_specs=(
            P("dp", "latent"),
            P("latent", None),
            P("latent"),
            P("latent"),
            P("latent", None),
            P("latent", None),
            P("latent"),
            P("latent"),
            P("latent"),
            P("latent"),
        ),
        out_specs=(
            P("latent", None),
            P("latent"),
            P("latent"),
            P("latent", None),
            P("latent", None),
            P("latent"),
            P("latent"),
            P("latent"),
            P("latent"),
            P(),
        ),
        check_vma=False,
    )
```

```python
import jax
import jax.numpy as jnp
from jax import lax
from jax.experimental import pallas as pl
from jax.experimental.pallas import tpu as pltpu
from jax.sharding import PartitionSpec as P

STEP = 1000
sparsity_coeff = 5.0
beta_one = 0.9
beta_two = 0.999
learn_rate = 0.001
adam_eps = 1e-08
norm_eps = 1e-06

TOK = 1152
WIDTH = 4096
ROWS = 288
CHUNK = 144
PART = 48
MAIN, SIDE = 64, 16
LAT = 256
VMEM_LIMIT = 40 * 1024 * 1024
F32 = jnp.float32
BF16 = jnp.bfloat16
MESH = pl.DeviceIdType.MESH


def adam_update(param, grad, mean, var):
    mean_new = beta_one * mean + (1.0 - beta_one) * grad
    var_new = beta_two * var + (1.0 - beta_two) * grad * grad
    rate = learn_rate / (1.0 - beta_one**STEP)
    scaled = var_new * (1.0 / (1.0 - beta_two**STEP))
    param_new = param - rate * mean_new / (scaled * lax.rsqrt(scaled) + adam_eps)
    return (param_new, mean_new, var_new)


def mod4(v):
    return lax.rem(v + 4, 4)


def dot(a, b):
    return jnp.dot(a, b, preferred_element_type=F32)


def dot_nt(a, b):
    return lax.dot_general(a, b, (((1,), (1,)), ((), ())), preferred_element_type=F32)


def kernel(
    inputs_hbm, center_hbm, offset_hbm, dict_ref,
    grad_ref, g_in, small_ref,
    inputs_ref, center_ref, offset_ref,
    weights, gx, ge, pre, dacc, acts, tmat, gacc,
    raw, raw_in, cen, cen_in, sm, sm_in, sums, sums_in,
    part, b0_out, b0_in, a0_out, a0_in, z_out, z_in,
    side, y_out, y_in, c1_out, c1_in, c2_out, c2_in,
    g_out,
    vx, vx_in, vz, vz_in,
    load_sem, pair_send, pair_recv,
    gx_send, gx_recv, ge_send, ge_recv, rs_send, rs_recv,
    g_send, g_recv, v_send, v_recv,
):
    h = lax.axis_index("dp")
    i = lax.axis_index("latent")
    core = lax.rem(i, 2)
    y = lax.rem(i // 2, 4)
    x = lax.rem(i // 8, 4)
    zl = i // 32
    z = 2 * h + zl

    def dev(xx, yy, zz, cc):
        return (zz // 2, ((lax.rem(zz, 2) * 4 + xx) * 4 + yy) * 2 + cc)

    coord = {"x": x, "y": y, "z": z}
    place = {(a, s): mod4(coord[a] + s) for a in coord for s in range(4)}
    near = {}
    for s in range(1, 4):
        near["x", s] = dev(place["x", s], y, z, core)
        near["y", s] = dev(x, place["y", s], z, core)
        near["z", s] = dev(x, y, place["z", s], core)

    def along(axis, step):
        return near[axis, step % 4]

    sibling = dev(x, y, z, 1 - core)
    far_z = 2 * h + 1 - zl
    other_z = dev(x, y, far_z, core)

    def rcopy(src, dst, ssem, rsem, device):
        return pltpu.make_async_remote_copy(
            src_ref=src, dst_ref=dst, send_sem=ssem, recv_sem=rsem,
            device_id=device, device_id_type=MESH,
        )

    def load(j):
        return pltpu.make_async_copy(
            dict_ref.at[:, pl.ds(512 * j, 512)], gacc.at[j], load_sem.at[j]
        )

    first_loads = [
        pltpu.make_async_copy(src, dst, load_sem.at[8 + k])
        for k, (src, dst) in enumerate(
            ((inputs_hbm, inputs_ref), (center_hbm, center_ref), (offset_hbm, offset_ref))
        )
    ]
    for c in first_loads:
        c.start()
    for j in range(8):
        load(j).start()

    plane = [
        dev(place["x", a], place["y", b], z, core) for a in range(4) for b in range(4) if a + b
    ]
    column = [
        dev(x, y, place["z", a], c)
        for a in range(4) for b, c in enumerate((core, 1 - core)) if a + b
    ]
    across = {
        axis: [near[axis, a] for a in range(1, 4)]
        + [
            dev(place["x", a], y, far_z, core) if axis == "x" else dev(x, place["y", a], far_z, core)
            for a in range(4)
        ]
        for axis in ("x", "y")
    }
    barrier = pltpu.get_barrier_semaphore()
    partners = plane + column + across["x"][4:] + across["y"][4:]
    for partner in partners:
        pl.semaphore_signal(barrier, inc=1, device_id=partner, device_id_type=MESH)

    for c in first_loads:
        c.wait()
    lane = lax.broadcasted_iota(jnp.int32, (1, 128), 1)
    mine = (lane // 64) == core
    both = inputs_ref[...].astype(F32)
    both = jnp.concatenate([both, both], axis=0).T
    raw[...] = jnp.where(mine, both, 0.0).astype(BF16).reshape(2, ROWS, 128)
    cboth = jnp.concatenate([center_ref[...], center_ref[...]], axis=1)
    cen[...] = jnp.broadcast_to(jnp.where(mine, cboth, 0.0), (8, 128))
    pl.semaphore_wait(barrier, len(partners))

    pair = [
        rcopy(raw.at[1 - core], raw_in, pair_send.at[0], pair_recv.at[0], sibling),
        rcopy(cen, cen_in, pair_send.at[1], pair_recv.at[1], sibling),
    ]
    for c in pair:
        c.start()
    for c in pair:
        c.wait_recv()
    center = cen[0:1, :] + cen_in[0:1, :]

    def own_rows(t):
        rows = pl.ds(CHUNK * t, CHUNK)
        return raw[core, rows].astype(F32) + raw_in[rows].astype(F32)

    sent = []

    def flush(log):
        for c in log:
            c.wait_send()
        log.clear()

    orders = (("y", "x", "z"), ("x", "z", "y"), ("z", "y", "x"))
    dirs = ((0, 1), (1, -1))

    def gather(buf, t, block, ssem, rsem, log):
        at = [tuple(coord[a] for a in reversed(o)) for o in orders]
        for p in range(3):
            buf[(t, p) + at[p]] = block[PART * p : PART * (p + 1)]

        def chunk(p, f, step):
            q = place[orders[p][f], step % 4]
            return (t, p) + at[p][: 2 - f] + (q,)

        def send(p, f, e, idx, step):
            ref = buf.at[idx]
            rcopy(
                ref, ref, ssem.at[t, p, f], rsem.at[t, p, e], along(orders[p][f], step)
            ).start()

        def whole(p, f, e, idx):
            ref = buf.at[idx]
            return rcopy(ref, ref, ssem.at[t, p, f], rsem.at[t, p, e], sibling)

        def triple(p, f):
            return (t, p) + at[p][: 2 - f] + (pl.ds(0, 3),)

        def double(p, f):
            return (t, p) + at[p][: 2 - f] + (pl.ds(0, 2),)

        def single(p, f):
            return (t, p) + at[p][: 2 - f] + (0,)

        for p in range(3):
            for step in (1, 3, 2):
                send(p, 0, 0, chunk(p, 0, 0), step)
            log.append(whole(p, 0, 0, triple(p, 0)))
        yield
        for p in range(3):
            whole(p, 0, 0, triple(p, 0)).wait_recv()
            for k, step in dirs:
                send(p, 1, 1, chunk(p, 1, 0), step)
            log.append(whole(p, 1, 1, triple(p, 1)))
        yield
        for p in range(3):
            whole(p, 1, 1, double(p, 1)).wait_recv()
            for k, step in dirs:
                send(p, 1, 2, chunk(p, 1, -step) + (pl.ds(2 * k, 2),), step)
        yield
        for p in range(3):
            whole(p, 1, 2, single(p, 1)).wait_recv()
            for k, step in dirs:
                send(p, 2, 3, chunk(p, 2, 0) + (pl.ds(2 * k, 2),), step)
            log.append(whole(p, 2, 3, triple(p, 2)))
        for p in range(3):
            for k, step in dirs:
                send(p, 2, 4, chunk(p, 2, 0) + (pl.ds(2 - 2 * k, 2),), step)
        yield
        for p in range(3):
            whole(p, 2, 3, single(p, 2)).wait_recv()
            for k, step in dirs:
                send(p, 2, 5, chunk(p, 2, -step) + (pl.ds(2 * k, 2),), step)
        yield
        for e in (4, 5):
            for p in range(3):
                whole(p, 2, e, single(p, 2)).wait_recv()

    def weight_copy(j):
        return rcopy(
            weights.at[0, j], weights.at[1, j], pair_send.at[2], pair_recv.at[2], sibling
        )

    all_weight_copies = rcopy(
        weights.at[0], weights.at[1], pair_send.at[2], pair_recv.at[2], sibling
    )

    small_copy = rcopy(sm, sm_in, pair_send.at[3], pair_recv.at[3], sibling)

    def prepare():
        sq = jnp.zeros((LAT, 1), F32)
        for j in range(8):
            load(j).wait()
            block = gacc[j]
            weights[0, j] = block.astype(BF16)
            weight_copy(j).start()
            sq = sq + jnp.sum(block * block, axis=1, keepdims=True)
        norm = jnp.sqrt(sq + norm_eps)
        sm[...] = jnp.zeros((8, LAT), F32)
        sm[0:1, :] = offset_ref[...]
        sm[1:2, :] = jnp.broadcast_to(norm, (LAT, 128)).T[0:1, :]
        small_copy.start()

    def slab(buf, t, j, blocks=(0, 1, 2, 3)):
        jz, jx = j // 4, j % 4
        rows = []
        for r in range(2):
            zz = 2 * (h if r == 0 else 1 - h) + jz
            for p in range(3):
                cols = []
                for yy in blocks:
                    idx = ((zz, jx, yy), (yy, zz, jx), (jx, yy, zz))[p]
                    cols.append(buf[(t, p) + idx])
                rows.append(jnp.concatenate(cols, axis=1))
        return jnp.concatenate(rows, axis=0)

    def all_weights(j):
        return jnp.concatenate([weights[0, j], weights[1, j]], axis=0)

    def project(buf, t, half):
        rows = jnp.concatenate([slab(buf, t, 4 * half + jx) for jx in range(4)], axis=1)
        cols = jnp.concatenate([all_weights(4 * half + jx) for jx in range(4)], axis=1)
        return dot_nt(rows, cols)

    def ring_first(src, lead, axis, b_out, b_in, sems, log):
        q = place[axis, 2]
        for k, step in dirs:
            b_out[k][...] = src[lead + (q, pl.ds(2 * k, 2))].astype(BF16)
            c = rcopy(b_out[k], b_in[k], sems[0][k], sems[1][k], along(axis, step))
            c.start()
            log.append(c)

    def ring_second(src, lead, axis, b_out, b_in, a_out, a_in, sems, log):
        for k, step in dirs:
            q = place[axis, step % 4]
            mix, rest = pl.ds(2 * k, 2), pl.ds(2 - 2 * k, 2)
            a_out[k][rest] = src[lead + (q, rest)].astype(BF16)
            rcopy(b_out[k], b_in[k], sems[0][k], sems[1][k], along(axis, step)).wait_recv()
            a_out[k][mix] = (src[lead + (q, mix)] + b_in[k][...].astype(F32)).astype(BF16)
            c = rcopy(a_out[k], a_in[k], sems[0][2 + k], sems[1][2 + k], along(axis, step))
            c.start()
            log.append(c)

    def ring_last(src, lead, axis, a_out, a_in, sems):
        for k, step in dirs:
            rcopy(a_out[k], a_in[k], sems[0][2 + k], sems[1][2 + k], along(axis, step)).wait_recv()
        return src[lead + (coord[axis],)] + a_in[0][...].astype(F32) + a_in[1][...].astype(F32)

    def direct_first(value, axis, out, into, sems, log):
        for k in range(3):
            out[k] = value(place[axis, k + 1]).astype(BF16)
            rcopy(out.at[k], into.at[k], sems[0][0], sems[1][0], along(axis, k + 1)).start()
        log.append(rcopy(out, into, sems[0][0], sems[1][0], sibling))

    def direct_last(value, axis, out, into, sems):
        rcopy(out, into, sems[0][0], sems[1][0], sibling).wait_recv()
        total = value(coord[axis])
        for k in range(3):
            total = total + into[k].astype(F32)
        return total

    def scatter(t, log):
        side_axes = ("x", "y") if t == 0 else ("y", "x")
        axes = (("x", "y"), ("y", "x"), side_axes)

        def some(ref, *lead):
            return [ref.at[lead + (k,)] for k in range(ref.shape[len(lead)])]

        def sems(p, s):
            return (
                [rs_send.at[t, p, 4 * s + e] for e in range(4)],
                [rs_recv.at[t, p, 4 * s + e] for e in range(4)],
            )

        def line_copy(p, e):
            src, dst = (z_out.at[t, p], z_in.at[t, p]) if e is None else (z_out.at[t, p, e], z_in.at[t, p, e])
            device = sibling if e is None else across[axes[p][1]][e]
            return rcopy(src, dst, rs_send.at[t, p, 4], rs_recv.at[t, p, 4], device)

        pair_copy = rcopy(
            y_out.at[t], y_in.at[t], rs_send.at[t, 2, 8], rs_recv.at[t, 2, 8], other_z
        )
        y_out[t] = side[t, 1 - zl].astype(BF16)
        pair_copy.start()
        ring = [
            (part, (t, p), axes[p][0], some(b0_out, t, p), some(b0_in, t, p), some(a0_out, t, p), some(a0_in, t, p), sems(p, 0))
            for p in range(2)
        ]
        for a in ring:
            ring_first(*a[:5], a[7], log)
        yield
        pair_copy.wait_recv()
        side[t, zl] = side[t, zl] + y_in[t].astype(F32)
        wide = (lambda q: side[t, zl, q], axes[2][0], c1_out.at[t], c1_in.at[t], sems(2, 0))
        direct_first(*wide, log)
        for a in ring:
            ring_second(*a, log)
        yield
        here = coord[axes[2][0]]
        side[t, zl, here] = direct_last(*wide)
        thin = (lambda q: side[t, zl, here, q], axes[2][1], c2_out.at[t], c2_in.at[t], sems(2, 1))
        direct_first(*thin, log)
        for p in range(2):
            first = coord[axes[p][0]]
            part[t, p, first] = ring_last(*ring[p][:3], *ring[p][5:])
            for e in range(7):
                a, w = (e + 1, zl) if e < 3 else (e - 3, 1 - zl)
                z_out[t, p, e] = part[t, p, first, place[axes[p][1], a], w].astype(BF16)
                line_copy(p, e).start()
            log.append(line_copy(p, None))
        yield
        out = []
        for p in range(2):
            total = part[t, p, coord[axes[p][0]], coord[axes[p][1]], zl]
            line_copy(p, None).wait_recv()
            for e in range(7):
                total = total + z_in[t, p, e].astype(F32)
            out.append(total)
        out.append(direct_last(*thin))
        log.append(pair_copy)
        result[t] = jnp.concatenate(out, axis=0)

    result, sq, err_sum, act_own, act_all, off_own, off_all = {}, {}, {}, {}, {}, {}, {}
    shared = {}

    def g_copy(j):
        cols = pl.ds(pl.multiple_of(512 * j, 512), 512)
        return rcopy(g_out.at[:, cols], g_in.at[:, cols], g_send.at[0], g_recv.at[0], sibling)

    def gradient(t, first, last):
        @pl.loop(first, last)
        def _(j):
            for k in range(2):
                blocks = (2 * k, 2 * k + 1)
                both = jnp.concatenate([slab(gx, t, j, blocks), slab(ge, t, j, blocks)], axis=0)
                out = dot(tmat[t], both)
                half = slice(256 * k, 256 * (k + 1))
                cols = pl.ds(pl.multiple_of(512 * j + 256 * k, 256), 256)
                if t == 0:
                    gacc[j, :, half] = out[LAT:]
                    grad_ref[:, cols] = out[:LAT]
                else:
                    g_out[:, cols] = (gacc[j, :, half] + out[LAT:]).astype(BF16)
                    grad_ref[:, cols] = grad_ref[:, cols] + out[:LAT]
            if t == 1:
                g_copy(j).start()

    def steps(t):
        centered = (own_rows(t) - center).astype(BF16)
        log_x, log_r, log_e = [], [], []
        yield from gather(gx, t, centered, gx_send, gx_recv, log_x)
        if t == 0:
            all_weight_copies.wait_recv()
            small_copy.wait_recv()
            shared["bias"] = jnp.concatenate([sm[0:1, :], sm_in[0:1, :]], axis=1)
            shared["norms"] = jnp.concatenate([sm[1:2, :], sm_in[1:2, :]], axis=1)
        norms = shared["norms"]
        pre[t] = project(gx, t, 0) + shared["bias"]
        yield
        pre[t] = pre[t] + project(gx, t, 1)
        yield
        acts[t] = jnp.maximum(pre[t], 0.0).astype(BF16)

        @pl.loop(0, 8, unroll=4)
        def _(j):
            jz, jx = j // 4, lax.rem(j, 4)
            out = dot(acts[t, :CHUNK], all_weights(j))
            for yy in range(4):
                cols = slice(128 * yy, 128 * (yy + 1))
                part[t, 0, jx, yy, jz] = out[:MAIN, cols]
                part[t, 1, yy, jx, jz] = out[MAIN : 2 * MAIN, cols]
                if t == 0:
                    side[t, jz, jx, yy] = out[2 * MAIN :, cols]
                else:
                    side[t, jz, yy, jx] = out[2 * MAIN :, cols]

        ready = scatter(t, log_r)
        next(ready)
        flush(log_x)
        act = acts[t]
        act_own[t] = jnp.sum(act[:CHUNK].astype(F32), axis=0, keepdims=True)
        act_all[t] = act_own[t] + jnp.sum(act[CHUNK:].astype(F32), axis=0, keepdims=True)
        yield
        yield from ready
        err = result[t] + center - own_rows(t)
        sq[t] = jnp.sum(err * err)
        err_sum[t] = jnp.sum(err, axis=0, keepdims=True)
        derr = (2.0 / TOK * err).astype(BF16)
        ready = gather(ge, t, derr, ge_send, ge_recv, log_e)
        next(ready)
        flush(log_r)
        yield
        yield from ready
        sent.extend(log_e)
        dacc[t] = project(ge, t, 0) + sparsity_coeff / TOK * norms
        yield
        dacts = dacc[t] + project(ge, t, 1)
        dpre = jnp.where(pre[t] > 0, dacts, 0.0).astype(BF16)
        tmat[t] = jnp.concatenate([dpre, acts[t]], axis=0).T
        off_own[t] = jnp.sum(dpre[:CHUNK].astype(F32), axis=0, keepdims=True)
        off_all[t] = off_own[t] + jnp.sum(dpre[CHUNK:].astype(F32), axis=0, keepdims=True)
        yield
        if t == 0:
            gradient(0, 0, 4)
            yield
            gradient(0, 4, 8)
            yield

    run = [steps(0), steps(1)]
    plan = "0101010w01001010110101010101010100011"
    for who in plan:
        if who == "w":
            prepare()
        else:
            next(run[int(who)])
    for one in run:
        assert next(one, one) is one
    off = off_own[0] + off_own[1]
    offs = off_all[0] + off_all[1]
    act_tot = act_all[0] + act_all[1]
    spars = jnp.sum((act_own[0] + act_own[1]) * shared["norms"])

    sums[...] = jnp.zeros((2, 8, LAT), F32)
    for k in range(2):
        sums[k, 0:1, :] = offs[:, LAT * k : LAT * (k + 1)]
        sums[k, 1:2, :] = act_tot[:, LAT * k : LAT * (k + 1)]
    sums_copy = rcopy(sums.at[1], sums_in, pair_send.at[4], pair_recv.at[4], sibling)
    sums_copy.start()

    hi = off.astype(BF16)
    rest = off - hi.astype(F32)
    mid = rest.astype(BF16)
    low = (rest - mid.astype(F32)).astype(BF16)
    row = lax.broadcasted_iota(jnp.int32, (16, 512), 0)
    terms = jnp.where(
        row == 0, hi.astype(F32),
        jnp.where(row == 1, mid.astype(F32), jnp.where(row == 2, low.astype(F32), 0.0)),
    ).astype(BF16)
    for j in range(8):
        enc = jnp.sum(dot(terms, all_weights(j)), axis=0, keepdims=True)
        for yy in range(4):
            vx[(j % 4) * 4 + yy, j // 4 : j // 4 + 1, :] = -enc[:, 128 * yy : 128 * (yy + 1)]
    scalars = jnp.where(lane == 0, sq[0] + sq[1], jnp.where(lane == 1, spars, 0.0))
    for k in range(16):
        vx[k, 2:8, :] = jnp.broadcast_to(scalars, (6, 128))
    here = x * 4 + y
    sub = lax.broadcasted_iota(jnp.int32, (8, 128), 0)
    vx[here] = vx[here] + jnp.where(sub == zl, 2.0 / TOK * (err_sum[0] + err_sum[1]), 0.0)

    def v_plane(e):
        a, b = (e + 1) // 4, (e + 1) % 4
        return rcopy(
            vx.at[place["x", a] * 4 + place["y", b]], vx_in.at[e], v_send.at[0], v_recv.at[0], plane[e]
        )

    def v_column(e):
        return rcopy(vz, vz_in.at[e], v_send.at[1], v_recv.at[1], column[e])

    v_planes = rcopy(vx_in, vx_in, v_send.at[0], v_recv.at[0], sibling)
    v_columns = rcopy(vz_in, vz_in, v_send.at[1], v_recv.at[1], sibling)

    for e in range(15):
        v_plane(e).start()
    gradient(1, 0, 4)
    total = vx[here]
    v_planes.wait_recv()
    for e in range(15):
        total = total + vx_in[e]
    vz[...] = total
    for e in range(7):
        v_column(e).start()
    gradient(1, 4, 8)
    v_columns.wait_recv()
    for e in range(7):
        total = total + vz_in[e]
    sums_copy.wait_recv()

    small_ref[...] = jnp.zeros((8, LAT), F32)
    small_ref[0:1, :] = sums[0, 0:1, :] + sums_in[0:1, :]
    small_ref[1:2, :] = sparsity_coeff / TOK * (sums[0, 1:2, :] + sums_in[1:2, :]) / sm[1:2, :]
    slot = jnp.where(zl == 0, total[0:1], total[1:2])
    small_ref[2:3, 0:64] = jnp.where(core == 0, slot[:, :64], slot[:, 64:])
    small_ref[3:4, 0:128] = total[2:3]

    flush(sent)
    for c in pair + [all_weight_copies, small_copy, sums_copy]:
        c.wait_send()
    v_planes.wait_send()
    v_columns.wait_send()
    all_g_copies = rcopy(g_out, g_in, g_send.at[0], g_recv.at[0], sibling)
    all_g_copies.wait_recv()
    all_g_copies.wait_send()


def step_kernel(inputs, center, offset, dictionary):
    vm = pltpu.VMEM
    dma = pltpu.SemaphoreType.DMA
    block = (PART, 128)
    main, side = (MAIN, 128), (SIDE, 128)
    return pl.pallas_call(
        kernel,
        out_shape=[
            jax.ShapeDtypeStruct((LAT, WIDTH), F32),
            jax.ShapeDtypeStruct((LAT, WIDTH), BF16),
            jax.ShapeDtypeStruct((8, LAT), F32),
        ],
        in_specs=[pl.BlockSpec(memory_space=pltpu.HBM)] * 4,
        out_specs=[pl.BlockSpec(memory_space=pltpu.VMEM)] * 3,
        scratch_shapes=[
            vm((64, 2 * ROWS), BF16),
            vm((1, 64), F32),
            vm((1, LAT), F32),
            vm((2, 8, LAT, 512), BF16),
            vm((2, 3, 4, 4, 4) + block, BF16),
            vm((2, 3, 4, 4, 4) + block, BF16),
            vm((2, 2 * CHUNK, 512), F32),
            vm((2, 2 * CHUNK, 512), F32),
            vm((2, 2 * CHUNK, 512), BF16),
            vm((2, 512, 4 * CHUNK), BF16),
            vm((8, LAT, 512), F32),
            vm((2, ROWS, 128), BF16),
            vm((ROWS, 128), BF16),
            vm((8, 128), F32),
            vm((8, 128), F32),
            vm((8, LAT), F32),
            vm((8, LAT), F32),
            vm((2, 8, LAT), F32),
            vm((8, LAT), F32),
            vm((2, 2, 4, 4, 2) + main, F32),
            vm((2, 2, 2, 2, 2) + main, BF16),
            vm((2, 2, 2, 2, 2) + main, BF16),
            vm((2, 2, 2, 4, 2) + main, BF16),
            vm((2, 2, 2, 4, 2) + main, BF16),
            vm((2, 2, 7) + main, BF16),
            vm((2, 2, 7) + main, BF16),
            vm((2, 2, 4, 4) + side, F32),
            vm((2, 4, 4) + side, BF16),
            vm((2, 4, 4) + side, BF16),
            vm((2, 3, 4) + side, BF16),
            vm((2, 3, 4) + side, BF16),
            vm((2, 3) + side, BF16),
            vm((2, 3) + side, BF16),
            vm((LAT, WIDTH), BF16),
            vm((16, 8, 128), F32),
            vm((15, 8, 128), F32),
            vm((8, 128), F32),
            vm((7, 8, 128), F32),
            dma((11,)),
            dma((5,)),
            dma((5,)),
            dma((2, 3, 3)),
            dma((2, 3, 6)),
            dma((2, 3, 3)),
            dma((2, 3, 6)),
            dma((2, 3, 9)),
            dma((2, 3, 9)),
            dma((1,)),
            dma((1,)),
            dma((2,)),
            dma((2,)),
        ],
        compiler_params=pltpu.CompilerParams(
            collective_id=0, has_side_effects=True, vmem_limit_bytes=VMEM_LIMIT
        ),
        cost_estimate=pl.CostEstimate(
            flops=12 * 2**30, bytes_accessed=160 * 2**20, transcendentals=0
        ),
        name="step",
    )(*[pltpu.with_memory_space_constraint(v, pltpu.HBM) for v in (inputs, center, offset, dictionary)])


def small_kernel(small, offset, offset_mean, offset_var, center, center_mean, center_var, *outs):
    rows = (
        (offset, small[0:1, :], offset_mean, offset_var),
        (center, small[2:3, 0:64], center_mean, center_var),
    )
    for k, (param, grad, mean, var) in enumerate(rows):
        new = adam_update(param[...], grad, mean[...], var[...])
        for n in range(3):
            outs[3 * k + n][...] = new[n]
    scalars = small[3:4, 0:128]
    lane = lax.broadcasted_iota(jnp.int32, (1, 128), 1)
    weight = jnp.where(lane == 0, 1.0, jnp.where(lane == 1, sparsity_coeff, 0.0))
    outs[6][...] = jnp.sum(scalars * weight, axis=1, keepdims=True) / (TOK * WIDTH)


def small_step(small, *rows):
    shapes = [(1, LAT)] * 3 + [(1, 64)] * 3 + [(1, 1)]
    return pl.pallas_call(
        small_kernel,
        out_shape=[jax.ShapeDtypeStruct(s, F32) for s in shapes],
        in_specs=[pl.BlockSpec(memory_space=pltpu.VMEM)] * 7,
        out_specs=[pl.BlockSpec(memory_space=pltpu.VMEM)] * 7,
        compiler_params=pltpu.CompilerParams(vmem_limit_bytes=2**20),
        name="small",
    )(small, *[r.reshape(1, -1) for r in rows])


def body(
    inputs,
    dictionary,
    offset,
    center,
    dict_mean,
    dict_var,
    offset_mean,
    offset_var,
    center_mean,
    center_var,
):
    grad, shared, small = step_kernel(
        inputs.T, center.reshape(1, -1), offset.reshape(1, -1), dictionary
    )
    g_dict = grad + shared.astype(F32) + small[1][:, None] * dictionary
    fresh_dict, mean_dict, var_dict = adam_update(dictionary, g_dict, dict_mean, dict_var)
    *rows, loss = small_step(
        small, offset, offset_mean, offset_var, center, center_mean, center_var
    )
    fresh_offset, mean_offset, var_offset, fresh_center, mean_center, var_center = [
        r.reshape(-1) for r in rows
    ]
    loss_value = loss.reshape(())
    return (
        fresh_dict,
        fresh_offset,
        fresh_center,
        mean_dict,
        var_dict,
        mean_offset,
        var_offset,
        mean_center,
        var_center,
        loss_value,
    )


def solution(mesh):
    return jax.shard_map(
        body,
        mesh=mesh,
        in_specs=(
            P("dp", "latent"),
            P("latent", None),
            P("latent"),
            P("latent"),
            P("latent", None),
            P("latent", None),
            P("latent"),
            P("latent"),
            P("latent"),
            P("latent"),
        ),
        out_specs=(
            P("latent", None),
            P("latent"),
            P("latent"),
            P("latent", None),
            P("latent", None),
            P("latent"),
            P("latent"),
            P("latent"),
            P("latent"),
            P(),
        ),
        check_vma=False,
    )
```

```python
import jax
import jax.numpy as jnp
from jax import lax
from jax.experimental import pallas as pl
from jax.experimental.pallas import tpu as pltpu
from jax.sharding import PartitionSpec as P

STEP = 1000
sparsity_coeff = 5.0
beta_one = 0.9
beta_two = 0.999
learn_rate = 0.001
adam_eps = 1e-08
norm_eps = 1e-06

TOK = 1152
WIDTH = 4096
ROWS = 288
CHUNK = 144
PART = 48
MAIN, SIDE = 64, 16
LAT = 256
VMEM_LIMIT = 40 * 1024 * 1024
F32 = jnp.float32
BF16 = jnp.bfloat16
MESH = pl.DeviceIdType.MESH


def adam_update(param, grad, mean, var):
    mean_new = beta_one * mean + (1.0 - beta_one) * grad
    var_new = beta_two * var + (1.0 - beta_two) * grad * grad
    rate = learn_rate / (1.0 - beta_one**STEP)
    scaled = var_new * (1.0 / (1.0 - beta_two**STEP))
    param_new = param - rate * mean_new / (scaled * lax.rsqrt(scaled) + adam_eps)
    return (param_new, mean_new, var_new)


def mod4(v):
    return lax.rem(v + 4, 4)


def dot(a, b):
    return jnp.dot(a, b, preferred_element_type=F32)


def dot_nt(a, b):
    return lax.dot_general(a, b, (((1,), (1,)), ((), ())), preferred_element_type=F32)


def kernel(
    inputs_hbm, center_hbm, offset_hbm, dict_ref,
    grad_ref, g_in, small_ref,
    inputs_ref, center_ref, offset_ref,
    weights, gx, ge, pre, dacc, acts, tmat, gacc,
    raw, raw_in, cen, cen_in, sm, sm_in, sums, sums_in,
    part, b0_out, b0_in, a0_out, a0_in, z_out, z_in,
    side, y_out, y_in, c1_out, c1_in, c2_out, c2_in,
    g_out,
    vx, vx_in, vz, vz_in,
    load_sem, pair_send, pair_recv,
    gx_send, gx_recv, ge_send, ge_recv, rs_send, rs_recv,
    g_send, g_recv, v_send, v_recv,
):
    h = lax.axis_index("dp")
    i = lax.axis_index("latent")
    core = lax.rem(i, 2)
    y = lax.rem(i // 2, 4)
    x = lax.rem(i // 8, 4)
    zl = i // 32
    z = 2 * h + zl

    def dev(xx, yy, zz, cc):
        return (zz // 2, ((lax.rem(zz, 2) * 4 + xx) * 4 + yy) * 2 + cc)

    coord = {"x": x, "y": y, "z": z}
    place = {(a, s): mod4(coord[a] + s) for a in coord for s in range(4)}
    near = {}
    for s in range(1, 4):
        near["x", s] = dev(place["x", s], y, z, core)
        near["y", s] = dev(x, place["y", s], z, core)
        near["z", s] = dev(x, y, place["z", s], core)

    def along(axis, step):
        return near[axis, step % 4]

    sibling = dev(x, y, z, 1 - core)
    far_z = 2 * h + 1 - zl
    other_z = dev(x, y, far_z, core)

    def rcopy(src, dst, ssem, rsem, device):
        return pltpu.make_async_remote_copy(
            src_ref=src, dst_ref=dst, send_sem=ssem, recv_sem=rsem,
            device_id=device, device_id_type=MESH,
        )

    def load(j):
        return pltpu.make_async_copy(
            dict_ref.at[:, pl.ds(512 * j, 512)], gacc.at[j], load_sem.at[j]
        )

    first_loads = [
        pltpu.make_async_copy(src, dst, load_sem.at[8 + k])
        for k, (src, dst) in enumerate(
            ((inputs_hbm, inputs_ref), (center_hbm, center_ref), (offset_hbm, offset_ref))
        )
    ]
    for c in first_loads:
        c.start()
    for j in range(8):
        load(j).start()

    plane = [
        dev(place["x", a], place["y", b], z, core) for a in range(4) for b in range(4) if a + b
    ]
    column = [
        dev(x, y, place["z", a], c)
        for a in range(4) for b, c in enumerate((core, 1 - core)) if a + b
    ]
    across = {
        axis: [near[axis, a] for a in range(1, 4)]
        + [
            dev(place["x", a], y, far_z, core) if axis == "x" else dev(x, place["y", a], far_z, core)
            for a in range(4)
        ]
        for axis in ("x", "y")
    }
    barrier = pltpu.get_barrier_semaphore()
    partners = plane + column + across["x"][4:] + across["y"][4:]
    for partner in partners:
        pl.semaphore_signal(barrier, inc=1, device_id=partner, device_id_type=MESH)

    for c in first_loads:
        c.wait()
    lane = lax.broadcasted_iota(jnp.int32, (1, 128), 1)
    mine = (lane // 64) == core
    both = inputs_ref[...].astype(F32)
    both = jnp.concatenate([both, both], axis=0).T
    raw[...] = jnp.where(mine, both, 0.0).astype(BF16).reshape(2, ROWS, 128)
    cboth = jnp.concatenate([center_ref[...], center_ref[...]], axis=1)
    cen[...] = jnp.broadcast_to(jnp.where(mine, cboth, 0.0), (8, 128))
    pl.semaphore_wait(barrier, len(partners))

    pair = [
        rcopy(raw.at[1 - core], raw_in, pair_send.at[0], pair_recv.at[0], sibling),
        rcopy(cen, cen_in, pair_send.at[1], pair_recv.at[1], sibling),
    ]
    for c in pair:
        c.start()
    for c in pair:
        c.wait_recv()
    center = cen[0:1, :] + cen_in[0:1, :]

    def own_rows(t):
        rows = pl.ds(CHUNK * t, CHUNK)
        return raw[core, rows].astype(F32) + raw_in[rows].astype(F32)

    sent = []

    def flush(log):
        for c in log:
            c.wait_send()
        log.clear()

    orders = (("y", "x", "z"), ("x", "z", "y"), ("z", "y", "x"))
    dirs = ((0, 1), (1, -1))

    def gather(buf, t, block, ssem, rsem, log):
        at = [tuple(coord[a] for a in reversed(o)) for o in orders]
        for p in range(3):
            buf[(t, p) + at[p]] = block[PART * p : PART * (p + 1)]

        def chunk(p, f, step):
            q = place[orders[p][f], step % 4]
            return (t, p) + at[p][: 2 - f] + (q,)

        def send(p, f, e, idx, step):
            ref = buf.at[idx]
            rcopy(
                ref, ref, ssem.at[t, p, f], rsem.at[t, p, e], along(orders[p][f], step)
            ).start()

        def whole(p, f, e, idx):
            ref = buf.at[idx]
            return rcopy(ref, ref, ssem.at[t, p, f], rsem.at[t, p, e], sibling)

        def triple(p, f):
            return (t, p) + at[p][: 2 - f] + (pl.ds(0, 3),)

        def double(p, f):
            return (t, p) + at[p][: 2 - f] + (pl.ds(0, 2),)

        def single(p, f):
            return (t, p) + at[p][: 2 - f] + (0,)

        for p in range(3):
            for step in (1, 3, 2):
                send(p, 0, 0, chunk(p, 0, 0), step)
            log.append(whole(p, 0, 0, triple(p, 0)))
        yield
        for p in range(3):
            whole(p, 0, 0, triple(p, 0)).wait_recv()
            for k, step in dirs:
                send(p, 1, 1, chunk(p, 1, 0), step)
            log.append(whole(p, 1, 1, triple(p, 1)))
        yield
        for p in range(3):
            whole(p, 1, 1, double(p, 1)).wait_recv()
            for k, step in dirs:
                send(p, 1, 2, chunk(p, 1, -step) + (pl.ds(2 * k, 2),), step)
        yield
        for p in range(3):
            whole(p, 1, 2, single(p, 1)).wait_recv()
            for k, step in dirs:
                send(p, 2, 3, chunk(p, 2, 0) + (pl.ds(2 * k, 2),), step)
            log.append(whole(p, 2, 3, triple(p, 2)))
        for p in range(3):
            for k, step in dirs:
                send(p, 2, 4, chunk(p, 2, 0) + (pl.ds(2 - 2 * k, 2),), step)
        yield
        for p in range(3):
            whole(p, 2, 3, single(p, 2)).wait_recv()
            for k, step in dirs:
                send(p, 2, 5, chunk(p, 2, -step) + (pl.ds(2 * k, 2),), step)
        yield
        for e in (4, 5):
            for p in range(3):
                whole(p, 2, e, single(p, 2)).wait_recv()

    def weight_copy(j):
        return rcopy(
            weights.at[0, j], weights.at[1, j], pair_send.at[2], pair_recv.at[2], sibling
        )

    all_weight_copies = rcopy(
        weights.at[0], weights.at[1], pair_send.at[2], pair_recv.at[2], sibling
    )

    small_copy = rcopy(sm, sm_in, pair_send.at[3], pair_recv.at[3], sibling)

    def prepare():
        sq = jnp.zeros((LAT, 1), F32)
        for j in range(8):
            load(j).wait()
            block = gacc[j]
            weights[0, j] = block.astype(BF16)
            weight_copy(j).start()
            sq = sq + jnp.sum(block * block, axis=1, keepdims=True)
        norm = jnp.sqrt(sq + norm_eps)
        sm[...] = jnp.zeros((8, LAT), F32)
        sm[0:1, :] = offset_ref[...]
        sm[1:2, :] = jnp.broadcast_to(norm, (LAT, 128)).T[0:1, :]
        small_copy.start()

    def slab(buf, t, j, blocks=(0, 1, 2, 3)):
        jz, jx = j // 4, j % 4
        rows = []
        for r in range(2):
            zz = 2 * (h if r == 0 else 1 - h) + jz
            for p in range(3):
                cols = []
                for yy in blocks:
                    idx = ((zz, jx, yy), (yy, zz, jx), (jx, yy, zz))[p]
                    cols.append(buf[(t, p) + idx])
                rows.append(jnp.concatenate(cols, axis=1))
        return jnp.concatenate(rows, axis=0)

    def all_weights(j):
        return jnp.concatenate([weights[0, j], weights[1, j]], axis=0)

    def project(buf, t, half):
        rows = jnp.concatenate([slab(buf, t, 4 * half + jx) for jx in range(4)], axis=1)
        cols = jnp.concatenate([all_weights(4 * half + jx) for jx in range(4)], axis=1)
        return dot_nt(rows, cols)

    def ring_first(src, lead, axis, b_out, b_in, sems, log):
        q = place[axis, 2]
        for k, step in dirs:
            b_out[k][...] = src[lead + (q, pl.ds(2 * k, 2))].astype(BF16)
            c = rcopy(b_out[k], b_in[k], sems[0][k], sems[1][k], along(axis, step))
            c.start()
            log.append(c)

    def ring_second(src, lead, axis, b_out, b_in, a_out, a_in, sems, log):
        for k, step in dirs:
            q = place[axis, step % 4]
            mix, rest = pl.ds(2 * k, 2), pl.ds(2 - 2 * k, 2)
            a_out[k][rest] = src[lead + (q, rest)].astype(BF16)
            rcopy(b_out[k], b_in[k], sems[0][k], sems[1][k], along(axis, step)).wait_recv()
            a_out[k][mix] = (src[lead + (q, mix)] + b_in[k][...].astype(F32)).astype(BF16)
            c = rcopy(a_out[k], a_in[k], sems[0][2 + k], sems[1][2 + k], along(axis, step))
            c.start()
            log.append(c)

    def ring_last(src, lead, axis, a_out, a_in, sems):
        for k, step in dirs:
            rcopy(a_out[k], a_in[k], sems[0][2 + k], sems[1][2 + k], along(axis, step)).wait_recv()
        return src[lead + (coord[axis],)] + a_in[0][...].astype(F32) + a_in[1][...].astype(F32)

    def direct_first(value, axis, out, into, sems, log):
        for k in range(3):
            out[k] = value(place[axis, k + 1]).astype(BF16)
            rcopy(out.at[k], into.at[k], sems[0][0], sems[1][0], along(axis, k + 1)).start()
        log.append(rcopy(out, into, sems[0][0], sems[1][0], sibling))

    def direct_last(value, axis, out, into, sems):
        rcopy(out, into, sems[0][0], sems[1][0], sibling).wait_recv()
        total = value(coord[axis])
        for k in range(3):
            total = total + into[k].astype(F32)
        return total

    def scatter(t, log):
        side_axes = ("x", "y") if t == 0 else ("y", "x")
        axes = (("x", "y"), ("y", "x"), side_axes)

        def some(ref, *lead):
            return [ref.at[lead + (k,)] for k in range(ref.shape[len(lead)])]

        def sems(p, s):
            return (
                [rs_send.at[t, p, 4 * s + e] for e in range(4)],
                [rs_recv.at[t, p, 4 * s + e] for e in range(4)],
            )

        def line_copy(p, e):
            src, dst = (z_out.at[t, p], z_in.at[t, p]) if e is None else (z_out.at[t, p, e], z_in.at[t, p, e])
            device = sibling if e is None else across[axes[p][1]][e]
            return rcopy(src, dst, rs_send.at[t, p, 4], rs_recv.at[t, p, 4], device)

        pair_copy = rcopy(
            y_out.at[t], y_in.at[t], rs_send.at[t, 2, 8], rs_recv.at[t, 2, 8], other_z
        )
        y_out[t] = side[t, 1 - zl].astype(BF16)
        pair_copy.start()
        ring = [
            (part, (t, p), axes[p][0], some(b0_out, t, p), some(b0_in, t, p), some(a0_out, t, p), some(a0_in, t, p), sems(p, 0))
            for p in range(2)
        ]
        for a in ring:
            ring_first(*a[:5], a[7], log)
        yield
        pair_copy.wait_recv()
        side[t, zl] = side[t, zl] + y_in[t].astype(F32)
        wide = (lambda q: side[t, zl, q], axes[2][0], c1_out.at[t], c1_in.at[t], sems(2, 0))
        direct_first(*wide, log)
        for a in ring:
            ring_second(*a, log)
        yield
        here = coord[axes[2][0]]
        side[t, zl, here] = direct_last(*wide)
        thin = (lambda q: side[t, zl, here, q], axes[2][1], c2_out.at[t], c2_in.at[t], sems(2, 1))
        direct_first(*thin, log)
        for p in range(2):
            first = coord[axes[p][0]]
            part[t, p, first] = ring_last(*ring[p][:3], *ring[p][5:])
            for e in range(7):
                a, w = (e + 1, zl) if e < 3 else (e - 3, 1 - zl)
                z_out[t, p, e] = part[t, p, first, place[axes[p][1], a], w].astype(BF16)
                line_copy(p, e).start()
            log.append(line_copy(p, None))
        yield
        out = []
        for p in range(2):
            total = part[t, p, coord[axes[p][0]], coord[axes[p][1]], zl]
            line_copy(p, None).wait_recv()
            for e in range(7):
                total = total + z_in[t, p, e].astype(F32)
            out.append(total)
        out.append(direct_last(*thin))
        log.append(pair_copy)
        result[t] = jnp.concatenate(out, axis=0)

    result, sq, err_sum, act_own, act_all, off_own, off_all = {}, {}, {}, {}, {}, {}, {}
    shared = {}

    def g_copy(j):
        cols = pl.ds(pl.multiple_of(512 * j, 512), 512)
        return rcopy(g_out.at[:, cols], g_in.at[:, cols], g_send.at[0], g_recv.at[0], sibling)

    def gradient(t, first, last):
        @pl.loop(first, last)
        def _(j):
            for k in range(2):
                blocks = (2 * k, 2 * k + 1)
                both = jnp.concatenate([slab(gx, t, j, blocks), slab(ge, t, j, blocks)], axis=0)
                out = dot(tmat[t], both)
                half = slice(256 * k, 256 * (k + 1))
                cols = pl.ds(pl.multiple_of(512 * j + 256 * k, 256), 256)
                if t == 0:
                    gacc[j, :, half] = out[LAT:]
                    grad_ref[:, cols] = out[:LAT]
                else:
                    g_out[:, cols] = (gacc[j, :, half] + out[LAT:]).astype(BF16)
                    grad_ref[:, cols] = grad_ref[:, cols] + out[:LAT]
            if t == 1:
                g_copy(j).start()

    def steps(t):
        centered = (own_rows(t) - center).astype(BF16)
        log_x, log_r, log_e = [], [], []
        yield from gather(gx, t, centered, gx_send, gx_recv, log_x)
        if t == 0:
            all_weight_copies.wait_recv()
            small_copy.wait_recv()
            shared["bias"] = jnp.concatenate([sm[0:1, :], sm_in[0:1, :]], axis=1)
            shared["norms"] = jnp.concatenate([sm[1:2, :], sm_in[1:2, :]], axis=1)
        norms = shared["norms"]
        pre[t] = project(gx, t, 0) + shared["bias"]
        yield
        pre[t] = pre[t] + project(gx, t, 1)
        yield
        acts[t] = jnp.maximum(pre[t], 0.0).astype(BF16)

        @pl.loop(0, 8, unroll=4)
        def _(j):
            jz, jx = j // 4, lax.rem(j, 4)
            out = dot(acts[t, :CHUNK], all_weights(j))
            for yy in range(4):
                cols = slice(128 * yy, 128 * (yy + 1))
                part[t, 0, jx, yy, jz] = out[:MAIN, cols]
                part[t, 1, yy, jx, jz] = out[MAIN : 2 * MAIN, cols]
                if t == 0:
                    side[t, jz, jx, yy] = out[2 * MAIN :, cols]
                else:
                    side[t, jz, yy, jx] = out[2 * MAIN :, cols]

        ready = scatter(t, log_r)
        next(ready)
        flush(log_x)
        act = acts[t]
        act_own[t] = jnp.sum(act[:CHUNK].astype(F32), axis=0, keepdims=True)
        act_all[t] = act_own[t] + jnp.sum(act[CHUNK:].astype(F32), axis=0, keepdims=True)
        yield
        yield from ready
        err = result[t] + center - own_rows(t)
        sq[t] = jnp.sum(err * err)
        err_sum[t] = jnp.sum(err, axis=0, keepdims=True)
        derr = (2.0 / TOK * err).astype(BF16)
        ready = gather(ge, t, derr, ge_send, ge_recv, log_e)
        next(ready)
        flush(log_r)
        yield
        yield from ready
        sent.extend(log_e)
        dacc[t] = project(ge, t, 0) + sparsity_coeff / TOK * norms
        yield
        dacts = dacc[t] + project(ge, t, 1)
        dpre = jnp.where(pre[t] > 0, dacts, 0.0).astype(BF16)
        tmat[t] = jnp.concatenate([dpre, acts[t]], axis=0).T
        off_own[t] = jnp.sum(dpre[:CHUNK].astype(F32), axis=0, keepdims=True)
        off_all[t] = off_own[t] + jnp.sum(dpre[CHUNK:].astype(F32), axis=0, keepdims=True)
        yield
        if t == 0:
            gradient(0, 0, 4)
            yield
            gradient(0, 4, 8)
            yield

    run = [steps(0), steps(1)]
    plan = "0101010w01001010110101010101010001011"
    for who in plan:
        if who == "w":
            prepare()
        else:
            next(run[int(who)])
    for one in run:
        assert next(one, one) is one
    off = off_own[0] + off_own[1]
    offs = off_all[0] + off_all[1]
    act_tot = act_all[0] + act_all[1]
    spars = jnp.sum((act_own[0] + act_own[1]) * shared["norms"])

    sums[...] = jnp.zeros((2, 8, LAT), F32)
    for k in range(2):
        sums[k, 0:1, :] = offs[:, LAT * k : LAT * (k + 1)]
        sums[k, 1:2, :] = act_tot[:, LAT * k : LAT * (k + 1)]
    sums_copy = rcopy(sums.at[1], sums_in, pair_send.at[4], pair_recv.at[4], sibling)
    sums_copy.start()

    hi = off.astype(BF16)
    rest = off - hi.astype(F32)
    mid = rest.astype(BF16)
    low = (rest - mid.astype(F32)).astype(BF16)
    row = lax.broadcasted_iota(jnp.int32, (16, 512), 0)
    terms = jnp.where(
        row == 0, hi.astype(F32),
        jnp.where(row == 1, mid.astype(F32), jnp.where(row == 2, low.astype(F32), 0.0)),
    ).astype(BF16)
    for j in range(8):
        enc = jnp.sum(dot(terms, all_weights(j)), axis=0, keepdims=True)
        for yy in range(4):
            vx[(j % 4) * 4 + yy, j // 4 : j // 4 + 1, :] = -enc[:, 128 * yy : 128 * (yy + 1)]
    scalars = jnp.where(lane == 0, sq[0] + sq[1], jnp.where(lane == 1, spars, 0.0))
    for k in range(16):
        vx[k, 2:8, :] = jnp.broadcast_to(scalars, (6, 128))
    here = x * 4 + y
    sub = lax.broadcasted_iota(jnp.int32, (8, 128), 0)
    vx[here] = vx[here] + jnp.where(sub == zl, 2.0 / TOK * (err_sum[0] + err_sum[1]), 0.0)

    def v_plane(e):
        a, b = (e + 1) // 4, (e + 1) % 4
        return rcopy(
            vx.at[place["x", a] * 4 + place["y", b]], vx_in.at[e], v_send.at[0], v_recv.at[0], plane[e]
        )

    def v_column(e):
        return rcopy(vz, vz_in.at[e], v_send.at[1], v_recv.at[1], column[e])

    v_planes = rcopy(vx_in, vx_in, v_send.at[0], v_recv.at[0], sibling)
    v_columns = rcopy(vz_in, vz_in, v_send.at[1], v_recv.at[1], sibling)

    for e in range(15):
        v_plane(e).start()
    gradient(1, 0, 4)
    total = vx[here]
    v_planes.wait_recv()
    for e in range(15):
        total = total + vx_in[e]
    vz[...] = total
    for e in range(7):
        v_column(e).start()
    gradient(1, 4, 8)
    v_columns.wait_recv()
    for e in range(7):
        total = total + vz_in[e]
    sums_copy.wait_recv()

    small_ref[...] = jnp.zeros((8, LAT), F32)
    small_ref[0:1, :] = sums[0, 0:1, :] + sums_in[0:1, :]
    small_ref[1:2, :] = sparsity_coeff / TOK * (sums[0, 1:2, :] + sums_in[1:2, :]) / sm[1:2, :]
    slot = jnp.where(zl == 0, total[0:1], total[1:2])
    small_ref[2:3, 0:64] = jnp.where(core == 0, slot[:, :64], slot[:, 64:])
    small_ref[3:4, 0:128] = total[2:3]

    flush(sent)
    for c in pair + [all_weight_copies, small_copy, sums_copy]:
        c.wait_send()
    v_planes.wait_send()
    v_columns.wait_send()
    all_g_copies = rcopy(g_out, g_in, g_send.at[0], g_recv.at[0], sibling)
    all_g_copies.wait_recv()
    all_g_copies.wait_send()


def step_kernel(inputs, center, offset, dictionary):
    vm = pltpu.VMEM
    dma = pltpu.SemaphoreType.DMA
    block = (PART, 128)
    main, side = (MAIN, 128), (SIDE, 128)
    return pl.pallas_call(
        kernel,
        out_shape=[
            jax.ShapeDtypeStruct((LAT, WIDTH), F32),
            jax.ShapeDtypeStruct((LAT, WIDTH), BF16),
            jax.ShapeDtypeStruct((8, LAT), F32),
        ],
        in_specs=[pl.BlockSpec(memory_space=pltpu.HBM)] * 4,
        out_specs=[pl.BlockSpec(memory_space=pltpu.VMEM)] * 3,
        scratch_shapes=[
            vm((64, 2 * ROWS), BF16),
            vm((1, 64), F32),
            vm((1, LAT), F32),
            vm((2, 8, LAT, 512), BF16),
            vm((2, 3, 4, 4, 4) + block, BF16),
            vm((2, 3, 4, 4, 4) + block, BF16),
            vm((2, 2 * CHUNK, 512), F32),
            vm((2, 2 * CHUNK, 512), F32),
            vm((2, 2 * CHUNK, 512), BF16),
            vm((2, 512, 4 * CHUNK), BF16),
            vm((8, LAT, 512), F32),
            vm((2, ROWS, 128), BF16),
            vm((ROWS, 128), BF16),
            vm((8, 128), F32),
            vm((8, 128), F32),
            vm((8, LAT), F32),
            vm((8, LAT), F32),
            vm((2, 8, LAT), F32),
            vm((8, LAT), F32),
            vm((2, 2, 4, 4, 2) + main, F32),
            vm((2, 2, 2, 2, 2) + main, BF16),
            vm((2, 2, 2, 2, 2) + main, BF16),
            vm((2, 2, 2, 4, 2) + main, BF16),
            vm((2, 2, 2, 4, 2) + main, BF16),
            vm((2, 2, 7) + main, BF16),
            vm((2, 2, 7) + main, BF16),
            vm((2, 2, 4, 4) + side, F32),
            vm((2, 4, 4) + side, BF16),
            vm((2, 4, 4) + side, BF16),
            vm((2, 3, 4) + side, BF16),
            vm((2, 3, 4) + side, BF16),
            vm((2, 3) + side, BF16),
            vm((2, 3) + side, BF16),
            vm((LAT, WIDTH), BF16),
            vm((16, 8, 128), F32),
            vm((15, 8, 128), F32),
            vm((8, 128), F32),
            vm((7, 8, 128), F32),
            dma((11,)),
            dma((5,)),
            dma((5,)),
            dma((2, 3, 3)),
            dma((2, 3, 6)),
            dma((2, 3, 3)),
            dma((2, 3, 6)),
            dma((2, 3, 9)),
            dma((2, 3, 9)),
            dma((1,)),
            dma((1,)),
            dma((2,)),
            dma((2,)),
        ],
        compiler_params=pltpu.CompilerParams(
            collective_id=0, has_side_effects=True, vmem_limit_bytes=VMEM_LIMIT
        ),
        cost_estimate=pl.CostEstimate(
            flops=12 * 2**30, bytes_accessed=160 * 2**20, transcendentals=0
        ),
        name="step",
    )(*[pltpu.with_memory_space_constraint(v, pltpu.HBM) for v in (inputs, center, offset, dictionary)])


def small_kernel(small, offset, offset_mean, offset_var, center, center_mean, center_var, *outs):
    rows = (
        (offset, small[0:1, :], offset_mean, offset_var),
        (center, small[2:3, 0:64], center_mean, center_var),
    )
    for k, (param, grad, mean, var) in enumerate(rows):
        new = adam_update(param[...], grad, mean[...], var[...])
        for n in range(3):
            outs[3 * k + n][...] = new[n]
    scalars = small[3:4, 0:128]
    lane = lax.broadcasted_iota(jnp.int32, (1, 128), 1)
    weight = jnp.where(lane == 0, 1.0, jnp.where(lane == 1, sparsity_coeff, 0.0))
    outs[6][...] = jnp.sum(scalars * weight, axis=1, keepdims=True) / (TOK * WIDTH)


def small_step(small, *rows):
    shapes = [(1, LAT)] * 3 + [(1, 64)] * 3 + [(1, 1)]
    return pl.pallas_call(
        small_kernel,
        out_shape=[jax.ShapeDtypeStruct(s, F32) for s in shapes],
        in_specs=[pl.BlockSpec(memory_space=pltpu.VMEM)] * 7,
        out_specs=[pl.BlockSpec(memory_space=pltpu.VMEM)] * 7,
        compiler_params=pltpu.CompilerParams(vmem_limit_bytes=2**20),
        name="small",
    )(small, *[r.reshape(1, -1) for r in rows])


def body(
    inputs,
    dictionary,
    offset,
    center,
    dict_mean,
    dict_var,
    offset_mean,
    offset_var,
    center_mean,
    center_var,
):
    grad, shared, small = step_kernel(
        inputs.T, center.reshape(1, -1), offset.reshape(1, -1), dictionary
    )
    g_dict = grad + shared.astype(F32) + small[1][:, None] * dictionary
    fresh_dict, mean_dict, var_dict = adam_update(dictionary, g_dict, dict_mean, dict_var)
    *rows, loss = small_step(
        small, offset, offset_mean, offset_var, center, center_mean, center_var
    )
    fresh_offset, mean_offset, var_offset, fresh_center, mean_center, var_center = [
        r.reshape(-1) for r in rows
    ]
    loss_value = loss.reshape(())
    return (
        fresh_dict,
        fresh_offset,
        fresh_center,
        mean_dict,
        var_dict,
        mean_offset,
        var_offset,
        mean_center,
        var_center,
        loss_value,
    )


def solution(mesh):
    return jax.shard_map(
        body,
        mesh=mesh,
        in_specs=(
            P("dp", "latent"),
            P("latent", None),
            P("latent"),
            P("latent"),
            P("latent", None),
            P("latent", None),
            P("latent"),
            P("latent"),
            P("latent"),
            P("latent"),
        ),
        out_specs=(
            P("latent", None),
            P("latent"),
            P("latent"),
            P("latent", None),
            P("latent", None),
            P("latent"),
            P("latent"),
            P("latent"),
            P("latent"),
            P(),
        ),
        check_vma=False,
    )
```
